32 devices in a mesh: chan: 8 (over y, x, core), tm: 4 (over z).
Axes of the slice: x: 2, y: 2, z: 4, core: 2. Of those that a mesh axis runs over, the one named last changes fastest.
Arguments:
- spectra: bfloat16 [2, 32, 2048, 128], P(None, 'tm', 'chan'), may hold values from -150 to 150
- quality: int32 [32, 128], P('tm'), may hold values 0 or 1
- offsets: int32 [4], replicated, may hold values from 1 to 4, as said below
Outputs:
- gathers: float32 [128, 4, 256], P('chan')
The draws below stay inside these ranges and needn't reach their ends.
Inputs may be any that keep to these rules, and one draw needn't show every extreme that they name: `offsets`: each offset lies from 1 to 4, and one of them equals 4.
All inputs are finite; a program needn't handle non-finite values. No bound on the sum of `quality` on one device may be relied on, other than what follows from the above.
Results may differ from the reference program's by a relative error of at most 0.0003.
Values may be sent and summed in bfloat16 or wider, within the bound.
No kernel may reach another device: no remote copies, remote signals or barrier semaphores. Data moves between devices by JAX's collectives and lax.ppermute only.
A program may use at most 64 MiB of HBM per device.

```python
import math
import jax
import jax.numpy as jnp
from jax import lax

F = 2048
LAGS = 256
NOFF = 4
CH_DEV = 16
NCH = 128
WINDOWS = 32
N_CHAN = 8


def draw_offsets(key, part):
    half_count = N_CHAN // 2
    others = jax.random.randint(jax.random.fold_in(key, 11), (NOFF - 1,), 1, half_count + 1).astype(jnp.int32)
    values = jnp.concatenate([jnp.full((1,), half_count, dtype=jnp.int32), others])
    return jax.random.permutation(jax.random.fold_in(key, 12), values)


def draw_spectra(key, part):
    subkeys = [jax.random.fold_in(key, 21 + number) for number in range(6)]
    chan_pos = jnp.arange(NCH, dtype=jnp.float32)
    freq_pos = jnp.arange(F, dtype=jnp.float32)
    chan_gain = jnp.exp(jax.random.uniform(subkeys[0], (NCH,), minval=0.0, maxval=math.log(10.0)))
    rough_gain = jnp.exp(jax.random.uniform(subkeys[1], (F,), minval=-0.7, maxval=0.7))
    tilt_rate = math.log(3.0)
    noise_part = jax.random.normal(subkeys[4], (2, WINDOWS, F, NCH))
    freq_gain = jnp.exp(tilt_rate * freq_pos / F) * rough_gain
    slowness = jax.random.uniform(subkeys[2], (), minval=0.02, maxval=0.1)
    phase = math.pi * freq_pos[:, None] * (chan_pos[None, :] * slowness) / F
    cosine = jnp.cos(phase)
    sine = jnp.sin(phase)
    source = jax.random.normal(subkeys[3], (2, WINDOWS, F, 1))
    coherent = jnp.stack([source[0] * cosine - source[1] * sine, source[0] * sine + source[1] * cosine])
    values = (coherent + noise_part) * freq_gain[None, None, :, None] * chan_gain[None, None, None, :]
    return jnp.clip(values, -150.0, 150.0).astype(jnp.bfloat16)


def plant(drawn, rng, smallest, top_value):
    dims = drawn.shape
    spot = [jax.random.randint(jax.random.fold_in(rng, axis), (), 0, dims[axis]) for axis in range(len(dims))]
    drawn = drawn.at[tuple(spot)].set(smallest)
    longest = dims.index(max(dims))
    spot[longest] = (spot[longest] + 1) % dims[longest]
    return drawn.at[tuple(spot)].set(top_value)


def setup_inputs(seed: int = 0) -> dict:
    streams_of = jax.random.split(jax.random.key(seed), 4)
    return {
        "spectra": draw_spectra(jax.random.fold_in(streams_of[3], 71), 0),
        "quality": plant((jax.random.randint(streams_of[1], (WINDOWS, NCH), 0, 8) < 7).astype(jnp.int32), jax.random.fold_in(streams_of[1], 1), 0, 1),
        "offsets": draw_offsets(jax.random.fold_in(streams_of[3], 71), 0),
    }


def lag_table(freq_count, lag_count):
    freq_index = jnp.arange(freq_count, dtype=jnp.int32)[:, None]
    double_lag = (2 * jnp.arange(lag_count, dtype=jnp.int32) - lag_count + 1)[None, :]
    turns = jnp.mod(freq_index * double_lag, 4 * freq_count)
    angles = turns.astype(jnp.float32) * (2.0 * math.pi / (4 * freq_count))
    cosine = jnp.cos(angles)
    sine = jnp.sin(angles)
    upper = jnp.concatenate([cosine, sine], axis=1)
    lower = jnp.concatenate([-sine, cosine], axis=1)
    return jnp.stack([upper, lower]).astype(jnp.bfloat16)

def whiten_parts(real_part, imag_part, magnitude, channel_level, usable):
    factor = usable.astype(jnp.float32)[:, None, :] / (magnitude + 0.5 * (channel_level + 1e-05))
    return jnp.stack([real_part * factor, imag_part * factor]).astype(jnp.bfloat16)

def cross_parts(own_real, own_imag, far_real, far_imag):
    own_real = own_real.astype(jnp.float32)
    own_imag = own_imag.astype(jnp.float32)
    far_real = far_real.astype(jnp.float32)
    far_imag = far_imag.astype(jnp.float32)
    return jnp.stack([own_real * far_real + own_imag * far_imag, own_imag * far_real - own_real * far_imag]).astype(jnp.bfloat16)

def pair_terms(corr_all):
    lag_count = corr_all.shape[-1] // 2
    real_corr = corr_all[..., :lag_count]
    imag_corr = corr_all[..., lag_count:]
    power = real_corr * real_corr + imag_corr * imag_corr
    mean_power = lax.optimization_barrier(jnp.mean(power, axis=-1, keepdims=True))
    denominator = jnp.sqrt(power + 0.25 * (mean_power + 1e-06))
    return (lax.optimization_barrier(jnp.sum(real_corr, axis=-3)), lax.optimization_barrier(jnp.sum(real_corr / denominator, axis=-3)), lax.optimization_barrier(jnp.sum(imag_corr / denominator, axis=-3)))

def reference(spectra, quality, offsets):
    real_part = spectra[0].astype(jnp.float32)
    imag_part = spectra[1].astype(jnp.float32)
    magnitude = jnp.sqrt(real_part * real_part + imag_part * imag_part)
    channel_level = lax.optimization_barrier(jnp.sum(magnitude, axis=1, keepdims=True)) / F
    whitened = whiten_parts(real_part, imag_part, magnitude, channel_level, quality)
    padded = jnp.pad(whitened, ((0, 0), (0, 0), (0, 0), (0, NCH)))
    table_wide = lag_table(F, LAGS).astype(jnp.float32)
    inv_root = 1.0 / math.sqrt(F)
    per_offset = []
    for offset_index in range(NOFF):
        shift_cells = (offsets[offset_index] * CH_DEV).astype(jnp.int32)

        def one_block(block, shift_cells=shift_cells):
            start = (block * CH_DEV).astype(jnp.int32)
            own = lax.dynamic_slice_in_dim(whitened, start, CH_DEV, 3)
            partner = lax.dynamic_slice_in_dim(padded, (start + shift_cells).astype(jnp.int32), CH_DEV, 3)
            crossed = cross_parts(own[0], own[1], partner[0], partner[1])
            corr_all = jnp.einsum('cwfh,cfl->whl', crossed.astype(jnp.float32), table_wide) * inv_root
            linear, real_phase, imag_phase = pair_terms(corr_all)
            linear = linear / WINDOWS
            real_phase = real_phase / WINDOWS
            imag_phase = imag_phase / WINDOWS
            return linear * (real_phase * real_phase + imag_phase * imag_phase)
        blocks = lax.map(one_block, jnp.arange(N_CHAN, dtype=jnp.int32))
        per_offset.append(blocks.reshape(NCH, LAGS))
    stacks = jnp.stack(per_offset, axis=1)
    shifted = jnp.pad(stacks, ((NCH, 0), (0, 0), (0, 0)))
    reverse_list = []
    for offset_index in range(NOFF):
        start = (NCH - offsets[offset_index] * CH_DEV).astype(jnp.int32)
        piece = lax.dynamic_slice_in_dim(shifted[:, offset_index], start, NCH, 0)
        reverse_list.append(jnp.flip(piece, axis=1))
    return stacks + jnp.stack(reverse_list, axis=1)
```

```python
import functools
import math

import jax
import jax.numpy as jnp
import numpy as np
from jax import lax
from jax.experimental import pallas as pl
from jax.experimental.pallas import tpu as pltpu
from jax.sharding import PartitionSpec as P

F = 2048
LAGS = 256
NOFF = 4
CH_DEV = 16
W_DEV = 8
VMEM_LIMIT = 48 * 1024 * 1024


def half_table(freq_count, lag_count):
    freq_index = np.arange(freq_count, dtype=np.int64)[None, :]
    double_lag = (2 * np.arange(lag_count // 2, lag_count, dtype=np.int64) - lag_count + 1)[:, None]
    turns = np.mod(freq_index * double_lag, 4 * freq_count).astype(np.float32)
    angles = turns * np.float32(2.0 * math.pi / (4 * freq_count))
    return np.concatenate([np.cos(angles), np.sin(angles)]).astype(jnp.bfloat16)


def window_kernel(offs_ref, where_ref, spec_ref, qual_ref, table_ref, out_ref, mag_ref, white_ref, cross_ref):
    sources, _, band, chans = spec_ref.shape
    freqs = sources * band
    groups, offset_count, _, lag_rows, _ = out_ref.shape
    half = groups * lag_rows
    step = 64

    def magnitudes(index, total):
        source, row = index // (band // step), index % (band // step) * step
        rows = pl.ds(pl.multiple_of(row, step), step)
        real = spec_ref[source, 0, rows, :].astype(jnp.float32)
        imag = spec_ref[source, 1, rows, :].astype(jnp.float32)
        magnitude = jnp.sqrt(real * real + imag * imag)
        mag_ref[pl.ds(pl.multiple_of(index * step, step), step), :] = magnitude
        return total + jnp.sum(magnitude.reshape(step // 8, 8, chans), axis=0)

    total = lax.fori_loop(0, freqs // step, magnitudes, jnp.zeros((8, chans), jnp.float32), unroll=4)
    level = jnp.sum(total, axis=0, keepdims=True) / freqs
    floor = 0.5 * (level + 1e-05)
    usable = qual_ref[pl.ds(where_ref[0], 1), :].astype(jnp.float32)

    def whiten(index, carry):
        source, row = index // (band // step), index % (band // step) * step
        rows = pl.ds(pl.multiple_of(row, step), step)
        held = pl.ds(pl.multiple_of(index * step, step), step)
        factor = usable / (mag_ref[held, :] + floor)
        for part in range(2):
            value = spec_ref[source, part, rows, :].astype(jnp.float32) * factor
            white_ref[part, held, :] = value.astype(jnp.bfloat16).astype(jnp.float32)
        return carry

    lax.fori_loop(0, freqs // step, whiten, 0, unroll=4)

    lane = lax.broadcasted_iota(jnp.int32, (1, chans), 1)
    scale = 1.0 / math.sqrt(freqs)
    for number in range(offset_count):
        ahead = offs_ref[number] * (chans // groups)
        turn = chans - ahead

        def cross(index, carry):
            held = pl.ds(pl.multiple_of(index * step, step), step)
            own_real, own_imag = white_ref[0, held, :], white_ref[1, held, :]
            far_real = pltpu.roll(own_real, turn, 1)
            far_imag = pltpu.roll(own_imag, turn, 1)
            cross_ref[held, pl.ds(0, chans)] = (own_real * far_real + own_imag * far_imag).astype(jnp.bfloat16)
            cross_ref[held, pl.ds(chans, chans)] = (own_imag * far_real - own_real * far_imag).astype(jnp.bfloat16)
            return carry

        lax.fori_loop(0, freqs // step, cross, 0, unroll=4)
        sums = jnp.dot(table_ref[...], cross_ref[...], preferred_element_type=jnp.float32)
        keep = jnp.where(lane < turn, scale, 0.0)
        cos_real, sin_real = sums[:half, :chans] * keep, sums[half:, :chans] * keep
        cos_imag, sin_imag = sums[:half, chans:] * keep, sums[half:, chans:] * keep
        corr = (
            (cos_real - sin_imag, sin_real + cos_imag),
            (cos_real + sin_imag, cos_imag - sin_real),
        )
        power = [real * real + imag * imag for real, imag in corr]
        mean_power = (jnp.sum(power[0], axis=0, keepdims=True) + jnp.sum(power[1], axis=0, keepdims=True)) / (2 * half)
        extra = 0.25 * (mean_power + 1e-06)
        for side in range(2):
            inverse = 1.0 / jnp.sqrt(power[side] + extra)
            real, imag = corr[side]
            for kind, value in enumerate((real, real * inverse, imag * inverse)):
                out_ref[:, number, 2 * kind + side, :, :] = value.reshape(groups, lag_rows, chans)


def stack_kernel(offs_ref, where_ref, sums_ref, out_ref, *, windows):
    blocks, copies, _, _ = out_ref.shape
    _, _, lag_rows, chans = sums_ref.shape
    total = jnp.sum(sums_ref[...], axis=0) / windows
    stacks = [
        total[side] * (total[2 + side] * total[2 + side] + total[4 + side] * total[4 + side]) for side in range(2)
    ]
    ahead = offs_ref[where_ref[0]] * (chans // blocks)
    lane = lax.broadcasted_iota(jnp.int32, (1, chans), 1)
    behind = [jnp.where(lane >= ahead, pltpu.roll(stack, ahead, 1), 0.0) for stack in stacks]
    both = jnp.concatenate([stacks[0] + behind[1], stacks[1] + behind[0]], axis=0)
    wide = 2 * lag_rows
    turned = jnp.concatenate([both] * (chans // wide), axis=0).T
    per_block = chans // blocks
    rows = per_block // 2
    for block in range(blocks):
        first = turned[block * per_block : block * per_block + rows, :]
        second = turned[block * per_block + rows : (block + 1) * per_block, :]
        piece = jnp.where(lane < wide, first, second)
        for copy in range(copies):
            out_ref[block, copy, :, :] = piece


def place_kernel(parts_ref, out_ref):
    groups, offset_count, rows, lanes = parts_ref.shape
    half = out_ref.shape[2] // 2
    lag_rows = half // groups
    lane = lax.broadcasted_iota(jnp.int32, (1, lanes), 1)
    mirror = (
        lax.broadcasted_iota(jnp.int32, (half, half), 0) + lax.broadcasted_iota(jnp.int32, (half, half), 1) == half - 1
    ).astype(jnp.float32)
    for number in range(offset_count):
        for part in range(2):
            ahead = jnp.zeros((rows, lanes), jnp.float32)
            back = jnp.zeros((rows, lanes), jnp.float32)
            for group in range(groups):
                piece = parts_ref[group, number]
                here = (lane >= group * lag_rows) & (lane < (group + 1) * lag_rows)
                begin = part * 2 * lag_rows
                ahead = jnp.where(here, pltpu.roll(piece, (group * lag_rows - begin) % lanes, 1), ahead)
                back = jnp.where(here, pltpu.roll(piece, (group * lag_rows - begin - lag_rows) % lanes, 1), back)
            back = jnp.dot(back, mirror, precision=lax.Precision.HIGHEST, preferred_element_type=jnp.float32)
            out_ref[part * rows : (part + 1) * rows, number, 0:half] = back
            out_ref[part * rows : (part + 1) * rows, number, half : 2 * half] = ahead


def window_shards(spectra, quality, offsets):
    chan_count = lax.axis_size("chan")
    tm_count = lax.axis_size("tm")
    _, windows, band, chans = spectra.shape
    freqs = band * chan_count
    half = LAGS // 2
    lag_rows = half // chan_count
    offset_count = offsets.shape[0]
    smem = pl.BlockSpec(memory_space=pltpu.SMEM)
    vmem = pl.BlockSpec(memory_space=pltpu.VMEM)
    params = pltpu.CompilerParams(vmem_limit_bytes=VMEM_LIMIT)
    table = jnp.asarray(half_table(freqs, LAGS))
    chan_index = lax.axis_index("chan").astype(jnp.int32).reshape(1)
    tm_index = lax.axis_index("tm").astype(jnp.int32).reshape(1)

    by_window = lax.all_to_all(jnp.transpose(spectra, (1, 0, 2, 3)), "chan", 0, 0, tiled=True)
    pairs = pl.pallas_call(
        window_kernel,
        out_shape=jax.ShapeDtypeStruct((chan_count, offset_count, 6, lag_rows, chans), jnp.float32),
        in_specs=[smem, smem, vmem, vmem, vmem],
        out_specs=vmem,
        scratch_shapes=[
            pltpu.VMEM((freqs, chans), jnp.float32),
            pltpu.VMEM((2, freqs, chans), jnp.float32),
            pltpu.VMEM((freqs, 2 * chans), jnp.bfloat16),
        ],
        compiler_params=params,
        name="window_pairs",
    )(offsets, chan_index, by_window, quality, table)
    by_lag = jnp.sum(lax.all_to_all(pairs, "chan", 0, 0, tiled=True), axis=0)
    by_offset = lax.all_to_all(by_lag, "tm", 0, 0, tiled=True)
    pieces = pl.pallas_call(
        functools.partial(stack_kernel, windows=windows * tm_count),
        out_shape=jax.ShapeDtypeStruct((chan_count, tm_count, CH_DEV // 2, chans), jnp.float32),
        in_specs=[smem, smem, vmem],
        out_specs=vmem,
        compiler_params=params,
        name="stack_pairs",
    )(offsets, tm_index, by_offset)
    shape = (chan_count * tm_count, CH_DEV // 2, chans)
    arrived = lax.all_to_all(pieces.reshape(shape), ("chan", "tm"), 0, 0, tiled=True)
    return pl.pallas_call(
        place_kernel,
        out_shape=jax.ShapeDtypeStruct((CH_DEV, offset_count, LAGS), jnp.float32),
        in_specs=[vmem],
        out_specs=vmem,
        compiler_params=params,
        name="place_lags",
    )(arrived.reshape(chan_count, tm_count, CH_DEV // 2, chans))


def shifted(value, axis, steps):
    count = lax.axis_size(axis)
    leading, last = (max(0, -steps), min(count, count - steps))
    return lax.ppermute(value, axis, [(source, source + steps) for source in range(leading, last)])


def lag_table(freq_count, lag_count):
    freq_index = jnp.arange(freq_count, dtype=jnp.int32)[:, None]
    double_lag = (2 * jnp.arange(lag_count, dtype=jnp.int32) - lag_count + 1)[None, :]
    turns = jnp.mod(freq_index * double_lag, 4 * freq_count)
    angles = turns.astype(jnp.float32) * (2.0 * math.pi / (4 * freq_count))
    cosine = jnp.cos(angles)
    sine = jnp.sin(angles)
    upper = jnp.concatenate([cosine, sine], axis=1)
    lower = jnp.concatenate([-sine, cosine], axis=1)
    return jnp.stack([upper, lower]).astype(jnp.bfloat16)


def whiten_parts(real_part, imag_part, magnitude, channel_level, usable):
    factor = usable.astype(jnp.float32)[:, None, :] / (magnitude + 0.5 * (channel_level + 1e-05))
    return jnp.stack([real_part * factor, imag_part * factor]).astype(jnp.bfloat16)


def cross_parts(own_real, own_imag, far_real, far_imag):
    own_real = own_real.astype(jnp.float32)
    own_imag = own_imag.astype(jnp.float32)
    far_real = far_real.astype(jnp.float32)
    far_imag = far_imag.astype(jnp.float32)
    return jnp.stack(
        [own_real * far_real + own_imag * far_imag, own_imag * far_real - own_real * far_imag]
    ).astype(jnp.bfloat16)


def pair_terms(corr_all):
    lag_count = corr_all.shape[-1] // 2
    real_corr = corr_all[..., :lag_count]
    imag_corr = corr_all[..., lag_count:]
    power = real_corr * real_corr + imag_corr * imag_corr
    mean_power = jnp.mean(power, axis=-1, keepdims=True)
    denominator = jnp.sqrt(power + 0.25 * (mean_power + 1e-06))
    return (
        jnp.sum(real_corr, axis=-3),
        jnp.sum(real_corr / denominator, axis=-3),
        jnp.sum(imag_corr / denominator, axis=-3),
    )


def shards(spectra, quality, offsets):
    chan_count = lax.axis_size("chan")
    tm_count = lax.axis_size("tm")
    levels = chan_count.bit_length() - 1
    table_bf = lag_table(F, LAGS)
    inv_root = 1.0 / math.sqrt(F)
    real_part = spectra[0].astype(jnp.float32)
    imag_part = spectra[1].astype(jnp.float32)
    magnitude = jnp.sqrt(real_part * real_part + imag_part * imag_part)
    band_total = lax.psum(jnp.sum(magnitude, axis=1), "chan")
    channel_level = (band_total / F)[:, None, :]
    whitened = whiten_parts(real_part, imag_part, magnitude, channel_level, quality)
    width_all = whitened.shape[3]
    padded = jnp.pad(whitened, ((0, 0), (0, 0), (0, 0), (0, width_all)))
    crossed_list = []
    for offset_index in range(NOFF):
        partner = lax.dynamic_slice_in_dim(padded, offsets[offset_index] * CH_DEV, width_all, 3)
        crossed_list.append(cross_parts(whitened[0], whitened[1], partner[0], partner[1]))
    crossed = jnp.stack(crossed_list, axis=1)
    corr_all = jnp.einsum(
        "cnwfh,cfl->nwhl",
        lax.all_to_all(crossed, "chan", split_axis=4, concat_axis=3, tiled=True),
        table_bf,
        preferred_element_type=jnp.float32,
    )
    linear_sum, real_sum, imag_sum = pair_terms(corr_all * inv_root)
    totals = lax.psum((linear_sum, real_sum, imag_sum), "tm")
    window_count = W_DEV * tm_count
    linear = totals[0] / window_count
    real_phase = totals[1] / window_count
    imag_phase = totals[2] / window_count
    stacks = jnp.transpose(linear * (real_phase * real_phase + imag_phase * imag_phase), (1, 0, 2))
    reverse_part = stacks
    for bit_index in range(levels):
        step_size = 1 << bit_index
        arrived = shifted(reverse_part, "chan", step_size)
        chosen = offsets // step_size % 2 == 1
        reverse_part = jnp.where(chosen[None, :, None], arrived, reverse_part)
    return stacks + jnp.flip(reverse_part, axis=2)


def solution(mesh):
    chan_count, tm_count = mesh.shape["chan"], mesh.shape["tm"]
    by_window = chan_count == W_DEV and tm_count == NOFF
    return jax.shard_map(
        window_shards if by_window else shards,
        mesh=mesh,
        in_specs=(P(None, "tm", "chan", None), P("tm", None), P()),
        out_specs=P("chan", None, None),
        check_vma=False,
    )
```

```python
import functools
import math

import jax
import jax.numpy as jnp
import numpy as np
from jax import lax
from jax.experimental import pallas as pl
from jax.experimental.pallas import tpu as pltpu
from jax.sharding import PartitionSpec as P

F = 2048
LAGS = 256
NOFF = 4
CH_DEV = 16
W_DEV = 8
VMEM_LIMIT = 48 * 1024 * 1024
CODE_TOP = 32767.0
OCTAVE = 256.0
LOWEST = -110.0


def encode(value):
    return jnp.round(value * CODE_TOP).astype(jnp.int32).astype(jnp.int16)


def decode(code):
    return code.astype(jnp.int32).astype(jnp.float32)


def level_code(peak):
    return jnp.ceil(jnp.maximum(jnp.log2(jnp.maximum(peak, 1e-30)), LOWEST) * OCTAVE) + 1.0


def level_of(code):
    return jnp.exp2(code * (1.0 / OCTAVE))


def half_table(freq_count, lag_count):
    freq_index = np.arange(freq_count, dtype=np.int64)[None, :]
    double_lag = (2 * np.arange(lag_count // 2, lag_count, dtype=np.int64) - lag_count + 1)[:, None]
    turns = np.mod(freq_index * double_lag, 4 * freq_count).astype(np.float32)
    angles = turns * np.float32(2.0 * math.pi / (4 * freq_count))
    return np.concatenate([np.cos(angles), np.sin(angles)]).astype(jnp.bfloat16)


def window_kernel(offs_ref, where_ref, spec_ref, qual_ref, table_ref, out_ref, mag_ref, white_ref, cross_ref):
    sources, _, band, chans = spec_ref.shape
    freqs = sources * band
    groups, blocks, lag_rows, _ = out_ref.shape
    offset_count = offs_ref.shape[0]
    half = groups * lag_rows
    step = 64

    def magnitudes(index, total):
        source, row = index // (band // step), index % (band // step) * step
        rows = pl.ds(pl.multiple_of(row, step), step)
        real = spec_ref[source, 0, rows, :].astype(jnp.float32)
        imag = spec_ref[source, 1, rows, :].astype(jnp.float32)
        magnitude = jnp.sqrt(real * real + imag * imag)
        mag_ref[pl.ds(pl.multiple_of(index * step, step), step), :] = magnitude
        return total + jnp.sum(magnitude.reshape(step // 8, 8, chans), axis=0)

    total = lax.fori_loop(0, freqs // step, magnitudes, jnp.zeros((8, chans), jnp.float32), unroll=4)
    level = jnp.sum(total, axis=0, keepdims=True) / freqs
    floor = 0.5 * (level + 1e-05)
    usable = qual_ref[pl.ds(where_ref[0], 1), :].astype(jnp.float32)

    def whiten(index, carry):
        source, row = index // (band // step), index % (band // step) * step
        rows = pl.ds(pl.multiple_of(row, step), step)
        held = pl.ds(pl.multiple_of(index * step, step), step)
        factor = usable / (mag_ref[held, :] + floor)
        for part in range(2):
            value = spec_ref[source, part, rows, :].astype(jnp.float32) * factor
            white_ref[part, held, :] = value.astype(jnp.bfloat16).astype(jnp.float32)
        return carry

    lax.fori_loop(0, freqs // step, whiten, 0, unroll=4)

    lane = lax.broadcasted_iota(jnp.int32, (1, chans), 1)
    row = lax.broadcasted_iota(jnp.int32, (lag_rows, chans), 0)
    levels = jnp.zeros((lag_rows, chans), jnp.float32)
    scale = 1.0 / math.sqrt(freqs)
    for number in range(offset_count):
        ahead = offs_ref[number] * (chans // groups)
        turn = chans - ahead

        def cross(index, carry):
            held = pl.ds(pl.multiple_of(index * step, step), step)
            own_real, own_imag = white_ref[0, held, :], white_ref[1, held, :]
            far_real = pltpu.roll(own_real, turn, 1)
            far_imag = pltpu.roll(own_imag, turn, 1)
            cross_ref[held, pl.ds(0, chans)] = (own_real * far_real + own_imag * far_imag).astype(jnp.bfloat16)
            cross_ref[held, pl.ds(chans, chans)] = (own_imag * far_real - own_real * far_imag).astype(jnp.bfloat16)
            return carry

        lax.fori_loop(0, freqs // step, cross, 0, unroll=4)
        sums = jnp.dot(table_ref[...], cross_ref[...], preferred_element_type=jnp.float32)
        keep = jnp.where(lane < turn, scale, 0.0)
        cos_real, sin_real = sums[:half, :chans] * keep, sums[half:, :chans] * keep
        cos_imag, sin_imag = sums[:half, chans:] * keep, sums[half:, chans:] * keep
        corr = (
            (cos_real - sin_imag, sin_real + cos_imag),
            (cos_real + sin_imag, cos_imag - sin_real),
        )
        power = [real * real + imag * imag for real, imag in corr]
        mean_power = (jnp.sum(power[0], axis=0, keepdims=True) + jnp.sum(power[1], axis=0, keepdims=True)) / (2 * half)
        extra = 0.25 * (mean_power + 1e-06)
        peak = jnp.max(jnp.maximum(jnp.abs(corr[0][0]), jnp.abs(corr[1][0])), axis=0, keepdims=True)
        code = level_code(peak)
        levels = jnp.where(row == number, code, levels)
        upscale = 1.0 / level_of(code)
        for side in range(2):
            inverse = 1.0 / jnp.sqrt(power[side] + extra)
            real, imag = corr[side]
            for kind, value in enumerate((real * upscale, real * inverse, imag * inverse)):
                out_ref[:, 6 * number + 2 * kind + side, :, :] = encode(value).reshape(groups, lag_rows, chans)
    for group in range(groups):
        out_ref[group, blocks - 1, :, :] = levels.astype(jnp.int32).astype(jnp.int16)


def sum_kernel(codes_ref, out_ref):
    sources, blocks, _, _ = codes_ref.shape
    offset_count = out_ref.shape[0]
    levels = [level_of(decode(codes_ref[source, blocks - 1])) / CODE_TOP for source in range(sources)]
    for number in range(offset_count):
        for block in range(6):
            total = 0.0
            for source in range(sources):
                value = decode(codes_ref[source, 6 * number + block])
                total += value * levels[source][number : number + 1, :] if block < 2 else value
            out_ref[number, block, :, :] = total if block < 2 else total / CODE_TOP


def stack_kernel(offs_ref, where_ref, sums_ref, out_ref, *, windows):
    blocks, copies, _, _ = out_ref.shape
    _, _, lag_rows, chans = sums_ref.shape
    total = jnp.sum(sums_ref[...], axis=0) / windows
    stacks = [
        total[side] * (total[2 + side] * total[2 + side] + total[4 + side] * total[4 + side]) for side in range(2)
    ]
    ahead = offs_ref[where_ref[0]] * (chans // blocks)
    lane = lax.broadcasted_iota(jnp.int32, (1, chans), 1)
    behind = [jnp.where(lane >= ahead, pltpu.roll(stack, ahead, 1), 0.0) for stack in stacks]
    both = jnp.concatenate([stacks[0] + behind[1], stacks[1] + behind[0]], axis=0)
    wide = 2 * lag_rows
    turned = jnp.concatenate([both] * (chans // wide), axis=0).T
    per_block = chans // blocks
    rows = per_block // 2
    for block in range(blocks):
        first = turned[block * per_block : block * per_block + rows, :]
        second = turned[block * per_block + rows : (block + 1) * per_block, :]
        piece = jnp.where(lane < wide, first, second)
        for copy in range(copies):
            out_ref[block, copy, :, :] = piece


def place_kernel(parts_ref, out_ref):
    groups, offset_count, rows, lanes = parts_ref.shape
    half = out_ref.shape[2] // 2
    lag_rows = half // groups
    lane = lax.broadcasted_iota(jnp.int32, (1, lanes), 1)
    mirror = (
        lax.broadcasted_iota(jnp.int32, (half, half), 0) + lax.broadcasted_iota(jnp.int32, (half, half), 1) == half - 1
    ).astype(jnp.float32)
    for number in range(offset_count):
        for part in range(2):
            ahead = jnp.zeros((rows, lanes), jnp.float32)
            back = jnp.zeros((rows, lanes), jnp.float32)
            for group in range(groups):
                piece = parts_ref[group, number]
                here = (lane >= group * lag_rows) & (lane < (group + 1) * lag_rows)
                begin = part * 2 * lag_rows
                ahead = jnp.where(here, pltpu.roll(piece, (group * lag_rows - begin) % lanes, 1), ahead)
                back = jnp.where(here, pltpu.roll(piece, (group * lag_rows - begin - lag_rows) % lanes, 1), back)
            back = jnp.dot(back, mirror, precision=lax.Precision.HIGHEST, preferred_element_type=jnp.float32)
            out_ref[part * rows : (part + 1) * rows, number, 0:half] = back
            out_ref[part * rows : (part + 1) * rows, number, half : 2 * half] = ahead


def window_shards(spectra, quality, offsets):
    chan_count = lax.axis_size("chan")
    tm_count = lax.axis_size("tm")
    _, windows, band, chans = spectra.shape
    freqs = band * chan_count
    half = LAGS // 2
    lag_rows = half // chan_count
    offset_count = offsets.shape[0]
    smem = pl.BlockSpec(memory_space=pltpu.SMEM)
    vmem = pl.BlockSpec(memory_space=pltpu.VMEM)
    params = pltpu.CompilerParams(vmem_limit_bytes=VMEM_LIMIT)
    table = jnp.asarray(half_table(freqs, LAGS))
    chan_index = lax.axis_index("chan").astype(jnp.int32).reshape(1)
    tm_index = lax.axis_index("tm").astype(jnp.int32).reshape(1)

    by_window = lax.all_to_all(jnp.transpose(spectra, (1, 0, 2, 3)), "chan", 0, 0, tiled=True)
    pairs = pl.pallas_call(
        window_kernel,
        out_shape=jax.ShapeDtypeStruct((chan_count, 6 * offset_count + 1, lag_rows, chans), jnp.int16),
        in_specs=[smem, smem, vmem, vmem, vmem],
        out_specs=vmem,
        scratch_shapes=[
            pltpu.VMEM((freqs, chans), jnp.float32),
            pltpu.VMEM((2, freqs, chans), jnp.float32),
            pltpu.VMEM((freqs, 2 * chans), jnp.bfloat16),
        ],
        compiler_params=params,
        name="window_pairs",
    )(offsets, chan_index, by_window, quality, table)
    by_lag = pl.pallas_call(
        sum_kernel,
        out_shape=jax.ShapeDtypeStruct((offset_count, 6, lag_rows, chans), jnp.float32),
        in_specs=[vmem],
        out_specs=vmem,
        compiler_params=params,
        name="sum_windows",
    )(lax.all_to_all(pairs, "chan", 0, 0, tiled=True))
    by_offset = lax.all_to_all(by_lag, "tm", 0, 0, tiled=True)
    pieces = pl.pallas_call(
        functools.partial(stack_kernel, windows=windows * tm_count),
        out_shape=jax.ShapeDtypeStruct((chan_count, tm_count, CH_DEV // 2, chans), jnp.float32),
        in_specs=[smem, smem, vmem],
        out_specs=vmem,
        compiler_params=params,
        name="stack_pairs",
    )(offsets, tm_index, by_offset)
    shape = (chan_count * tm_count, CH_DEV // 2, chans)
    arrived = lax.all_to_all(pieces.reshape(shape), ("chan", "tm"), 0, 0, tiled=True)
    return pl.pallas_call(
        place_kernel,
        out_shape=jax.ShapeDtypeStruct((CH_DEV, offset_count, LAGS), jnp.float32),
        in_specs=[vmem],
        out_specs=vmem,
        compiler_params=params,
        name="place_lags",
    )(arrived.reshape(chan_count, tm_count, CH_DEV // 2, chans))


def shifted(value, axis, steps):
    count = lax.axis_size(axis)
    leading, last = (max(0, -steps), min(count, count - steps))
    return lax.ppermute(value, axis, [(source, source + steps) for source in range(leading, last)])


def lag_table(freq_count, lag_count):
    freq_index = jnp.arange(freq_count, dtype=jnp.int32)[:, None]
    double_lag = (2 * jnp.arange(lag_count, dtype=jnp.int32) - lag_count + 1)[None, :]
    turns = jnp.mod(freq_index * double_lag, 4 * freq_count)
    angles = turns.astype(jnp.float32) * (2.0 * math.pi / (4 * freq_count))
    cosine = jnp.cos(angles)
    sine = jnp.sin(angles)
    upper = jnp.concatenate([cosine, sine], axis=1)
    lower = jnp.concatenate([-sine, cosine], axis=1)
    return jnp.stack([upper, lower]).astype(jnp.bfloat16)


def whiten_parts(real_part, imag_part, magnitude, channel_level, usable):
    factor = usable.astype(jnp.float32)[:, None, :] / (magnitude + 0.5 * (channel_level + 1e-05))
    return jnp.stack([real_part * factor, imag_part * factor]).astype(jnp.bfloat16)


def cross_parts(own_real, own_imag, far_real, far_imag):
    own_real = own_real.astype(jnp.float32)
    own_imag = own_imag.astype(jnp.float32)
    far_real = far_real.astype(jnp.float32)
    far_imag = far_imag.astype(jnp.float32)
    return jnp.stack(
        [own_real * far_real + own_imag * far_imag, own_imag * far_real - own_real * far_imag]
    ).astype(jnp.bfloat16)


def pair_terms(corr_all):
    lag_count = corr_all.shape[-1] // 2
    real_corr = corr_all[..., :lag_count]
    imag_corr = corr_all[..., lag_count:]
    power = real_corr * real_corr + imag_corr * imag_corr
    mean_power = jnp.mean(power, axis=-1, keepdims=True)
    denominator = jnp.sqrt(power + 0.25 * (mean_power + 1e-06))
    return (
        jnp.sum(real_corr, axis=-3),
        jnp.sum(real_corr / denominator, axis=-3),
        jnp.sum(imag_corr / denominator, axis=-3),
    )


def shards(spectra, quality, offsets):
    chan_count = lax.axis_size("chan")
    tm_count = lax.axis_size("tm")
    levels = chan_count.bit_length() - 1
    table_bf = lag_table(F, LAGS)
    inv_root = 1.0 / math.sqrt(F)
    real_part = spectra[0].astype(jnp.float32)
    imag_part = spectra[1].astype(jnp.float32)
    magnitude = jnp.sqrt(real_part * real_part + imag_part * imag_part)
    band_total = lax.psum(jnp.sum(magnitude, axis=1), "chan")
    channel_level = (band_total / F)[:, None, :]
    whitened = whiten_parts(real_part, imag_part, magnitude, channel_level, quality)
    width_all = whitened.shape[3]
    padded = jnp.pad(whitened, ((0, 0), (0, 0), (0, 0), (0, width_all)))
    crossed_list = []
    for offset_index in range(NOFF):
        partner = lax.dynamic_slice_in_dim(padded, offsets[offset_index] * CH_DEV, width_all, 3)
        crossed_list.append(cross_parts(whitened[0], whitened[1], partner[0], partner[1]))
    crossed = jnp.stack(crossed_list, axis=1)
    corr_all = jnp.einsum(
        "cnwfh,cfl->nwhl",
        lax.all_to_all(crossed, "chan", split_axis=4, concat_axis=3, tiled=True),
        table_bf,
        preferred_element_type=jnp.float32,
    )
    linear_sum, real_sum, imag_sum = pair_terms(corr_all * inv_root)
    totals = lax.psum((linear_sum, real_sum, imag_sum), "tm")
    window_count = W_DEV * tm_count
    linear = totals[0] / window_count
    real_phase = totals[1] / window_count
    imag_phase = totals[2] / window_count
    stacks = jnp.transpose(linear * (real_phase * real_phase + imag_phase * imag_phase), (1, 0, 2))
    reverse_part = stacks
    for bit_index in range(levels):
        step_size = 1 << bit_index
        arrived = shifted(reverse_part, "chan", step_size)
        chosen = offsets // step_size % 2 == 1
        reverse_part = jnp.where(chosen[None, :, None], arrived, reverse_part)
    return stacks + jnp.flip(reverse_part, axis=2)


def solution(mesh):
    chan_count, tm_count = mesh.shape["chan"], mesh.shape["tm"]
    by_window = chan_count == W_DEV and tm_count == NOFF
    return jax.shard_map(
        window_shards if by_window else shards,
        mesh=mesh,
        in_specs=(P(None, "tm", "chan", None), P("tm", None), P()),
        out_specs=P("chan", None, None),
        check_vma=False,
    )
```

```python
import functools
import math

import jax
import jax.numpy as jnp
import numpy as np
from jax import lax
from jax.experimental import pallas as pl
from jax.experimental.pallas import tpu as pltpu
from jax.sharding import PartitionSpec as P

F = 2048
LAGS = 256
NOFF = 4
CH_DEV = 16
W_DEV = 8
VMEM_LIMIT = 48 * 1024 * 1024
CODE_TOP = 32767.0
OCTAVE = 256.0
LOWEST = -110.0


def encode(value):
    return jnp.round(value * CODE_TOP).astype(jnp.int32).astype(jnp.int16)


def decode(code):
    return code.astype(jnp.int32).astype(jnp.float32)


def level_code(peak):
    return jnp.ceil(jnp.maximum(jnp.log2(jnp.maximum(peak, 1e-30)), LOWEST) * OCTAVE) + 1.0


def level_of(code):
    return jnp.exp2(code * (1.0 / OCTAVE))


def half_table(freq_count, lag_count):
    freq_index = np.arange(freq_count, dtype=np.int64)[None, :]
    double_lag = (2 * np.arange(lag_count // 2, lag_count, dtype=np.int64) - lag_count + 1)[:, None]
    turns = np.mod(freq_index * double_lag, 4 * freq_count).astype(np.float32)
    angles = turns * np.float32(2.0 * math.pi / (4 * freq_count))
    return np.concatenate([np.cos(angles), np.sin(angles)]).astype(jnp.bfloat16)


def window_kernel(chan_count, offs_ref, where_ref, *refs):
    spec_refs, (qual_ref, table_ref) = refs[:chan_count], refs[chan_count : chan_count + 2]
    out_refs = refs[chan_count + 2 : 2 * chan_count + 2]
    mag_ref, white_ref, cross_ref = refs[2 * chan_count + 2 :]
    me = where_ref[0]
    _, band, chans = spec_refs[0].shape
    freqs = chan_count * band
    blocks, lag_rows, _ = out_refs[0].shape
    offset_count = offs_ref.shape[0]
    half = chan_count * lag_rows
    step = 64

    total = jnp.zeros((8, chans), jnp.float32)
    for partner, spec_ref in enumerate(spec_refs):

        def magnitudes(index, total, spec_ref=spec_ref, base=(me ^ partner) * band):
            rows = pl.ds(pl.multiple_of(index * step, step), step)
            real = spec_ref[0, rows, :].astype(jnp.float32)
            imag = spec_ref[1, rows, :].astype(jnp.float32)
            magnitude = jnp.sqrt(real * real + imag * imag)
            mag_ref[pl.ds(pl.multiple_of(base + index * step, step), step), :] = magnitude
            return total + jnp.sum(magnitude.reshape(step // 8, 8, chans), axis=0)

        total = lax.fori_loop(0, band // step, magnitudes, total, unroll=True)
    level = jnp.sum(total, axis=0, keepdims=True) / freqs
    floor = 0.5 * (level + 1e-05)
    usable = qual_ref[pl.ds(me, 1), :].astype(jnp.float32)

    for partner, spec_ref in enumerate(spec_refs):

        def whiten(index, carry, spec_ref=spec_ref, base=(me ^ partner) * band):
            rows = pl.ds(pl.multiple_of(index * step, step), step)
            held = pl.ds(pl.multiple_of(base + index * step, step), step)
            factor = usable / (mag_ref[held, :] + floor)
            for part in range(2):
                value = spec_ref[part, rows, :].astype(jnp.float32) * factor
                white_ref[part, held, :] = value.astype(jnp.bfloat16).astype(jnp.float32)
            return carry

        lax.fori_loop(0, band // step, whiten, 0, unroll=True)

    lane = lax.broadcasted_iota(jnp.int32, (1, chans), 1)
    row = lax.broadcasted_iota(jnp.int32, (lag_rows, chans), 0)
    levels = jnp.zeros((lag_rows, chans), jnp.float32)
    scale = 1.0 / math.sqrt(freqs)
    table = jnp.concatenate([table_ref[side, me ^ k] for side in range(2) for k in range(chan_count)], axis=0)
    for number in range(offset_count):
        ahead = offs_ref[number] * (chans // chan_count)
        turn = chans - ahead

        def cross(index, carry):
            held = pl.ds(pl.multiple_of(index * step, step), step)
            own_real, own_imag = white_ref[0, held, :], white_ref[1, held, :]
            far_real = pltpu.roll(own_real, turn, 1)
            far_imag = pltpu.roll(own_imag, turn, 1)
            cross_ref[held, pl.ds(0, chans)] = (own_real * far_real + own_imag * far_imag).astype(jnp.bfloat16)
            cross_ref[held, pl.ds(chans, chans)] = (own_imag * far_real - own_real * far_imag).astype(jnp.bfloat16)
            return carry

        lax.fori_loop(0, freqs // step, cross, 0, unroll=4)
        sums = jnp.dot(table, cross_ref[...], preferred_element_type=jnp.float32)
        keep = jnp.where(lane < turn, scale, 0.0)
        cos_real, sin_real = sums[:half, :chans] * keep, sums[half:, :chans] * keep
        cos_imag, sin_imag = sums[:half, chans:] * keep, sums[half:, chans:] * keep
        corr = (
            (cos_real - sin_imag, sin_real + cos_imag),
            (cos_real + sin_imag, cos_imag - sin_real),
        )
        power = [real * real + imag * imag for real, imag in corr]
        mean_power = (jnp.sum(power[0], axis=0, keepdims=True) + jnp.sum(power[1], axis=0, keepdims=True)) / (2 * half)
        extra = 0.25 * (mean_power + 1e-06)
        peak = jnp.max(jnp.maximum(jnp.abs(corr[0][0]), jnp.abs(corr[1][0])), axis=0, keepdims=True)
        code = level_code(peak)
        levels = jnp.where(row == number, code, levels)
        upscale = 1.0 / level_of(code)
        for side in range(2):
            inverse = 1.0 / jnp.sqrt(power[side] + extra)
            real, imag = corr[side]
            for kind, value in enumerate((real * upscale, real * inverse, imag * inverse)):
                coded = encode(value).reshape(chan_count, lag_rows, chans)
                for k in range(chan_count):
                    out_refs[k][6 * number + 2 * kind + side, :, :] = coded[k]
    for k in range(chan_count):
        out_refs[k][blocks - 1, :, :] = levels.astype(jnp.int32).astype(jnp.int16)


def sum_kernel(chan_count, where_ref, *refs):
    code_refs, out_refs = refs[:chan_count], refs[chan_count:]
    blocks = code_refs[0].shape[0]
    levels = [level_of(decode(codes_ref[blocks - 1])) / CODE_TOP for codes_ref in code_refs]
    row = lax.broadcasted_iota(jnp.int32, levels[0].shape, 0)
    for k, out_ref in enumerate(out_refs):
        number = where_ref[0] ^ k
        own = [jnp.sum(jnp.where(row == number, level, 0.0), axis=0, keepdims=True) for level in levels]
        for block in range(6):
            total = 0.0
            for codes_ref, level in zip(code_refs, own):
                value = decode(codes_ref[6 * number + block])
                total += value * level if block < 2 else value
            out_ref[block, :, :] = total if block < 2 else total / CODE_TOP


def exchange(pieces, axis):
    count = lax.axis_size(axis)
    return [pieces[0]] + [
        lax.ppermute(pieces[k], axis, [(source, source ^ k) for source in range(count)]) for k in range(1, count)
    ]


def stack_kernel(windows, offs_ref, where_ref, *refs):
    sums_refs, out_ref = refs[:-1], refs[-1]
    blocks, copies, _, _ = out_ref.shape
    _, lag_rows, chans = sums_refs[0].shape
    total = sum(sums_ref[...] for sums_ref in sums_refs) / windows
    stacks = [
        total[side] * (total[2 + side] * total[2 + side] + total[4 + side] * total[4 + side]) for side in range(2)
    ]
    ahead = offs_ref[where_ref[0]] * (chans // blocks)
    lane = lax.broadcasted_iota(jnp.int32, (1, chans), 1)
    behind = [jnp.where(lane >= ahead, pltpu.roll(stack, ahead, 1), 0.0) for stack in stacks]
    both = jnp.concatenate([stacks[0] + behind[1], stacks[1] + behind[0]], axis=0)
    wide = 2 * lag_rows
    turned = jnp.concatenate([both] * (chans // wide), axis=0).T
    per_block = chans // blocks
    rows = per_block // 2
    for block in range(blocks):
        first = turned[block * per_block : block * per_block + rows, :]
        second = turned[block * per_block + rows : (block + 1) * per_block, :]
        piece = jnp.where(lane < wide, first, second)
        for copy in range(copies):
            out_ref[block, copy, :, :] = piece


def place_kernel(parts_ref, out_ref):
    groups, offset_count, rows, lanes = parts_ref.shape
    half = out_ref.shape[2] // 2
    lag_rows = half // groups
    lane = lax.broadcasted_iota(jnp.int32, (1, lanes), 1)
    mirror = (
        lax.broadcasted_iota(jnp.int32, (half, half), 0) + lax.broadcasted_iota(jnp.int32, (half, half), 1) == half - 1
    ).astype(jnp.float32)
    for number in range(offset_count):
        for part in range(2):
            ahead = jnp.zeros((rows, lanes), jnp.float32)
            back = jnp.zeros((rows, lanes), jnp.float32)
            for group in range(groups):
                piece = parts_ref[group, number]
                here = (lane >= group * lag_rows) & (lane < (group + 1) * lag_rows)
                begin = part * 2 * lag_rows
                ahead = jnp.where(here, pltpu.roll(piece, (group * lag_rows - begin) % lanes, 1), ahead)
                back = jnp.where(here, pltpu.roll(piece, (group * lag_rows - begin - lag_rows) % lanes, 1), back)
            back = jnp.dot(back, mirror, precision=lax.Precision.HIGHEST, preferred_element_type=jnp.float32)
            out_ref[part * rows : (part + 1) * rows, number, 0:half] = back
            out_ref[part * rows : (part + 1) * rows, number, half : 2 * half] = ahead


def window_shards(spectra, quality, offsets):
    chan_count = lax.axis_size("chan")
    tm_count = lax.axis_size("tm")
    _, windows, band, chans = spectra.shape
    freqs = band * chan_count
    half = LAGS // 2
    lag_rows = half // chan_count
    offset_count = offsets.shape[0]
    smem = pl.BlockSpec(memory_space=pltpu.SMEM)
    vmem = pl.BlockSpec(memory_space=pltpu.VMEM)
    params = pltpu.CompilerParams(vmem_limit_bytes=VMEM_LIMIT)
    table = jnp.asarray(half_table(freqs, LAGS).reshape(2, chan_count, lag_rows, freqs))
    chan_index = lax.axis_index("chan").astype(jnp.int32)
    tm_index = lax.axis_index("tm").astype(jnp.int32)
    chan_where, tm_where = chan_index.reshape(1), tm_index.reshape(1)

    pieces = [
        lax.dynamic_index_in_dim(spectra, chan_index ^ k, 1, keepdims=False) for k in range(chan_count)
    ]
    pairs = pl.pallas_call(
        functools.partial(window_kernel, chan_count),
        out_shape=[jax.ShapeDtypeStruct((6 * offset_count + 1, lag_rows, chans), jnp.int16)] * chan_count,
        in_specs=[smem, smem] + [vmem] * (chan_count + 2),
        out_specs=[vmem] * chan_count,
        scratch_shapes=[
            pltpu.VMEM((freqs, chans), jnp.float32),
            pltpu.VMEM((2, freqs, chans), jnp.float32),
            pltpu.VMEM((freqs, 2 * chans), jnp.bfloat16),
        ],
        compiler_params=params,
        name="window_pairs",
    )(offsets, chan_where, *exchange(pieces, "chan"), quality, table)
    sums = pl.pallas_call(
        functools.partial(sum_kernel, chan_count),
        out_shape=[jax.ShapeDtypeStruct((6, lag_rows, chans), jnp.float32)] * tm_count,
        in_specs=[smem] + [vmem] * chan_count,
        out_specs=[vmem] * tm_count,
        compiler_params=params,
        name="sum_windows",
    )(tm_where, *exchange(pairs, "chan"))
    pieces = pl.pallas_call(
        functools.partial(stack_kernel, windows * tm_count),
        out_shape=jax.ShapeDtypeStruct((chan_count, tm_count, CH_DEV // 2, chans), jnp.float32),
        in_specs=[smem, smem] + [vmem] * tm_count,
        out_specs=vmem,
        compiler_params=params,
        name="stack_pairs",
    )(offsets, tm_where, *exchange(sums, "tm"))
    shape = (chan_count * tm_count, CH_DEV // 2, chans)
    arrived = lax.all_to_all(pieces.reshape(shape), ("chan", "tm"), 0, 0, tiled=True)
    return pl.pallas_call(
        place_kernel,
        out_shape=jax.ShapeDtypeStruct((CH_DEV, offset_count, LAGS), jnp.float32),
        in_specs=[vmem],
        out_specs=vmem,
        compiler_params=params,
        name="place_lags",
    )(arrived.reshape(chan_count, tm_count, CH_DEV // 2, chans))


def shifted(value, axis, steps):
    count = lax.axis_size(axis)
    leading, last = (max(0, -steps), min(count, count - steps))
    return lax.ppermute(value, axis, [(source, source + steps) for source in range(leading, last)])


def lag_table(freq_count, lag_count):
    freq_index = jnp.arange(freq_count, dtype=jnp.int32)[:, None]
    double_lag = (2 * jnp.arange(lag_count, dtype=jnp.int32) - lag_count + 1)[None, :]
    turns = jnp.mod(freq_index * double_lag, 4 * freq_count)
    angles = turns.astype(jnp.float32) * (2.0 * math.pi / (4 * freq_count))
    cosine = jnp.cos(angles)
    sine = jnp.sin(angles)
    upper = jnp.concatenate([cosine, sine], axis=1)
    lower = jnp.concatenate([-sine, cosine], axis=1)
    return jnp.stack([upper, lower]).astype(jnp.bfloat16)


def whiten_parts(real_part, imag_part, magnitude, channel_level, usable):
    factor = usable.astype(jnp.float32)[:, None, :] / (magnitude + 0.5 * (channel_level + 1e-05))
    return jnp.stack([real_part * factor, imag_part * factor]).astype(jnp.bfloat16)


def cross_parts(own_real, own_imag, far_real, far_imag):
    own_real = own_real.astype(jnp.float32)
    own_imag = own_imag.astype(jnp.float32)
    far_real = far_real.astype(jnp.float32)
    far_imag = far_imag.astype(jnp.float32)
    return jnp.stack(
        [own_real * far_real + own_imag * far_imag, own_imag * far_real - own_real * far_imag]
    ).astype(jnp.bfloat16)


def pair_terms(corr_all):
    lag_count = corr_all.shape[-1] // 2
    real_corr = corr_all[..., :lag_count]
    imag_corr = corr_all[..., lag_count:]
    power = real_corr * real_corr + imag_corr * imag_corr
    mean_power = jnp.mean(power, axis=-1, keepdims=True)
    denominator = jnp.sqrt(power + 0.25 * (mean_power + 1e-06))
    return (
        jnp.sum(real_corr, axis=-3),
        jnp.sum(real_corr / denominator, axis=-3),
        jnp.sum(imag_corr / denominator, axis=-3),
    )


def shards(spectra, quality, offsets):
    chan_count = lax.axis_size("chan")
    tm_count = lax.axis_size("tm")
    levels = chan_count.bit_length() - 1
    table_bf = lag_table(F, LAGS)
    inv_root = 1.0 / math.sqrt(F)
    real_part = spectra[0].astype(jnp.float32)
    imag_part = spectra[1].astype(jnp.float32)
    magnitude = jnp.sqrt(real_part * real_part + imag_part * imag_part)
    band_total = lax.psum(jnp.sum(magnitude, axis=1), "chan")
    channel_level = (band_total / F)[:, None, :]
    whitened = whiten_parts(real_part, imag_part, magnitude, channel_level, quality)
    width_all = whitened.shape[3]
    padded = jnp.pad(whitened, ((0, 0), (0, 0), (0, 0), (0, width_all)))
    crossed_list = []
    for offset_index in range(NOFF):
        partner = lax.dynamic_slice_in_dim(padded, offsets[offset_index] * CH_DEV, width_all, 3)
        crossed_list.append(cross_parts(whitened[0], whitened[1], partner[0], partner[1]))
    crossed = jnp.stack(crossed_list, axis=1)
    corr_all = jnp.einsum(
        "cnwfh,cfl->nwhl",
        lax.all_to_all(crossed, "chan", split_axis=4, concat_axis=3, tiled=True),
        table_bf,
        preferred_element_type=jnp.float32,
    )
    linear_sum, real_sum, imag_sum = pair_terms(corr_all * inv_root)
    totals = lax.psum((linear_sum, real_sum, imag_sum), "tm")
    window_count = W_DEV * tm_count
    linear = totals[0] / window_count
    real_phase = totals[1] / window_count
    imag_phase = totals[2] / window_count
    stacks = jnp.transpose(linear * (real_phase * real_phase + imag_phase * imag_phase), (1, 0, 2))
    reverse_part = stacks
    for bit_index in range(levels):
        step_size = 1 << bit_index
        arrived = shifted(reverse_part, "chan", step_size)
        chosen = offsets // step_size % 2 == 1
        reverse_part = jnp.where(chosen[None, :, None], arrived, reverse_part)
    return stacks + jnp.flip(reverse_part, axis=2)


def solution(mesh):
    chan_count, tm_count = mesh.shape["chan"], mesh.shape["tm"]
    by_window = chan_count == W_DEV and tm_count == NOFF
    return jax.shard_map(
        window_shards if by_window else shards,
        mesh=mesh,
        in_specs=(P(None, "tm", "chan", None), P("tm", None), P()),
        out_specs=P("chan", None, None),
        check_vma=False,
    )
```

```python
import functools
import math

import jax
import jax.numpy as jnp
import numpy as np
from jax import lax
from jax.experimental import pallas as pl
from jax.experimental.pallas import tpu as pltpu
from jax.sharding import PartitionSpec as P

F = 2048
LAGS = 256
NOFF = 4
CH_DEV = 16
W_DEV = 8
VMEM_LIMIT = 48 * 1024 * 1024
CODE_TOP = 32767.0
OCTAVE = 256.0
LOWEST = -110.0


def encode(value):
    return jnp.round(value * CODE_TOP).astype(jnp.int32).astype(jnp.int16)


def decode(code):
    return code.astype(jnp.int32).astype(jnp.float32)


def level_code(peak):
    return jnp.ceil(jnp.maximum(jnp.log2(jnp.maximum(peak, 1e-30)), LOWEST) * OCTAVE) + 1.0


def level_of(code):
    return jnp.exp2(code * (1.0 / OCTAVE))


def half_table(freq_count, lag_count):
    freq_index = np.arange(freq_count, dtype=np.int64)[None, :]
    double_lag = (2 * np.arange(lag_count // 2, lag_count, dtype=np.int64) - lag_count + 1)[:, None]
    turns = np.mod(freq_index * double_lag, 4 * freq_count).astype(np.float32)
    angles = turns * np.float32(2.0 * math.pi / (4 * freq_count))
    return np.concatenate([np.cos(angles), np.sin(angles)]).astype(jnp.bfloat16)


def window_kernel(order, offs_ref, where_ref, *refs):
    chan_count = len(order)
    spec_refs, (qual_ref, table_ref) = refs[:chan_count], refs[chan_count : chan_count + 2]
    out_refs = refs[chan_count + 2 : 2 * chan_count + 2]
    mag_ref, white_ref, cross_ref = refs[2 * chan_count + 2 :]
    me = where_ref[0]
    _, band, chans = spec_refs[0].shape
    freqs = chan_count * band
    blocks, lag_rows, _ = out_refs[0].shape
    offset_count = offs_ref.shape[0]
    half = chan_count * lag_rows
    step = 64

    total = jnp.zeros((8, chans), jnp.float32)
    for partner, spec_ref in zip(order, spec_refs):

        def magnitudes(index, total, spec_ref=spec_ref, base=(me ^ partner) * band):
            rows = pl.ds(pl.multiple_of(index * step, step), step)
            real = spec_ref[0, rows, :].astype(jnp.float32)
            imag = spec_ref[1, rows, :].astype(jnp.float32)
            magnitude = jnp.sqrt(real * real + imag * imag)
            mag_ref[pl.ds(pl.multiple_of(base + index * step, step), step), :] = magnitude
            return total + jnp.sum(magnitude.reshape(step // 8, 8, chans), axis=0)

        total = lax.fori_loop(0, band // step, magnitudes, total, unroll=True)
    level = jnp.sum(total, axis=0, keepdims=True) / freqs
    floor = 0.5 * (level + 1e-05)
    usable = qual_ref[pl.ds(me, 1), :].astype(jnp.float32)

    for partner, spec_ref in zip(order, spec_refs):

        def whiten(index, carry, spec_ref=spec_ref, base=(me ^ partner) * band):
            rows = pl.ds(pl.multiple_of(index * step, step), step)
            held = pl.ds(pl.multiple_of(base + index * step, step), step)
            factor = usable / (mag_ref[held, :] + floor)
            for part in range(2):
                value = spec_ref[part, rows, :].astype(jnp.float32) * factor
                white_ref[part, held, :] = value.astype(jnp.bfloat16).astype(jnp.float32)
            return carry

        lax.fori_loop(0, band // step, whiten, 0, unroll=True)

    lane = lax.broadcasted_iota(jnp.int32, (1, chans), 1)
    row = lax.broadcasted_iota(jnp.int32, (lag_rows, chans), 0)
    levels = jnp.zeros((lag_rows, chans), jnp.float32)
    scale = 1.0 / math.sqrt(freqs)
    table = jnp.concatenate([table_ref[side, me ^ k] for side in range(2) for k in order], axis=0)
    for number in range(offset_count):
        ahead = offs_ref[number] * (chans // chan_count)
        turn = chans - ahead

        def cross(index, carry):
            held = pl.ds(pl.multiple_of(index * step, step), step)
            own_real, own_imag = white_ref[0, held, :], white_ref[1, held, :]
            far_real = pltpu.roll(own_real, turn, 1)
            far_imag = pltpu.roll(own_imag, turn, 1)
            cross_ref[held, pl.ds(0, chans)] = (own_real * far_real + own_imag * far_imag).astype(jnp.bfloat16)
            cross_ref[held, pl.ds(chans, chans)] = (own_imag * far_real - own_real * far_imag).astype(jnp.bfloat16)
            return carry

        lax.fori_loop(0, freqs // step, cross, 0, unroll=4)
        sums = jnp.dot(table, cross_ref[...], preferred_element_type=jnp.float32)
        keep = jnp.where(lane < turn, scale, 0.0)
        cos_real, sin_real = sums[:half, :chans] * keep, sums[half:, :chans] * keep
        cos_imag, sin_imag = sums[:half, chans:] * keep, sums[half:, chans:] * keep
        corr = (
            (cos_real - sin_imag, sin_real + cos_imag),
            (cos_real + sin_imag, cos_imag - sin_real),
        )
        power = [real * real + imag * imag for real, imag in corr]
        mean_power = (jnp.sum(power[0], axis=0, keepdims=True) + jnp.sum(power[1], axis=0, keepdims=True)) / (2 * half)
        extra = 0.25 * (mean_power + 1e-06)
        peak = jnp.max(jnp.maximum(jnp.abs(corr[0][0]), jnp.abs(corr[1][0])), axis=0, keepdims=True)
        code = level_code(peak)
        levels = jnp.where(row == number, code, levels)
        upscale = 1.0 / level_of(code)
        for side in range(2):
            inverse = 1.0 / jnp.sqrt(power[side] + extra)
            real, imag = corr[side]
            for kind, value in enumerate((real * upscale, real * inverse, imag * inverse)):
                coded = encode(value).reshape(chan_count, lag_rows, chans)
                for k in range(chan_count):
                    out_refs[k][6 * number + 2 * kind + side, :, :] = coded[k]
    for k in range(chan_count):
        out_refs[k][blocks - 1, :, :] = levels.astype(jnp.int32).astype(jnp.int16)


def sum_kernel(order, where_ref, *refs):
    code_refs, out_refs = refs[: -len(order)], refs[-len(order) :]
    blocks = code_refs[0].shape[0]
    levels = [level_of(decode(codes_ref[blocks - 1])) / CODE_TOP for codes_ref in code_refs]
    row = lax.broadcasted_iota(jnp.int32, levels[0].shape, 0)
    for k, out_ref in zip(order, out_refs):
        number = where_ref[0] ^ k
        own = [jnp.sum(jnp.where(row == number, level, 0.0), axis=0, keepdims=True) for level in levels]
        for block in range(6):
            total = 0.0
            for codes_ref, level in zip(code_refs, own):
                value = decode(codes_ref[6 * number + block])
                total += value * level if block < 2 else value
            out_ref[block, :, :] = total if block < 2 else total / CODE_TOP


def partners(count):
    return sorted(range(1, count), key=lambda k: (-(k >> 1).bit_count(), k & 1, k)) + [0]


def exchange(pieces, axis):
    count = lax.axis_size(axis)
    return [
        lax.ppermute(piece, axis, [(source, source ^ k) for source in range(count)]) if k else piece
        for k, piece in zip(partners(count), pieces)
    ]


def split_kernel(order, where_ref, spec_ref, *refs):
    out_refs, sems = refs[:-1], refs[-1]
    copies = [
        pltpu.make_async_copy(spec_ref.at[:, where_ref[0] ^ k], out_ref, sems.at[number])
        for number, (k, out_ref) in enumerate(zip(order, out_refs))
    ]
    for copy in copies:
        copy.start()
    for copy in copies:
        copy.wait()


def stack_kernel(windows, offs_ref, where_ref, *refs):
    sums_refs, out_ref = refs[:-1], refs[-1]
    blocks, copies, _, _ = out_ref.shape
    _, lag_rows, chans = sums_refs[0].shape
    total = sum(sums_ref[...] for sums_ref in sums_refs) / windows
    stacks = [
        total[side] * (total[2 + side] * total[2 + side] + total[4 + side] * total[4 + side]) for side in range(2)
    ]
    ahead = offs_ref[where_ref[0]] * (chans // blocks)
    lane = lax.broadcasted_iota(jnp.int32, (1, chans), 1)
    behind = [jnp.where(lane >= ahead, pltpu.roll(stack, ahead, 1), 0.0) for stack in stacks]
    both = jnp.concatenate([stacks[0] + behind[1], stacks[1] + behind[0]], axis=0)
    wide = 2 * lag_rows
    turned = jnp.concatenate([both] * (chans // wide), axis=0).T
    per_block = chans // blocks
    rows = per_block // 2
    for block in range(blocks):
        first = turned[block * per_block : block * per_block + rows, :]
        second = turned[block * per_block + rows : (block + 1) * per_block, :]
        piece = jnp.where(lane < wide, first, second)
        for copy in range(copies):
            out_ref[block, copy, :, :] = piece


def place_kernel(parts_ref, out_ref):
    groups, offset_count, rows, lanes = parts_ref.shape
    half = out_ref.shape[2] // 2
    lag_rows = half // groups
    lane = lax.broadcasted_iota(jnp.int32, (1, lanes), 1)
    mirror = (
        lax.broadcasted_iota(jnp.int32, (half, half), 0) + lax.broadcasted_iota(jnp.int32, (half, half), 1) == half - 1
    ).astype(jnp.float32)
    for number in range(offset_count):
        for part in range(2):
            ahead = jnp.zeros((rows, lanes), jnp.float32)
            back = jnp.zeros((rows, lanes), jnp.float32)
            for group in range(groups):
                piece = parts_ref[group, number]
                here = (lane >= group * lag_rows) & (lane < (group + 1) * lag_rows)
                begin = part * 2 * lag_rows
                ahead = jnp.where(here, pltpu.roll(piece, (group * lag_rows - begin) % lanes, 1), ahead)
                back = jnp.where(here, pltpu.roll(piece, (group * lag_rows - begin - lag_rows) % lanes, 1), back)
            back = jnp.dot(back, mirror, precision=lax.Precision.HIGHEST, preferred_element_type=jnp.float32)
            out_ref[part * rows : (part + 1) * rows, number, 0:half] = back
            out_ref[part * rows : (part + 1) * rows, number, half : 2 * half] = ahead


def window_shards(spectra, quality, offsets):
    chan_count = lax.axis_size("chan")
    tm_count = lax.axis_size("tm")
    _, windows, band, chans = spectra.shape
    freqs = band * chan_count
    half = LAGS // 2
    lag_rows = half // chan_count
    offset_count = offsets.shape[0]
    smem = pl.BlockSpec(memory_space=pltpu.SMEM)
    vmem = pl.BlockSpec(memory_space=pltpu.VMEM)
    params = pltpu.CompilerParams(vmem_limit_bytes=VMEM_LIMIT)
    table = jnp.asarray(half_table(freqs, LAGS).reshape(2, chan_count, lag_rows, freqs))
    chan_index = lax.axis_index("chan").astype(jnp.int32)
    tm_index = lax.axis_index("tm").astype(jnp.int32)
    chan_where, tm_where = chan_index.reshape(1), tm_index.reshape(1)

    chan_order, tm_order = partners(chan_count), partners(tm_count)
    pieces = pl.pallas_call(
        functools.partial(split_kernel, chan_order),
        out_shape=[jax.ShapeDtypeStruct((2, band, chans), spectra.dtype)] * chan_count,
        in_specs=[smem, pl.BlockSpec(memory_space=pl.ANY)],
        out_specs=[pl.BlockSpec(memory_space=pl.ANY)] * chan_count,
        scratch_shapes=[pltpu.SemaphoreType.DMA((chan_count,))],
        compiler_params=params,
        name="split_windows",
    )(chan_where, spectra)
    pairs = pl.pallas_call(
        functools.partial(window_kernel, chan_order),
        out_shape=[jax.ShapeDtypeStruct((6 * offset_count + 1, lag_rows, chans), jnp.int16)] * chan_count,
        in_specs=[smem, smem] + [vmem] * (chan_count + 2),
        out_specs=[vmem] * chan_count,
        scratch_shapes=[
            pltpu.VMEM((freqs, chans), jnp.float32),
            pltpu.VMEM((2, freqs, chans), jnp.float32),
            pltpu.VMEM((freqs, 2 * chans), jnp.bfloat16),
        ],
        compiler_params=params,
        name="window_pairs",
    )(offsets, chan_where, *exchange(pieces, "chan"), quality, table)
    sums = pl.pallas_call(
        functools.partial(sum_kernel, tm_order),
        out_shape=[jax.ShapeDtypeStruct((6, lag_rows, chans), jnp.float32)] * tm_count,
        in_specs=[smem] + [vmem] * chan_count,
        out_specs=[vmem] * tm_count,
        compiler_params=params,
        name="sum_windows",
    )(tm_where, *exchange(pairs, "chan"))
    pieces = pl.pallas_call(
        functools.partial(stack_kernel, windows * tm_count),
        out_shape=jax.ShapeDtypeStruct((chan_count, tm_count, CH_DEV // 2, chans), jnp.float32),
        in_specs=[smem, smem] + [vmem] * tm_count,
        out_specs=vmem,
        compiler_params=params,
        name="stack_pairs",
    )(offsets, tm_where, *exchange(sums, "tm"))
    shape = (chan_count * tm_count, CH_DEV // 2, chans)
    arrived = lax.all_to_all(pieces.reshape(shape), ("chan", "tm"), 0, 0, tiled=True)
    return pl.pallas_call(
        place_kernel,
        out_shape=jax.ShapeDtypeStruct((CH_DEV, offset_count, LAGS), jnp.float32),
        in_specs=[vmem],
        out_specs=vmem,
        compiler_params=params,
        name="place_lags",
    )(arrived.reshape(chan_count, tm_count, CH_DEV // 2, chans))


def shifted(value, axis, steps):
    count = lax.axis_size(axis)
    leading, last = (max(0, -steps), min(count, count - steps))
    return lax.ppermute(value, axis, [(source, source + steps) for source in range(leading, last)])


def lag_table(freq_count, lag_count):
    freq_index = jnp.arange(freq_count, dtype=jnp.int32)[:, None]
    double_lag = (2 * jnp.arange(lag_count, dtype=jnp.int32) - lag_count + 1)[None, :]
    turns = jnp.mod(freq_index * double_lag, 4 * freq_count)
    angles = turns.astype(jnp.float32) * (2.0 * math.pi / (4 * freq_count))
    cosine = jnp.cos(angles)
    sine = jnp.sin(angles)
    upper = jnp.concatenate([cosine, sine], axis=1)
    lower = jnp.concatenate([-sine, cosine], axis=1)
    return jnp.stack([upper, lower]).astype(jnp.bfloat16)


def whiten_parts(real_part, imag_part, magnitude, channel_level, usable):
    factor = usable.astype(jnp.float32)[:, None, :] / (magnitude + 0.5 * (channel_level + 1e-05))
    return jnp.stack([real_part * factor, imag_part * factor]).astype(jnp.bfloat16)


def cross_parts(own_real, own_imag, far_real, far_imag):
    own_real = own_real.astype(jnp.float32)
    own_imag = own_imag.astype(jnp.float32)
    far_real = far_real.astype(jnp.float32)
    far_imag = far_imag.astype(jnp.float32)
    return jnp.stack(
        [own_real * far_real + own_imag * far_imag, own_imag * far_real - own_real * far_imag]
    ).astype(jnp.bfloat16)


def pair_terms(corr_all):
    lag_count = corr_all.shape[-1] // 2
    real_corr = corr_all[..., :lag_count]
    imag_corr = corr_all[..., lag_count:]
    power = real_corr * real_corr + imag_corr * imag_corr
    mean_power = jnp.mean(power, axis=-1, keepdims=True)
    denominator = jnp.sqrt(power + 0.25 * (mean_power + 1e-06))
    return (
        jnp.sum(real_corr, axis=-3),
        jnp.sum(real_corr / denominator, axis=-3),
        jnp.sum(imag_corr / denominator, axis=-3),
    )


def shards(spectra, quality, offsets):
    chan_count = lax.axis_size("chan")
    tm_count = lax.axis_size("tm")
    levels = chan_count.bit_length() - 1
    table_bf = lag_table(F, LAGS)
    inv_root = 1.0 / math.sqrt(F)
    real_part = spectra[0].astype(jnp.float32)
    imag_part = spectra[1].astype(jnp.float32)
    magnitude = jnp.sqrt(real_part * real_part + imag_part * imag_part)
    band_total = lax.psum(jnp.sum(magnitude, axis=1), "chan")
    channel_level = (band_total / F)[:, None, :]
    whitened = whiten_parts(real_part, imag_part, magnitude, channel_level, quality)
    width_all = whitened.shape[3]
    padded = jnp.pad(whitened, ((0, 0), (0, 0), (0, 0), (0, width_all)))
    crossed_list = []
    for offset_index in range(NOFF):
        partner = lax.dynamic_slice_in_dim(padded, offsets[offset_index] * CH_DEV, width_all, 3)
        crossed_list.append(cross_parts(whitened[0], whitened[1], partner[0], partner[1]))
    crossed = jnp.stack(crossed_list, axis=1)
    corr_all = jnp.einsum(
        "cnwfh,cfl->nwhl",
        lax.all_to_all(crossed, "chan", split_axis=4, concat_axis=3, tiled=True),
        table_bf,
        preferred_element_type=jnp.float32,
    )
    linear_sum, real_sum, imag_sum = pair_terms(corr_all * inv_root)
    totals = lax.psum((linear_sum, real_sum, imag_sum), "tm")
    window_count = W_DEV * tm_count
    linear = totals[0] / window_count
    real_phase = totals[1] / window_count
    imag_phase = totals[2] / window_count
    stacks = jnp.transpose(linear * (real_phase * real_phase + imag_phase * imag_phase), (1, 0, 2))
    reverse_part = stacks
    for bit_index in range(levels):
        step_size = 1 << bit_index
        arrived = shifted(reverse_part, "chan", step_size)
        chosen = offsets // step_size % 2 == 1
        reverse_part = jnp.where(chosen[None, :, None], arrived, reverse_part)
    return stacks + jnp.flip(reverse_part, axis=2)


def solution(mesh):
    chan_count, tm_count = mesh.shape["chan"], mesh.shape["tm"]
    by_window = chan_count == W_DEV and tm_count == NOFF
    return jax.shard_map(
        window_shards if by_window else shards,
        mesh=mesh,
        in_specs=(P(None, "tm", "chan", None), P("tm", None), P()),
        out_specs=P("chan", None, None),
        check_vma=False,
    )
```

```python
import functools
import math

import jax
import jax.numpy as jnp
import numpy as np
from jax import lax
from jax.experimental import pallas as pl
from jax.experimental.pallas import tpu as pltpu
from jax.sharding import PartitionSpec as P

F = 2048
LAGS = 256
NOFF = 4
CH_DEV = 16
W_DEV = 8
VMEM_LIMIT = 48 * 1024 * 1024
CODE_TOP = 32767.0
OCTAVE = 256.0
LOWEST = -110.0


def encode(value):
    return jnp.round(value).astype(jnp.int32).astype(jnp.int16)


def decode(code):
    return code.astype(jnp.int32).astype(jnp.float32)


def level_code(peak):
    return jnp.ceil(jnp.maximum(jnp.log2(jnp.maximum(peak, 1e-30)), LOWEST) * OCTAVE) + 1.0


def level_of(code):
    return jnp.exp2(code * (1.0 / OCTAVE))


def half_table(freq_count, lag_count):
    freq_index = np.arange(freq_count, dtype=np.int64)[None, :]
    double_lag = (2 * np.arange(lag_count // 2, lag_count, dtype=np.int64) - lag_count + 1)[:, None]
    turns = np.mod(freq_index * double_lag, 4 * freq_count).astype(np.float32)
    angles = turns * np.float32(2.0 * math.pi / (4 * freq_count))
    return np.concatenate([np.cos(angles), np.sin(angles)]).astype(jnp.bfloat16)


def window_kernel(order, offs_ref, where_ref, *refs):
    chan_count = len(order)
    spec_refs, (qual_ref, table_ref) = refs[:chan_count], refs[chan_count : chan_count + 2]
    out_refs = refs[chan_count + 2 : 2 * chan_count + 2]
    mag_ref, white_ref, cross_ref = refs[2 * chan_count + 2 :]
    me = where_ref[0]
    _, band, chans = spec_refs[0].shape
    freqs = chan_count * band
    blocks, lag_rows, _ = out_refs[0].shape
    offset_count = offs_ref.shape[0]
    half = chan_count * lag_rows
    step = 64

    total = jnp.zeros((8, chans), jnp.float32)
    for partner, spec_ref in zip(order, spec_refs):
        base = (me ^ partner) * band
        for row in range(0, band, step):
            real = spec_ref[0, row : row + step, :].astype(jnp.float32)
            imag = spec_ref[1, row : row + step, :].astype(jnp.float32)
            square = real * real + imag * imag
            magnitude = square * lax.rsqrt(jnp.maximum(square, 1e-30))
            mag_ref[pl.ds(pl.multiple_of(base + row, step), step), :] = magnitude
            total += jnp.sum(magnitude.reshape(step // 8, 8, chans), axis=0)
    level = jnp.sum(total, axis=0, keepdims=True) * (1.0 / freqs)
    floor = 0.5 * (level + 1e-05)

    for partner, spec_ref in zip(order, spec_refs):
        base = (me ^ partner) * band
        for row in range(0, band, step):
            held = pl.ds(pl.multiple_of(base + row, step), step)
            factor = pl.reciprocal(mag_ref[held, :] + floor, approx=True)
            for part in range(2):
                value = spec_ref[part, row : row + step, :].astype(jnp.float32) * factor
                white_ref[part, held, :] = value.astype(jnp.bfloat16)

    lane = lax.broadcasted_iota(jnp.int32, (1, chans), 1)
    line = lax.broadcasted_iota(jnp.int32, (lag_rows, chans), 0)
    usable = qual_ref[pl.ds(me, 1), :].astype(jnp.float32)
    levels = jnp.zeros((lag_rows, chans), jnp.float32)
    table = jnp.concatenate([table_ref[side, me ^ k] for side in range(2) for k in order], axis=0)
    for number in range(offset_count):
        turn = chans - offs_ref[number] * (chans // chan_count)
        slot = number % 2
        for row in range(0, freqs, step):
            own = [white_ref[part, row : row + step, :] for part in range(2)]
            far_real, far_imag = (pltpu.roll(value, turn, 1).astype(jnp.float32) for value in own)
            own_real, own_imag = (value.astype(jnp.float32) for value in own)
            real = own_real * far_real + own_imag * far_imag
            imag = own_imag * far_real - own_real * far_imag
            cross_ref[slot, row : row + step, 0:chans] = real.astype(jnp.bfloat16)
            cross_ref[slot, row : row + step, chans : 2 * chans] = imag.astype(jnp.bfloat16)
        sums = jnp.dot(table, cross_ref[slot], preferred_element_type=jnp.float32)
        cos_real, sin_real = sums[:half, :chans], sums[half:, :chans]
        cos_imag, sin_imag = sums[:half, chans:], sums[half:, chans:]
        corr = (
            (cos_real - sin_imag, sin_real + cos_imag),
            (cos_real + sin_imag, cos_imag - sin_real),
        )
        power = [real * real + imag * imag for real, imag in corr]
        mean_power = jnp.sum(power[0] + power[1], axis=0, keepdims=True) * (1.0 / (2 * half))
        extra = 0.25 * (mean_power + 1e-06 * freqs)
        peak = jnp.max(jnp.maximum(jnp.abs(corr[0][0]), jnp.abs(corr[1][0])), axis=0, keepdims=True)
        code = level_code(peak)
        levels = jnp.where(line == number, code, levels)
        keep = jnp.where(lane < turn, usable * pltpu.roll(usable, turn, 1), 0.0) * CODE_TOP
        upscale = keep / level_of(code)
        for side in range(2):
            inverse = lax.rsqrt(power[side] + extra) * keep
            real, imag = corr[side]
            for kind, value in enumerate((real * upscale, real * inverse, imag * inverse)):
                coded = encode(value).reshape(chan_count, lag_rows, chans)
                for k in range(chan_count):
                    out_refs[k][6 * number + 2 * kind + side, :, :] = coded[k]
    for k in range(chan_count):
        out_refs[k][blocks - 1, :, :] = encode(levels)


def sum_kernel(order, scale, where_ref, *refs):
    code_refs, out_refs = refs[: -len(order)], refs[-len(order) :]
    blocks = code_refs[0].shape[0]
    levels = [level_of(decode(codes_ref[blocks - 1])) * scale for codes_ref in code_refs]
    row = lax.broadcasted_iota(jnp.int32, levels[0].shape, 0)
    for k, out_ref in zip(order, out_refs):
        number = where_ref[0] ^ k
        own = [jnp.sum(jnp.where(row == number, level, 0.0), axis=0, keepdims=True) for level in levels]
        for block in range(6):
            total = 0.0
            for codes_ref, level in zip(code_refs, own):
                value = decode(codes_ref[6 * number + block])
                total += value * level if block < 2 else value
            out_ref[block, :, :] = total if block < 2 else total / CODE_TOP


def partners(count):
    return sorted(range(1, count), key=lambda k: (-(k >> 1).bit_count(), k & 1, k)) + [0]


def exchange(pieces, axis):
    count = lax.axis_size(axis)
    return [
        lax.ppermute(piece, axis, [(source, source ^ k) for source in range(count)]) if k else piece
        for k, piece in zip(partners(count), pieces)
    ]


def split_kernel(order, where_ref, spec_ref, *refs):
    out_refs, sems = refs[:-1], refs[-1]
    copies = [
        pltpu.make_async_copy(spec_ref.at[:, where_ref[0] ^ k], out_ref, sems.at[number])
        for number, (k, out_ref) in enumerate(zip(order, out_refs))
    ]
    for copy in copies:
        copy.start()
    for copy in copies:
        copy.wait()


def stack_kernel(windows, offs_ref, where_ref, *refs):
    sums_refs, out_ref = refs[:-1], refs[-1]
    blocks, copies, _, _ = out_ref.shape
    _, lag_rows, chans = sums_refs[0].shape
    total = sum(sums_ref[...] for sums_ref in sums_refs) / windows
    stacks = [
        total[side] * (total[2 + side] * total[2 + side] + total[4 + side] * total[4 + side]) for side in range(2)
    ]
    ahead = offs_ref[where_ref[0]] * (chans // blocks)
    lane = lax.broadcasted_iota(jnp.int32, (1, chans), 1)
    behind = [jnp.where(lane >= ahead, pltpu.roll(stack, ahead, 1), 0.0) for stack in stacks]
    both = jnp.concatenate([stacks[0] + behind[1], stacks[1] + behind[0]], axis=0)
    wide = 2 * lag_rows
    turned = jnp.concatenate([both] * (chans // wide), axis=0).T
    per_block = chans // blocks
    rows = per_block // 2
    for block in range(blocks):
        first = turned[block * per_block : block * per_block + rows, :]
        second = turned[block * per_block + rows : (block + 1) * per_block, :]
        piece = jnp.where(lane < wide, first, second)
        for copy in range(copies):
            out_ref[block, copy, :, :] = piece


def place_kernel(parts_ref, out_ref):
    groups, offset_count, rows, lanes = parts_ref.shape
    half = out_ref.shape[2] // 2
    lag_rows = half // groups
    lane = lax.broadcasted_iota(jnp.int32, (1, lanes), 1)
    mirror = (
        lax.broadcasted_iota(jnp.int32, (half, half), 0) + lax.broadcasted_iota(jnp.int32, (half, half), 1) == half - 1
    ).astype(jnp.float32)
    for number in range(offset_count):
        for part in range(2):
            ahead = jnp.zeros((rows, lanes), jnp.float32)
            back = jnp.zeros((rows, lanes), jnp.float32)
            for group in range(groups):
                piece = parts_ref[group, number]
                here = (lane >= group * lag_rows) & (lane < (group + 1) * lag_rows)
                begin = part * 2 * lag_rows
                ahead = jnp.where(here, pltpu.roll(piece, (group * lag_rows - begin) % lanes, 1), ahead)
                back = jnp.where(here, pltpu.roll(piece, (group * lag_rows - begin - lag_rows) % lanes, 1), back)
            back = jnp.dot(back, mirror, precision=lax.Precision.HIGHEST, preferred_element_type=jnp.float32)
            out_ref[part * rows : (part + 1) * rows, number, 0:half] = back
            out_ref[part * rows : (part + 1) * rows, number, half : 2 * half] = ahead


def window_shards(spectra, quality, offsets):
    chan_count = lax.axis_size("chan")
    tm_count = lax.axis_size("tm")
    _, windows, band, chans = spectra.shape
    freqs = band * chan_count
    half = LAGS // 2
    lag_rows = half // chan_count
    offset_count = offsets.shape[0]
    smem = pl.BlockSpec(memory_space=pltpu.SMEM)
    vmem = pl.BlockSpec(memory_space=pltpu.VMEM)
    params = pltpu.CompilerParams(vmem_limit_bytes=VMEM_LIMIT)
    table = jnp.asarray(half_table(freqs, LAGS).reshape(2, chan_count, lag_rows, freqs))
    chan_index = lax.axis_index("chan").astype(jnp.int32)
    tm_index = lax.axis_index("tm").astype(jnp.int32)
    chan_where, tm_where = chan_index.reshape(1), tm_index.reshape(1)

    chan_order, tm_order = partners(chan_count), partners(tm_count)
    pieces = pl.pallas_call(
        functools.partial(split_kernel, chan_order),
        out_shape=[jax.ShapeDtypeStruct((2, band, chans), spectra.dtype)] * chan_count,
        in_specs=[smem, pl.BlockSpec(memory_space=pltpu.HBM)],
        out_specs=[pl.BlockSpec(memory_space=pl.ANY)] * chan_count,
        scratch_shapes=[pltpu.SemaphoreType.DMA((chan_count,))],
        compiler_params=params,
        name="split_windows",
    )(chan_where, spectra)
    pairs = pl.pallas_call(
        functools.partial(window_kernel, chan_order),
        out_shape=[jax.ShapeDtypeStruct((6 * offset_count + 1, lag_rows, chans), jnp.int16)] * chan_count,
        in_specs=[smem, smem] + [vmem] * (chan_count + 2),
        out_specs=[vmem] * chan_count,
        scratch_shapes=[
            pltpu.VMEM((freqs, chans), jnp.float32),
            pltpu.VMEM((2, freqs, chans), jnp.bfloat16),
            pltpu.VMEM((2, freqs, 2 * chans), jnp.bfloat16),
        ],
        compiler_params=params,
        name="window_pairs",
    )(offsets, chan_where, *exchange(pieces, "chan"), quality, table)
    sums = pl.pallas_call(
        functools.partial(sum_kernel, tm_order, 1.0 / (CODE_TOP * math.sqrt(freqs))),
        out_shape=[jax.ShapeDtypeStruct((6, lag_rows, chans), jnp.float32)] * tm_count,
        in_specs=[smem] + [vmem] * chan_count,
        out_specs=[vmem] * tm_count,
        compiler_params=params,
        name="sum_windows",
    )(tm_where, *exchange(pairs, "chan"))
    pieces = pl.pallas_call(
        functools.partial(stack_kernel, windows * tm_count),
        out_shape=jax.ShapeDtypeStruct((chan_count, tm_count, CH_DEV // 2, chans), jnp.float32),
        in_specs=[smem, smem] + [vmem] * tm_count,
        out_specs=vmem,
        compiler_params=params,
        name="stack_pairs",
    )(offsets, tm_where, *exchange(sums, "tm"))
    shape = (chan_count * tm_count, CH_DEV // 2, chans)
    arrived = lax.all_to_all(pieces.reshape(shape), ("chan", "tm"), 0, 0, tiled=True)
    return pl.pallas_call(
        place_kernel,
        out_shape=jax.ShapeDtypeStruct((CH_DEV, offset_count, LAGS), jnp.float32),
        in_specs=[vmem],
        out_specs=vmem,
        compiler_params=params,
        name="place_lags",
    )(arrived.reshape(chan_count, tm_count, CH_DEV // 2, chans))


def shifted(value, axis, steps):
    count = lax.axis_size(axis)
    leading, last = (max(0, -steps), min(count, count - steps))
    return lax.ppermute(value, axis, [(source, source + steps) for source in range(leading, last)])


def lag_table(freq_count, lag_count):
    freq_index = jnp.arange(freq_count, dtype=jnp.int32)[:, None]
    double_lag = (2 * jnp.arange(lag_count, dtype=jnp.int32) - lag_count + 1)[None, :]
    turns = jnp.mod(freq_index * double_lag, 4 * freq_count)
    angles = turns.astype(jnp.float32) * (2.0 * math.pi / (4 * freq_count))
    cosine = jnp.cos(angles)
    sine = jnp.sin(angles)
    upper = jnp.concatenate([cosine, sine], axis=1)
    lower = jnp.concatenate([-sine, cosine], axis=1)
    return jnp.stack([upper, lower]).astype(jnp.bfloat16)


def whiten_parts(real_part, imag_part, magnitude, channel_level, usable):
    factor = usable.astype(jnp.float32)[:, None, :] / (magnitude + 0.5 * (channel_level + 1e-05))
    return jnp.stack([real_part * factor, imag_part * factor]).astype(jnp.bfloat16)


def cross_parts(own_real, own_imag, far_real, far_imag):
    own_real = own_real.astype(jnp.float32)
    own_imag = own_imag.astype(jnp.float32)
    far_real = far_real.astype(jnp.float32)
    far_imag = far_imag.astype(jnp.float32)
    return jnp.stack(
        [own_real * far_real + own_imag * far_imag, own_imag * far_real - own_real * far_imag]
    ).astype(jnp.bfloat16)


def pair_terms(corr_all):
    lag_count = corr_all.shape[-1] // 2
    real_corr = corr_all[..., :lag_count]
    imag_corr = corr_all[..., lag_count:]
    power = real_corr * real_corr + imag_corr * imag_corr
    mean_power = jnp.mean(power, axis=-1, keepdims=True)
    denominator = jnp.sqrt(power + 0.25 * (mean_power + 1e-06))
    return (
        jnp.sum(real_corr, axis=-3),
        jnp.sum(real_corr / denominator, axis=-3),
        jnp.sum(imag_corr / denominator, axis=-3),
    )


def shards(spectra, quality, offsets):
    chan_count = lax.axis_size("chan")
    tm_count = lax.axis_size("tm")
    levels = chan_count.bit_length() - 1
    table_bf = lag_table(F, LAGS)
    inv_root = 1.0 / math.sqrt(F)
    real_part = spectra[0].astype(jnp.float32)
    imag_part = spectra[1].astype(jnp.float32)
    magnitude = jnp.sqrt(real_part * real_part + imag_part * imag_part)
    band_total = lax.psum(jnp.sum(magnitude, axis=1), "chan")
    channel_level = (band_total / F)[:, None, :]
    whitened = whiten_parts(real_part, imag_part, magnitude, channel_level, quality)
    width_all = whitened.shape[3]
    padded = jnp.pad(whitened, ((0, 0), (0, 0), (0, 0), (0, width_all)))
    crossed_list = []
    for offset_index in range(NOFF):
        partner = lax.dynamic_slice_in_dim(padded, offsets[offset_index] * CH_DEV, width_all, 3)
        crossed_list.append(cross_parts(whitened[0], whitened[1], partner[0], partner[1]))
    crossed = jnp.stack(crossed_list, axis=1)
    corr_all = jnp.einsum(
        "cnwfh,cfl->nwhl",
        lax.all_to_all(crossed, "chan", split_axis=4, concat_axis=3, tiled=True),
        table_bf,
        preferred_element_type=jnp.float32,
    )
    linear_sum, real_sum, imag_sum = pair_terms(corr_all * inv_root)
    totals = lax.psum((linear_sum, real_sum, imag_sum), "tm")
    window_count = W_DEV * tm_count
    linear = totals[0] / window_count
    real_phase = totals[1] / window_count
    imag_phase = totals[2] / window_count
    stacks = jnp.transpose(linear * (real_phase * real_phase + imag_phase * imag_phase), (1, 0, 2))
    reverse_part = stacks
    for bit_index in range(levels):
        step_size = 1 << bit_index
        arrived = shifted(reverse_part, "chan", step_size)
        chosen = offsets // step_size % 2 == 1
        reverse_part = jnp.where(chosen[None, :, None], arrived, reverse_part)
    return stacks + jnp.flip(reverse_part, axis=2)


def solution(mesh):
    chan_count, tm_count = mesh.shape["chan"], mesh.shape["tm"]
    by_window = chan_count == W_DEV and tm_count == NOFF
    return jax.shard_map(
        window_shards if by_window else shards,
        mesh=mesh,
        in_specs=(P(None, "tm", "chan", None), P("tm", None), P()),
        out_specs=P("chan", None, None),
        check_vma=False,
    )
```

```python
import functools
import math

import jax
import jax.numpy as jnp
import numpy as np
from jax import lax
from jax.experimental import pallas as pl
from jax.experimental.pallas import tpu as pltpu
from jax.sharding import PartitionSpec as P

F = 2048
LAGS = 256
NOFF = 4
CH_DEV = 16
W_DEV = 8
VMEM_LIMIT = 48 * 1024 * 1024
CODE_TOP = 32767.0
OCTAVE = 256.0
LOWEST = -110.0


def encode(value):
    return jnp.round(value).astype(jnp.int32).astype(jnp.int16)


def decode(code):
    return code.astype(jnp.int32).astype(jnp.float32)


def level_code(peak):
    return jnp.ceil(jnp.maximum(jnp.log2(jnp.maximum(peak, 1e-30)), LOWEST) * OCTAVE) + 1.0


def level_of(code):
    return jnp.exp2(code * (1.0 / OCTAVE))


def half_table(freq_count, lag_count):
    freq_index = np.arange(freq_count, dtype=np.int64)[None, :]
    double_lag = (2 * np.arange(lag_count // 2, lag_count, dtype=np.int64) - lag_count + 1)[:, None]
    turns = np.mod(freq_index * double_lag, 4 * freq_count).astype(np.float32)
    angles = turns * np.float32(2.0 * math.pi / (4 * freq_count))
    return np.concatenate([np.cos(angles), np.sin(angles)]).astype(jnp.bfloat16)


def window_kernel(order, offs_ref, where_ref, *refs):
    chan_count = len(order)
    spec_refs, (qual_ref, table_ref) = refs[:chan_count], refs[chan_count : chan_count + 2]
    out_refs = refs[chan_count + 2 : 2 * chan_count + 2]
    mag_ref, white_ref, cross_ref = refs[2 * chan_count + 2 :]
    me = where_ref[0]
    _, band, chans = spec_refs[0].shape
    freqs = chan_count * band
    blocks, lag_rows, _ = out_refs[0].shape
    offset_count = offs_ref.shape[0]
    half = chan_count * lag_rows
    step = 64

    total = jnp.zeros((8, chans), jnp.float32)
    for partner, spec_ref in zip(order, spec_refs):
        base = (me ^ partner) * band
        for row in range(0, band, step):
            real = spec_ref[0, row : row + step, :].astype(jnp.float32)
            imag = spec_ref[1, row : row + step, :].astype(jnp.float32)
            square = real * real + imag * imag
            magnitude = square * lax.rsqrt(jnp.maximum(square, 1e-30))
            mag_ref[pl.ds(pl.multiple_of(base + row, step), step), :] = magnitude
            total += jnp.sum(magnitude.reshape(step // 8, 8, chans), axis=0)
    level = jnp.sum(total, axis=0, keepdims=True) * (1.0 / freqs)
    floor = 0.5 * (level + 1e-05)

    for partner, spec_ref in zip(order, spec_refs):
        base = (me ^ partner) * band
        for row in range(0, band, step):
            held = pl.ds(pl.multiple_of(base + row, step), step)
            factor = pl.reciprocal(mag_ref[held, :] + floor, approx=True)
            for part in range(2):
                value = spec_ref[part, row : row + step, :].astype(jnp.float32) * factor
                white_ref[part, held, :] = value.astype(jnp.bfloat16)

    lane = lax.broadcasted_iota(jnp.int32, (1, chans), 1)
    line = lax.broadcasted_iota(jnp.int32, (lag_rows, chans), 0)
    usable = qual_ref[pl.ds(me, 1), :].astype(jnp.float32)
    levels = jnp.zeros((lag_rows, chans), jnp.float32)
    table = jnp.concatenate([table_ref[side, me ^ k] for side in range(2) for k in order], axis=0)
    for number in range(offset_count):
        turn = chans - offs_ref[number] * (chans // chan_count)
        slot = number % 2
        for row in range(0, freqs, step):
            own = [white_ref[part, row : row + step, :] for part in range(2)]
            far_real, far_imag = (pltpu.roll(value, turn, 1).astype(jnp.float32) for value in own)
            own_real, own_imag = (value.astype(jnp.float32) for value in own)
            real = own_real * far_real + own_imag * far_imag
            imag = own_imag * far_real - own_real * far_imag
            cross_ref[slot, row : row + step, 0:chans] = real.astype(jnp.bfloat16)
            cross_ref[slot, row : row + step, chans : 2 * chans] = imag.astype(jnp.bfloat16)
        sums = jnp.dot(table, cross_ref[slot], preferred_element_type=jnp.float32)
        cos_real, sin_real = sums[:half, :chans], sums[half:, :chans]
        cos_imag, sin_imag = sums[:half, chans:], sums[half:, chans:]
        corr = (
            (cos_real - sin_imag, sin_real + cos_imag),
            (cos_real + sin_imag, cos_imag - sin_real),
        )
        power = [real * real + imag * imag for real, imag in corr]
        mean_power = jnp.sum(power[0] + power[1], axis=0, keepdims=True) * (1.0 / (2 * half))
        extra = 0.25 * (mean_power + 1e-06 * freqs)
        peak = jnp.max(jnp.maximum(jnp.abs(corr[0][0]), jnp.abs(corr[1][0])), axis=0, keepdims=True)
        code = level_code(peak)
        levels = jnp.where(line == number, code, levels)
        keep = jnp.where(lane < turn, usable * pltpu.roll(usable, turn, 1), 0.0) * CODE_TOP
        upscale = keep / level_of(code)
        for side in range(2):
            inverse = lax.rsqrt(power[side] + extra) * keep
            real, imag = corr[side]
            for kind, value in enumerate((real * upscale, real * inverse, imag * inverse)):
                coded = encode(value).reshape(chan_count, lag_rows, chans)
                for k in range(chan_count):
                    out_refs[k][6 * number + 2 * kind + side, :, :] = coded[k]
    for k in range(chan_count):
        out_refs[k][blocks - 1, :, :] = encode(levels)


def sum_kernel(order, scale, where_ref, *refs):
    code_refs, out_refs = refs[: -len(order)], refs[-len(order) :]
    blocks = code_refs[0].shape[0]
    levels = [level_of(decode(codes_ref[blocks - 1])) * scale for codes_ref in code_refs]
    row = lax.broadcasted_iota(jnp.int32, levels[0].shape, 0)
    for k, out_ref in zip(order, out_refs):
        number = where_ref[0] ^ k
        own = [jnp.sum(jnp.where(row == number, level, 0.0), axis=0, keepdims=True) for level in levels]
        for block in range(6):
            total = 0.0
            for codes_ref, level in zip(code_refs, own):
                value = decode(codes_ref[6 * number + block])
                total += value * level if block < 2 else value
            out_ref[block, :, :] = total if block < 2 else total / CODE_TOP


def partners(count):
    return sorted(range(1, count), key=lambda k: (-(k >> 1).bit_count(), k & 1, k)) + [0]


def exchange(pieces, axis):
    count = lax.axis_size(axis)
    return [
        lax.ppermute(piece, axis, [(source, source ^ k) for source in range(count)]) if k else piece
        for k, piece in zip(partners(count), pieces)
    ]


def split_kernel(order, where_ref, spec_ref, *refs):
    out_refs, sems = refs[:-1], refs[-1]
    copies = [
        pltpu.make_async_copy(spec_ref.at[:, where_ref[0] ^ k], out_ref, sems.at[number])
        for number, (k, out_ref) in enumerate(zip(order, out_refs))
    ]
    for copy in copies:
        copy.start()
    for copy in copies:
        copy.wait()


def stack_kernel(windows, offs_ref, where_ref, *refs):
    sums_refs, out_ref = refs[:-1], refs[-1]
    blocks, copies, _, _ = out_ref.shape
    _, lag_rows, chans = sums_refs[0].shape
    total = sum(sums_ref[...] for sums_ref in sums_refs) / windows
    stacks = [
        total[side] * (total[2 + side] * total[2 + side] + total[4 + side] * total[4 + side]) for side in range(2)
    ]
    ahead = offs_ref[where_ref[0]] * (chans // blocks)
    lane = lax.broadcasted_iota(jnp.int32, (1, chans), 1)
    behind = [jnp.where(lane >= ahead, pltpu.roll(stack, ahead, 1), 0.0) for stack in stacks]
    both = jnp.concatenate([stacks[0] + behind[1], stacks[1] + behind[0]], axis=0)
    wide = 2 * lag_rows
    turned = jnp.concatenate([both] * (chans // wide), axis=0).T
    per_block = chans // blocks
    rows = per_block // 2
    for block in range(blocks):
        first = turned[block * per_block : block * per_block + rows, :]
        second = turned[block * per_block + rows : (block + 1) * per_block, :]
        piece = jnp.where(lane < wide, first, second)
        for copy in range(copies):
            out_ref[block, copy, :, :] = piece


def place_kernel(parts_ref, out_ref):
    groups, offset_count, rows, lanes = parts_ref.shape
    half = out_ref.shape[2] // 2
    lag_rows = half // groups
    lane = lax.broadcasted_iota(jnp.int32, (1, lanes), 1)
    mirror = (
        lax.broadcasted_iota(jnp.int32, (half, half), 0) + lax.broadcasted_iota(jnp.int32, (half, half), 1) == half - 1
    ).astype(jnp.float32)
    for number in range(offset_count):
        for part in range(2):
            ahead = jnp.zeros((rows, lanes), jnp.float32)
            back = jnp.zeros((rows, lanes), jnp.float32)
            for group in range(groups):
                piece = parts_ref[group, number]
                here = (lane >= group * lag_rows) & (lane < (group + 1) * lag_rows)
                begin = part * 2 * lag_rows
                ahead = jnp.where(here, pltpu.roll(piece, (group * lag_rows - begin) % lanes, 1), ahead)
                back = jnp.where(here, pltpu.roll(piece, (group * lag_rows - begin - lag_rows) % lanes, 1), back)
            back = jnp.dot(back, mirror, precision=lax.Precision.HIGHEST, preferred_element_type=jnp.float32)
            out_ref[part * rows : (part + 1) * rows, number, 0:half] = back
            out_ref[part * rows : (part + 1) * rows, number, half : 2 * half] = ahead


def window_shards(spectra, quality, offsets):
    chan_count = lax.axis_size("chan")
    tm_count = lax.axis_size("tm")
    _, windows, band, chans = spectra.shape
    freqs = band * chan_count
    half = LAGS // 2
    lag_rows = half // chan_count
    offset_count = offsets.shape[0]
    smem = pl.BlockSpec(memory_space=pltpu.SMEM)
    vmem = pl.BlockSpec(memory_space=pltpu.VMEM)
    params = pltpu.CompilerParams(vmem_limit_bytes=VMEM_LIMIT)
    table = jnp.asarray(half_table(freqs, LAGS).reshape(2, chan_count, lag_rows, freqs))
    chan_index = lax.axis_index("chan").astype(jnp.int32)
    tm_index = lax.axis_index("tm").astype(jnp.int32)
    chan_where, tm_where = chan_index.reshape(1), tm_index.reshape(1)

    chan_order, tm_order = partners(chan_count), partners(tm_count)
    pieces = pl.pallas_call(
        functools.partial(split_kernel, chan_order),
        out_shape=[jax.ShapeDtypeStruct((2, band, chans), spectra.dtype)] * chan_count,
        in_specs=[smem, pl.BlockSpec(memory_space=pltpu.HBM)],
        out_specs=[pl.BlockSpec(memory_space=pl.ANY)] * chan_count,
        scratch_shapes=[pltpu.SemaphoreType.DMA((chan_count,))],
        compiler_params=params,
        name="split_windows",
    )(chan_where, pltpu.with_memory_space_constraint(spectra, pltpu.HBM))
    pairs = pl.pallas_call(
        functools.partial(window_kernel, chan_order),
        out_shape=[jax.ShapeDtypeStruct((6 * offset_count + 1, lag_rows, chans), jnp.int16)] * chan_count,
        in_specs=[smem, smem] + [vmem] * (chan_count + 2),
        out_specs=[vmem] * chan_count,
        scratch_shapes=[
            pltpu.VMEM((freqs, chans), jnp.float32),
            pltpu.VMEM((2, freqs, chans), jnp.bfloat16),
            pltpu.VMEM((2, freqs, 2 * chans), jnp.bfloat16),
        ],
        compiler_params=params,
        name="window_pairs",
    )(offsets, chan_where, *exchange(pieces, "chan"), quality, table)
    sums = pl.pallas_call(
        functools.partial(sum_kernel, tm_order, 1.0 / (CODE_TOP * math.sqrt(freqs))),
        out_shape=[jax.ShapeDtypeStruct((6, lag_rows, chans), jnp.float32)] * tm_count,
        in_specs=[smem] + [vmem] * chan_count,
        out_specs=[vmem] * tm_count,
        compiler_params=params,
        name="sum_windows",
    )(tm_where, *exchange(pairs, "chan"))
    pieces = pl.pallas_call(
        functools.partial(stack_kernel, windows * tm_count),
        out_shape=jax.ShapeDtypeStruct((chan_count, tm_count, CH_DEV // 2, chans), jnp.float32),
        in_specs=[smem, smem] + [vmem] * tm_count,
        out_specs=vmem,
        compiler_params=params,
        name="stack_pairs",
    )(offsets, tm_where, *exchange(sums, "tm"))
    shape = (chan_count * tm_count, CH_DEV // 2, chans)
    arrived = lax.all_to_all(pieces.reshape(shape), ("chan", "tm"), 0, 0, tiled=True)
    return pl.pallas_call(
        place_kernel,
        out_shape=jax.ShapeDtypeStruct((CH_DEV, offset_count, LAGS), jnp.float32),
        in_specs=[vmem],
        out_specs=vmem,
        compiler_params=params,
        name="place_lags",
    )(arrived.reshape(chan_count, tm_count, CH_DEV // 2, chans))


def shifted(value, axis, steps):
    count = lax.axis_size(axis)
    leading, last = (max(0, -steps), min(count, count - steps))
    return lax.ppermute(value, axis, [(source, source + steps) for source in range(leading, last)])


def lag_table(freq_count, lag_count):
    freq_index = jnp.arange(freq_count, dtype=jnp.int32)[:, None]
    double_lag = (2 * jnp.arange(lag_count, dtype=jnp.int32) - lag_count + 1)[None, :]
    turns = jnp.mod(freq_index * double_lag, 4 * freq_count)
    angles = turns.astype(jnp.float32) * (2.0 * math.pi / (4 * freq_count))
    cosine = jnp.cos(angles)
    sine = jnp.sin(angles)
    upper = jnp.concatenate([cosine, sine], axis=1)
    lower = jnp.concatenate([-sine, cosine], axis=1)
    return jnp.stack([upper, lower]).astype(jnp.bfloat16)


def whiten_parts(real_part, imag_part, magnitude, channel_level, usable):
    factor = usable.astype(jnp.float32)[:, None, :] / (magnitude + 0.5 * (channel_level + 1e-05))
    return jnp.stack([real_part * factor, imag_part * factor]).astype(jnp.bfloat16)


def cross_parts(own_real, own_imag, far_real, far_imag):
    own_real = own_real.astype(jnp.float32)
    own_imag = own_imag.astype(jnp.float32)
    far_real = far_real.astype(jnp.float32)
    far_imag = far_imag.astype(jnp.float32)
    return jnp.stack(
        [own_real * far_real + own_imag * far_imag, own_imag * far_real - own_real * far_imag]
    ).astype(jnp.bfloat16)


def pair_terms(corr_all):
    lag_count = corr_all.shape[-1] // 2
    real_corr = corr_all[..., :lag_count]
    imag_corr = corr_all[..., lag_count:]
    power = real_corr * real_corr + imag_corr * imag_corr
    mean_power = jnp.mean(power, axis=-1, keepdims=True)
    denominator = jnp.sqrt(power + 0.25 * (mean_power + 1e-06))
    return (
        jnp.sum(real_corr, axis=-3),
        jnp.sum(real_corr / denominator, axis=-3),
        jnp.sum(imag_corr / denominator, axis=-3),
    )


def shards(spectra, quality, offsets):
    chan_count = lax.axis_size("chan")
    tm_count = lax.axis_size("tm")
    levels = chan_count.bit_length() - 1
    table_bf = lag_table(F, LAGS)
    inv_root = 1.0 / math.sqrt(F)
    real_part = spectra[0].astype(jnp.float32)
    imag_part = spectra[1].astype(jnp.float32)
    magnitude = jnp.sqrt(real_part * real_part + imag_part * imag_part)
    band_total = lax.psum(jnp.sum(magnitude, axis=1), "chan")
    channel_level = (band_total / F)[:, None, :]
    whitened = whiten_parts(real_part, imag_part, magnitude, channel_level, quality)
    width_all = whitened.shape[3]
    padded = jnp.pad(whitened, ((0, 0), (0, 0), (0, 0), (0, width_all)))
    crossed_list = []
    for offset_index in range(NOFF):
        partner = lax.dynamic_slice_in_dim(padded, offsets[offset_index] * CH_DEV, width_all, 3)
        crossed_list.append(cross_parts(whitened[0], whitened[1], partner[0], partner[1]))
    crossed = jnp.stack(crossed_list, axis=1)
    corr_all = jnp.einsum(
        "cnwfh,cfl->nwhl",
        lax.all_to_all(crossed, "chan", split_axis=4, concat_axis=3, tiled=True),
        table_bf,
        preferred_element_type=jnp.float32,
    )
    linear_sum, real_sum, imag_sum = pair_terms(corr_all * inv_root)
    totals = lax.psum((linear_sum, real_sum, imag_sum), "tm")
    window_count = W_DEV * tm_count
    linear = totals[0] / window_count
    real_phase = totals[1] / window_count
    imag_phase = totals[2] / window_count
    stacks = jnp.transpose(linear * (real_phase * real_phase + imag_phase * imag_phase), (1, 0, 2))
    reverse_part = stacks
    for bit_index in range(levels):
        step_size = 1 << bit_index
        arrived = shifted(reverse_part, "chan", step_size)
        chosen = offsets // step_size % 2 == 1
        reverse_part = jnp.where(chosen[None, :, None], arrived, reverse_part)
    return stacks + jnp.flip(reverse_part, axis=2)


def solution(mesh):
    chan_count, tm_count = mesh.shape["chan"], mesh.shape["tm"]
    by_window = chan_count == W_DEV and tm_count == NOFF
    return jax.shard_map(
        window_shards if by_window else shards,
        mesh=mesh,
        in_specs=(P(None, "tm", "chan", None), P("tm", None), P()),
        out_specs=P("chan", None, None),
        check_vma=False,
    )
```

```python
import functools
import math

import jax
import jax.numpy as jnp
import numpy as np
from jax import lax
from jax.experimental import pallas as pl
from jax.experimental.pallas import tpu as pltpu
from jax.sharding import PartitionSpec as P

F = 2048
LAGS = 256
NOFF = 4
CH_DEV = 16
W_DEV = 8
VMEM_LIMIT = 48 * 1024 * 1024
CODE_TOP = 32767.0
OCTAVE = 256.0
LOWEST = -110.0


def encode(value):
    return jnp.round(value).astype(jnp.int32).astype(jnp.int16)


def decode(code):
    return code.astype(jnp.int32).astype(jnp.float32)


def level_code(peak):
    return jnp.ceil(jnp.maximum(jnp.log2(jnp.maximum(peak, 1e-30)), LOWEST) * OCTAVE) + 1.0


def level_of(code):
    return jnp.exp2(code * (1.0 / OCTAVE))


def half_table(freq_count, lag_count):
    freq_index = np.arange(freq_count, dtype=np.int64)[None, :]
    double_lag = (2 * np.arange(lag_count // 2, lag_count, dtype=np.int64) - lag_count + 1)[:, None]
    turns = np.mod(freq_index * double_lag, 4 * freq_count).astype(np.float32)
    angles = turns * np.float32(2.0 * math.pi / (4 * freq_count))
    return np.concatenate([np.cos(angles), np.sin(angles)]).astype(jnp.bfloat16)


def window_kernel(order, offs_ref, where_ref, *refs):
    chan_count = len(order)
    spec_refs, (qual_ref, table_ref) = refs[:chan_count], refs[chan_count : chan_count + 2]
    out_refs = refs[chan_count + 2 : 2 * chan_count + 2]
    mag_ref, white_ref, cross_ref = refs[2 * chan_count + 2 :]
    me = where_ref[0]
    _, band, chans = spec_refs[0].shape
    freqs = chan_count * band
    blocks, block, half = out_refs[0].shape
    offset_count = offs_ref.shape[0]
    step = 64

    total = jnp.zeros((8, chans), jnp.float32)
    for number, spec_ref in enumerate(spec_refs):
        for row in range(0, band, step):
            real = spec_ref[0, row : row + step, :].astype(jnp.float32)
            imag = spec_ref[1, row : row + step, :].astype(jnp.float32)
            square = real * real + imag * imag
            magnitude = square * lax.rsqrt(jnp.maximum(square, 1e-30))
            mag_ref[number * band + row : number * band + row + step, :] = magnitude
            total += jnp.sum(magnitude.reshape(step // 8, 8, chans), axis=0)
    level = jnp.sum(total, axis=0, keepdims=True) * (1.0 / freqs)
    floor = 0.5 * (level + 1e-05)
    usable = qual_ref[pl.ds(me, 1), :].astype(jnp.float32)

    width = 128
    for number, spec_ref in enumerate(spec_refs):
        for row in range(0, band, width):
            start = number * band + row
            factor = usable * pl.reciprocal(mag_ref[start : start + width, :] + floor, approx=True)
            for part in range(2):
                value = spec_ref[part, row : row + width, :].astype(jnp.float32) * factor
                white_ref[part, 0:chans, start : start + width] = value.astype(jnp.bfloat16).T
    white_ref[:, chans:, :] = jnp.zeros((2, white_ref.shape[1] - chans, freqs), jnp.bfloat16)

    lane = lax.broadcasted_iota(jnp.int32, (1, half), 1)
    levels = jnp.zeros((chans, half), jnp.float32)
    table = jnp.concatenate([table_ref[me ^ k] for k in order], axis=0)
    span = min(512, freqs)
    for number in range(offset_count):
        slot = number % 2
        for place, k in enumerate(order):
            own_rows = pl.ds(pl.multiple_of((me ^ k) * block, block), block)
            far_rows = pl.ds(pl.multiple_of(((me ^ k) + offs_ref[number]) * block, block), block)
            for start in range(0, freqs, span):
                lanes = slice(start, start + span)
                own_real, own_imag = (white_ref[part, own_rows, lanes].astype(jnp.float32) for part in range(2))
                far_real, far_imag = (white_ref[part, far_rows, lanes].astype(jnp.float32) for part in range(2))
                real = own_real * far_real + own_imag * far_imag
                imag = own_imag * far_real - own_real * far_imag
                cross_ref[slot, place * block : (place + 1) * block, lanes] = real.astype(jnp.bfloat16)
                cross_ref[slot, chans + place * block : chans + (place + 1) * block, lanes] = imag.astype(jnp.bfloat16)
        sums = jnp.dot(cross_ref[slot], table, preferred_element_type=jnp.float32)
        cos_real, sin_real = sums[:chans, :half], sums[:chans, half:]
        cos_imag, sin_imag = sums[chans:, :half], sums[chans:, half:]
        corr = (
            (cos_real - sin_imag, sin_real + cos_imag),
            (cos_real + sin_imag, cos_imag - sin_real),
        )
        power = [real * real + imag * imag for real, imag in corr]
        mean_power = jnp.sum(power[0] + power[1], axis=1, keepdims=True) * (1.0 / (2 * half))
        extra = 0.25 * (mean_power + 1e-06 * freqs)
        peak = jnp.max(jnp.maximum(jnp.abs(corr[0][0]), jnp.abs(corr[1][0])), axis=1, keepdims=True)
        code = level_code(peak)
        levels = jnp.where(lane == number, code, levels)
        upscale = CODE_TOP / level_of(code)
        for side in range(2):
            inverse = lax.rsqrt(power[side] + extra) * CODE_TOP
            real, imag = corr[side]
            for kind, value in enumerate((real * upscale, real * inverse, imag * inverse)):
                coded = encode(value)
                for place, out_ref in enumerate(out_refs):
                    out_ref[6 * number + 2 * kind + side, :, :] = coded[place * block : (place + 1) * block]
    for place, out_ref in enumerate(out_refs):
        out_ref[blocks - 1, :, :] = encode(levels[place * block : (place + 1) * block])


def sum_kernel(order, scale, where_ref, *refs):
    code_refs, out_refs = refs[: -len(order)], refs[-len(order) :]
    blocks, _, half = code_refs[0].shape
    levels = [level_of(decode(codes_ref[blocks - 1])) * scale for codes_ref in code_refs]
    lane = lax.broadcasted_iota(jnp.int32, (1, half), 1)
    for k, out_ref in zip(order, out_refs):
        number = where_ref[0] ^ k
        own = [jnp.sum(jnp.where(lane == number, level, 0.0), axis=1, keepdims=True) for level in levels]
        linear = [
            sum(decode(codes_ref[6 * number + side]) * level for codes_ref, level in zip(code_refs, own))
            for side in range(2)
        ]
        peak = jnp.max(jnp.maximum(jnp.abs(linear[0]), jnp.abs(linear[1])), axis=1, keepdims=True)
        code = level_code(jnp.broadcast_to(peak, linear[0].shape))
        upscale = CODE_TOP / level_of(code)
        for side in range(2):
            out_ref[side, :, :] = encode(linear[side] * upscale)
        for part in range(2, 6):
            total = sum(decode(codes_ref[6 * number + part]) for codes_ref in code_refs)
            out_ref[part, :, :] = encode(total * (1.0 / len(code_refs)))
        out_ref[6, :, :] = encode(code)


def partners(count):
    return sorted(range(1, count), key=lambda k: (-(k >> 1).bit_count(), k & 1, k)) + [0]


def exchange(pieces, axis):
    count = lax.axis_size(axis)
    return [
        lax.ppermute(piece, axis, [(source, source ^ k) for source in range(count)]) if k else piece
        for k, piece in zip(partners(count), pieces)
    ]


def split_kernel(order, where_ref, spec_ref, *refs):
    out_refs, sems = refs[:-1], refs[-1]
    copies = [
        pltpu.make_async_copy(spec_ref.at[:, where_ref[0] ^ k], out_ref, sems.at[number])
        for number, (k, out_ref) in enumerate(zip(order, out_refs))
    ]
    for copy in copies:
        copy.start()
    for copy in copies:
        copy.wait()


def stack_kernel(windows, *refs):
    sums_refs, out_ref = refs[:-1], refs[-1]
    per_sum = windows // len(sums_refs)
    levels = [level_of(decode(sums_ref[6])) * (1.0 / (CODE_TOP * windows)) for sums_ref in sums_refs]
    for side in range(2):
        linear = sum(decode(sums_ref[side]) * level for sums_ref, level in zip(sums_refs, levels))
        real, imag = (
            sum(decode(sums_ref[part + side]) for sums_ref in sums_refs) * (per_sum / (CODE_TOP * windows))
            for part in (2, 4)
        )
        out_ref[side, :, :] = linear * (real * real + imag * imag)


def pair_kernel(offs_ref, where_ref, stack_ref, *refs):
    shift_refs, out_ref = refs[:-1], refs[-1]
    half = stack_ref.shape[2]
    ahead = offs_ref[where_ref[0]]
    behind = [
        sum(jnp.where(ahead == number + 1, shift_ref[side], 0.0) for number, shift_ref in enumerate(shift_refs))
        for side in range(2)
    ]
    mirror = (
        lax.broadcasted_iota(jnp.int32, (half, half), 0) + lax.broadcasted_iota(jnp.int32, (half, half), 1) == half - 1
    ).astype(jnp.float32)
    back = stack_ref[1] + behind[0]
    out_ref[:, 0:half] = jnp.dot(back, mirror, precision=lax.Precision.HIGHEST, preferred_element_type=jnp.float32)
    out_ref[:, half : 2 * half] = stack_ref[0] + behind[1]


def place_kernel(order, where_ref, *refs):
    part_refs, out_ref = refs[:-1], refs[-1]
    for number in range(out_ref.shape[1]):
        out_ref[:, number, :] = sum(
            jnp.where(where_ref[0] ^ k == number, part_ref[...], 0.0) for k, part_ref in zip(order, part_refs)
        )


def window_shards(spectra, quality, offsets):
    chan_count = lax.axis_size("chan")
    tm_count = lax.axis_size("tm")
    _, windows, band, chans = spectra.shape
    freqs = band * chan_count
    half = LAGS // 2
    block = chans // chan_count
    reach = chan_count // 2
    offset_count = offsets.shape[0]
    smem = pl.BlockSpec(memory_space=pltpu.SMEM)
    vmem = pl.BlockSpec(memory_space=pltpu.VMEM)
    params = pltpu.CompilerParams(vmem_limit_bytes=VMEM_LIMIT)
    table = jnp.asarray(half_table(freqs, LAGS).T.reshape(chan_count, band, LAGS))
    chan_where = lax.axis_index("chan").astype(jnp.int32).reshape(1)
    tm_where = lax.axis_index("tm").astype(jnp.int32).reshape(1)
    chan_order, tm_order = partners(chan_count), partners(tm_count)

    pieces = pl.pallas_call(
        functools.partial(split_kernel, chan_order),
        out_shape=[jax.ShapeDtypeStruct((2, band, chans), spectra.dtype)] * chan_count,
        in_specs=[smem, pl.BlockSpec(memory_space=pltpu.HBM)],
        out_specs=[pl.BlockSpec(memory_space=pl.ANY)] * chan_count,
        scratch_shapes=[pltpu.SemaphoreType.DMA((chan_count,))],
        compiler_params=params,
        name="split_windows",
    )(chan_where, pltpu.with_memory_space_constraint(spectra, pltpu.HBM))
    pairs = pl.pallas_call(
        functools.partial(window_kernel, chan_order),
        out_shape=[jax.ShapeDtypeStruct((6 * offset_count + 1, block, half), jnp.int16)] * chan_count,
        in_specs=[smem, smem] + [vmem] * (chan_count + 2),
        out_specs=[vmem] * chan_count,
        scratch_shapes=[
            pltpu.VMEM((freqs, chans), jnp.float32),
            pltpu.VMEM((2, chans + reach * block, freqs), jnp.bfloat16),
            pltpu.VMEM((2, 2 * chans, freqs), jnp.bfloat16),
        ],
        compiler_params=params,
        name="window_pairs",
    )(offsets, chan_where, *exchange(pieces, "chan"), quality, table)
    sums = pl.pallas_call(
        functools.partial(sum_kernel, tm_order, 1.0 / (CODE_TOP * math.sqrt(freqs))),
        out_shape=[jax.ShapeDtypeStruct((7, block, half), jnp.int16)] * tm_count,
        in_specs=[smem] + [vmem] * chan_count,
        out_specs=[vmem] * tm_count,
        compiler_params=params,
        name="sum_windows",
    )(tm_where, *exchange(pairs, "chan"))
    stacks = pl.pallas_call(
        functools.partial(stack_kernel, windows * tm_count),
        out_shape=jax.ShapeDtypeStruct((2, block, half), jnp.float32),
        in_specs=[vmem] * tm_count,
        out_specs=vmem,
        compiler_params=params,
        name="stack_pairs",
    )(*exchange(sums, "tm"))
    shifts = [shifted(stacks, "chan", steps) for steps in range(1, reach + 1)]
    gathers = pl.pallas_call(
        pair_kernel,
        out_shape=jax.ShapeDtypeStruct((block, LAGS), jnp.float32),
        in_specs=[smem, smem] + [vmem] * (reach + 1),
        out_specs=vmem,
        compiler_params=params,
        name="add_reverse",
    )(offsets, tm_where, stacks, *shifts)
    return pl.pallas_call(
        functools.partial(place_kernel, tm_order),
        out_shape=jax.ShapeDtypeStruct((block, offset_count, LAGS), jnp.float32),
        in_specs=[smem] + [vmem] * tm_count,
        out_specs=vmem,
        compiler_params=params,
        name="place_offsets",
    )(tm_where, *exchange([gathers] * tm_count, "tm"))


def shifted(value, axis, steps):
    count = lax.axis_size(axis)
    leading, last = (max(0, -steps), min(count, count - steps))
    return lax.ppermute(value, axis, [(source, source + steps) for source in range(leading, last)])


def lag_table(freq_count, lag_count):
    freq_index = jnp.arange(freq_count, dtype=jnp.int32)[:, None]
    double_lag = (2 * jnp.arange(lag_count, dtype=jnp.int32) - lag_count + 1)[None, :]
    turns = jnp.mod(freq_index * double_lag, 4 * freq_count)
    angles = turns.astype(jnp.float32) * (2.0 * math.pi / (4 * freq_count))
    cosine = jnp.cos(angles)
    sine = jnp.sin(angles)
    upper = jnp.concatenate([cosine, sine], axis=1)
    lower = jnp.concatenate([-sine, cosine], axis=1)
    return jnp.stack([upper, lower]).astype(jnp.bfloat16)


def whiten_parts(real_part, imag_part, magnitude, channel_level, usable):
    factor = usable.astype(jnp.float32)[:, None, :] / (magnitude + 0.5 * (channel_level + 1e-05))
    return jnp.stack([real_part * factor, imag_part * factor]).astype(jnp.bfloat16)


def cross_parts(own_real, own_imag, far_real, far_imag):
    own_real = own_real.astype(jnp.float32)
    own_imag = own_imag.astype(jnp.float32)
    far_real = far_real.astype(jnp.float32)
    far_imag = far_imag.astype(jnp.float32)
    return jnp.stack(
        [own_real * far_real + own_imag * far_imag, own_imag * far_real - own_real * far_imag]
    ).astype(jnp.bfloat16)


def pair_terms(corr_all):
    lag_count = corr_all.shape[-1] // 2
    real_corr = corr_all[..., :lag_count]
    imag_corr = corr_all[..., lag_count:]
    power = real_corr * real_corr + imag_corr * imag_corr
    mean_power = jnp.mean(power, axis=-1, keepdims=True)
    denominator = jnp.sqrt(power + 0.25 * (mean_power + 1e-06))
    return (
        jnp.sum(real_corr, axis=-3),
        jnp.sum(real_corr / denominator, axis=-3),
        jnp.sum(imag_corr / denominator, axis=-3),
    )


def shards(spectra, quality, offsets):
    chan_count = lax.axis_size("chan")
    tm_count = lax.axis_size("tm")
    levels = chan_count.bit_length() - 1
    table_bf = lag_table(F, LAGS)
    inv_root = 1.0 / math.sqrt(F)
    real_part = spectra[0].astype(jnp.float32)
    imag_part = spectra[1].astype(jnp.float32)
    magnitude = jnp.sqrt(real_part * real_part + imag_part * imag_part)
    band_total = lax.psum(jnp.sum(magnitude, axis=1), "chan")
    channel_level = (band_total / F)[:, None, :]
    whitened = whiten_parts(real_part, imag_part, magnitude, channel_level, quality)
    width_all = whitened.shape[3]
    padded = jnp.pad(whitened, ((0, 0), (0, 0), (0, 0), (0, width_all)))
    crossed_list = []
    for offset_index in range(NOFF):
        partner = lax.dynamic_slice_in_dim(padded, offsets[offset_index] * CH_DEV, width_all, 3)
        crossed_list.append(cross_parts(whitened[0], whitened[1], partner[0], partner[1]))
    crossed = jnp.stack(crossed_list, axis=1)
    corr_all = jnp.einsum(
        "cnwfh,cfl->nwhl",
        lax.all_to_all(crossed, "chan", split_axis=4, concat_axis=3, tiled=True),
        table_bf,
        preferred_element_type=jnp.float32,
    )
    linear_sum, real_sum, imag_sum = pair_terms(corr_all * inv_root)
    totals = lax.psum((linear_sum, real_sum, imag_sum), "tm")
    window_count = W_DEV * tm_count
    linear = totals[0] / window_count
    real_phase = totals[1] / window_count
    imag_phase = totals[2] / window_count
    stacks = jnp.transpose(linear * (real_phase * real_phase + imag_phase * imag_phase), (1, 0, 2))
    reverse_part = stacks
    for bit_index in range(levels):
        step_size = 1 << bit_index
        arrived = shifted(reverse_part, "chan", step_size)
        chosen = offsets // step_size % 2 == 1
        reverse_part = jnp.where(chosen[None, :, None], arrived, reverse_part)
    return stacks + jnp.flip(reverse_part, axis=2)


def solution(mesh):
    chan_count, tm_count = mesh.shape["chan"], mesh.shape["tm"]
    by_window = chan_count == W_DEV and tm_count == NOFF
    return jax.shard_map(
        window_shards if by_window else shards,
        mesh=mesh,
        in_specs=(P(None, "tm", "chan", None), P("tm", None), P()),
        out_specs=P("chan", None, None),
        check_vma=False,
    )
```

```python
import functools
import math

import jax
import jax.numpy as jnp
import numpy as np
from jax import lax
from jax.experimental import pallas as pl
from jax.experimental.pallas import tpu as pltpu
from jax.sharding import PartitionSpec as P

F = 2048
LAGS = 256
NOFF = 4
CH_DEV = 16
W_DEV = 8
VMEM_LIMIT = 48 * 1024 * 1024
CODE_TOP = 32767.0
OCTAVE = 256.0
LOWEST = -110.0


def encode(value):
    return jnp.round(value).astype(jnp.int32).astype(jnp.int16)


def decode(code):
    return code.astype(jnp.int32).astype(jnp.float32)


def level_code(peak):
    return jnp.ceil(jnp.maximum(jnp.log2(jnp.maximum(peak, 1e-30)), LOWEST) * OCTAVE) + 1.0


def level_of(code):
    return jnp.exp2(code * (1.0 / OCTAVE))


def half_table(freq_count, lag_count):
    freq_index = np.arange(freq_count, dtype=np.int64)[None, :]
    double_lag = (2 * np.arange(lag_count // 2, lag_count, dtype=np.int64) - lag_count + 1)[:, None]
    turns = np.mod(freq_index * double_lag, 4 * freq_count).astype(np.float32)
    angles = turns * np.float32(2.0 * math.pi / (4 * freq_count))
    return np.concatenate([np.cos(angles), np.sin(angles)]).astype(jnp.bfloat16)


def window_kernel(order, offs_ref, where_ref, *refs):
    chan_count = len(order)
    spec_refs, (qual_ref, table_ref) = refs[:chan_count], refs[chan_count : chan_count + 2]
    out_refs = refs[chan_count + 2 : 2 * chan_count + 2]
    mag_ref, white_ref, cross_ref = refs[2 * chan_count + 2 :]
    me = where_ref[0]
    _, band, chans = spec_refs[0].shape
    freqs = chan_count * band
    blocks, lag_rows, _ = out_refs[0].shape
    offset_count = offs_ref.shape[0]
    half = chan_count * lag_rows
    step = 64

    total = jnp.zeros((8, chans), jnp.float32)
    for partner, spec_ref in zip(order, spec_refs):
        base = (me ^ partner) * band
        for row in range(0, band, step):
            real = spec_ref[0, row : row + step, :].astype(jnp.float32)
            imag = spec_ref[1, row : row + step, :].astype(jnp.float32)
            square = real * real + imag * imag
            magnitude = square * lax.rsqrt(jnp.maximum(square, 1e-30))
            mag_ref[pl.ds(pl.multiple_of(base + row, step), step), :] = magnitude
            total += jnp.sum(magnitude.reshape(step // 8, 8, chans), axis=0)
    level = jnp.sum(total, axis=0, keepdims=True) * (1.0 / freqs)
    floor = 0.5 * (level + 1e-05)

    for partner, spec_ref in zip(order, spec_refs):
        base = (me ^ partner) * band
        for row in range(0, band, step):
            held = pl.ds(pl.multiple_of(base + row, step), step)
            factor = pl.reciprocal(mag_ref[held, :] + floor, approx=True)
            for part in range(2):
                value = spec_ref[part, row : row + step, :].astype(jnp.float32) * factor
                white_ref[part, held, :] = value.astype(jnp.bfloat16)

    lane = lax.broadcasted_iota(jnp.int32, (1, chans), 1)
    line = lax.broadcasted_iota(jnp.int32, (lag_rows, chans), 0)
    usable = qual_ref[pl.ds(me, 1), :].astype(jnp.float32)
    levels = jnp.zeros((lag_rows, chans), jnp.float32)
    table = jnp.concatenate([table_ref[side, me ^ k] for side in range(2) for k in order], axis=0)
    for number in range(offset_count):
        turn = chans - offs_ref[number] * (chans // chan_count)
        slot = number % 2
        for row in range(0, freqs, step):
            own = [white_ref[part, row : row + step, :] for part in range(2)]
            far_real, far_imag = (pltpu.roll(value, turn, 1).astype(jnp.float32) for value in own)
            own_real, own_imag = (value.astype(jnp.float32) for value in own)
            real = own_real * far_real + own_imag * far_imag
            imag = own_imag * far_real - own_real * far_imag
            cross_ref[slot, row : row + step, 0:chans] = real.astype(jnp.bfloat16)
            cross_ref[slot, row : row + step, chans : 2 * chans] = imag.astype(jnp.bfloat16)
        sums = jnp.dot(table, cross_ref[slot], preferred_element_type=jnp.float32)
        cos_real, sin_real = sums[:half, :chans], sums[half:, :chans]
        cos_imag, sin_imag = sums[:half, chans:], sums[half:, chans:]
        corr = (
            (cos_real - sin_imag, sin_real + cos_imag),
            (cos_real + sin_imag, cos_imag - sin_real),
        )
        power = [real * real + imag * imag for real, imag in corr]
        mean_power = jnp.sum(power[0] + power[1], axis=0, keepdims=True) * (1.0 / (2 * half))
        extra = 0.25 * (mean_power + 1e-06 * freqs)
        peak = jnp.max(jnp.maximum(jnp.abs(corr[0][0]), jnp.abs(corr[1][0])), axis=0, keepdims=True)
        code = level_code(peak)
        levels = jnp.where(line == number, code, levels)
        keep = jnp.where(lane < turn, usable * pltpu.roll(usable, turn, 1), 0.0) * CODE_TOP
        upscale = keep / level_of(code)
        for side in range(2):
            inverse = lax.rsqrt(power[side] + extra) * keep
            real, imag = corr[side]
            for kind, value in enumerate((real * upscale, real * inverse, imag * inverse)):
                coded = encode(value).reshape(chan_count, lag_rows, chans)
                for k in range(chan_count):
                    out_refs[k][6 * number + 2 * kind + side, :, :] = coded[k]
    for k in range(chan_count):
        out_refs[k][blocks - 1, :, :] = encode(levels)


def sum_kernel(order, scale, where_ref, *refs):
    code_refs, out_refs = refs[: -len(order)], refs[-len(order) :]
    blocks = code_refs[0].shape[0]
    levels = [level_of(decode(codes_ref[blocks - 1])) * scale for codes_ref in code_refs]
    line = lax.broadcasted_iota(jnp.int32, levels[0].shape, 0)
    for k, out_ref in zip(order, out_refs):
        number = where_ref[0] ^ k
        own = [jnp.sum(jnp.where(line == number, level, 0.0), axis=0, keepdims=True) for level in levels]
        linear = [
            sum(decode(codes_ref[6 * number + side]) * level for codes_ref, level in zip(code_refs, own))
            for side in range(2)
        ]
        peak = jnp.max(jnp.maximum(jnp.abs(linear[0]), jnp.abs(linear[1])), axis=0, keepdims=True)
        code = level_code(jnp.broadcast_to(peak, linear[0].shape))
        upscale = CODE_TOP / level_of(code)
        for side in range(2):
            out_ref[side, :, :] = encode(linear[side] * upscale)
        for part in range(2, 6):
            total = sum(decode(codes_ref[6 * number + part]) for codes_ref in code_refs)
            out_ref[part, :, :] = encode(total * (1.0 / len(code_refs)))
        out_ref[6, :, :] = encode(code)


def partners(count):
    return sorted(range(1, count), key=lambda k: (-(k >> 1).bit_count(), k & 1, k)) + [0]


def exchange(pieces, axis):
    count = lax.axis_size(axis)
    return [
        lax.ppermute(piece, axis, [(source, source ^ k) for source in range(count)]) if k else piece
        for k, piece in zip(partners(count), pieces)
    ]


def split_kernel(order, where_ref, spec_ref, *refs):
    out_refs, sems = refs[:-1], refs[-1]
    copies = [
        pltpu.make_async_copy(spec_ref.at[:, where_ref[0] ^ k], out_ref, sems.at[number])
        for number, (k, out_ref) in enumerate(zip(order, out_refs))
    ]
    for copy in copies:
        copy.start()
    for copy in copies:
        copy.wait()


def stack_kernel(windows, offs_ref, where_ref, *refs):
    sums_refs, out_ref = refs[:-1], refs[-1]
    blocks, copies, rows, _ = out_ref.shape
    _, lag_rows, chans = sums_refs[0].shape
    per_sum = windows // len(sums_refs)
    levels = [level_of(decode(sums_ref[6])) * (1.0 / (CODE_TOP * windows)) for sums_ref in sums_refs]
    stacks = []
    for side in range(2):
        linear = sum(decode(sums_ref[side]) * level for sums_ref, level in zip(sums_refs, levels))
        real, imag = (
            sum(decode(sums_ref[part + side]) for sums_ref in sums_refs) * (per_sum / (CODE_TOP * windows))
            for part in (2, 4)
        )
        stacks.append(linear * (real * real + imag * imag))
    ahead = offs_ref[where_ref[0]] * (chans // blocks)
    lane = lax.broadcasted_iota(jnp.int32, (1, chans), 1)
    behind = [jnp.where(lane >= ahead, pltpu.roll(stack, ahead, 1), 0.0) for stack in stacks]
    back = stacks[1] + behind[0]
    both = jnp.concatenate(
        [stacks[0] + behind[1]] + [back[row : row + 1, :] for row in reversed(range(lag_rows))], axis=0
    )
    wide = 2 * lag_rows
    parts = chans // wide
    turned = jnp.concatenate([both] * parts, axis=0).T
    per_block = chans // blocks
    for block in range(blocks):
        piece = jnp.zeros((rows, chans), jnp.float32)
        for part in range(parts):
            begin = block * per_block + part * rows
            piece = jnp.where(lane // wide == part, turned[begin : begin + rows, :], piece)
        for copy in range(copies):
            out_ref[block, copy, :, :] = piece


def place_kernel(parts_ref, out_ref):
    groups, offset_count, rows, lanes = parts_ref.shape
    half = out_ref.shape[2] // 2
    lag_rows = half // groups
    parts = out_ref.shape[0] // rows
    lane = lax.broadcasted_iota(jnp.int32, (1, lanes), 1)
    for number in range(offset_count):
        for part in range(parts):
            ahead = jnp.zeros((rows, lanes), jnp.float32)
            back = jnp.zeros((rows, lanes), jnp.float32)
            begin = part * 2 * lag_rows
            for group in range(groups):
                piece = parts_ref[group, number]
                first, last = group * lag_rows, half - (group + 1) * lag_rows
                ahead = jnp.where(lane // lag_rows == group, pltpu.roll(piece, (first - begin) % lanes, 1), ahead)
                back = jnp.where(
                    lane // lag_rows == groups - 1 - group, pltpu.roll(piece, (last - begin - lag_rows) % lanes, 1), back
                )
            out_ref[part * rows : (part + 1) * rows, number, 0:half] = back
            out_ref[part * rows : (part + 1) * rows, number, half : 2 * half] = ahead


def window_shards(spectra, quality, offsets):
    chan_count = lax.axis_size("chan")
    tm_count = lax.axis_size("tm")
    _, windows, band, chans = spectra.shape
    freqs = band * chan_count
    half = LAGS // 2
    lag_rows = half // chan_count
    offset_count = offsets.shape[0]
    piece_rows = 2 * lag_rows // chan_count
    smem = pl.BlockSpec(memory_space=pltpu.SMEM)
    vmem = pl.BlockSpec(memory_space=pltpu.VMEM)
    params = pltpu.CompilerParams(vmem_limit_bytes=VMEM_LIMIT)
    table = jnp.asarray(half_table(freqs, LAGS).reshape(2, chan_count, lag_rows, freqs))
    chan_index = lax.axis_index("chan").astype(jnp.int32)
    tm_index = lax.axis_index("tm").astype(jnp.int32)
    chan_where, tm_where = chan_index.reshape(1), tm_index.reshape(1)

    chan_order, tm_order = partners(chan_count), partners(tm_count)
    pieces = pl.pallas_call(
        functools.partial(split_kernel, chan_order),
        out_shape=[jax.ShapeDtypeStruct((2, band, chans), spectra.dtype)] * chan_count,
        in_specs=[smem, pl.BlockSpec(memory_space=pltpu.HBM)],
        out_specs=[pl.BlockSpec(memory_space=pl.ANY)] * chan_count,
        scratch_shapes=[pltpu.SemaphoreType.DMA((chan_count,))],
        compiler_params=params,
        name="split_windows",
    )(chan_where, pltpu.with_memory_space_constraint(spectra, pltpu.HBM))
    pairs = pl.pallas_call(
        functools.partial(window_kernel, chan_order),
        out_shape=[jax.ShapeDtypeStruct((6 * offset_count + 1, lag_rows, chans), jnp.int16)] * chan_count,
        in_specs=[smem, smem] + [vmem] * (chan_count + 2),
        out_specs=[vmem] * chan_count,
        scratch_shapes=[
            pltpu.VMEM((freqs, chans), jnp.float32),
            pltpu.VMEM((2, freqs, chans), jnp.bfloat16),
            pltpu.VMEM((2, freqs, 2 * chans), jnp.bfloat16),
        ],
        compiler_params=params,
        name="window_pairs",
    )(offsets, chan_where, *exchange(pieces, "chan"), quality, table)
    sums = pl.pallas_call(
        functools.partial(sum_kernel, tm_order, 1.0 / (CODE_TOP * math.sqrt(freqs))),
        out_shape=[jax.ShapeDtypeStruct((7, lag_rows, chans), jnp.int16)] * tm_count,
        in_specs=[smem] + [vmem] * chan_count,
        out_specs=[vmem] * tm_count,
        compiler_params=params,
        name="sum_windows",
    )(tm_where, *exchange(pairs, "chan"))
    pieces = pl.pallas_call(
        functools.partial(stack_kernel, windows * tm_count),
        out_shape=jax.ShapeDtypeStruct((chan_count, tm_count, piece_rows, chans), jnp.float32),
        in_specs=[smem, smem] + [vmem] * tm_count,
        out_specs=vmem,
        compiler_params=params,
        name="stack_pairs",
    )(offsets, tm_where, *exchange(sums, "tm"))
    shape = (chan_count * tm_count, piece_rows, chans)
    arrived = lax.all_to_all(pieces.reshape(shape), ("chan", "tm"), 0, 0, tiled=True)
    return pl.pallas_call(
        place_kernel,
        out_shape=jax.ShapeDtypeStruct((CH_DEV, offset_count, LAGS), jnp.float32),
        in_specs=[vmem],
        out_specs=vmem,
        compiler_params=params,
        name="place_lags",
    )(arrived.reshape(chan_count, tm_count, piece_rows, chans))


def shifted(value, axis, steps):
    count = lax.axis_size(axis)
    leading, last = (max(0, -steps), min(count, count - steps))
    return lax.ppermute(value, axis, [(source, source + steps) for source in range(leading, last)])


def lag_table(freq_count, lag_count):
    freq_index = jnp.arange(freq_count, dtype=jnp.int32)[:, None]
    double_lag = (2 * jnp.arange(lag_count, dtype=jnp.int32) - lag_count + 1)[None, :]
    turns = jnp.mod(freq_index * double_lag, 4 * freq_count)
    angles = turns.astype(jnp.float32) * (2.0 * math.pi / (4 * freq_count))
    cosine = jnp.cos(angles)
    sine = jnp.sin(angles)
    upper = jnp.concatenate([cosine, sine], axis=1)
    lower = jnp.concatenate([-sine, cosine], axis=1)
    return jnp.stack([upper, lower]).astype(jnp.bfloat16)


def whiten_parts(real_part, imag_part, magnitude, channel_level, usable):
    factor = usable.astype(jnp.float32)[:, None, :] / (magnitude + 0.5 * (channel_level + 1e-05))
    return jnp.stack([real_part * factor, imag_part * factor]).astype(jnp.bfloat16)


def cross_parts(own_real, own_imag, far_real, far_imag):
    own_real = own_real.astype(jnp.float32)
    own_imag = own_imag.astype(jnp.float32)
    far_real = far_real.astype(jnp.float32)
    far_imag = far_imag.astype(jnp.float32)
    return jnp.stack(
        [own_real * far_real + own_imag * far_imag, own_imag * far_real - own_real * far_imag]
    ).astype(jnp.bfloat16)


def pair_terms(corr_all):
    lag_count = corr_all.shape[-1] // 2
    real_corr = corr_all[..., :lag_count]
    imag_corr = corr_all[..., lag_count:]
    power = real_corr * real_corr + imag_corr * imag_corr
    mean_power = jnp.mean(power, axis=-1, keepdims=True)
    denominator = jnp.sqrt(power + 0.25 * (mean_power + 1e-06))
    return (
        jnp.sum(real_corr, axis=-3),
        jnp.sum(real_corr / denominator, axis=-3),
        jnp.sum(imag_corr / denominator, axis=-3),
    )


def shards(spectra, quality, offsets):
    chan_count = lax.axis_size("chan")
    tm_count = lax.axis_size("tm")
    levels = chan_count.bit_length() - 1
    table_bf = lag_table(F, LAGS)
    inv_root = 1.0 / math.sqrt(F)
    real_part = spectra[0].astype(jnp.float32)
    imag_part = spectra[1].astype(jnp.float32)
    magnitude = jnp.sqrt(real_part * real_part + imag_part * imag_part)
    band_total = lax.psum(jnp.sum(magnitude, axis=1), "chan")
    channel_level = (band_total / F)[:, None, :]
    whitened = whiten_parts(real_part, imag_part, magnitude, channel_level, quality)
    width_all = whitened.shape[3]
    padded = jnp.pad(whitened, ((0, 0), (0, 0), (0, 0), (0, width_all)))
    crossed_list = []
    for offset_index in range(NOFF):
        partner = lax.dynamic_slice_in_dim(padded, offsets[offset_index] * CH_DEV, width_all, 3)
        crossed_list.append(cross_parts(whitened[0], whitened[1], partner[0], partner[1]))
    crossed = jnp.stack(crossed_list, axis=1)
    corr_all = jnp.einsum(
        "cnwfh,cfl->nwhl",
        lax.all_to_all(crossed, "chan", split_axis=4, concat_axis=3, tiled=True),
        table_bf,
        preferred_element_type=jnp.float32,
    )
    linear_sum, real_sum, imag_sum = pair_terms(corr_all * inv_root)
    totals = lax.psum((linear_sum, real_sum, imag_sum), "tm")
    window_count = W_DEV * tm_count
    linear = totals[0] / window_count
    real_phase = totals[1] / window_count
    imag_phase = totals[2] / window_count
    stacks = jnp.transpose(linear * (real_phase * real_phase + imag_phase * imag_phase), (1, 0, 2))
    reverse_part = stacks
    for bit_index in range(levels):
        step_size = 1 << bit_index
        arrived = shifted(reverse_part, "chan", step_size)
        chosen = offsets // step_size % 2 == 1
        reverse_part = jnp.where(chosen[None, :, None], arrived, reverse_part)
    return stacks + jnp.flip(reverse_part, axis=2)


def solution(mesh):
    chan_count, tm_count = mesh.shape["chan"], mesh.shape["tm"]
    by_window = chan_count == W_DEV and tm_count == NOFF
    return jax.shard_map(
        window_shards if by_window else shards,
        mesh=mesh,
        in_specs=(P(None, "tm", "chan", None), P("tm", None), P()),
        out_specs=P("chan", None, None),
        check_vma=False,
    )
```

```python
import functools
import math

import jax
import jax.numpy as jnp
import numpy as np
from jax import lax
from jax.experimental import pallas as pl
from jax.experimental.pallas import tpu as pltpu
from jax.sharding import PartitionSpec as P

F = 2048
LAGS = 256
NOFF = 4
CH_DEV = 16
W_DEV = 8
VMEM_LIMIT = 48 * 1024 * 1024
CODE_TOP = 32767.0
OCTAVE = 256.0
LOWEST = -110.0


def encode(value):
    return jnp.round(value).astype(jnp.int32).astype(jnp.int16)


def decode(code):
    return code.astype(jnp.int32).astype(jnp.float32)


def level_code(peak):
    return jnp.ceil(jnp.maximum(jnp.log2(jnp.maximum(peak, 1e-30)), LOWEST) * OCTAVE) + 1.0


def level_of(code):
    return jnp.exp2(code * (1.0 / OCTAVE))


def half_table(freq_count, lag_count):
    freq_index = np.arange(freq_count, dtype=np.int64)[None, :]
    double_lag = (2 * np.arange(lag_count // 2, lag_count, dtype=np.int64) - lag_count + 1)[:, None]
    turns = np.mod(freq_index * double_lag, 4 * freq_count).astype(np.float32)
    angles = turns * np.float32(2.0 * math.pi / (4 * freq_count))
    return np.concatenate([np.cos(angles), np.sin(angles)]).astype(jnp.bfloat16)


def window_kernel(order, offs_ref, where_ref, *refs):
    chan_count = len(order)
    spec_refs, (qual_ref, table_ref) = refs[:chan_count], refs[chan_count : chan_count + 2]
    out_refs = refs[chan_count + 2 : chan_count + 4]
    mag_ref, white_ref, cross_ref = refs[chan_count + 4 :]
    me = where_ref[0]
    _, band, chans = spec_refs[0].shape
    freqs = chan_count * band
    chip_count, blocks, lag_rows, _ = out_refs[0].shape
    offset_count = offs_ref.shape[0]
    half = chan_count * lag_rows
    step = 64

    total = jnp.zeros((8, chans), jnp.float32)
    for partner, spec_ref in zip(order, spec_refs):
        base = (me ^ partner) * band
        for row in range(0, band, step):
            real = spec_ref[0, row : row + step, :].astype(jnp.float32)
            imag = spec_ref[1, row : row + step, :].astype(jnp.float32)
            square = real * real + imag * imag
            magnitude = square * lax.rsqrt(jnp.maximum(square, 1e-30))
            mag_ref[pl.ds(pl.multiple_of(base + row, step), step), :] = magnitude
            total += jnp.sum(magnitude.reshape(step // 8, 8, chans), axis=0)
    level = jnp.sum(total, axis=0, keepdims=True) * (1.0 / freqs)
    floor = 0.5 * (level + 1e-05)

    for partner, spec_ref in zip(order, spec_refs):
        base = (me ^ partner) * band
        for row in range(0, band, step):
            held = pl.ds(pl.multiple_of(base + row, step), step)
            factor = pl.reciprocal(mag_ref[held, :] + floor, approx=True)
            for part in range(2):
                value = spec_ref[part, row : row + step, :].astype(jnp.float32) * factor
                white_ref[part, held, :] = value.astype(jnp.bfloat16)

    lane = lax.broadcasted_iota(jnp.int32, (1, chans), 1)
    line = lax.broadcasted_iota(jnp.int32, (lag_rows, chans), 0)
    usable = qual_ref[pl.ds(me, 1), :].astype(jnp.float32)
    levels = jnp.zeros((lag_rows, chans), jnp.float32)
    groups = [k ^ core for core in range(2) for k in chips(chan_count)]
    table = jnp.concatenate([table_ref[side, me ^ k] for side in range(2) for k in groups], axis=0)
    for number in range(offset_count):
        turn = chans - offs_ref[number] * (chans // chan_count)
        slot = number % 2
        for row in range(0, freqs, step):
            own = [white_ref[part, row : row + step, :] for part in range(2)]
            far_real, far_imag = (pltpu.roll(value, turn, 1).astype(jnp.float32) for value in own)
            own_real, own_imag = (value.astype(jnp.float32) for value in own)
            real = own_real * far_real + own_imag * far_imag
            imag = own_imag * far_real - own_real * far_imag
            cross_ref[slot, row : row + step, 0:chans] = real.astype(jnp.bfloat16)
            cross_ref[slot, row : row + step, chans : 2 * chans] = imag.astype(jnp.bfloat16)
        sums = jnp.dot(table, cross_ref[slot], preferred_element_type=jnp.float32)
        cos_real, sin_real = sums[:half, :chans], sums[half:, :chans]
        cos_imag, sin_imag = sums[:half, chans:], sums[half:, chans:]
        corr = (
            (cos_real - sin_imag, sin_real + cos_imag),
            (cos_real + sin_imag, cos_imag - sin_real),
        )
        power = [real * real + imag * imag for real, imag in corr]
        mean_power = jnp.sum(power[0] + power[1], axis=0, keepdims=True) * (1.0 / (2 * half))
        extra = 0.25 * (mean_power + 1e-06 * freqs)
        peak = jnp.max(jnp.maximum(jnp.abs(corr[0][0]), jnp.abs(corr[1][0])), axis=0, keepdims=True)
        code = level_code(peak)
        levels = jnp.where(line == number, code, levels)
        keep = jnp.where(lane < turn, usable * pltpu.roll(usable, turn, 1), 0.0) * CODE_TOP
        upscale = keep / level_of(code)
        for side in range(2):
            inverse = lax.rsqrt(power[side] + extra) * keep
            real, imag = corr[side]
            for kind, value in enumerate((real * upscale, real * inverse, imag * inverse)):
                coded = encode(value).reshape(chan_count, lag_rows, chans)
                for core in range(2):
                    rows = slice(core * chip_count, (core + 1) * chip_count)
                    out_refs[core][:, 6 * number + 2 * kind + side, :, :] = coded[rows]
    for out_ref in out_refs:
        for chip in range(chip_count):
            out_ref[chip, blocks - 1, :, :] = encode(levels)


def merge_kernel(own_ref, far_ref, *out_refs):
    blocks = own_ref.shape[1]
    for chip, out_ref in enumerate(out_refs):
        levels = [level_of(decode(ref[chip, blocks - 1])) for ref in (own_ref, far_ref)]
        code = level_code(levels[0] + levels[1])
        shares = [level / level_of(code) for level in levels]
        out_ref[blocks - 1, :, :] = encode(code)
        for block in range(blocks - 1):
            number, part = divmod(block, 6)
            own, far = decode(own_ref[chip, block]), decode(far_ref[chip, block])
            if part < 2:
                total = own * shares[0][number : number + 1, :] + far * shares[1][number : number + 1, :]
            else:
                total = (own + far) * 0.5
            out_ref[block, :, :] = encode(total)


def sum_kernel(order, scale, where_ref, *refs):
    code_refs, out_refs = refs[: -len(order)], refs[-len(order) :]
    blocks = code_refs[0].shape[0]
    levels = [level_of(decode(codes_ref[blocks - 1])) * scale for codes_ref in code_refs]
    line = lax.broadcasted_iota(jnp.int32, levels[0].shape, 0)
    for k, out_ref in zip(order, out_refs):
        number = where_ref[0] ^ k
        own = [jnp.sum(jnp.where(line == number, level, 0.0), axis=0, keepdims=True) for level in levels]
        linear = [
            sum(decode(codes_ref[6 * number + side]) * level for codes_ref, level in zip(code_refs, own))
            for side in range(2)
        ]
        peak = jnp.max(jnp.maximum(jnp.abs(linear[0]), jnp.abs(linear[1])), axis=0, keepdims=True)
        code = level_code(jnp.broadcast_to(peak, linear[0].shape))
        upscale = CODE_TOP / level_of(code)
        for side in range(2):
            out_ref[side, :, :] = encode(linear[side] * upscale)
        for part in range(2, 6):
            total = sum(decode(codes_ref[6 * number + part]) for codes_ref in code_refs)
            out_ref[part, :, :] = encode(total * (1.0 / len(code_refs)))
        out_ref[6, :, :] = encode(code)


def partners(count):
    return sorted(range(1, count), key=lambda k: (-(k >> 1).bit_count(), k & 1, k)) + [0]


def chips(count):
    return [k for k in partners(count) if k % 2 == 0]


def exchange(pieces, axis, order):
    count = lax.axis_size(axis)
    return [
        lax.ppermute(piece, axis, [(source, source ^ k) for source in range(count)]) if k else piece
        for k, piece in zip(order, pieces)
    ]


def split_kernel(order, where_ref, spec_ref, *refs):
    out_refs, sems = refs[:-1], refs[-1]
    copies = [
        pltpu.make_async_copy(spec_ref.at[:, where_ref[0] ^ k], out_ref, sems.at[number])
        for number, (k, out_ref) in enumerate(zip(order, out_refs))
    ]
    for copy in copies:
        copy.start()
    for copy in copies:
        copy.wait()


def stack_kernel(windows, offs_ref, where_ref, *refs):
    sums_refs, out_ref = refs[:-1], refs[-1]
    blocks, copies, rows, _ = out_ref.shape
    _, lag_rows, chans = sums_refs[0].shape
    per_sum = windows // len(sums_refs)
    levels = [level_of(decode(sums_ref[6])) * (1.0 / (CODE_TOP * windows)) for sums_ref in sums_refs]
    stacks = []
    for side in range(2):
        linear = sum(decode(sums_ref[side]) * level for sums_ref, level in zip(sums_refs, levels))
        real, imag = (
            sum(decode(sums_ref[part + side]) for sums_ref in sums_refs) * (per_sum / (CODE_TOP * windows))
            for part in (2, 4)
        )
        stacks.append(linear * (real * real + imag * imag))
    ahead = offs_ref[where_ref[0]] * (chans // blocks)
    lane = lax.broadcasted_iota(jnp.int32, (1, chans), 1)
    behind = [jnp.where(lane >= ahead, pltpu.roll(stack, ahead, 1), 0.0) for stack in stacks]
    back = stacks[1] + behind[0]
    both = jnp.concatenate(
        [stacks[0] + behind[1]] + [back[row : row + 1, :] for row in reversed(range(lag_rows))], axis=0
    )
    wide = 2 * lag_rows
    parts = chans // wide
    turned = jnp.concatenate([both] * parts, axis=0).T
    per_block = chans // blocks
    for block in range(blocks):
        piece = jnp.zeros((rows, chans), jnp.float32)
        for part in range(parts):
            begin = block * per_block + part * rows
            piece = jnp.where(lane // wide == part, turned[begin : begin + rows, :], piece)
        for copy in range(copies):
            out_ref[block, copy, :, :] = piece


def place_kernel(parts_ref, out_ref):
    groups, offset_count, rows, lanes = parts_ref.shape
    half = out_ref.shape[2] // 2
    lag_rows = half // groups
    parts = out_ref.shape[0] // rows
    lane = lax.broadcasted_iota(jnp.int32, (1, lanes), 1)
    for number in range(offset_count):
        for part in range(parts):
            ahead = jnp.zeros((rows, lanes), jnp.float32)
            back = jnp.zeros((rows, lanes), jnp.float32)
            begin = part * 2 * lag_rows
            for group in range(groups):
                piece = parts_ref[group, number]
                first, last = group * lag_rows, half - (group + 1) * lag_rows
                ahead = jnp.where(lane // lag_rows == group, pltpu.roll(piece, (first - begin) % lanes, 1), ahead)
                back = jnp.where(
                    lane // lag_rows == groups - 1 - group, pltpu.roll(piece, (last - begin - lag_rows) % lanes, 1), back
                )
            out_ref[part * rows : (part + 1) * rows, number, 0:half] = back
            out_ref[part * rows : (part + 1) * rows, number, half : 2 * half] = ahead


def window_shards(spectra, quality, offsets):
    chan_count = lax.axis_size("chan")
    tm_count = lax.axis_size("tm")
    _, windows, band, chans = spectra.shape
    freqs = band * chan_count
    half = LAGS // 2
    lag_rows = half // chan_count
    offset_count = offsets.shape[0]
    piece_rows = 2 * lag_rows // chan_count
    smem = pl.BlockSpec(memory_space=pltpu.SMEM)
    vmem = pl.BlockSpec(memory_space=pltpu.VMEM)
    params = pltpu.CompilerParams(vmem_limit_bytes=VMEM_LIMIT)
    table = jnp.asarray(half_table(freqs, LAGS).reshape(2, chan_count, lag_rows, freqs))
    chan_index = lax.axis_index("chan").astype(jnp.int32)
    tm_index = lax.axis_index("tm").astype(jnp.int32)
    chan_where, tm_where = chan_index.reshape(1), tm_index.reshape(1)

    chan_order, tm_order = partners(chan_count), partners(tm_count)
    pieces = pl.pallas_call(
        functools.partial(split_kernel, chan_order),
        out_shape=[jax.ShapeDtypeStruct((2, band, chans), spectra.dtype)] * chan_count,
        in_specs=[smem, pl.BlockSpec(memory_space=pltpu.HBM)],
        out_specs=[pl.BlockSpec(memory_space=pl.ANY)] * chan_count,
        scratch_shapes=[pltpu.SemaphoreType.DMA((chan_count,))],
        compiler_params=params,
        name="split_windows",
    )(chan_where, pltpu.with_memory_space_constraint(spectra, pltpu.HBM))
    chip_order = chips(chan_count)
    pair_shape = (6 * offset_count + 1, lag_rows, chans)
    own, far = pl.pallas_call(
        functools.partial(window_kernel, chan_order),
        out_shape=[jax.ShapeDtypeStruct((len(chip_order), *pair_shape), jnp.int16)] * 2,
        in_specs=[smem, smem] + [vmem] * (chan_count + 2),
        out_specs=[vmem] * 2,
        scratch_shapes=[
            pltpu.VMEM((freqs, chans), jnp.float32),
            pltpu.VMEM((2, freqs, chans), jnp.bfloat16),
            pltpu.VMEM((2, freqs, 2 * chans), jnp.bfloat16),
        ],
        compiler_params=params,
        name="window_pairs",
    )(offsets, chan_where, *exchange(pieces, "chan", chan_order), quality, table)
    pairs = pl.pallas_call(
        merge_kernel,
        out_shape=[jax.ShapeDtypeStruct(pair_shape, jnp.int16)] * len(chip_order),
        in_specs=[vmem] * 2,
        out_specs=[vmem] * len(chip_order),
        compiler_params=params,
        name="merge_windows",
    )(own, *exchange([far], "chan", [1]))
    sums = pl.pallas_call(
        functools.partial(sum_kernel, tm_order, 1.0 / (CODE_TOP * math.sqrt(freqs))),
        out_shape=[jax.ShapeDtypeStruct((7, lag_rows, chans), jnp.int16)] * tm_count,
        in_specs=[smem] + [vmem] * len(chip_order),
        out_specs=[vmem] * tm_count,
        compiler_params=params,
        name="sum_windows",
    )(tm_where, *exchange(pairs, "chan", chip_order))
    pieces = pl.pallas_call(
        functools.partial(stack_kernel, windows * tm_count),
        out_shape=jax.ShapeDtypeStruct((chan_count, tm_count, piece_rows, chans), jnp.float32),
        in_specs=[smem, smem] + [vmem] * tm_count,
        out_specs=vmem,
        compiler_params=params,
        name="stack_pairs",
    )(offsets, tm_where, *exchange(sums, "tm", tm_order))
    shape = (chan_count * tm_count, piece_rows, chans)
    arrived = lax.all_to_all(pieces.reshape(shape), ("chan", "tm"), 0, 0, tiled=True)
    return pl.pallas_call(
        place_kernel,
        out_shape=jax.ShapeDtypeStruct((CH_DEV, offset_count, LAGS), jnp.float32),
        in_specs=[vmem],
        out_specs=vmem,
        compiler_params=params,
        name="place_lags",
    )(arrived.reshape(chan_count, tm_count, piece_rows, chans))


def shifted(value, axis, steps):
    count = lax.axis_size(axis)
    leading, last = (max(0, -steps), min(count, count - steps))
    return lax.ppermute(value, axis, [(source, source + steps) for source in range(leading, last)])


def lag_table(freq_count, lag_count):
    freq_index = jnp.arange(freq_count, dtype=jnp.int32)[:, None]
    double_lag = (2 * jnp.arange(lag_count, dtype=jnp.int32) - lag_count + 1)[None, :]
    turns = jnp.mod(freq_index * double_lag, 4 * freq_count)
    angles = turns.astype(jnp.float32) * (2.0 * math.pi / (4 * freq_count))
    cosine = jnp.cos(angles)
    sine = jnp.sin(angles)
    upper = jnp.concatenate([cosine, sine], axis=1)
    lower = jnp.concatenate([-sine, cosine], axis=1)
    return jnp.stack([upper, lower]).astype(jnp.bfloat16)


def whiten_parts(real_part, imag_part, magnitude, channel_level, usable):
    factor = usable.astype(jnp.float32)[:, None, :] / (magnitude + 0.5 * (channel_level + 1e-05))
    return jnp.stack([real_part * factor, imag_part * factor]).astype(jnp.bfloat16)


def cross_parts(own_real, own_imag, far_real, far_imag):
    own_real = own_real.astype(jnp.float32)
    own_imag = own_imag.astype(jnp.float32)
    far_real = far_real.astype(jnp.float32)
    far_imag = far_imag.astype(jnp.float32)
    return jnp.stack(
        [own_real * far_real + own_imag * far_imag, own_imag * far_real - own_real * far_imag]
    ).astype(jnp.bfloat16)


def pair_terms(corr_all):
    lag_count = corr_all.shape[-1] // 2
    real_corr = corr_all[..., :lag_count]
    imag_corr = corr_all[..., lag_count:]
    power = real_corr * real_corr + imag_corr * imag_corr
    mean_power = jnp.mean(power, axis=-1, keepdims=True)
    denominator = jnp.sqrt(power + 0.25 * (mean_power + 1e-06))
    return (
        jnp.sum(real_corr, axis=-3),
        jnp.sum(real_corr / denominator, axis=-3),
        jnp.sum(imag_corr / denominator, axis=-3),
    )


def shards(spectra, quality, offsets):
    chan_count = lax.axis_size("chan")
    tm_count = lax.axis_size("tm")
    levels = chan_count.bit_length() - 1
    table_bf = lag_table(F, LAGS)
    inv_root = 1.0 / math.sqrt(F)
    real_part = spectra[0].astype(jnp.float32)
    imag_part = spectra[1].astype(jnp.float32)
    magnitude = jnp.sqrt(real_part * real_part + imag_part * imag_part)
    band_total = lax.psum(jnp.sum(magnitude, axis=1), "chan")
    channel_level = (band_total / F)[:, None, :]
    whitened = whiten_parts(real_part, imag_part, magnitude, channel_level, quality)
    width_all = whitened.shape[3]
    padded = jnp.pad(whitened, ((0, 0), (0, 0), (0, 0), (0, width_all)))
    crossed_list = []
    for offset_index in range(NOFF):
        partner = lax.dynamic_slice_in_dim(padded, offsets[offset_index] * CH_DEV, width_all, 3)
        crossed_list.append(cross_parts(whitened[0], whitened[1], partner[0], partner[1]))
    crossed = jnp.stack(crossed_list, axis=1)
    corr_all = jnp.einsum(
        "cnwfh,cfl->nwhl",
        lax.all_to_all(crossed, "chan", split_axis=4, concat_axis=3, tiled=True),
        table_bf,
        preferred_element_type=jnp.float32,
    )
    linear_sum, real_sum, imag_sum = pair_terms(corr_all * inv_root)
    totals = lax.psum((linear_sum, real_sum, imag_sum), "tm")
    window_count = W_DEV * tm_count
    linear = totals[0] / window_count
    real_phase = totals[1] / window_count
    imag_phase = totals[2] / window_count
    stacks = jnp.transpose(linear * (real_phase * real_phase + imag_phase * imag_phase), (1, 0, 2))
    reverse_part = stacks
    for bit_index in range(levels):
        step_size = 1 << bit_index
        arrived = shifted(reverse_part, "chan", step_size)
        chosen = offsets // step_size % 2 == 1
        reverse_part = jnp.where(chosen[None, :, None], arrived, reverse_part)
    return stacks + jnp.flip(reverse_part, axis=2)


def solution(mesh):
    chan_count, tm_count = mesh.shape["chan"], mesh.shape["tm"]
    by_window = chan_count == W_DEV and tm_count == NOFF
    return jax.shard_map(
        window_shards if by_window else shards,
        mesh=mesh,
        in_specs=(P(None, "tm", "chan", None), P("tm", None), P()),
        out_specs=P("chan", None, None),
        check_vma=False,
    )
```

```python
import functools
import math

import jax
import jax.numpy as jnp
import numpy as np
from jax import lax
from jax.experimental import pallas as pl
from jax.experimental.pallas import tpu as pltpu
from jax.sharding import PartitionSpec as P

F = 2048
LAGS = 256
NOFF = 4
CH_DEV = 16
W_DEV = 8
VMEM_LIMIT = 48 * 1024 * 1024
CODE_TOP = 32767.0
OCTAVE = 256.0
LOWEST = -110.0


def encode(value):
    return jnp.round(value).astype(jnp.int32).astype(jnp.int16)


def decode(code):
    return code.astype(jnp.int32).astype(jnp.float32)


def level_code(peak):
    return jnp.ceil(jnp.maximum(jnp.log2(jnp.maximum(peak, 1e-30)), LOWEST) * OCTAVE) + 1.0


def level_of(code):
    return jnp.exp2(code * (1.0 / OCTAVE))


def half_table(freq_count, lag_count):
    freq_index = np.arange(freq_count, dtype=np.int64)[None, :]
    double_lag = (2 * np.arange(lag_count // 2, lag_count, dtype=np.int64) - lag_count + 1)[:, None]
    turns = np.mod(freq_index * double_lag, 4 * freq_count).astype(np.float32)
    angles = turns * np.float32(2.0 * math.pi / (4 * freq_count))
    return np.concatenate([np.cos(angles), np.sin(angles)]).astype(jnp.bfloat16)


def window_kernel(order, offs_ref, where_ref, *refs):
    chan_count = len(order)
    spec_refs, (qual_ref, table_ref) = refs[:chan_count], refs[chan_count : chan_count + 2]
    out_refs = refs[chan_count + 2 : chan_count + 4]
    mag_ref, white_ref, cross_ref = refs[chan_count + 4 :]
    me = where_ref[0]
    _, band, chans = spec_refs[0].shape
    freqs = chan_count * band
    chip_count, blocks, lag_rows, _ = out_refs[0].shape
    offset_count = offs_ref.shape[0]
    half = chan_count * lag_rows
    step = 64

    total = jnp.zeros((8, chans), jnp.float32)
    for partner, spec_ref in zip(order, spec_refs):
        base = (me ^ partner) * band
        for row in range(0, band, step):
            real = spec_ref[0, row : row + step, :].astype(jnp.float32)
            imag = spec_ref[1, row : row + step, :].astype(jnp.float32)
            square = real * real + imag * imag
            magnitude = square * lax.rsqrt(jnp.maximum(square, 1e-30))
            mag_ref[pl.ds(pl.multiple_of(base + row, step), step), :] = magnitude
            total += jnp.sum(magnitude.reshape(step // 8, 8, chans), axis=0)
    level = jnp.sum(total, axis=0, keepdims=True) * (1.0 / freqs)
    floor = 0.5 * (level + 1e-05)

    for partner, spec_ref in zip(order, spec_refs):
        base = (me ^ partner) * band
        for row in range(0, band, step):
            held = pl.ds(pl.multiple_of(base + row, step), step)
            factor = pl.reciprocal(mag_ref[held, :] + floor, approx=True)
            for part in range(2):
                value = spec_ref[part, row : row + step, :].astype(jnp.float32) * factor
                white_ref[part, held, :] = value.astype(jnp.bfloat16)

    lane = lax.broadcasted_iota(jnp.int32, (1, chans), 1)
    line = lax.broadcasted_iota(jnp.int32, (lag_rows, chans), 0)
    usable = qual_ref[pl.ds(me, 1), :].astype(jnp.float32)
    levels = jnp.zeros((lag_rows, chans), jnp.float32)
    groups = [k ^ core for core in range(2) for k in chips(chan_count)]
    table = jnp.concatenate([table_ref[side, me ^ k] for side in range(2) for k in groups], axis=0)
    for number in range(offset_count):
        turn = chans - offs_ref[number] * (chans // chan_count)
        slot = number % 2
        for row in range(0, freqs, step):
            own = [white_ref[part, row : row + step, :] for part in range(2)]
            far_real, far_imag = (pltpu.roll(value, turn, 1).astype(jnp.float32) for value in own)
            own_real, own_imag = (value.astype(jnp.float32) for value in own)
            real = own_real * far_real + own_imag * far_imag
            imag = own_imag * far_real - own_real * far_imag
            cross_ref[slot, row : row + step, 0:chans] = real.astype(jnp.bfloat16)
            cross_ref[slot, row : row + step, chans : 2 * chans] = imag.astype(jnp.bfloat16)
        sums = jnp.dot(table, cross_ref[slot], preferred_element_type=jnp.float32)
        cos_real, sin_real = sums[:half, :chans], sums[half:, :chans]
        cos_imag, sin_imag = sums[:half, chans:], sums[half:, chans:]
        corr = (
            (cos_real - sin_imag, sin_real + cos_imag),
            (cos_real + sin_imag, cos_imag - sin_real),
        )
        power = [real * real + imag * imag for real, imag in corr]
        mean_power = jnp.sum(power[0] + power[1], axis=0, keepdims=True) * (1.0 / (2 * half))
        extra = 0.25 * (mean_power + 1e-06 * freqs)
        peak = jnp.max(jnp.maximum(jnp.abs(corr[0][0]), jnp.abs(corr[1][0])), axis=0, keepdims=True)
        code = level_code(peak)
        levels = jnp.where(line == number, code, levels)
        keep = jnp.where(lane < turn, usable * pltpu.roll(usable, turn, 1), 0.0) * CODE_TOP
        upscale = keep / level_of(code)
        for side in range(2):
            inverse = lax.rsqrt(power[side] + extra) * keep
            real, imag = corr[side]
            for kind, value in enumerate((real * upscale, real * inverse, imag * inverse)):
                coded = encode(value).reshape(chan_count, lag_rows, chans)
                for core in range(2):
                    rows = slice(core * chip_count, (core + 1) * chip_count)
                    out_refs[core][:, 6 * number + 2 * kind + side, :, :] = coded[rows]
    for out_ref in out_refs:
        for chip in range(chip_count):
            out_ref[chip, blocks - 1, :, :] = encode(levels)


def merge_kernel(own_ref, far_ref, *out_refs):
    blocks = own_ref.shape[1]
    for chip, out_ref in enumerate(out_refs):
        levels = [level_of(decode(ref[chip, blocks - 1])) for ref in (own_ref, far_ref)]
        code = level_code(levels[0] + levels[1])
        shares = [level / level_of(code) for level in levels]
        out_ref[blocks - 1, :, :] = encode(code)
        for block in range(blocks - 1):
            number, part = divmod(block, 6)
            own, far = decode(own_ref[chip, block]), decode(far_ref[chip, block])
            if part < 2:
                total = own * shares[0][number : number + 1, :] + far * shares[1][number : number + 1, :]
            else:
                total = (own + far) * 0.5
            out_ref[block, :, :] = encode(total)


def sum_kernel(order, scale, where_ref, *refs):
    code_refs, out_refs = refs[: -len(order)], refs[-len(order) :]
    blocks = code_refs[0].shape[0]
    levels = [level_of(decode(codes_ref[blocks - 1])) * scale for codes_ref in code_refs]
    line = lax.broadcasted_iota(jnp.int32, levels[0].shape, 0)
    for k, out_ref in zip(order, out_refs):
        number = where_ref[0] ^ k
        own = [jnp.sum(jnp.where(line == number, level, 0.0), axis=0, keepdims=True) for level in levels]
        linear = [
            sum(decode(codes_ref[6 * number + side]) * level for codes_ref, level in zip(code_refs, own))
            for side in range(2)
        ]
        peak = jnp.max(jnp.maximum(jnp.abs(linear[0]), jnp.abs(linear[1])), axis=0, keepdims=True)
        code = level_code(jnp.broadcast_to(peak, linear[0].shape))
        upscale = CODE_TOP / level_of(code)
        for side in range(2):
            out_ref[side, :, :] = encode(linear[side] * upscale)
        for part in range(2, 6):
            total = sum(decode(codes_ref[6 * number + part]) for codes_ref in code_refs)
            out_ref[part, :, :] = encode(total * (1.0 / len(code_refs)))
        out_ref[6, :, :] = encode(code)


def partners(count):
    return sorted(range(1, count), key=lambda k: (-(k >> 1).bit_count(), k & 1, k)) + [0]


def chips(count):
    return [k for k in partners(count) if k % 2 == 0]


def exchange(pieces, axis, order):
    count = lax.axis_size(axis)
    return [
        lax.ppermute(piece, axis, [(source, source ^ k) for source in range(count)]) if k else piece
        for k, piece in zip(order, pieces)
    ]


def split_kernel(order, where_ref, spec_ref, *refs):
    out_refs, sems = refs[:-1], refs[-1]
    copies = [
        pltpu.make_async_copy(spec_ref.at[:, where_ref[0] ^ k], out_ref, sems.at[number])
        for number, (k, out_ref) in enumerate(zip(order, out_refs))
    ]
    for copy in copies:
        copy.start()
    for copy in copies:
        copy.wait()


def stack_kernel(windows, offs_ref, where_ref, *refs):
    sums_refs, out_ref = refs[:-1], refs[-1]
    blocks, copies, rows, _ = out_ref.shape
    _, lag_rows, chans = sums_refs[0].shape
    per_sum = windows // len(sums_refs)
    levels = [level_of(decode(sums_ref[6])) * (1.0 / (CODE_TOP * windows)) for sums_ref in sums_refs]
    stacks = []
    for side in range(2):
        linear = sum(decode(sums_ref[side]) * level for sums_ref, level in zip(sums_refs, levels))
        real, imag = (
            sum(decode(sums_ref[part + side]) for sums_ref in sums_refs) * (per_sum / (CODE_TOP * windows))
            for part in (2, 4)
        )
        stacks.append(linear * (real * real + imag * imag))
    ahead = offs_ref[where_ref[0]] * (chans // blocks)
    lane = lax.broadcasted_iota(jnp.int32, (1, chans), 1)
    behind = [jnp.where(lane >= ahead, pltpu.roll(stack, ahead, 1), 0.0) for stack in stacks]
    back = stacks[1] + behind[0]
    both = jnp.concatenate(
        [stacks[0] + behind[1]] + [back[row : row + 1, :] for row in reversed(range(lag_rows))], axis=0
    )
    wide = 2 * lag_rows
    parts = chans // wide
    turned = jnp.concatenate([both] * parts, axis=0).T
    per_block = chans // blocks
    for block in range(blocks):
        piece = jnp.zeros((rows, chans), jnp.float32)
        for part in range(parts):
            begin = block * per_block + part * rows
            piece = jnp.where(lane // wide == part, turned[begin : begin + rows, :], piece)
        for copy in range(copies):
            out_ref[block, copy, :, :] = piece


def place_kernel(parts_ref, out_ref):
    groups, offset_count, rows, lanes = parts_ref.shape
    half = out_ref.shape[2] // 2
    lag_rows = half // groups
    parts = out_ref.shape[0] // rows
    lane = lax.broadcasted_iota(jnp.int32, (1, lanes), 1)
    for number in range(offset_count):
        for part in range(parts):
            ahead = jnp.zeros((rows, lanes), jnp.float32)
            back = jnp.zeros((rows, lanes), jnp.float32)
            begin = part * 2 * lag_rows
            for group in range(groups):
                piece = parts_ref[group, number]
                first, last = group * lag_rows, half - (group + 1) * lag_rows
                ahead = jnp.where(lane // lag_rows == group, pltpu.roll(piece, (first - begin) % lanes, 1), ahead)
                back = jnp.where(
                    lane // lag_rows == groups - 1 - group, pltpu.roll(piece, (last - begin - lag_rows) % lanes, 1), back
                )
            out_ref[part * rows : (part + 1) * rows, number, 0:half] = back
            out_ref[part * rows : (part + 1) * rows, number, half : 2 * half] = ahead


def window_shards(spectra, quality, offsets):
    chan_count = lax.axis_size("chan")
    tm_count = lax.axis_size("tm")
    _, windows, band, chans = spectra.shape
    freqs = band * chan_count
    half = LAGS // 2
    lag_rows = half // chan_count
    offset_count = offsets.shape[0]
    piece_rows = 2 * lag_rows // chan_count
    smem = pl.BlockSpec(memory_space=pltpu.SMEM)
    vmem = pl.BlockSpec(memory_space=pltpu.VMEM)
    params = pltpu.CompilerParams(vmem_limit_bytes=VMEM_LIMIT)
    table = jnp.asarray(half_table(freqs, LAGS).reshape(2, chan_count, lag_rows, freqs))
    chan_index = lax.axis_index("chan").astype(jnp.int32)
    tm_index = lax.axis_index("tm").astype(jnp.int32)
    chan_where, tm_where = chan_index.reshape(1), tm_index.reshape(1)

    chan_order, tm_order = partners(chan_count), partners(tm_count)
    spectra = pltpu.with_memory_space_constraint(spectra, pltpu.HBM)
    pieces = []
    for part in (chan_order[:2], chan_order[2:]):
        pieces += pl.pallas_call(
            functools.partial(split_kernel, part),
            out_shape=[jax.ShapeDtypeStruct((2, band, chans), spectra.dtype)] * len(part),
            in_specs=[smem, pl.BlockSpec(memory_space=pltpu.HBM)],
            out_specs=[pl.BlockSpec(memory_space=pl.ANY)] * len(part),
            scratch_shapes=[pltpu.SemaphoreType.DMA((len(part),))],
            compiler_params=params,
            name="split_windows",
        )(chan_where, spectra)
    chip_order = chips(chan_count)
    pair_shape = (6 * offset_count + 1, lag_rows, chans)
    own, far = pl.pallas_call(
        functools.partial(window_kernel, chan_order),
        out_shape=[jax.ShapeDtypeStruct((len(chip_order), *pair_shape), jnp.int16)] * 2,
        in_specs=[smem, smem] + [vmem] * (chan_count + 2),
        out_specs=[vmem] * 2,
        scratch_shapes=[
            pltpu.VMEM((freqs, chans), jnp.float32),
            pltpu.VMEM((2, freqs, chans), jnp.bfloat16),
            pltpu.VMEM((2, freqs, 2 * chans), jnp.bfloat16),
        ],
        compiler_params=params,
        name="window_pairs",
    )(offsets, chan_where, *exchange(pieces, "chan", chan_order), quality, table)
    pairs = pl.pallas_call(
        merge_kernel,
        out_shape=[jax.ShapeDtypeStruct(pair_shape, jnp.int16)] * len(chip_order),
        in_specs=[vmem] * 2,
        out_specs=[vmem] * len(chip_order),
        compiler_params=params,
        name="merge_windows",
    )(own, *exchange([far], "chan", [1]))
    sums = pl.pallas_call(
        functools.partial(sum_kernel, tm_order, 1.0 / (CODE_TOP * math.sqrt(freqs))),
        out_shape=[jax.ShapeDtypeStruct((7, lag_rows, chans), jnp.int16)] * tm_count,
        in_specs=[smem] + [vmem] * len(chip_order),
        out_specs=[vmem] * tm_count,
        compiler_params=params,
        name="sum_windows",
    )(tm_where, *exchange(pairs, "chan", chip_order))
    pieces = pl.pallas_call(
        functools.partial(stack_kernel, windows * tm_count),
        out_shape=jax.ShapeDtypeStruct((chan_count, tm_count, piece_rows, chans), jnp.float32),
        in_specs=[smem, smem] + [vmem] * tm_count,
        out_specs=vmem,
        compiler_params=params,
        name="stack_pairs",
    )(offsets, tm_where, *exchange(sums, "tm", tm_order))
    shape = (chan_count * tm_count, piece_rows, chans)
    arrived = lax.all_to_all(pieces.reshape(shape), ("chan", "tm"), 0, 0, tiled=True)
    return pl.pallas_call(
        place_kernel,
        out_shape=jax.ShapeDtypeStruct((CH_DEV, offset_count, LAGS), jnp.float32),
        in_specs=[vmem],
        out_specs=vmem,
        compiler_params=params,
        name="place_lags",
    )(arrived.reshape(chan_count, tm_count, piece_rows, chans))


def shifted(value, axis, steps):
    count = lax.axis_size(axis)
    leading, last = (max(0, -steps), min(count, count - steps))
    return lax.ppermute(value, axis, [(source, source + steps) for source in range(leading, last)])


def lag_table(freq_count, lag_count):
    freq_index = jnp.arange(freq_count, dtype=jnp.int32)[:, None]
    double_lag = (2 * jnp.arange(lag_count, dtype=jnp.int32) - lag_count + 1)[None, :]
    turns = jnp.mod(freq_index * double_lag, 4 * freq_count)
    angles = turns.astype(jnp.float32) * (2.0 * math.pi / (4 * freq_count))
    cosine = jnp.cos(angles)
    sine = jnp.sin(angles)
    upper = jnp.concatenate([cosine, sine], axis=1)
    lower = jnp.concatenate([-sine, cosine], axis=1)
    return jnp.stack([upper, lower]).astype(jnp.bfloat16)


def whiten_parts(real_part, imag_part, magnitude, channel_level, usable):
    factor = usable.astype(jnp.float32)[:, None, :] / (magnitude + 0.5 * (channel_level + 1e-05))
    return jnp.stack([real_part * factor, imag_part * factor]).astype(jnp.bfloat16)


def cross_parts(own_real, own_imag, far_real, far_imag):
    own_real = own_real.astype(jnp.float32)
    own_imag = own_imag.astype(jnp.float32)
    far_real = far_real.astype(jnp.float32)
    far_imag = far_imag.astype(jnp.float32)
    return jnp.stack(
        [own_real * far_real + own_imag * far_imag, own_imag * far_real - own_real * far_imag]
    ).astype(jnp.bfloat16)


def pair_terms(corr_all):
    lag_count = corr_all.shape[-1] // 2
    real_corr = corr_all[..., :lag_count]
    imag_corr = corr_all[..., lag_count:]
    power = real_corr * real_corr + imag_corr * imag_corr
    mean_power = jnp.mean(power, axis=-1, keepdims=True)
    denominator = jnp.sqrt(power + 0.25 * (mean_power + 1e-06))
    return (
        jnp.sum(real_corr, axis=-3),
        jnp.sum(real_corr / denominator, axis=-3),
        jnp.sum(imag_corr / denominator, axis=-3),
    )


def shards(spectra, quality, offsets):
    chan_count = lax.axis_size("chan")
    tm_count = lax.axis_size("tm")
    levels = chan_count.bit_length() - 1
    table_bf = lag_table(F, LAGS)
    inv_root = 1.0 / math.sqrt(F)
    real_part = spectra[0].astype(jnp.float32)
    imag_part = spectra[1].astype(jnp.float32)
    magnitude = jnp.sqrt(real_part * real_part + imag_part * imag_part)
    band_total = lax.psum(jnp.sum(magnitude, axis=1), "chan")
    channel_level = (band_total / F)[:, None, :]
    whitened = whiten_parts(real_part, imag_part, magnitude, channel_level, quality)
    width_all = whitened.shape[3]
    padded = jnp.pad(whitened, ((0, 0), (0, 0), (0, 0), (0, width_all)))
    crossed_list = []
    for offset_index in range(NOFF):
        partner = lax.dynamic_slice_in_dim(padded, offsets[offset_index] * CH_DEV, width_all, 3)
        crossed_list.append(cross_parts(whitened[0], whitened[1], partner[0], partner[1]))
    crossed = jnp.stack(crossed_list, axis=1)
    corr_all = jnp.einsum(
        "cnwfh,cfl->nwhl",
        lax.all_to_all(crossed, "chan", split_axis=4, concat_axis=3, tiled=True),
        table_bf,
        preferred_element_type=jnp.float32,
    )
    linear_sum, real_sum, imag_sum = pair_terms(corr_all * inv_root)
    totals = lax.psum((linear_sum, real_sum, imag_sum), "tm")
    window_count = W_DEV * tm_count
    linear = totals[0] / window_count
    real_phase = totals[1] / window_count
    imag_phase = totals[2] / window_count
    stacks = jnp.transpose(linear * (real_phase * real_phase + imag_phase * imag_phase), (1, 0, 2))
    reverse_part = stacks
    for bit_index in range(levels):
        step_size = 1 << bit_index
        arrived = shifted(reverse_part, "chan", step_size)
        chosen = offsets // step_size % 2 == 1
        reverse_part = jnp.where(chosen[None, :, None], arrived, reverse_part)
    return stacks + jnp.flip(reverse_part, axis=2)


def solution(mesh):
    chan_count, tm_count = mesh.shape["chan"], mesh.shape["tm"]
    by_window = chan_count == W_DEV and tm_count == NOFF
    return jax.shard_map(
        window_shards if by_window else shards,
        mesh=mesh,
        in_specs=(P(None, "tm", "chan", None), P("tm", None), P()),
        out_specs=P("chan", None, None),
        check_vma=False,
    )
```

```python
import functools
import math

import jax
import jax.numpy as jnp
import numpy as np
from jax import lax
from jax.experimental import pallas as pl
from jax.experimental.pallas import tpu as pltpu
from jax.sharding import PartitionSpec as P

F = 2048
LAGS = 256
NOFF = 4
CH_DEV = 16
W_DEV = 8
VMEM_LIMIT = 48 * 1024 * 1024
CODE_TOP = 32767.0
OCTAVE = 256.0
LOWEST = -110.0


def encode(value):
    return jnp.round(value).astype(jnp.int32).astype(jnp.int16)


def decode(code):
    return code.astype(jnp.int32).astype(jnp.float32)


def level_code(peak):
    return jnp.ceil(jnp.maximum(jnp.log2(jnp.maximum(peak, 1e-30)), LOWEST) * OCTAVE) + 1.0


def level_of(code):
    return jnp.exp2(code * (1.0 / OCTAVE))


def half_table(freq_count, lag_count):
    freq_index = np.arange(freq_count, dtype=np.int64)[None, :]
    double_lag = (2 * np.arange(lag_count // 2, lag_count, dtype=np.int64) - lag_count + 1)[:, None]
    turns = np.mod(freq_index * double_lag, 4 * freq_count).astype(np.float32)
    angles = turns * np.float32(2.0 * math.pi / (4 * freq_count))
    return np.concatenate([np.cos(angles), np.sin(angles)]).astype(jnp.bfloat16)


def widest(offs_ref, reach):
    last = offs_ref.shape[0] - 1
    found = last
    for number in reversed(range(last)):
        found = jnp.where(offs_ref[number] == reach, number, found)
    return found


def offset_of(slot, offs_ref, reach):
    last, wide = offs_ref.shape[0] - 1, widest(offs_ref, reach)
    return offs_ref[jnp.where(slot == wide, last, jnp.where(slot == last, wide, slot))]


def window_kernel(order, offs_ref, where_ref, *refs):
    chan_count = len(order)
    spec_refs, (qual_ref, table_ref) = refs[:chan_count], refs[chan_count : chan_count + 2]
    out_refs = refs[chan_count + 2 : chan_count + 4]
    mag_ref, white_ref, cross_ref = refs[chan_count + 4 :]
    me = where_ref[0]
    _, band, chans = spec_refs[0].shape
    freqs = chan_count * band
    chip_count, blocks, lag_rows, _ = out_refs[0].shape
    offset_count = offs_ref.shape[0]
    half = chan_count * lag_rows
    step = 64

    total = jnp.zeros((8, chans), jnp.float32)
    for partner, spec_ref in zip(order, spec_refs):
        base = (me ^ partner) * band
        for row in range(0, band, step):
            real = spec_ref[0, row : row + step, :].astype(jnp.float32)
            imag = spec_ref[1, row : row + step, :].astype(jnp.float32)
            square = real * real + imag * imag
            magnitude = square * lax.rsqrt(jnp.maximum(square, 1e-30))
            mag_ref[pl.ds(pl.multiple_of(base + row, step), step), :] = magnitude
            total += jnp.sum(magnitude.reshape(step // 8, 8, chans), axis=0)
    level = jnp.sum(total, axis=0, keepdims=True) * (1.0 / freqs)
    floor = 0.5 * (level + 1e-05)

    for partner, spec_ref in zip(order, spec_refs):
        base = (me ^ partner) * band
        for row in range(0, band, step):
            held = pl.ds(pl.multiple_of(base + row, step), step)
            factor = pl.reciprocal(mag_ref[held, :] + floor, approx=True)
            for part in range(2):
                value = spec_ref[part, row : row + step, :].astype(jnp.float32) * factor
                white_ref[part, held, :] = value.astype(jnp.bfloat16)

    lane = lax.broadcasted_iota(jnp.int32, (1, chans), 1)
    line = lax.broadcasted_iota(jnp.int32, (lag_rows, chans), 0)
    usable = qual_ref[pl.ds(me, 1), :].astype(jnp.float32)
    levels = jnp.zeros((lag_rows, chans), jnp.float32)
    groups = [k ^ core for core in range(2) for k in chips(chan_count)]
    table = jnp.concatenate([table_ref[side, me ^ k] for side in range(2) for k in groups], axis=0)
    for number in range(offset_count):
        turn = chans - offset_of(number, offs_ref, chan_count // 2) * (chans // chan_count)
        slot = number % 2
        for row in range(0, freqs, step):
            own = [white_ref[part, row : row + step, :] for part in range(2)]
            far_real, far_imag = (pltpu.roll(value, turn, 1).astype(jnp.float32) for value in own)
            own_real, own_imag = (value.astype(jnp.float32) for value in own)
            real = own_real * far_real + own_imag * far_imag
            imag = own_imag * far_real - own_real * far_imag
            cross_ref[slot, row : row + step, 0:chans] = real.astype(jnp.bfloat16)
            cross_ref[slot, row : row + step, chans : 2 * chans] = imag.astype(jnp.bfloat16)
        sums = jnp.dot(table, cross_ref[slot], preferred_element_type=jnp.float32)
        cos_real, sin_real = sums[:half, :chans], sums[half:, :chans]
        cos_imag, sin_imag = sums[:half, chans:], sums[half:, chans:]
        corr = (
            (cos_real - sin_imag, sin_real + cos_imag),
            (cos_real + sin_imag, cos_imag - sin_real),
        )
        power = [real * real + imag * imag for real, imag in corr]
        mean_power = jnp.sum(power[0] + power[1], axis=0, keepdims=True) * (1.0 / (2 * half))
        extra = 0.25 * (mean_power + 1e-06 * freqs)
        peak = jnp.max(jnp.maximum(jnp.abs(corr[0][0]), jnp.abs(corr[1][0])), axis=0, keepdims=True)
        code = level_code(peak)
        keep = jnp.where(lane < turn, usable * pltpu.roll(usable, turn, 1), 0.0) * CODE_TOP
        upscale = keep / level_of(code)
        inverse = [lax.rsqrt(side + extra) * keep for side in power]
        kinds = [
            [real * upscale for real, _ in corr],
            [real * scale for (real, _), scale in zip(corr, inverse)],
            [imag * scale for (_, imag), scale in zip(corr, inverse)],
        ]
        if number == offset_count - 1:
            code = jnp.where(lane < chans // 2, code, pltpu.roll(code, chans // 2, 1))
            kinds = [[jnp.where(lane < chans // 2, ahead, pltpu.roll(back, chans // 2, 1))] for ahead, back in kinds]
        levels = jnp.where(line == number, code, levels)
        for place, value in enumerate(value for kind in kinds for value in kind):
            coded = encode(value).reshape(chan_count, lag_rows, chans)
            for core in range(2):
                rows = slice(core * chip_count, (core + 1) * chip_count)
                out_refs[core][:, 6 * number + place, :, :] = coded[rows]
    for out_ref in out_refs:
        for chip in range(chip_count):
            out_ref[chip, blocks - 1, :, :] = encode(levels)


def merge_kernel(own_ref, far_ref, *out_refs):
    blocks = own_ref.shape[1]
    for chip, out_ref in enumerate(out_refs):
        levels = [level_of(decode(ref[chip, blocks - 1])) for ref in (own_ref, far_ref)]
        code = level_code(levels[0] + levels[1])
        shares = [level / level_of(code) for level in levels]
        out_ref[blocks - 1, :, :] = encode(code)
        for block in range(blocks - 1):
            number, part = divmod(block, 6)
            linear = part < (2 if blocks - 1 - 6 * number > 3 else 1)
            own, far = decode(own_ref[chip, block]), decode(far_ref[chip, block])
            if linear:
                total = own * shares[0][number : number + 1, :] + far * shares[1][number : number + 1, :]
            else:
                total = (own + far) * 0.5
            out_ref[block, :, :] = encode(total)


def sum_kernel(order, scale, where_ref, *refs):
    code_refs, out_refs, held_ref = refs[: -len(order) - 1], refs[-len(order) - 1 : -1], refs[-1]
    blocks, _, chans = code_refs[0].shape
    slots = held_ref.shape[0]
    levels = [level_of(decode(codes_ref[blocks - 1])) * scale for codes_ref in code_refs]
    low = lax.broadcasted_iota(jnp.int32, (1, chans), 1) < chans // 2
    for number in range(slots):
        sides = 2 if number < slots - 1 else 1
        own = [level[number : number + 1, :] for level in levels]
        sums = []
        for place in range(3 * sides):
            codes = [decode(codes_ref[6 * number + place]) for codes_ref in code_refs]
            if place < sides:
                sums.append(sum(code * level for code, level in zip(codes, own)))
            else:
                sums.append(sum(codes) * (1.0 / len(code_refs)))
        if sides == 1:
            sums = [
                jnp.where(low, side, 0.0) for value in sums for side in (value, pltpu.roll(value, chans // 2, 1))
            ]
        peak = jnp.max(jnp.maximum(jnp.abs(sums[0]), jnp.abs(sums[1])), axis=0, keepdims=True)
        code = level_code(jnp.broadcast_to(peak, sums[0].shape))
        upscale = CODE_TOP / level_of(code)
        for part, value in enumerate([sums[0] * upscale, sums[1] * upscale, *sums[2:], code]):
            held_ref[number, part, :, :] = encode(value)
    for k, out_ref in zip(order, out_refs):
        out_ref[...] = held_ref[where_ref[0] ^ k]


def partners(count):
    return sorted(range(1, count), key=lambda k: (-(k >> 1).bit_count(), k & 1, k)) + [0]


def chips(count):
    return [k for k in partners(count) if k % 2 == 0]


def exchange(pieces, axis, order):
    count = lax.axis_size(axis)
    return [
        lax.ppermute(piece, axis, [(source, source ^ k) for source in range(count)]) if k else piece
        for k, piece in zip(order, pieces)
    ]


def split_kernel(order, where_ref, spec_ref, *refs):
    out_refs, sems = refs[:-1], refs[-1]
    copies = [
        pltpu.make_async_copy(spec_ref.at[:, where_ref[0] ^ k], out_ref, sems.at[number])
        for number, (k, out_ref) in enumerate(zip(order, out_refs))
    ]
    for copy in copies:
        copy.start()
    for copy in copies:
        copy.wait()


def stack_kernel(windows, offs_ref, where_ref, *refs):
    sums_refs, out_ref = refs[:-1], refs[-1]
    blocks, copies, rows, _ = out_ref.shape
    _, lag_rows, chans = sums_refs[0].shape
    per_sum = windows // len(sums_refs)
    levels = [level_of(decode(sums_ref[6])) * (1.0 / (CODE_TOP * windows)) for sums_ref in sums_refs]
    stacks = []
    for side in range(2):
        linear = sum(decode(sums_ref[side]) * level for sums_ref, level in zip(sums_refs, levels))
        real, imag = (
            sum(decode(sums_ref[part + side]) for sums_ref in sums_refs) * (per_sum / (CODE_TOP * windows))
            for part in (2, 4)
        )
        stacks.append(linear * (real * real + imag * imag))
    ahead = offset_of(where_ref[0], offs_ref, blocks // 2) * (chans // blocks)
    lane = lax.broadcasted_iota(jnp.int32, (1, chans), 1)
    behind = [jnp.where(lane >= ahead, pltpu.roll(stack, ahead, 1), 0.0) for stack in stacks]
    back = stacks[1] + behind[0]
    both = jnp.concatenate(
        [stacks[0] + behind[1]] + [back[row : row + 1, :] for row in reversed(range(lag_rows))], axis=0
    )
    wide = 2 * lag_rows
    parts = chans // wide
    turned = jnp.concatenate([both] * parts, axis=0).T
    per_block = chans // blocks
    for block in range(blocks):
        piece = jnp.zeros((rows, chans), jnp.float32)
        for part in range(parts):
            begin = block * per_block + part * rows
            piece = jnp.where(lane // wide == part, turned[begin : begin + rows, :], piece)
        for copy in range(copies):
            out_ref[block, copy, :, :] = piece


def place_kernel(offs_ref, parts_ref, out_ref):
    groups, offset_count, rows, lanes = parts_ref.shape
    half = out_ref.shape[2] // 2
    lag_rows = half // groups
    parts = out_ref.shape[0] // rows
    lane = lax.broadcasted_iota(jnp.int32, (1, lanes), 1)
    last, wide = offset_count - 1, widest(offs_ref, groups // 2)
    for part in range(parts):
        begin = part * 2 * lag_rows
        slots = []
        for number in range(offset_count):
            ahead = jnp.zeros((rows, lanes), jnp.float32)
            back = jnp.zeros((rows, lanes), jnp.float32)
            for group in range(groups):
                piece = parts_ref[group, number]
                first, end = group * lag_rows, half - (group + 1) * lag_rows
                ahead = jnp.where(lane // lag_rows == group, pltpu.roll(piece, (first - begin) % lanes, 1), ahead)
                back = jnp.where(
                    lane // lag_rows == groups - 1 - group, pltpu.roll(piece, (end - begin - lag_rows) % lanes, 1), back
                )
            slots.append((back, ahead))
        for number in range(offset_count):
            for side in range(2):
                value = slots[number][side]
                for other in range(last) if number == last else [last]:
                    value = jnp.where(wide == min(number, other), slots[other][side], value)
                out_ref[part * rows : (part + 1) * rows, number, side * half : (side + 1) * half] = value


def window_shards(spectra, quality, offsets):
    chan_count = lax.axis_size("chan")
    tm_count = lax.axis_size("tm")
    _, windows, band, chans = spectra.shape
    freqs = band * chan_count
    half = LAGS // 2
    lag_rows = half // chan_count
    offset_count = offsets.shape[0]
    piece_rows = 2 * lag_rows // chan_count
    smem = pl.BlockSpec(memory_space=pltpu.SMEM)
    vmem = pl.BlockSpec(memory_space=pltpu.VMEM)
    params = pltpu.CompilerParams(vmem_limit_bytes=VMEM_LIMIT)
    table = jnp.asarray(half_table(freqs, LAGS).reshape(2, chan_count, lag_rows, freqs))
    chan_index = lax.axis_index("chan").astype(jnp.int32)
    tm_index = lax.axis_index("tm").astype(jnp.int32)
    chan_where, tm_where = chan_index.reshape(1), tm_index.reshape(1)

    chan_order, tm_order = partners(chan_count), partners(tm_count)
    spectra = pltpu.with_memory_space_constraint(spectra, pltpu.HBM)
    pieces = []
    for part in (chan_order[:2], chan_order[2:]):
        pieces += pl.pallas_call(
            functools.partial(split_kernel, part),
            out_shape=[jax.ShapeDtypeStruct((2, band, chans), spectra.dtype)] * len(part),
            in_specs=[smem, pl.BlockSpec(memory_space=pltpu.HBM)],
            out_specs=[pl.BlockSpec(memory_space=pl.ANY)] * len(part),
            scratch_shapes=[pltpu.SemaphoreType.DMA((len(part),))],
            compiler_params=params,
            name="split_windows",
        )(chan_where, spectra)
    chip_order = chips(chan_count)
    pair_shape = (6 * offset_count - 2, lag_rows, chans)
    own, far = pl.pallas_call(
        functools.partial(window_kernel, chan_order),
        out_shape=[jax.ShapeDtypeStruct((len(chip_order), *pair_shape), jnp.int16)] * 2,
        in_specs=[smem, smem] + [vmem] * (chan_count + 2),
        out_specs=[vmem] * 2,
        scratch_shapes=[
            pltpu.VMEM((freqs, chans), jnp.float32),
            pltpu.VMEM((2, freqs, chans), jnp.bfloat16),
            pltpu.VMEM((2, freqs, 2 * chans), jnp.bfloat16),
        ],
        compiler_params=params,
        name="window_pairs",
    )(offsets, chan_where, *exchange(pieces, "chan", chan_order), quality, table)
    pairs = pl.pallas_call(
        merge_kernel,
        out_shape=[jax.ShapeDtypeStruct(pair_shape, jnp.int16)] * len(chip_order),
        in_specs=[vmem] * 2,
        out_specs=[vmem] * len(chip_order),
        compiler_params=params,
        name="merge_windows",
    )(own, *exchange([far], "chan", [1]))
    sums = pl.pallas_call(
        functools.partial(sum_kernel, tm_order, 1.0 / (CODE_TOP * math.sqrt(freqs))),
        out_shape=[jax.ShapeDtypeStruct((7, lag_rows, chans), jnp.int16)] * tm_count,
        in_specs=[smem] + [vmem] * len(chip_order),
        out_specs=[vmem] * tm_count,
        scratch_shapes=[pltpu.VMEM((offset_count, 7, lag_rows, chans), jnp.int16)],
        compiler_params=params,
        name="sum_windows",
    )(tm_where, *exchange(pairs, "chan", chip_order))
    pieces = pl.pallas_call(
        functools.partial(stack_kernel, windows * tm_count),
        out_shape=jax.ShapeDtypeStruct((chan_count, tm_count, piece_rows, chans), jnp.float32),
        in_specs=[smem, smem] + [vmem] * tm_count,
        out_specs=vmem,
        compiler_params=params,
        name="stack_pairs",
    )(offsets, tm_where, *exchange(sums, "tm", tm_order))
    shape = (chan_count * tm_count, piece_rows, chans)
    arrived = lax.all_to_all(pieces.reshape(shape), ("chan", "tm"), 0, 0, tiled=True)
    return pl.pallas_call(
        place_kernel,
        out_shape=jax.ShapeDtypeStruct((CH_DEV, offset_count, LAGS), jnp.float32),
        in_specs=[smem, vmem],
        out_specs=vmem,
        compiler_params=params,
        name="place_lags",
    )(offsets, arrived.reshape(chan_count, tm_count, piece_rows, chans))


def shifted(value, axis, steps):
    count = lax.axis_size(axis)
    leading, last = (max(0, -steps), min(count, count - steps))
    return lax.ppermute(value, axis, [(source, source + steps) for source in range(leading, last)])


def lag_table(freq_count, lag_count):
    freq_index = jnp.arange(freq_count, dtype=jnp.int32)[:, None]
    double_lag = (2 * jnp.arange(lag_count, dtype=jnp.int32) - lag_count + 1)[None, :]
    turns = jnp.mod(freq_index * double_lag, 4 * freq_count)
    angles = turns.astype(jnp.float32) * (2.0 * math.pi / (4 * freq_count))
    cosine = jnp.cos(angles)
    sine = jnp.sin(angles)
    upper = jnp.concatenate([cosine, sine], axis=1)
    lower = jnp.concatenate([-sine, cosine], axis=1)
    return jnp.stack([upper, lower]).astype(jnp.bfloat16)


def whiten_parts(real_part, imag_part, magnitude, channel_level, usable):
    factor = usable.astype(jnp.float32)[:, None, :] / (magnitude + 0.5 * (channel_level + 1e-05))
    return jnp.stack([real_part * factor, imag_part * factor]).astype(jnp.bfloat16)


def cross_parts(own_real, own_imag, far_real, far_imag):
    own_real = own_real.astype(jnp.float32)
    own_imag = own_imag.astype(jnp.float32)
    far_real = far_real.astype(jnp.float32)
    far_imag = far_imag.astype(jnp.float32)
    return jnp.stack(
        [own_real * far_real + own_imag * far_imag, own_imag * far_real - own_real * far_imag]
    ).astype(jnp.bfloat16)


def pair_terms(corr_all):
    lag_count = corr_all.shape[-1] // 2
    real_corr = corr_all[..., :lag_count]
    imag_corr = corr_all[..., lag_count:]
    power = real_corr * real_corr + imag_corr * imag_corr
    mean_power = jnp.mean(power, axis=-1, keepdims=True)
    denominator = jnp.sqrt(power + 0.25 * (mean_power + 1e-06))
    return (
        jnp.sum(real_corr, axis=-3),
        jnp.sum(real_corr / denominator, axis=-3),
        jnp.sum(imag_corr / denominator, axis=-3),
    )


def shards(spectra, quality, offsets):
    chan_count = lax.axis_size("chan")
    tm_count = lax.axis_size("tm")
    levels = chan_count.bit_length() - 1
    table_bf = lag_table(F, LAGS)
    inv_root = 1.0 / math.sqrt(F)
    real_part = spectra[0].astype(jnp.float32)
    imag_part = spectra[1].astype(jnp.float32)
    magnitude = jnp.sqrt(real_part * real_part + imag_part * imag_part)
    band_total = lax.psum(jnp.sum(magnitude, axis=1), "chan")
    channel_level = (band_total / F)[:, None, :]
    whitened = whiten_parts(real_part, imag_part, magnitude, channel_level, quality)
    width_all = whitened.shape[3]
    padded = jnp.pad(whitened, ((0, 0), (0, 0), (0, 0), (0, width_all)))
    crossed_list = []
    for offset_index in range(NOFF):
        partner = lax.dynamic_slice_in_dim(padded, offsets[offset_index] * CH_DEV, width_all, 3)
        crossed_list.append(cross_parts(whitened[0], whitened[1], partner[0], partner[1]))
    crossed = jnp.stack(crossed_list, axis=1)
    corr_all = jnp.einsum(
        "cnwfh,cfl->nwhl",
        lax.all_to_all(crossed, "chan", split_axis=4, concat_axis=3, tiled=True),
        table_bf,
        preferred_element_type=jnp.float32,
    )
    linear_sum, real_sum, imag_sum = pair_terms(corr_all * inv_root)
    totals = lax.psum((linear_sum, real_sum, imag_sum), "tm")
    window_count = W_DEV * tm_count
    linear = totals[0] / window_count
    real_phase = totals[1] / window_count
    imag_phase = totals[2] / window_count
    stacks = jnp.transpose(linear * (real_phase * real_phase + imag_phase * imag_phase), (1, 0, 2))
    reverse_part = stacks
    for bit_index in range(levels):
        step_size = 1 << bit_index
        arrived = shifted(reverse_part, "chan", step_size)
        chosen = offsets // step_size % 2 == 1
        reverse_part = jnp.where(chosen[None, :, None], arrived, reverse_part)
    return stacks + jnp.flip(reverse_part, axis=2)


def solution(mesh):
    chan_count, tm_count = mesh.shape["chan"], mesh.shape["tm"]
    by_window = chan_count == W_DEV and tm_count == NOFF
    return jax.shard_map(
        window_shards if by_window else shards,
        mesh=mesh,
        in_specs=(P(None, "tm", "chan", None), P("tm", None), P()),
        out_specs=P("chan", None, None),
        check_vma=False,
    )
```

```python
import functools
import math

import jax
import jax.numpy as jnp
import numpy as np
from jax import lax
from jax.experimental import pallas as pl
from jax.experimental.pallas import tpu as pltpu
from jax.sharding import PartitionSpec as P

F = 2048
LAGS = 256
NOFF = 4
CH_DEV = 16
W_DEV = 8
VMEM_LIMIT = 48 * 1024 * 1024
CODE_TOP = 32767.0
OCTAVE = 256.0
LOWEST = -110.0


def encode(value):
    return jnp.round(value).astype(jnp.int32).astype(jnp.int16)


def decode(code):
    return code.astype(jnp.int32).astype(jnp.float32)


def level_code(peak):
    return jnp.ceil(jnp.maximum(jnp.log2(jnp.maximum(peak, 1e-30)), LOWEST) * OCTAVE) + 1.0


def level_of(code):
    return jnp.exp2(code * (1.0 / OCTAVE))


def half_table(freq_count, lag_count):
    freq_index = np.arange(freq_count, dtype=np.int64)[None, :]
    double_lag = (2 * np.arange(lag_count // 2, lag_count, dtype=np.int64) - lag_count + 1)[:, None]
    turns = np.mod(freq_index * double_lag, 4 * freq_count).astype(np.float32)
    angles = turns * np.float32(2.0 * math.pi / (4 * freq_count))
    return np.concatenate([np.cos(angles), np.sin(angles)]).astype(jnp.bfloat16)


def widest(offs_ref, reach):
    last = offs_ref.shape[0] - 1
    found = last
    for number in reversed(range(last)):
        found = jnp.where(offs_ref[number] == reach, number, found)
    return found


def offset_of(slot, offs_ref, reach):
    last, wide = offs_ref.shape[0] - 1, widest(offs_ref, reach)
    return offs_ref[jnp.where(slot == wide, last, jnp.where(slot == last, wide, slot))]


def window_kernel(order, offs_hbm_ref, where_ref, *refs):
    chan_count = len(order)
    spec_refs, (qual_ref, table_ref) = refs[:chan_count], refs[chan_count : chan_count + 2]
    out_refs = refs[chan_count + 2 : chan_count + 4]
    mag_ref, white_ref, cross_ref, offs_ref, offs_sem = refs[chan_count + 4 :]
    fetch = pltpu.make_async_copy(offs_hbm_ref, offs_ref, offs_sem)
    fetch.start()
    me = where_ref[0]
    _, band, chans = spec_refs[0].shape
    freqs = chan_count * band
    chip_count, blocks, lag_rows, _ = out_refs[0].shape
    offset_count = offs_ref.shape[0]
    half = chan_count * lag_rows
    step = 64

    total = jnp.zeros((8, chans), jnp.float32)
    for partner, spec_ref in zip(order, spec_refs):
        base = (me ^ partner) * band
        for row in range(0, band, step):
            real = spec_ref[0, row : row + step, :].astype(jnp.float32)
            imag = spec_ref[1, row : row + step, :].astype(jnp.float32)
            square = real * real + imag * imag
            magnitude = square * lax.rsqrt(jnp.maximum(square, 1e-30))
            mag_ref[pl.ds(pl.multiple_of(base + row, step), step), :] = magnitude
            total += jnp.sum(magnitude.reshape(step // 8, 8, chans), axis=0)
    level = jnp.sum(total, axis=0, keepdims=True) * (1.0 / freqs)
    floor = 0.5 * (level + 1e-05)

    for partner, spec_ref in zip(order, spec_refs):
        base = (me ^ partner) * band
        for row in range(0, band, step):
            held = pl.ds(pl.multiple_of(base + row, step), step)
            factor = pl.reciprocal(mag_ref[held, :] + floor, approx=True)
            for part in range(2):
                value = spec_ref[part, row : row + step, :].astype(jnp.float32) * factor
                white_ref[part, held, :] = value.astype(jnp.bfloat16)

    lane = lax.broadcasted_iota(jnp.int32, (1, chans), 1)
    line = lax.broadcasted_iota(jnp.int32, (lag_rows, chans), 0)
    usable = qual_ref[pl.ds(me, 1), :].astype(jnp.float32)
    levels = jnp.zeros((lag_rows, chans), jnp.float32)
    groups = [k ^ core for core in range(2) for k in chips(chan_count)]
    fetch.wait()
    table = jnp.concatenate([table_ref[side, me ^ k] for side in range(2) for k in groups], axis=0)
    for number in range(offset_count):
        turn = chans - offset_of(number, offs_ref, chan_count // 2) * (chans // chan_count)
        slot = number % 2
        for row in range(0, freqs, step):
            own = [white_ref[part, row : row + step, :] for part in range(2)]
            far_real, far_imag = (pltpu.roll(value, turn, 1).astype(jnp.float32) for value in own)
            own_real, own_imag = (value.astype(jnp.float32) for value in own)
            real = own_real * far_real + own_imag * far_imag
            imag = own_imag * far_real - own_real * far_imag
            cross_ref[slot, row : row + step, 0:chans] = real.astype(jnp.bfloat16)
            cross_ref[slot, row : row + step, chans : 2 * chans] = imag.astype(jnp.bfloat16)
        sums = jnp.dot(table, cross_ref[slot], preferred_element_type=jnp.float32)
        cos_real, sin_real = sums[:half, :chans], sums[half:, :chans]
        cos_imag, sin_imag = sums[:half, chans:], sums[half:, chans:]
        corr = (
            (cos_real - sin_imag, sin_real + cos_imag),
            (cos_real + sin_imag, cos_imag - sin_real),
        )
        power = [real * real + imag * imag for real, imag in corr]
        mean_power = jnp.sum(power[0] + power[1], axis=0, keepdims=True) * (1.0 / (2 * half))
        extra = 0.25 * (mean_power + 1e-06 * freqs)
        peak = jnp.max(jnp.maximum(jnp.abs(corr[0][0]), jnp.abs(corr[1][0])), axis=0, keepdims=True)
        code = level_code(peak)
        keep = jnp.where(lane < turn, usable * pltpu.roll(usable, turn, 1), 0.0) * CODE_TOP
        upscale = keep / level_of(code)
        inverse = [lax.rsqrt(side + extra) * keep for side in power]
        kinds = [
            [real * upscale for real, _ in corr],
            [real * scale for (real, _), scale in zip(corr, inverse)],
            [imag * scale for (_, imag), scale in zip(corr, inverse)],
        ]
        if number == offset_count - 1:
            code = jnp.where(lane < chans // 2, code, pltpu.roll(code, chans // 2, 1))
            kinds = [[jnp.where(lane < chans // 2, ahead, pltpu.roll(back, chans // 2, 1))] for ahead, back in kinds]
        levels = jnp.where(line == number, code, levels)
        for place, value in enumerate(value for kind in kinds for value in kind):
            coded = encode(value).reshape(chan_count, lag_rows, chans)
            for core in range(2):
                rows = slice(core * chip_count, (core + 1) * chip_count)
                out_refs[core][:, 6 * number + place, :, :] = coded[rows]
    for number in range(offset_count):
        levels = jnp.where(line == offset_count + number, offs_ref[number].astype(jnp.float32), levels)
    wide = widest(offs_ref, chan_count // 2).astype(jnp.float32)
    levels = jnp.where(line == 2 * offset_count, wide, levels)
    for out_ref in out_refs:
        for chip in range(chip_count):
            out_ref[chip, blocks - 1, :, :] = encode(levels)


def merge_kernel(slots, own_ref, far_ref, *out_refs):
    blocks = own_ref.shape[1]
    for chip, out_ref in enumerate(out_refs):
        codes = [decode(ref[chip, blocks - 1]) for ref in (own_ref, far_ref)]
        levels = [level_of(code) for code in codes]
        code = level_code(levels[0] + levels[1])
        shares = [level / level_of(code) for level in levels]
        line = lax.broadcasted_iota(jnp.int32, code.shape, 0)
        out_ref[blocks - 1, :, :] = encode(jnp.where(line < slots, code, codes[0]))
        for block in range(blocks - 1):
            number, part = divmod(block, 6)
            linear = part < (2 if blocks - 1 - 6 * number > 3 else 1)
            own, far = decode(own_ref[chip, block]), decode(far_ref[chip, block])
            if linear:
                total = own * shares[0][number : number + 1, :] + far * shares[1][number : number + 1, :]
            else:
                total = (own + far) * 0.5
            out_ref[block, :, :] = encode(total)


def sum_kernel(order, scale, where_ref, *refs):
    code_refs, out_refs, held_ref = refs[: -len(order) - 1], refs[-len(order) - 1 : -1], refs[-1]
    blocks, _, chans = code_refs[0].shape
    slots = held_ref.shape[0]
    heads = [decode(codes_ref[blocks - 1]) for codes_ref in code_refs]
    levels = [level_of(head) * scale for head in heads]
    offsets = [heads[0][slots + number : slots + number + 1, :] for number in range(slots)]
    wide = heads[0][2 * slots : 2 * slots + 1, :]
    low = lax.broadcasted_iota(jnp.int32, (1, chans), 1) < chans // 2
    all_sums = []
    for number in range(slots):
        sides = 2 if number < slots - 1 else 1
        own = [level[number : number + 1, :] for level in levels]
        sums = []
        for place in range(3 * sides):
            codes = [decode(codes_ref[6 * number + place]) for codes_ref in code_refs]
            if place < sides:
                sums.append(sum(code * level for code, level in zip(codes, own)))
            else:
                sums.append(sum(codes) * (1.0 / len(code_refs)))
        if sides == 1:
            sums = [
                jnp.where(low, side, 0.0) for value in sums for side in (value, pltpu.roll(value, chans // 2, 1))
            ]
        all_sums.append(sums)
    line = lax.broadcasted_iota(jnp.int32, levels[0].shape, 0)
    last = slots - 1
    for number in range(slots):
        sums = all_sums[number]
        for other in range(last) if number == last else [last]:
            swap = wide == min(number, other)
            sums = [jnp.where(swap, value, kept) for value, kept in zip(all_sums[other], sums)]
        peak = jnp.max(jnp.maximum(jnp.abs(sums[0]), jnp.abs(sums[1])), axis=0, keepdims=True)
        code = level_code(peak)
        upscale = CODE_TOP / level_of(code)
        head = jnp.where(line == 0, code, offsets[number])
        for part, value in enumerate([sums[0] * upscale, sums[1] * upscale, *sums[2:], head]):
            held_ref[number, part, :, :] = encode(value)
    for k, out_ref in zip(order, out_refs):
        out_ref[...] = held_ref[where_ref[0] ^ k]


def partners(count):
    return sorted(range(1, count), key=lambda k: (-(k >> 1).bit_count(), k & 1, k)) + [0]


def chips(count):
    return [k for k in partners(count) if k % 2 == 0]


def exchange(pieces, axis, order):
    count = lax.axis_size(axis)
    return [
        lax.ppermute(piece, axis, [(source, source ^ k) for source in range(count)]) if k else piece
        for k, piece in zip(order, pieces)
    ]


def split_kernel(order, where_ref, spec_ref, *refs):
    out_refs, sems = refs[:-1], refs[-1]
    copies = [
        pltpu.make_async_copy(spec_ref.at[:, where_ref[0] ^ k], out_ref, sems.at[number])
        for number, (k, out_ref) in enumerate(zip(order, out_refs))
    ]
    for copy in copies:
        copy.start()
    for copy in copies:
        copy.wait()


def stack_kernel(windows, *refs):
    sums_refs, out_ref = refs[:-1], refs[-1]
    blocks, copies, rows, _ = out_ref.shape
    _, lag_rows, chans = sums_refs[0].shape
    per_sum = windows // len(sums_refs)
    heads = [decode(sums_ref[6]) for sums_ref in sums_refs]
    levels = [level_of(head[0:1, :]) * (1.0 / (CODE_TOP * windows)) for head in heads]
    stacks = []
    for side in range(2):
        linear = sum(decode(sums_ref[side]) * level for sums_ref, level in zip(sums_refs, levels))
        real, imag = (
            sum(decode(sums_ref[part + side]) for sums_ref in sums_refs) * (per_sum / (CODE_TOP * windows))
            for part in (2, 4)
        )
        stacks.append(linear * (real * real + imag * imag))
    offset = heads[0][1:2, :]
    lane = lax.broadcasted_iota(jnp.int32, (1, chans), 1)
    behind = [jnp.zeros_like(stack) for stack in stacks]
    for steps in range(1, blocks // 2 + 1):
        ahead = steps * (chans // blocks)
        chosen = (offset == steps) & (lane >= ahead)
        behind = [jnp.where(chosen, pltpu.roll(stack, ahead, 1), kept) for stack, kept in zip(stacks, behind)]
    back = stacks[1] + behind[0]
    both = jnp.concatenate(
        [stacks[0] + behind[1]] + [back[row : row + 1, :] for row in reversed(range(lag_rows))], axis=0
    )
    wide = 2 * lag_rows
    parts = chans // wide
    turned = jnp.concatenate([both] * parts, axis=0).T
    per_block = chans // blocks
    for block in range(blocks):
        piece = jnp.zeros((rows, chans), jnp.float32)
        for part in range(parts):
            begin = block * per_block + part * rows
            piece = jnp.where(lane // wide == part, turned[begin : begin + rows, :], piece)
        for copy in range(copies):
            out_ref[block, copy, :, :] = piece


def place_kernel(parts_ref, out_ref):
    groups, offset_count, rows, lanes = parts_ref.shape
    half = out_ref.shape[2] // 2
    lag_rows = half // groups
    parts = out_ref.shape[0] // rows
    lane = lax.broadcasted_iota(jnp.int32, (1, lanes), 1)
    for number in range(offset_count):
        for part in range(parts):
            ahead = jnp.zeros((rows, lanes), jnp.float32)
            back = jnp.zeros((rows, lanes), jnp.float32)
            begin = part * 2 * lag_rows
            for group in range(groups):
                piece = parts_ref[group, number]
                first, last = group * lag_rows, half - (group + 1) * lag_rows
                ahead = jnp.where(lane // lag_rows == group, pltpu.roll(piece, (first - begin) % lanes, 1), ahead)
                back = jnp.where(
                    lane // lag_rows == groups - 1 - group, pltpu.roll(piece, (last - begin - lag_rows) % lanes, 1), back
                )
            out_ref[part * rows : (part + 1) * rows, number, 0:half] = back
            out_ref[part * rows : (part + 1) * rows, number, half : 2 * half] = ahead


def window_shards(spectra, quality, offsets):
    chan_count = lax.axis_size("chan")
    tm_count = lax.axis_size("tm")
    _, windows, band, chans = spectra.shape
    freqs = band * chan_count
    half = LAGS // 2
    lag_rows = half // chan_count
    offset_count = offsets.shape[0]
    piece_rows = 2 * lag_rows // chan_count
    smem = pl.BlockSpec(memory_space=pltpu.SMEM)
    vmem = pl.BlockSpec(memory_space=pltpu.VMEM)
    params = pltpu.CompilerParams(vmem_limit_bytes=VMEM_LIMIT)
    table = jnp.asarray(half_table(freqs, LAGS).reshape(2, chan_count, lag_rows, freqs))
    chan_index = lax.axis_index("chan").astype(jnp.int32)
    tm_index = lax.axis_index("tm").astype(jnp.int32)
    chan_where, tm_where = chan_index.reshape(1), tm_index.reshape(1)

    chan_order, tm_order = partners(chan_count), partners(tm_count)
    kept = pl.BlockSpec(memory_space=pltpu.HBM)
    spectra = pltpu.with_memory_space_constraint(spectra, pltpu.HBM)
    pieces = []
    for part in (chan_order[:2], chan_order[2:]):
        pieces += pl.pallas_call(
            functools.partial(split_kernel, part),
            out_shape=[jax.ShapeDtypeStruct((2, band, chans), spectra.dtype)] * len(part),
            in_specs=[smem, kept],
            out_specs=[pl.BlockSpec(memory_space=pl.ANY)] * len(part),
            scratch_shapes=[pltpu.SemaphoreType.DMA((len(part),))],
            compiler_params=params,
            name="split_windows",
        )(chan_where, spectra)
    chip_order = chips(chan_count)
    pair_shape = (6 * offset_count - 2, lag_rows, chans)
    own, far = pl.pallas_call(
        functools.partial(window_kernel, chan_order),
        out_shape=[jax.ShapeDtypeStruct((len(chip_order), *pair_shape), jnp.int16)] * 2,
        in_specs=[kept, smem] + [vmem] * (chan_count + 2),
        out_specs=[vmem] * 2,
        scratch_shapes=[
            pltpu.VMEM((freqs, chans), jnp.float32),
            pltpu.VMEM((2, freqs, chans), jnp.bfloat16),
            pltpu.VMEM((2, freqs, 2 * chans), jnp.bfloat16),
            pltpu.SMEM(offsets.shape, jnp.int32),
            pltpu.SemaphoreType.DMA(()),
        ],
        compiler_params=params,
        name="window_pairs",
    )(pltpu.with_memory_space_constraint(offsets, pltpu.HBM), chan_where, *exchange(pieces, "chan", chan_order), quality, table)
    pairs = pl.pallas_call(
        functools.partial(merge_kernel, offset_count),
        out_shape=[jax.ShapeDtypeStruct(pair_shape, jnp.int16)] * len(chip_order),
        in_specs=[vmem] * 2,
        out_specs=[vmem] * len(chip_order),
        compiler_params=params,
        name="merge_windows",
    )(own, *exchange([far], "chan", [1]))
    sums = pl.pallas_call(
        functools.partial(sum_kernel, tm_order, 1.0 / (CODE_TOP * math.sqrt(freqs))),
        out_shape=[jax.ShapeDtypeStruct((7, lag_rows, chans), jnp.int16)] * tm_count,
        in_specs=[smem] + [vmem] * len(chip_order),
        out_specs=[vmem] * tm_count,
        scratch_shapes=[pltpu.VMEM((offset_count, 7, lag_rows, chans), jnp.int16)],
        compiler_params=params,
        name="sum_windows",
    )(tm_where, *exchange(pairs, "chan", chip_order))
    pieces = pl.pallas_call(
        functools.partial(stack_kernel, windows * tm_count),
        out_shape=jax.ShapeDtypeStruct((chan_count, tm_count, piece_rows, chans), jnp.float32),
        in_specs=[vmem] * tm_count,
        out_specs=vmem,
        compiler_params=params,
        name="stack_pairs",
    )(*exchange(sums, "tm", tm_order))
    shape = (chan_count * tm_count, piece_rows, chans)
    arrived = lax.all_to_all(pieces.reshape(shape), ("chan", "tm"), 0, 0, tiled=True)
    return pl.pallas_call(
        place_kernel,
        out_shape=jax.ShapeDtypeStruct((CH_DEV, offset_count, LAGS), jnp.float32),
        in_specs=[vmem],
        out_specs=vmem,
        compiler_params=params,
        name="place_lags",
    )(arrived.reshape(chan_count, tm_count, piece_rows, chans))


def shifted(value, axis, steps):
    count = lax.axis_size(axis)
    leading, last = (max(0, -steps), min(count, count - steps))
    return lax.ppermute(value, axis, [(source, source + steps) for source in range(leading, last)])


def lag_table(freq_count, lag_count):
    freq_index = jnp.arange(freq_count, dtype=jnp.int32)[:, None]
    double_lag = (2 * jnp.arange(lag_count, dtype=jnp.int32) - lag_count + 1)[None, :]
    turns = jnp.mod(freq_index * double_lag, 4 * freq_count)
    angles = turns.astype(jnp.float32) * (2.0 * math.pi / (4 * freq_count))
    cosine = jnp.cos(angles)
    sine = jnp.sin(angles)
    upper = jnp.concatenate([cosine, sine], axis=1)
    lower = jnp.concatenate([-sine, cosine], axis=1)
    return jnp.stack([upper, lower]).astype(jnp.bfloat16)


def whiten_parts(real_part, imag_part, magnitude, channel_level, usable):
    factor = usable.astype(jnp.float32)[:, None, :] / (magnitude + 0.5 * (channel_level + 1e-05))
    return jnp.stack([real_part * factor, imag_part * factor]).astype(jnp.bfloat16)


def cross_parts(own_real, own_imag, far_real, far_imag):
    own_real = own_real.astype(jnp.float32)
    own_imag = own_imag.astype(jnp.float32)
    far_real = far_real.astype(jnp.float32)
    far_imag = far_imag.astype(jnp.float32)
    return jnp.stack(
        [own_real * far_real + own_imag * far_imag, own_imag * far_real - own_real * far_imag]
    ).astype(jnp.bfloat16)


def pair_terms(corr_all):
    lag_count = corr_all.shape[-1] // 2
    real_corr = corr_all[..., :lag_count]
    imag_corr = corr_all[..., lag_count:]
    power = real_corr * real_corr + imag_corr * imag_corr
    mean_power = jnp.mean(power, axis=-1, keepdims=True)
    denominator = jnp.sqrt(power + 0.25 * (mean_power + 1e-06))
    return (
        jnp.sum(real_corr, axis=-3),
        jnp.sum(real_corr / denominator, axis=-3),
        jnp.sum(imag_corr / denominator, axis=-3),
    )


def shards(spectra, quality, offsets):
    chan_count = lax.axis_size("chan")
    tm_count = lax.axis_size("tm")
    levels = chan_count.bit_length() - 1
    table_bf = lag_table(F, LAGS)
    inv_root = 1.0 / math.sqrt(F)
    real_part = spectra[0].astype(jnp.float32)
    imag_part = spectra[1].astype(jnp.float32)
    magnitude = jnp.sqrt(real_part * real_part + imag_part * imag_part)
    band_total = lax.psum(jnp.sum(magnitude, axis=1), "chan")
    channel_level = (band_total / F)[:, None, :]
    whitened = whiten_parts(real_part, imag_part, magnitude, channel_level, quality)
    width_all = whitened.shape[3]
    padded = jnp.pad(whitened, ((0, 0), (0, 0), (0, 0), (0, width_all)))
    crossed_list = []
    for offset_index in range(NOFF):
        partner = lax.dynamic_slice_in_dim(padded, offsets[offset_index] * CH_DEV, width_all, 3)
        crossed_list.append(cross_parts(whitened[0], whitened[1], partner[0], partner[1]))
    crossed = jnp.stack(crossed_list, axis=1)
    corr_all = jnp.einsum(
        "cnwfh,cfl->nwhl",
        lax.all_to_all(crossed, "chan", split_axis=4, concat_axis=3, tiled=True),
        table_bf,
        preferred_element_type=jnp.float32,
    )
    linear_sum, real_sum, imag_sum = pair_terms(corr_all * inv_root)
    totals = lax.psum((linear_sum, real_sum, imag_sum), "tm")
    window_count = W_DEV * tm_count
    linear = totals[0] / window_count
    real_phase = totals[1] / window_count
    imag_phase = totals[2] / window_count
    stacks = jnp.transpose(linear * (real_phase * real_phase + imag_phase * imag_phase), (1, 0, 2))
    reverse_part = stacks
    for bit_index in range(levels):
        step_size = 1 << bit_index
        arrived = shifted(reverse_part, "chan", step_size)
        chosen = offsets // step_size % 2 == 1
        reverse_part = jnp.where(chosen[None, :, None], arrived, reverse_part)
    return stacks + jnp.flip(reverse_part, axis=2)


def solution(mesh):
    chan_count, tm_count = mesh.shape["chan"], mesh.shape["tm"]
    by_window = chan_count == W_DEV and tm_count == NOFF
    return jax.shard_map(
        window_shards if by_window else shards,
        mesh=mesh,
        in_specs=(P(None, "tm", "chan", None), P("tm", None), P()),
        out_specs=P("chan", None, None),
        check_vma=False,
    )
```

```python
import functools
import math

import jax
import jax.numpy as jnp
import numpy as np
from jax import lax
from jax.experimental import pallas as pl
from jax.experimental.pallas import tpu as pltpu
from jax.sharding import PartitionSpec as P

F = 2048
LAGS = 256
NOFF = 4
CH_DEV = 16
W_DEV = 8
VMEM_LIMIT = 48 * 1024 * 1024
CODE_TOP = 32767.0
OCTAVE = 256.0
LOWEST = -110.0


def encode(value):
    return jnp.round(value).astype(jnp.int32).astype(jnp.int16)


def decode(code):
    return code.astype(jnp.int32).astype(jnp.float32)


def level_code(peak):
    return jnp.ceil(jnp.maximum(jnp.log2(jnp.maximum(peak, 1e-30)), LOWEST) * OCTAVE) + 1.0


def level_of(code):
    return jnp.exp2(code * (1.0 / OCTAVE))


def half_table(freq_count, lag_count):
    freq_index = np.arange(freq_count, dtype=np.int64)[None, :]
    double_lag = (2 * np.arange(lag_count // 2, lag_count, dtype=np.int64) - lag_count + 1)[:, None]
    turns = np.mod(freq_index * double_lag, 4 * freq_count).astype(np.float32)
    angles = turns * np.float32(2.0 * math.pi / (4 * freq_count))
    return np.concatenate([np.cos(angles), np.sin(angles)]).astype(jnp.bfloat16)


def widest(offs_ref, reach):
    last = offs_ref.shape[0] - 1
    found = last
    for number in reversed(range(last)):
        found = jnp.where(offs_ref[number] == reach, number, found)
    return found


def offset_of(slot, offs_ref, reach):
    last, wide = offs_ref.shape[0] - 1, widest(offs_ref, reach)
    return offs_ref[jnp.where(slot == wide, last, jnp.where(slot == last, wide, slot))]


def window_kernel(order, offs_hbm_ref, where_ref, *refs):
    chan_count = len(order)
    spec_refs, (qual_ref, table_ref) = refs[:chan_count], refs[chan_count : chan_count + 2]
    out_refs = refs[chan_count + 2 : chan_count + 4]
    mag_ref, white_ref, cross_ref, offs_ref, offs_sem = refs[chan_count + 4 :]
    fetch = pltpu.make_async_copy(offs_hbm_ref, offs_ref, offs_sem)
    fetch.start()
    me = where_ref[0]
    _, band, chans = spec_refs[0].shape
    freqs = chan_count * band
    chip_count, blocks, lag_rows, _ = out_refs[0].shape
    offset_count = offs_ref.shape[0]
    half = chan_count * lag_rows
    step = 64

    total = jnp.zeros((8, chans), jnp.float32)
    for partner, spec_ref in zip(order, spec_refs):
        base = (me ^ partner) * band
        for row in range(0, band, step):
            real = spec_ref[0, row : row + step, :].astype(jnp.float32)
            imag = spec_ref[1, row : row + step, :].astype(jnp.float32)
            square = real * real + imag * imag
            magnitude = square * lax.rsqrt(jnp.maximum(square, 1e-30))
            mag_ref[pl.ds(pl.multiple_of(base + row, step), step), :] = magnitude
            total += jnp.sum(magnitude.reshape(step // 8, 8, chans), axis=0)
    level = jnp.sum(total, axis=0, keepdims=True) * (1.0 / freqs)
    floor = 0.5 * (level + 1e-05)

    for partner, spec_ref in zip(order, spec_refs):
        base = (me ^ partner) * band
        for row in range(0, band, step):
            held = pl.ds(pl.multiple_of(base + row, step), step)
            factor = pl.reciprocal(mag_ref[held, :] + floor, approx=True)
            for part in range(2):
                value = spec_ref[part, row : row + step, :].astype(jnp.float32) * factor
                white_ref[part, held, :] = value.astype(jnp.bfloat16)

    lane = lax.broadcasted_iota(jnp.int32, (1, chans), 1)
    line = lax.broadcasted_iota(jnp.int32, (lag_rows, chans), 0)
    usable = qual_ref[pl.ds(me, 1), :].astype(jnp.float32)
    levels = jnp.zeros((lag_rows, chans), jnp.float32)
    groups = [k ^ core for core in range(2) for k in chips(chan_count)]
    fetch.wait()
    table = jnp.concatenate([table_ref[side, me ^ k] for side in range(2) for k in groups], axis=0)
    turns = [chans - offset_of(number, offs_ref, chan_count // 2) * (chans // chan_count) for number in range(offset_count)]

    def cross(number):
        for row in range(0, freqs, step):
            own = [white_ref[part, row : row + step, :] for part in range(2)]
            far_real, far_imag = (pltpu.roll(value, turns[number], 1).astype(jnp.float32) for value in own)
            own_real, own_imag = (value.astype(jnp.float32) for value in own)
            real = own_real * far_real + own_imag * far_imag
            imag = own_imag * far_real - own_real * far_imag
            cross_ref[number, row : row + step, 0:chans] = real.astype(jnp.bfloat16)
            cross_ref[number, row : row + step, chans : 2 * chans] = imag.astype(jnp.bfloat16)

    def code_pairs(number, sums, levels):
        cos_real, sin_real = sums[:half, :chans], sums[half:, :chans]
        cos_imag, sin_imag = sums[:half, chans:], sums[half:, chans:]
        corr = (
            (cos_real - sin_imag, sin_real + cos_imag),
            (cos_real + sin_imag, cos_imag - sin_real),
        )
        power = [real * real + imag * imag for real, imag in corr]
        mean_power = jnp.sum(power[0] + power[1], axis=0, keepdims=True) * (1.0 / (2 * half))
        extra = 0.25 * (mean_power + 1e-06 * freqs)
        peak = jnp.max(jnp.maximum(jnp.abs(corr[0][0]), jnp.abs(corr[1][0])), axis=0, keepdims=True)
        code = level_code(peak)
        keep = jnp.where(lane < turns[number], usable * pltpu.roll(usable, turns[number], 1), 0.0) * CODE_TOP
        upscale = keep / level_of(code)
        inverse = [lax.rsqrt(side + extra) * keep for side in power]
        kinds = [
            [real * upscale for real, _ in corr],
            [real * scale for (real, _), scale in zip(corr, inverse)],
            [imag * scale for (_, imag), scale in zip(corr, inverse)],
        ]
        if number == offset_count - 1:
            code = jnp.where(lane < chans // 2, code, pltpu.roll(code, chans // 2, 1))
            kinds = [[jnp.where(lane < chans // 2, ahead, pltpu.roll(back, chans // 2, 1))] for ahead, back in kinds]
        for place, value in enumerate(value for kind in kinds for value in kind):
            coded = encode(value).reshape(chan_count, lag_rows, chans)
            for core in range(2):
                rows = slice(core * chip_count, (core + 1) * chip_count)
                out_refs[core][:, 6 * number + place, :, :] = coded[rows]
        return jnp.where(line == number, code, levels)

    waiting = []
    for number in range(offset_count + 2):
        if number < offset_count:
            cross(number)
        if 0 < number <= offset_count:
            waiting.append(jnp.dot(table, cross_ref[number - 1], preferred_element_type=jnp.float32))
        if number > 1:
            levels = code_pairs(number - 2, waiting[number - 2], levels)
    for number in range(offset_count):
        levels = jnp.where(line == offset_count + number, offs_ref[number].astype(jnp.float32), levels)
    wide = widest(offs_ref, chan_count // 2).astype(jnp.float32)
    levels = jnp.where(line == 2 * offset_count, wide, levels)
    for out_ref in out_refs:
        for chip in range(chip_count):
            out_ref[chip, blocks - 1, :, :] = encode(levels)


def merge_kernel(slots, own_ref, far_ref, *out_refs):
    blocks = own_ref.shape[1]
    for chip, out_ref in enumerate(out_refs):
        codes = [decode(ref[chip, blocks - 1]) for ref in (own_ref, far_ref)]
        levels = [level_of(code) for code in codes]
        code = level_code(levels[0] + levels[1])
        shares = [level / level_of(code) for level in levels]
        line = lax.broadcasted_iota(jnp.int32, code.shape, 0)
        out_ref[blocks - 1, :, :] = encode(jnp.where(line < slots, code, codes[0]))
        for block in range(blocks - 1):
            number, part = divmod(block, 6)
            linear = part < (2 if blocks - 1 - 6 * number > 3 else 1)
            own, far = decode(own_ref[chip, block]), decode(far_ref[chip, block])
            if linear:
                total = own * shares[0][number : number + 1, :] + far * shares[1][number : number + 1, :]
            else:
                total = (own + far) * 0.5
            out_ref[block, :, :] = encode(total)


def sum_kernel(order, scale, where_ref, *refs):
    code_refs, out_refs, held_ref = refs[: -len(order) - 1], refs[-len(order) - 1 : -1], refs[-1]
    blocks, _, chans = code_refs[0].shape
    slots = held_ref.shape[0]
    heads = [decode(codes_ref[blocks - 1]) for codes_ref in code_refs]
    levels = [level_of(head) * scale for head in heads]
    offsets = [heads[0][slots + number : slots + number + 1, :] for number in range(slots)]
    wide = heads[0][2 * slots : 2 * slots + 1, :]
    low = lax.broadcasted_iota(jnp.int32, (1, chans), 1) < chans // 2
    all_sums = []
    for number in range(slots):
        sides = 2 if number < slots - 1 else 1
        own = [level[number : number + 1, :] for level in levels]
        sums = []
        for place in range(3 * sides):
            codes = [decode(codes_ref[6 * number + place]) for codes_ref in code_refs]
            if place < sides:
                sums.append(sum(code * level for code, level in zip(codes, own)))
            else:
                sums.append(sum(codes) * (1.0 / len(code_refs)))
        if sides == 1:
            sums = [
                jnp.where(low, side, 0.0) for value in sums for side in (value, pltpu.roll(value, chans // 2, 1))
            ]
        all_sums.append(sums)
    line = lax.broadcasted_iota(jnp.int32, levels[0].shape, 0)
    last = slots - 1
    for number in range(slots):
        sums = all_sums[number]
        for other in range(last) if number == last else [last]:
            swap = wide == min(number, other)
            sums = [jnp.where(swap, value, kept) for value, kept in zip(all_sums[other], sums)]
        peak = jnp.max(jnp.maximum(jnp.abs(sums[0]), jnp.abs(sums[1])), axis=0, keepdims=True)
        code = level_code(peak)
        upscale = CODE_TOP / level_of(code)
        head = jnp.where(line == 0, code, offsets[number])
        for part, value in enumerate([sums[0] * upscale, sums[1] * upscale, *sums[2:], head]):
            held_ref[number, part, :, :] = encode(value)
    for k, out_ref in zip(order, out_refs):
        out_ref[...] = held_ref[where_ref[0] ^ k]


def partners(count):
    return sorted(range(1, count), key=lambda k: (-(k >> 1).bit_count(), k & 1, k)) + [0]


def chips(count):
    return [k for k in partners(count) if k % 2 == 0]


def exchange(pieces, axis, order):
    count = lax.axis_size(axis)
    return [
        lax.ppermute(piece, axis, [(source, source ^ k) for source in range(count)]) if k else piece
        for k, piece in zip(order, pieces)
    ]


def split_kernel(order, where_ref, spec_ref, *refs):
    out_refs, sems = refs[:-1], refs[-1]
    copies = [
        pltpu.make_async_copy(spec_ref.at[:, where_ref[0] ^ k], out_ref, sems.at[number])
        for number, (k, out_ref) in enumerate(zip(order, out_refs))
    ]
    for copy in copies:
        copy.start()
    for copy in copies:
        copy.wait()


def stack_kernel(windows, *refs):
    sums_refs, out_ref = refs[:-1], refs[-1]
    blocks, copies, rows, _ = out_ref.shape
    _, lag_rows, chans = sums_refs[0].shape
    per_sum = windows // len(sums_refs)
    heads = [decode(sums_ref[6]) for sums_ref in sums_refs]
    levels = [level_of(head[0:1, :]) * (1.0 / (CODE_TOP * windows)) for head in heads]
    stacks = []
    for side in range(2):
        linear = sum(decode(sums_ref[side]) * level for sums_ref, level in zip(sums_refs, levels))
        real, imag = (
            sum(decode(sums_ref[part + side]) for sums_ref in sums_refs) * (per_sum / (CODE_TOP * windows))
            for part in (2, 4)
        )
        stacks.append(linear * (real * real + imag * imag))
    offset = heads[0][1:2, :]
    lane = lax.broadcasted_iota(jnp.int32, (1, chans), 1)
    behind = [jnp.zeros_like(stack) for stack in stacks]
    for steps in range(1, blocks // 2 + 1):
        ahead = steps * (chans // blocks)
        chosen = (offset == steps) & (lane >= ahead)
        behind = [jnp.where(chosen, pltpu.roll(stack, ahead, 1), kept) for stack, kept in zip(stacks, behind)]
    back = stacks[1] + behind[0]
    both = jnp.concatenate(
        [stacks[0] + behind[1]] + [back[row : row + 1, :] for row in reversed(range(lag_rows))], axis=0
    )
    wide = 2 * lag_rows
    parts = chans // wide
    turned = jnp.concatenate([both] * parts, axis=0).T
    per_block = chans // blocks
    for block in range(blocks):
        piece = jnp.zeros((rows, chans), jnp.float32)
        for part in range(parts):
            begin = block * per_block + part * rows
            piece = jnp.where(lane // wide == part, turned[begin : begin + rows, :], piece)
        for copy in range(copies):
            out_ref[block, copy, :, :] = piece


def place_kernel(parts_ref, out_ref):
    groups, offset_count, rows, lanes = parts_ref.shape
    half = out_ref.shape[2] // 2
    lag_rows = half // groups
    parts = out_ref.shape[0] // rows
    lane = lax.broadcasted_iota(jnp.int32, (1, lanes), 1)
    for number in range(offset_count):
        for part in range(parts):
            ahead = jnp.zeros((rows, lanes), jnp.float32)
            back = jnp.zeros((rows, lanes), jnp.float32)
            begin = part * 2 * lag_rows
            for group in range(groups):
                piece = parts_ref[group, number]
                first, last = group * lag_rows, half - (group + 1) * lag_rows
                ahead = jnp.where(lane // lag_rows == group, pltpu.roll(piece, (first - begin) % lanes, 1), ahead)
                back = jnp.where(
                    lane // lag_rows == groups - 1 - group, pltpu.roll(piece, (last - begin - lag_rows) % lanes, 1), back
                )
            out_ref[part * rows : (part + 1) * rows, number, 0:half] = back
            out_ref[part * rows : (part + 1) * rows, number, half : 2 * half] = ahead


def window_shards(spectra, quality, offsets):
    chan_count = lax.axis_size("chan")
    tm_count = lax.axis_size("tm")
    _, windows, band, chans = spectra.shape
    freqs = band * chan_count
    half = LAGS // 2
    lag_rows = half // chan_count
    offset_count = offsets.shape[0]
    piece_rows = 2 * lag_rows // chan_count
    smem = pl.BlockSpec(memory_space=pltpu.SMEM)
    vmem = pl.BlockSpec(memory_space=pltpu.VMEM)
    params = pltpu.CompilerParams(vmem_limit_bytes=VMEM_LIMIT)
    table = jnp.asarray(half_table(freqs, LAGS).reshape(2, chan_count, lag_rows, freqs))
    chan_index = lax.axis_index("chan").astype(jnp.int32)
    tm_index = lax.axis_index("tm").astype(jnp.int32)
    chan_where, tm_where = chan_index.reshape(1), tm_index.reshape(1)

    chan_order, tm_order = partners(chan_count), partners(tm_count)
    kept = pl.BlockSpec(memory_space=pltpu.HBM)
    spectra = pltpu.with_memory_space_constraint(spectra, pltpu.HBM)
    pieces = []
    for part in (chan_order[:2], chan_order[2:]):
        pieces += pl.pallas_call(
            functools.partial(split_kernel, part),
            out_shape=[jax.ShapeDtypeStruct((2, band, chans), spectra.dtype)] * len(part),
            in_specs=[smem, kept],
            out_specs=[pl.BlockSpec(memory_space=pl.ANY)] * len(part),
            scratch_shapes=[pltpu.SemaphoreType.DMA((len(part),))],
            compiler_params=params,
            name="split_windows",
        )(chan_where, spectra)
    chip_order = chips(chan_count)
    pair_shape = (6 * offset_count - 2, lag_rows, chans)
    own, far = pl.pallas_call(
        functools.partial(window_kernel, chan_order),
        out_shape=[jax.ShapeDtypeStruct((len(chip_order), *pair_shape), jnp.int16)] * 2,
        in_specs=[kept, smem] + [vmem] * (chan_count + 2),
        out_specs=[vmem] * 2,
        scratch_shapes=[
            pltpu.VMEM((freqs, chans), jnp.float32),
            pltpu.VMEM((2, freqs, chans), jnp.bfloat16),
            pltpu.VMEM((offset_count, freqs, 2 * chans), jnp.bfloat16),
            pltpu.SMEM(offsets.shape, jnp.int32),
            pltpu.SemaphoreType.DMA(()),
        ],
        compiler_params=params,
        name="window_pairs",
    )(pltpu.with_memory_space_constraint(offsets, pltpu.HBM), chan_where, *exchange(pieces, "chan", chan_order), quality, table)
    pairs = pl.pallas_call(
        functools.partial(merge_kernel, offset_count),
        out_shape=[jax.ShapeDtypeStruct(pair_shape, jnp.int16)] * len(chip_order),
        in_specs=[vmem] * 2,
        out_specs=[vmem] * len(chip_order),
        compiler_params=params,
        name="merge_windows",
    )(own, *exchange([far], "chan", [1]))
    sums = pl.pallas_call(
        functools.partial(sum_kernel, tm_order, 1.0 / (CODE_TOP * math.sqrt(freqs))),
        out_shape=[jax.ShapeDtypeStruct((7, lag_rows, chans), jnp.int16)] * tm_count,
        in_specs=[smem] + [vmem] * len(chip_order),
        out_specs=[vmem] * tm_count,
        scratch_shapes=[pltpu.VMEM((offset_count, 7, lag_rows, chans), jnp.int16)],
        compiler_params=params,
        name="sum_windows",
    )(tm_where, *exchange(pairs, "chan", chip_order))
    pieces = pl.pallas_call(
        functools.partial(stack_kernel, windows * tm_count),
        out_shape=jax.ShapeDtypeStruct((chan_count, tm_count, piece_rows, chans), jnp.float32),
        in_specs=[vmem] * tm_count,
        out_specs=vmem,
        compiler_params=params,
        name="stack_pairs",
    )(*exchange(sums, "tm", tm_order))
    shape = (chan_count * tm_count, piece_rows, chans)
    arrived = lax.all_to_all(pieces.reshape(shape), ("chan", "tm"), 0, 0, tiled=True)
    return pl.pallas_call(
        place_kernel,
        out_shape=jax.ShapeDtypeStruct((CH_DEV, offset_count, LAGS), jnp.float32),
        in_specs=[vmem],
        out_specs=vmem,
        compiler_params=params,
        name="place_lags",
    )(arrived.reshape(chan_count, tm_count, piece_rows, chans))


def shifted(value, axis, steps):
    count = lax.axis_size(axis)
    leading, last = (max(0, -steps), min(count, count - steps))
    return lax.ppermute(value, axis, [(source, source + steps) for source in range(leading, last)])


def lag_table(freq_count, lag_count):
    freq_index = jnp.arange(freq_count, dtype=jnp.int32)[:, None]
    double_lag = (2 * jnp.arange(lag_count, dtype=jnp.int32) - lag_count + 1)[None, :]
    turns = jnp.mod(freq_index * double_lag, 4 * freq_count)
    angles = turns.astype(jnp.float32) * (2.0 * math.pi / (4 * freq_count))
    cosine = jnp.cos(angles)
    sine = jnp.sin(angles)
    upper = jnp.concatenate([cosine, sine], axis=1)
    lower = jnp.concatenate([-sine, cosine], axis=1)
    return jnp.stack([upper, lower]).astype(jnp.bfloat16)


def whiten_parts(real_part, imag_part, magnitude, channel_level, usable):
    factor = usable.astype(jnp.float32)[:, None, :] / (magnitude + 0.5 * (channel_level + 1e-05))
    return jnp.stack([real_part * factor, imag_part * factor]).astype(jnp.bfloat16)


def cross_parts(own_real, own_imag, far_real, far_imag):
    own_real = own_real.astype(jnp.float32)
    own_imag = own_imag.astype(jnp.float32)
    far_real = far_real.astype(jnp.float32)
    far_imag = far_imag.astype(jnp.float32)
    return jnp.stack(
        [own_real * far_real + own_imag * far_imag, own_imag * far_real - own_real * far_imag]
    ).astype(jnp.bfloat16)


def pair_terms(corr_all):
    lag_count = corr_all.shape[-1] // 2
    real_corr = corr_all[..., :lag_count]
    imag_corr = corr_all[..., lag_count:]
    power = real_corr * real_corr + imag_corr * imag_corr
    mean_power = jnp.mean(power, axis=-1, keepdims=True)
    denominator = jnp.sqrt(power + 0.25 * (mean_power + 1e-06))
    return (
        jnp.sum(real_corr, axis=-3),
        jnp.sum(real_corr / denominator, axis=-3),
        jnp.sum(imag_corr / denominator, axis=-3),
    )


def shards(spectra, quality, offsets):
    chan_count = lax.axis_size("chan")
    tm_count = lax.axis_size("tm")
    levels = chan_count.bit_length() - 1
    table_bf = lag_table(F, LAGS)
    inv_root = 1.0 / math.sqrt(F)
    real_part = spectra[0].astype(jnp.float32)
    imag_part = spectra[1].astype(jnp.float32)
    magnitude = jnp.sqrt(real_part * real_part + imag_part * imag_part)
    band_total = lax.psum(jnp.sum(magnitude, axis=1), "chan")
    channel_level = (band_total / F)[:, None, :]
    whitened = whiten_parts(real_part, imag_part, magnitude, channel_level, quality)
    width_all = whitened.shape[3]
    padded = jnp.pad(whitened, ((0, 0), (0, 0), (0, 0), (0, width_all)))
    crossed_list = []
    for offset_index in range(NOFF):
        partner = lax.dynamic_slice_in_dim(padded, offsets[offset_index] * CH_DEV, width_all, 3)
        crossed_list.append(cross_parts(whitened[0], whitened[1], partner[0], partner[1]))
    crossed = jnp.stack(crossed_list, axis=1)
    corr_all = jnp.einsum(
        "cnwfh,cfl->nwhl",
        lax.all_to_all(crossed, "chan", split_axis=4, concat_axis=3, tiled=True),
        table_bf,
        preferred_element_type=jnp.float32,
    )
    linear_sum, real_sum, imag_sum = pair_terms(corr_all * inv_root)
    totals = lax.psum((linear_sum, real_sum, imag_sum), "tm")
    window_count = W_DEV * tm_count
    linear = totals[0] / window_count
    real_phase = totals[1] / window_count
    imag_phase = totals[2] / window_count
    stacks = jnp.transpose(linear * (real_phase * real_phase + imag_phase * imag_phase), (1, 0, 2))
    reverse_part = stacks
    for bit_index in range(levels):
        step_size = 1 << bit_index
        arrived = shifted(reverse_part, "chan", step_size)
        chosen = offsets // step_size % 2 == 1
        reverse_part = jnp.where(chosen[None, :, None], arrived, reverse_part)
    return stacks + jnp.flip(reverse_part, axis=2)


def solution(mesh):
    chan_count, tm_count = mesh.shape["chan"], mesh.shape["tm"]
    by_window = chan_count == W_DEV and tm_count == NOFF
    return jax.shard_map(
        window_shards if by_window else shards,
        mesh=mesh,
        in_specs=(P(None, "tm", "chan", None), P("tm", None), P()),
        out_specs=P("chan", None, None),
        check_vma=False,
    )
```

```python
import functools
import math

import jax
import jax.numpy as jnp
import numpy as np
from jax import lax
from jax.experimental import pallas as pl
from jax.experimental.pallas import tpu as pltpu
from jax.sharding import PartitionSpec as P

F = 2048
LAGS = 256
NOFF = 4
CH_DEV = 16
W_DEV = 8
VMEM_LIMIT = 48 * 1024 * 1024
CODE_TOP = 32767.0
OCTAVE = 256.0
LOWEST = -110.0


def encode(value):
    return jnp.round(value).astype(jnp.int32).astype(jnp.int16)


def decode(code):
    return code.astype(jnp.int32).astype(jnp.float32)


def level_code(peak):
    return jnp.ceil(jnp.maximum(jnp.log2(jnp.maximum(peak, 1e-30)), LOWEST) * OCTAVE) + 1.0


def level_of(code):
    return jnp.exp2(code * (1.0 / OCTAVE))


def half_table(freq_count, lag_count):
    freq_index = np.arange(freq_count, dtype=np.int64)[None, :]
    double_lag = (2 * np.arange(lag_count // 2, lag_count, dtype=np.int64) - lag_count + 1)[:, None]
    turns = np.mod(freq_index * double_lag, 4 * freq_count).astype(np.float32)
    angles = turns * np.float32(2.0 * math.pi / (4 * freq_count))
    return np.concatenate([np.cos(angles), np.sin(angles)]).astype(jnp.bfloat16)


def widest(offs_ref, reach):
    last = offs_ref.shape[0] - 1
    found = last
    for number in reversed(range(last)):
        found = jnp.where(offs_ref[number] == reach, number, found)
    return found


def offset_of(slot, offs_ref, reach):
    last, wide = offs_ref.shape[0] - 1, widest(offs_ref, reach)
    return offs_ref[jnp.where(slot == wide, last, jnp.where(slot == last, wide, slot))]


def window_kernel(order, offs_hbm_ref, where_ref, *refs):
    chan_count = len(order)
    spec_refs, (qual_ref, table_ref) = refs[:chan_count], refs[chan_count : chan_count + 2]
    out_refs = refs[chan_count + 2 : chan_count + 4]
    mag_ref, white_ref, cross_ref, offs_ref, offs_sem = refs[chan_count + 4 :]
    fetch = pltpu.make_async_copy(offs_hbm_ref, offs_ref, offs_sem)
    fetch.start()
    me = where_ref[0]
    _, band, chans = spec_refs[0].shape
    freqs = chan_count * band
    chip_count, blocks, lag_rows, _ = out_refs[0].shape
    offset_count = offs_ref.shape[0]
    half = chan_count * lag_rows
    step = 64

    total = jnp.zeros((8, chans), jnp.float32)
    for partner, spec_ref in zip(order, spec_refs):
        base = (me ^ partner) * band
        for row in range(0, band, step):
            real = spec_ref[0, row : row + step, :].astype(jnp.float32)
            imag = spec_ref[1, row : row + step, :].astype(jnp.float32)
            square = real * real + imag * imag
            magnitude = square * lax.rsqrt(jnp.maximum(square, 1e-30))
            mag_ref[pl.ds(pl.multiple_of(base + row, step), step), :] = magnitude
            total += jnp.sum(magnitude.reshape(step // 8, 8, chans), axis=0)
    level = jnp.sum(total, axis=0, keepdims=True) * (1.0 / freqs)
    floor = 0.5 * (level + 1e-05)

    for partner, spec_ref in zip(order, spec_refs):
        base = (me ^ partner) * band
        for row in range(0, band, step):
            held = pl.ds(pl.multiple_of(base + row, step), step)
            factor = pl.reciprocal(mag_ref[held, :] + floor, approx=True)
            for part in range(2):
                value = spec_ref[part, row : row + step, :].astype(jnp.float32) * factor
                white_ref[part, held, :] = value.astype(jnp.bfloat16)

    lane = lax.broadcasted_iota(jnp.int32, (1, chans), 1)
    line = lax.broadcasted_iota(jnp.int32, (lag_rows, chans), 0)
    usable = qual_ref[pl.ds(me, 1), :].astype(jnp.float32)
    levels = jnp.zeros((lag_rows, chans), jnp.float32)
    groups = [k ^ core for core in range(2) for k in chips(chan_count)]
    fetch.wait()
    table = jnp.concatenate([table_ref[side, me ^ k] for side in range(2) for k in groups], axis=0)
    for number in range(offset_count):
        turn = chans - offset_of(number, offs_ref, chan_count // 2) * (chans // chan_count)
        slot = number % 2
        for row in range(0, freqs, step):
            own_real, own_imag = (white_ref[part, row : row + step, :].astype(jnp.float32) for part in range(2))
            far_real, far_imag = (pltpu.roll(value, turn, 1) for value in (own_real, own_imag))
            real = own_real * far_real + own_imag * far_imag
            imag = own_imag * far_real - own_real * far_imag
            cross_ref[slot, row : row + step, 0:chans] = real.astype(jnp.bfloat16)
            cross_ref[slot, row : row + step, chans : 2 * chans] = imag.astype(jnp.bfloat16)
        sums = jnp.dot(table, cross_ref[slot], preferred_element_type=jnp.float32)
        cos_real, sin_real = sums[:half, :chans], sums[half:, :chans]
        cos_imag, sin_imag = sums[:half, chans:], sums[half:, chans:]
        corr = (
            (cos_real - sin_imag, sin_real + cos_imag),
            (cos_real + sin_imag, cos_imag - sin_real),
        )
        power = [real * real + imag * imag for real, imag in corr]
        mean_power = jnp.sum(power[0] + power[1], axis=0, keepdims=True) * (1.0 / (2 * half))
        extra = 0.25 * (mean_power + 1e-06 * freqs)
        peak = jnp.max(jnp.maximum(jnp.abs(corr[0][0]), jnp.abs(corr[1][0])), axis=0, keepdims=True)
        code = level_code(peak)
        keep = jnp.where(lane < turn, usable * pltpu.roll(usable, turn, 1), 0.0) * CODE_TOP
        upscale = keep / level_of(code)
        inverse = [lax.rsqrt(side + extra) * keep for side in power]
        kinds = [
            [real * upscale for real, _ in corr],
            [real * scale for (real, _), scale in zip(corr, inverse)],
            [imag * scale for (_, imag), scale in zip(corr, inverse)],
        ]
        if number == offset_count - 1:
            code = jnp.where(lane < chans // 2, code, pltpu.roll(code, chans // 2, 1))
            kinds = [[jnp.where(lane < chans // 2, ahead, pltpu.roll(back, chans // 2, 1))] for ahead, back in kinds]
        levels = jnp.where(line == number, code, levels)
        for place, value in enumerate(value for kind in kinds for value in kind):
            coded = encode(value).reshape(chan_count, lag_rows, chans)
            for core in range(2):
                rows = slice(core * chip_count, (core + 1) * chip_count)
                out_refs[core][:, 6 * number + place, :, :] = coded[rows]
    for number in range(offset_count):
        levels = jnp.where(line == offset_count + number, offs_ref[number].astype(jnp.float32), levels)
    wide = widest(offs_ref, chan_count // 2).astype(jnp.float32)
    levels = jnp.where(line == 2 * offset_count, wide, levels)
    for out_ref in out_refs:
        for chip in range(chip_count):
            out_ref[chip, blocks - 1, :, :] = encode(levels)


def merge_kernel(slots, own_ref, far_ref, *out_refs):
    blocks = own_ref.shape[1]
    for chip, out_ref in enumerate(out_refs):
        codes = [decode(ref[chip, blocks - 1]) for ref in (own_ref, far_ref)]
        levels = [level_of(code) for code in codes]
        code = level_code(levels[0] + levels[1])
        shares = [level / level_of(code) for level in levels]
        line = lax.broadcasted_iota(jnp.int32, code.shape, 0)
        out_ref[blocks - 1, :, :] = encode(jnp.where(line < slots, code, codes[0]))
        for block in range(blocks - 1):
            number, part = divmod(block, 6)
            linear = part < (2 if blocks - 1 - 6 * number > 3 else 1)
            own, far = decode(own_ref[chip, block]), decode(far_ref[chip, block])
            if linear:
                total = own * shares[0][number : number + 1, :] + far * shares[1][number : number + 1, :]
            else:
                total = (own + far) * 0.5
            out_ref[block, :, :] = encode(total)


def sum_kernel(order, scale, where_ref, *refs):
    code_refs, out_refs, held_ref = refs[: -len(order) - 1], refs[-len(order) - 1 : -1], refs[-1]
    blocks, _, chans = code_refs[0].shape
    slots = held_ref.shape[0]
    heads = [decode(codes_ref[blocks - 1]) for codes_ref in code_refs]
    levels = [level_of(head) * scale for head in heads]
    offsets = [heads[0][slots + number : slots + number + 1, :] for number in range(slots)]
    wide = heads[0][2 * slots : 2 * slots + 1, :]
    low = lax.broadcasted_iota(jnp.int32, (1, chans), 1) < chans // 2
    all_sums = []
    for number in range(slots):
        sides = 2 if number < slots - 1 else 1
        own = [level[number : number + 1, :] for level in levels]
        sums = []
        for place in range(3 * sides):
            codes = [decode(codes_ref[6 * number + place]) for codes_ref in code_refs]
            if place < sides:
                sums.append(sum(code * level for code, level in zip(codes, own)))
            else:
                sums.append(sum(codes) * (1.0 / len(code_refs)))
        if sides == 1:
            sums = [
                jnp.where(low, side, 0.0) for value in sums for side in (value, pltpu.roll(value, chans // 2, 1))
            ]
        all_sums.append(sums)
    line = lax.broadcasted_iota(jnp.int32, levels[0].shape, 0)
    last = slots - 1
    for number in range(slots):
        sums = all_sums[number]
        for other in range(last) if number == last else [last]:
            swap = wide == min(number, other)
            sums = [jnp.where(swap, value, kept) for value, kept in zip(all_sums[other], sums)]
        peak = jnp.max(jnp.maximum(jnp.abs(sums[0]), jnp.abs(sums[1])), axis=0, keepdims=True)
        code = level_code(peak)
        upscale = CODE_TOP / level_of(code)
        head = jnp.where(line == 0, code, offsets[number])
        for part, value in enumerate([sums[0] * upscale, sums[1] * upscale, *sums[2:], head]):
            held_ref[number, part, :, :] = encode(value)
    for k, out_ref in zip(order, out_refs):
        out_ref[...] = held_ref[where_ref[0] ^ k]


def partners(count):
    return sorted(range(1, count), key=lambda k: (-(k >> 1).bit_count(), k & 1, k)) + [0]


def chips(count):
    return [k for k in partners(count) if k % 2 == 0]


def exchange(pieces, axis, order):
    count = lax.axis_size(axis)
    return [
        lax.ppermute(piece, axis, [(source, source ^ k) for source in range(count)]) if k else piece
        for k, piece in zip(order, pieces)
    ]


def split_kernel(order, where_ref, spec_ref, *refs):
    out_refs, sems = refs[:-1], refs[-1]
    copies = [
        pltpu.make_async_copy(spec_ref.at[:, where_ref[0] ^ k], out_ref, sems.at[number])
        for number, (k, out_ref) in enumerate(zip(order, out_refs))
    ]
    for copy in copies:
        copy.start()
    for copy in copies:
        copy.wait()


def stack_kernel(windows, *refs):
    sums_refs, out_ref = refs[:-1], refs[-1]
    blocks, copies, rows, _ = out_ref.shape
    _, lag_rows, chans = sums_refs[0].shape
    per_sum = windows // len(sums_refs)
    heads = [decode(sums_ref[6]) for sums_ref in sums_refs]
    levels = [level_of(head[0:1, :]) * (1.0 / (CODE_TOP * windows)) for head in heads]
    stacks = []
    for side in range(2):
        linear = sum(decode(sums_ref[side]) * level for sums_ref, level in zip(sums_refs, levels))
        real, imag = (
            sum(decode(sums_ref[part + side]) for sums_ref in sums_refs) * (per_sum / (CODE_TOP * windows))
            for part in (2, 4)
        )
        stacks.append(linear * (real * real + imag * imag))
    offset = heads[0][1:2, :]
    lane = lax.broadcasted_iota(jnp.int32, (1, chans), 1)
    behind = [jnp.zeros_like(stack) for stack in stacks]
    for steps in range(1, blocks // 2 + 1):
        ahead = steps * (chans // blocks)
        chosen = (offset == steps) & (lane >= ahead)
        behind = [jnp.where(chosen, pltpu.roll(stack, ahead, 1), kept) for stack, kept in zip(stacks, behind)]
    back = stacks[1] + behind[0]
    both = jnp.concatenate(
        [stacks[0] + behind[1]] + [back[row : row + 1, :] for row in reversed(range(lag_rows))], axis=0
    )
    wide = 2 * lag_rows
    parts = chans // wide
    turned = jnp.concatenate([both] * parts, axis=0).T
    per_block = chans // blocks
    for block in range(blocks):
        piece = jnp.zeros((rows, chans), jnp.float32)
        for part in range(parts):
            begin = block * per_block + part * rows
            piece = jnp.where(lane // wide == part, turned[begin : begin + rows, :], piece)
        for copy in range(copies):
            out_ref[block, copy, :, :] = piece


def place_kernel(parts_ref, out_ref):
    groups, offset_count, rows, lanes = parts_ref.shape
    half = out_ref.shape[2] // 2
    lag_rows = half // groups
    parts = out_ref.shape[0] // rows
    lane = lax.broadcasted_iota(jnp.int32, (1, lanes), 1)
    for number in range(offset_count):
        for part in range(parts):
            ahead = jnp.zeros((rows, lanes), jnp.float32)
            back = jnp.zeros((rows, lanes), jnp.float32)
            begin = part * 2 * lag_rows
            for group in range(groups):
                piece = parts_ref[group, number]
                first, last = group * lag_rows, half - (group + 1) * lag_rows
                ahead = jnp.where(lane // lag_rows == group, pltpu.roll(piece, (first - begin) % lanes, 1), ahead)
                back = jnp.where(
                    lane // lag_rows == groups - 1 - group, pltpu.roll(piece, (last - begin - lag_rows) % lanes, 1), back
                )
            out_ref[part * rows : (part + 1) * rows, number, 0:half] = back
            out_ref[part * rows : (part + 1) * rows, number, half : 2 * half] = ahead


def window_shards(spectra, quality, offsets):
    chan_count = lax.axis_size("chan")
    tm_count = lax.axis_size("tm")
    _, windows, band, chans = spectra.shape
    freqs = band * chan_count
    half = LAGS // 2
    lag_rows = half // chan_count
    offset_count = offsets.shape[0]
    piece_rows = 2 * lag_rows // chan_count
    smem = pl.BlockSpec(memory_space=pltpu.SMEM)
    vmem = pl.BlockSpec(memory_space=pltpu.VMEM)
    params = pltpu.CompilerParams(vmem_limit_bytes=VMEM_LIMIT)
    table = jnp.asarray(half_table(freqs, LAGS).reshape(2, chan_count, lag_rows, freqs))
    chan_index = lax.axis_index("chan").astype(jnp.int32)
    tm_index = lax.axis_index("tm").astype(jnp.int32)
    chan_where, tm_where = chan_index.reshape(1), tm_index.reshape(1)

    chan_order, tm_order = partners(chan_count), partners(tm_count)
    kept = pl.BlockSpec(memory_space=pltpu.HBM)
    spectra = pltpu.with_memory_space_constraint(spectra, pltpu.HBM)
    pieces = []
    for part in (chan_order[:2], chan_order[2:]):
        pieces += pl.pallas_call(
            functools.partial(split_kernel, part),
            out_shape=[jax.ShapeDtypeStruct((2, band, chans), spectra.dtype)] * len(part),
            in_specs=[smem, kept],
            out_specs=[pl.BlockSpec(memory_space=pl.ANY)] * len(part),
            scratch_shapes=[pltpu.SemaphoreType.DMA((len(part),))],
            compiler_params=params,
            name="split_windows",
        )(chan_where, spectra)
    chip_order = chips(chan_count)
    pair_shape = (6 * offset_count - 2, lag_rows, chans)
    own, far = pl.pallas_call(
        functools.partial(window_kernel, chan_order),
        out_shape=[jax.ShapeDtypeStruct((len(chip_order), *pair_shape), jnp.int16)] * 2,
        in_specs=[kept, smem] + [vmem] * (chan_count + 2),
        out_specs=[vmem] * 2,
        scratch_shapes=[
            pltpu.VMEM((freqs, chans), jnp.float32),
            pltpu.VMEM((2, freqs, chans), jnp.bfloat16),
            pltpu.VMEM((2, freqs, 2 * chans), jnp.bfloat16),
            pltpu.SMEM(offsets.shape, jnp.int32),
            pltpu.SemaphoreType.DMA(()),
        ],
        compiler_params=params,
        name="window_pairs",
    )(pltpu.with_memory_space_constraint(offsets, pltpu.HBM), chan_where, *exchange(pieces, "chan", chan_order), quality, table)
    pairs = pl.pallas_call(
        functools.partial(merge_kernel, offset_count),
        out_shape=[jax.ShapeDtypeStruct(pair_shape, jnp.int16)] * len(chip_order),
        in_specs=[vmem] * 2,
        out_specs=[vmem] * len(chip_order),
        compiler_params=params,
        name="merge_windows",
    )(own, *exchange([far], "chan", [1]))
    sums = pl.pallas_call(
        functools.partial(sum_kernel, tm_order, 1.0 / (CODE_TOP * math.sqrt(freqs))),
        out_shape=[jax.ShapeDtypeStruct((7, lag_rows, chans), jnp.int16)] * tm_count,
        in_specs=[smem] + [vmem] * len(chip_order),
        out_specs=[vmem] * tm_count,
        scratch_shapes=[pltpu.VMEM((offset_count, 7, lag_rows, chans), jnp.int16)],
        compiler_params=params,
        name="sum_windows",
    )(tm_where, *exchange(pairs, "chan", chip_order))
    pieces = pl.pallas_call(
        functools.partial(stack_kernel, windows * tm_count),
        out_shape=jax.ShapeDtypeStruct((chan_count, tm_count, piece_rows, chans), jnp.float32),
        in_specs=[vmem] * tm_count,
        out_specs=vmem,
        compiler_params=params,
        name="stack_pairs",
    )(*exchange(sums, "tm", tm_order))
    shape = (chan_count * tm_count, piece_rows, chans)
    arrived = lax.all_to_all(pieces.reshape(shape), ("chan", "tm"), 0, 0, tiled=True)
    return pl.pallas_call(
        place_kernel,
        out_shape=jax.ShapeDtypeStruct((CH_DEV, offset_count, LAGS), jnp.float32),
        in_specs=[vmem],
        out_specs=vmem,
        compiler_params=params,
        name="place_lags",
    )(arrived.reshape(chan_count, tm_count, piece_rows, chans))


def shifted(value, axis, steps):
    count = lax.axis_size(axis)
    leading, last = (max(0, -steps), min(count, count - steps))
    return lax.ppermute(value, axis, [(source, source + steps) for source in range(leading, last)])


def lag_table(freq_count, lag_count):
    freq_index = jnp.arange(freq_count, dtype=jnp.int32)[:, None]
    double_lag = (2 * jnp.arange(lag_count, dtype=jnp.int32) - lag_count + 1)[None, :]
    turns = jnp.mod(freq_index * double_lag, 4 * freq_count)
    angles = turns.astype(jnp.float32) * (2.0 * math.pi / (4 * freq_count))
    cosine = jnp.cos(angles)
    sine = jnp.sin(angles)
    upper = jnp.concatenate([cosine, sine], axis=1)
    lower = jnp.concatenate([-sine, cosine], axis=1)
    return jnp.stack([upper, lower]).astype(jnp.bfloat16)


def whiten_parts(real_part, imag_part, magnitude, channel_level, usable):
    factor = usable.astype(jnp.float32)[:, None, :] / (magnitude + 0.5 * (channel_level + 1e-05))
    return jnp.stack([real_part * factor, imag_part * factor]).astype(jnp.bfloat16)


def cross_parts(own_real, own_imag, far_real, far_imag):
    own_real = own_real.astype(jnp.float32)
    own_imag = own_imag.astype(jnp.float32)
    far_real = far_real.astype(jnp.float32)
    far_imag = far_imag.astype(jnp.float32)
    return jnp.stack(
        [own_real * far_real + own_imag * far_imag, own_imag * far_real - own_real * far_imag]
    ).astype(jnp.bfloat16)


def pair_terms(corr_all):
    lag_count = corr_all.shape[-1] // 2
    real_corr = corr_all[..., :lag_count]
    imag_corr = corr_all[..., lag_count:]
    power = real_corr * real_corr + imag_corr * imag_corr
    mean_power = jnp.mean(power, axis=-1, keepdims=True)
    denominator = jnp.sqrt(power + 0.25 * (mean_power + 1e-06))
    return (
        jnp.sum(real_corr, axis=-3),
        jnp.sum(real_corr / denominator, axis=-3),
        jnp.sum(imag_corr / denominator, axis=-3),
    )


def shards(spectra, quality, offsets):
    chan_count = lax.axis_size("chan")
    tm_count = lax.axis_size("tm")
    levels = chan_count.bit_length() - 1
    table_bf = lag_table(F, LAGS)
    inv_root = 1.0 / math.sqrt(F)
    real_part = spectra[0].astype(jnp.float32)
    imag_part = spectra[1].astype(jnp.float32)
    magnitude = jnp.sqrt(real_part * real_part + imag_part * imag_part)
    band_total = lax.psum(jnp.sum(magnitude, axis=1), "chan")
    channel_level = (band_total / F)[:, None, :]
    whitened = whiten_parts(real_part, imag_part, magnitude, channel_level, quality)
    width_all = whitened.shape[3]
    padded = jnp.pad(whitened, ((0, 0), (0, 0), (0, 0), (0, width_all)))
    crossed_list = []
    for offset_index in range(NOFF):
        partner = lax.dynamic_slice_in_dim(padded, offsets[offset_index] * CH_DEV, width_all, 3)
        crossed_list.append(cross_parts(whitened[0], whitened[1], partner[0], partner[1]))
    crossed = jnp.stack(crossed_list, axis=1)
    corr_all = jnp.einsum(
        "cnwfh,cfl->nwhl",
        lax.all_to_all(crossed, "chan", split_axis=4, concat_axis=3, tiled=True),
        table_bf,
        preferred_element_type=jnp.float32,
    )
    linear_sum, real_sum, imag_sum = pair_terms(corr_all * inv_root)
    totals = lax.psum((linear_sum, real_sum, imag_sum), "tm")
    window_count = W_DEV * tm_count
    linear = totals[0] / window_count
    real_phase = totals[1] / window_count
    imag_phase = totals[2] / window_count
    stacks = jnp.transpose(linear * (real_phase * real_phase + imag_phase * imag_phase), (1, 0, 2))
    reverse_part = stacks
    for bit_index in range(levels):
        step_size = 1 << bit_index
        arrived = shifted(reverse_part, "chan", step_size)
        chosen = offsets // step_size % 2 == 1
        reverse_part = jnp.where(chosen[None, :, None], arrived, reverse_part)
    return stacks + jnp.flip(reverse_part, axis=2)


def solution(mesh):
    chan_count, tm_count = mesh.shape["chan"], mesh.shape["tm"]
    by_window = chan_count == W_DEV and tm_count == NOFF
    return jax.shard_map(
        window_shards if by_window else shards,
        mesh=mesh,
        in_specs=(P(None, "tm", "chan", None), P("tm", None), P()),
        out_specs=P("chan", None, None),
        check_vma=False,
    )
```

```python
import functools
import math

import jax
import jax.numpy as jnp
import numpy as np
from jax import lax
from jax.experimental import pallas as pl
from jax.experimental.pallas import tpu as pltpu
from jax.sharding import PartitionSpec as P

F = 2048
LAGS = 256
NOFF = 4
CH_DEV = 16
W_DEV = 8
VMEM_LIMIT = 48 * 1024 * 1024
CODE_TOP = 32767.0
OCTAVE = 256.0
LOWEST = -110.0


def encode(value):
    return jnp.round(value).astype(jnp.int32).astype(jnp.int16)


def decode(code):
    return code.astype(jnp.int32).astype(jnp.float32)


def level_code(peak):
    return jnp.ceil(jnp.maximum(jnp.log2(jnp.maximum(peak, 1e-30)), LOWEST) * OCTAVE) + 1.0


def level_of(code):
    return jnp.exp2(code * (1.0 / OCTAVE))


def half_table(freq_count, lag_count):
    freq_index = np.arange(freq_count, dtype=np.int64)[None, :]
    double_lag = (2 * np.arange(lag_count // 2, lag_count, dtype=np.int64) - lag_count + 1)[:, None]
    turns = np.mod(freq_index * double_lag, 4 * freq_count).astype(np.float32)
    angles = turns * np.float32(2.0 * math.pi / (4 * freq_count))
    return np.concatenate([np.cos(angles), np.sin(angles)]).astype(jnp.bfloat16)


def widest(offs_ref, reach):
    last = offs_ref.shape[0] - 1
    found = last
    for number in reversed(range(last)):
        found = jnp.where(offs_ref[number] == reach, number, found)
    return found


def offset_of(slot, offs_ref, reach):
    last, wide = offs_ref.shape[0] - 1, widest(offs_ref, reach)
    return offs_ref[jnp.where(slot == wide, last, jnp.where(slot == last, wide, slot))]


def window_kernel(order, offs_hbm_ref, where_ref, *refs):
    chan_count = len(order)
    spec_refs, (qual_ref, table_ref) = refs[:chan_count], refs[chan_count : chan_count + 2]
    out_refs = refs[chan_count + 2 : chan_count + 4]
    mag_ref, white_ref, cross_ref, offs_ref, offs_sem = refs[chan_count + 4 :]
    fetch = pltpu.make_async_copy(offs_hbm_ref, offs_ref, offs_sem)
    fetch.start()
    me = where_ref[0]
    _, band, chans = spec_refs[0].shape
    freqs = chan_count * band
    chip_count, blocks, lag_rows, _ = out_refs[0].shape
    offset_count = offs_ref.shape[0]
    half = chan_count * lag_rows
    step = 64

    total = jnp.zeros((8, chans), jnp.float32)
    for partner, spec_ref in zip(order, spec_refs):
        base = (me ^ partner) * band
        for row in range(0, band, step):
            real = spec_ref[0, row : row + step, :].astype(jnp.float32)
            imag = spec_ref[1, row : row + step, :].astype(jnp.float32)
            square = real * real + imag * imag
            magnitude = square * lax.rsqrt(jnp.maximum(square, 1e-30))
            mag_ref[pl.ds(pl.multiple_of(base + row, step), step), :] = magnitude
            total += jnp.sum(magnitude.reshape(step // 8, 8, chans), axis=0)
    level = jnp.sum(total, axis=0, keepdims=True) * (1.0 / freqs)
    floor = 0.5 * (level + 1e-05)

    for partner, spec_ref in zip(order, spec_refs):
        base = (me ^ partner) * band
        for row in range(0, band, step):
            held = pl.ds(pl.multiple_of(base + row, step), step)
            factor = pl.reciprocal(mag_ref[held, :] + floor, approx=True)
            for part in range(2):
                value = spec_ref[part, row : row + step, :].astype(jnp.float32) * factor
                white_ref[part, held, :] = value.astype(jnp.bfloat16)

    lane = lax.broadcasted_iota(jnp.int32, (1, chans), 1)
    line = lax.broadcasted_iota(jnp.int32, (lag_rows, chans), 0)
    usable = qual_ref[pl.ds(me, 1), :].astype(jnp.float32)
    levels = jnp.zeros((lag_rows, chans), jnp.float32)
    groups = [k ^ core for core in range(2) for k in chips(chan_count)]
    fetch.wait()
    table = jnp.concatenate([table_ref[side, me ^ k] for side in range(2) for k in groups], axis=0)
    for number in range(offset_count):
        turn = chans - offset_of(number, offs_ref, chan_count // 2) * (chans // chan_count)
        slot = number % 2

        def cross(index, carry, slot=slot, turn=turn):
            rows = pl.ds(pl.multiple_of(index * step, step), step)
            own = [white_ref[part, rows, :] for part in range(2)]
            far_real, far_imag = (pltpu.roll(value, turn, 1).astype(jnp.float32) for value in own)
            own_real, own_imag = (value.astype(jnp.float32) for value in own)
            real = own_real * far_real + own_imag * far_imag
            imag = own_imag * far_real - own_real * far_imag
            cross_ref[slot, rows, 0:chans] = real.astype(jnp.bfloat16)
            cross_ref[slot, rows, chans : 2 * chans] = imag.astype(jnp.bfloat16)
            return carry

        lax.fori_loop(0, freqs // step, cross, 0, unroll=4)
        sums = jnp.dot(table, cross_ref[slot], preferred_element_type=jnp.float32)
        cos_real, sin_real = sums[:half, :chans], sums[half:, :chans]
        cos_imag, sin_imag = sums[:half, chans:], sums[half:, chans:]
        corr = (
            (cos_real - sin_imag, sin_real + cos_imag),
            (cos_real + sin_imag, cos_imag - sin_real),
        )
        power = [real * real + imag * imag for real, imag in corr]
        mean_power = jnp.sum(power[0] + power[1], axis=0, keepdims=True) * (1.0 / (2 * half))
        extra = 0.25 * (mean_power + 1e-06 * freqs)
        peak = jnp.max(jnp.maximum(jnp.abs(corr[0][0]), jnp.abs(corr[1][0])), axis=0, keepdims=True)
        code = level_code(peak)
        keep = jnp.where(lane < turn, usable * pltpu.roll(usable, turn, 1), 0.0) * CODE_TOP
        upscale = keep / level_of(code)
        inverse = [lax.rsqrt(side + extra) * keep for side in power]
        kinds = [
            [real * upscale for real, _ in corr],
            [real * scale for (real, _), scale in zip(corr, inverse)],
            [imag * scale for (_, imag), scale in zip(corr, inverse)],
        ]
        if number == offset_count - 1:
            code = jnp.where(lane < chans // 2, code, pltpu.roll(code, chans // 2, 1))
            kinds = [[jnp.where(lane < chans // 2, ahead, pltpu.roll(back, chans // 2, 1))] for ahead, back in kinds]
        levels = jnp.where(line == number, code, levels)
        for place, value in enumerate(value for kind in kinds for value in kind):
            coded = encode(value).reshape(chan_count, lag_rows, chans)
            for core in range(2):
                rows = slice(core * chip_count, (core + 1) * chip_count)
                out_refs[core][:, 6 * number + place, :, :] = coded[rows]
    for number in range(offset_count):
        levels = jnp.where(line == offset_count + number, offs_ref[number].astype(jnp.float32), levels)
    wide = widest(offs_ref, chan_count // 2).astype(jnp.float32)
    levels = jnp.where(line == 2 * offset_count, wide, levels)
    for out_ref in out_refs:
        for chip in range(chip_count):
            out_ref[chip, blocks - 1, :, :] = encode(levels)


def merge_kernel(slots, own_ref, far_ref, *out_refs):
    blocks = own_ref.shape[1]
    for chip, out_ref in enumerate(out_refs):
        codes = [decode(ref[chip, blocks - 1]) for ref in (own_ref, far_ref)]
        levels = [level_of(code) for code in codes]
        code = level_code(levels[0] + levels[1])
        shares = [level / level_of(code) for level in levels]
        line = lax.broadcasted_iota(jnp.int32, code.shape, 0)
        out_ref[blocks - 1, :, :] = encode(jnp.where(line < slots, code, codes[0]))
        for block in range(blocks - 1):
            number, part = divmod(block, 6)
            linear = part < (2 if blocks - 1 - 6 * number > 3 else 1)
            own, far = decode(own_ref[chip, block]), decode(far_ref[chip, block])
            if linear:
                total = own * shares[0][number : number + 1, :] + far * shares[1][number : number + 1, :]
            else:
                total = (own + far) * 0.5
            out_ref[block, :, :] = encode(total)


def sum_kernel(order, scale, where_ref, *refs):
    code_refs, out_refs, held_ref = refs[: -len(order) - 1], refs[-len(order) - 1 : -1], refs[-1]
    blocks, _, chans = code_refs[0].shape
    slots = held_ref.shape[0]
    heads = [decode(codes_ref[blocks - 1]) for codes_ref in code_refs]
    levels = [level_of(head) * scale for head in heads]
    offsets = [heads[0][slots + number : slots + number + 1, :] for number in range(slots)]
    wide = heads[0][2 * slots : 2 * slots + 1, :]
    low = lax.broadcasted_iota(jnp.int32, (1, chans), 1) < chans // 2
    all_sums = []
    for number in range(slots):
        sides = 2 if number < slots - 1 else 1
        own = [level[number : number + 1, :] for level in levels]
        sums = []
        for place in range(3 * sides):
            codes = [decode(codes_ref[6 * number + place]) for codes_ref in code_refs]
            if place < sides:
                sums.append(sum(code * level for code, level in zip(codes, own)))
            else:
                sums.append(sum(codes) * (1.0 / len(code_refs)))
        if sides == 1:
            sums = [
                jnp.where(low, side, 0.0) for value in sums for side in (value, pltpu.roll(value, chans // 2, 1))
            ]
        all_sums.append(sums)
    line = lax.broadcasted_iota(jnp.int32, levels[0].shape, 0)
    last = slots - 1
    for number in range(slots):
        sums = all_sums[number]
        for other in range(last) if number == last else [last]:
            swap = wide == min(number, other)
            sums = [jnp.where(swap, value, kept) for value, kept in zip(all_sums[other], sums)]
        peak = jnp.max(jnp.maximum(jnp.abs(sums[0]), jnp.abs(sums[1])), axis=0, keepdims=True)
        code = level_code(peak)
        upscale = CODE_TOP / level_of(code)
        head = jnp.where(line == 0, code, offsets[number])
        for part, value in enumerate([sums[0] * upscale, sums[1] * upscale, *sums[2:], head]):
            held_ref[number, part, :, :] = encode(value)
    for k, out_ref in zip(order, out_refs):
        out_ref[...] = held_ref[where_ref[0] ^ k]


def partners(count):
    return sorted(range(1, count), key=lambda k: (-(k >> 1).bit_count(), k & 1, k)) + [0]


def chips(count):
    return [k for k in partners(count) if k % 2 == 0]


def exchange(pieces, axis, order):
    count = lax.axis_size(axis)
    return [
        lax.ppermute(piece, axis, [(source, source ^ k) for source in range(count)]) if k else piece
        for k, piece in zip(order, pieces)
    ]


def split_kernel(order, where_ref, spec_ref, *refs):
    out_refs, sems = refs[:-1], refs[-1]
    copies = [
        pltpu.make_async_copy(spec_ref.at[:, where_ref[0] ^ k], out_ref, sems.at[number])
        for number, (k, out_ref) in enumerate(zip(order, out_refs))
    ]
    for copy in copies:
        copy.start()
    for copy in copies:
        copy.wait()


def stack_kernel(windows, *refs):
    sums_refs, out_ref = refs[:-1], refs[-1]
    blocks, copies, rows, _ = out_ref.shape
    _, lag_rows, chans = sums_refs[0].shape
    per_sum = windows // len(sums_refs)
    heads = [decode(sums_ref[6]) for sums_ref in sums_refs]
    levels = [level_of(head[0:1, :]) * (1.0 / (CODE_TOP * windows)) for head in heads]
    stacks = []
    for side in range(2):
        linear = sum(decode(sums_ref[side]) * level for sums_ref, level in zip(sums_refs, levels))
        real, imag = (
            sum(decode(sums_ref[part + side]) for sums_ref in sums_refs) * (per_sum / (CODE_TOP * windows))
            for part in (2, 4)
        )
        stacks.append(linear * (real * real + imag * imag))
    offset = heads[0][1:2, :]
    lane = lax.broadcasted_iota(jnp.int32, (1, chans), 1)
    behind = [jnp.zeros_like(stack) for stack in stacks]
    for steps in range(1, blocks // 2 + 1):
        ahead = steps * (chans // blocks)
        chosen = (offset == steps) & (lane >= ahead)
        behind = [jnp.where(chosen, pltpu.roll(stack, ahead, 1), kept) for stack, kept in zip(stacks, behind)]
    back = stacks[1] + behind[0]
    both = jnp.concatenate(
        [stacks[0] + behind[1]] + [back[row : row + 1, :] for row in reversed(range(lag_rows))], axis=0
    )
    wide = 2 * lag_rows
    parts = chans // wide
    turned = jnp.concatenate([both] * parts, axis=0).T
    per_block = chans // blocks
    for block in range(blocks):
        piece = jnp.zeros((rows, chans), jnp.float32)
        for part in range(parts):
            begin = block * per_block + part * rows
            piece = jnp.where(lane // wide == part, turned[begin : begin + rows, :], piece)
        for copy in range(copies):
            out_ref[block, copy, :, :] = piece


def place_kernel(parts_ref, out_ref):
    groups, offset_count, rows, lanes = parts_ref.shape
    half = out_ref.shape[2] // 2
    lag_rows = half // groups
    parts = out_ref.shape[0] // rows
    lane = lax.broadcasted_iota(jnp.int32, (1, lanes), 1)
    for number in range(offset_count):
        for part in range(parts):
            ahead = jnp.zeros((rows, lanes), jnp.float32)
            back = jnp.zeros((rows, lanes), jnp.float32)
            begin = part * 2 * lag_rows
            for group in range(groups):
                piece = parts_ref[group, number]
                first, last = group * lag_rows, half - (group + 1) * lag_rows
                ahead = jnp.where(lane // lag_rows == group, pltpu.roll(piece, (first - begin) % lanes, 1), ahead)
                back = jnp.where(
                    lane // lag_rows == groups - 1 - group, pltpu.roll(piece, (last - begin - lag_rows) % lanes, 1), back
                )
            out_ref[part * rows : (part + 1) * rows, number, 0:half] = back
            out_ref[part * rows : (part + 1) * rows, number, half : 2 * half] = ahead


def window_shards(spectra, quality, offsets):
    chan_count = lax.axis_size("chan")
    tm_count = lax.axis_size("tm")
    _, windows, band, chans = spectra.shape
    freqs = band * chan_count
    half = LAGS // 2
    lag_rows = half // chan_count
    offset_count = offsets.shape[0]
    piece_rows = 2 * lag_rows // chan_count
    smem = pl.BlockSpec(memory_space=pltpu.SMEM)
    vmem = pl.BlockSpec(memory_space=pltpu.VMEM)
    params = pltpu.CompilerParams(vmem_limit_bytes=VMEM_LIMIT)
    table = jnp.asarray(half_table(freqs, LAGS).reshape(2, chan_count, lag_rows, freqs))
    chan_index = lax.axis_index("chan").astype(jnp.int32)
    tm_index = lax.axis_index("tm").astype(jnp.int32)
    chan_where, tm_where = chan_index.reshape(1), tm_index.reshape(1)

    chan_order, tm_order = partners(chan_count), partners(tm_count)
    kept = pl.BlockSpec(memory_space=pltpu.HBM)
    spectra = pltpu.with_memory_space_constraint(spectra, pltpu.HBM)
    pieces = []
    for part in (chan_order[:2], chan_order[2:]):
        pieces += pl.pallas_call(
            functools.partial(split_kernel, part),
            out_shape=[jax.ShapeDtypeStruct((2, band, chans), spectra.dtype)] * len(part),
            in_specs=[smem, kept],
            out_specs=[pl.BlockSpec(memory_space=pl.ANY)] * len(part),
            scratch_shapes=[pltpu.SemaphoreType.DMA((len(part),))],
            compiler_params=params,
            name="split_windows",
        )(chan_where, spectra)
    chip_order = chips(chan_count)
    pair_shape = (6 * offset_count - 2, lag_rows, chans)
    own, far = pl.pallas_call(
        functools.partial(window_kernel, chan_order),
        out_shape=[jax.ShapeDtypeStruct((len(chip_order), *pair_shape), jnp.int16)] * 2,
        in_specs=[kept, smem] + [vmem] * (chan_count + 2),
        out_specs=[vmem] * 2,
        scratch_shapes=[
            pltpu.VMEM((freqs, chans), jnp.float32),
            pltpu.VMEM((2, freqs, chans), jnp.bfloat16),
            pltpu.VMEM((2, freqs, 2 * chans), jnp.bfloat16),
            pltpu.SMEM(offsets.shape, jnp.int32),
            pltpu.SemaphoreType.DMA(()),
        ],
        compiler_params=params,
        name="window_pairs",
    )(pltpu.with_memory_space_constraint(offsets, pltpu.HBM), chan_where, *exchange(pieces, "chan", chan_order), quality, table)
    pairs = pl.pallas_call(
        functools.partial(merge_kernel, offset_count),
        out_shape=[jax.ShapeDtypeStruct(pair_shape, jnp.int16)] * len(chip_order),
        in_specs=[vmem] * 2,
        out_specs=[vmem] * len(chip_order),
        compiler_params=params,
        name="merge_windows",
    )(own, *exchange([far], "chan", [1]))
    sums = pl.pallas_call(
        functools.partial(sum_kernel, tm_order, 1.0 / (CODE_TOP * math.sqrt(freqs))),
        out_shape=[jax.ShapeDtypeStruct((7, lag_rows, chans), jnp.int16)] * tm_count,
        in_specs=[smem] + [vmem] * len(chip_order),
        out_specs=[vmem] * tm_count,
        scratch_shapes=[pltpu.VMEM((offset_count, 7, lag_rows, chans), jnp.int16)],
        compiler_params=params,
        name="sum_windows",
    )(tm_where, *exchange(pairs, "chan", chip_order))
    pieces = pl.pallas_call(
        functools.partial(stack_kernel, windows * tm_count),
        out_shape=jax.ShapeDtypeStruct((chan_count, tm_count, piece_rows, chans), jnp.float32),
        in_specs=[vmem] * tm_count,
        out_specs=vmem,
        compiler_params=params,
        name="stack_pairs",
    )(*exchange(sums, "tm", tm_order))
    shape = (chan_count * tm_count, piece_rows, chans)
    arrived = lax.all_to_all(pieces.reshape(shape), ("chan", "tm"), 0, 0, tiled=True)
    return pl.pallas_call(
        place_kernel,
        out_shape=jax.ShapeDtypeStruct((CH_DEV, offset_count, LAGS), jnp.float32),
        in_specs=[vmem],
        out_specs=vmem,
        compiler_params=params,
        name="place_lags",
    )(arrived.reshape(chan_count, tm_count, piece_rows, chans))


def shifted(value, axis, steps):
    count = lax.axis_size(axis)
    leading, last = (max(0, -steps), min(count, count - steps))
    return lax.ppermute(value, axis, [(source, source + steps) for source in range(leading, last)])


def lag_table(freq_count, lag_count):
    freq_index = jnp.arange(freq_count, dtype=jnp.int32)[:, None]
    double_lag = (2 * jnp.arange(lag_count, dtype=jnp.int32) - lag_count + 1)[None, :]
    turns = jnp.mod(freq_index * double_lag, 4 * freq_count)
    angles = turns.astype(jnp.float32) * (2.0 * math.pi / (4 * freq_count))
    cosine = jnp.cos(angles)
    sine = jnp.sin(angles)
    upper = jnp.concatenate([cosine, sine], axis=1)
    lower = jnp.concatenate([-sine, cosine], axis=1)
    return jnp.stack([upper, lower]).astype(jnp.bfloat16)


def whiten_parts(real_part, imag_part, magnitude, channel_level, usable):
    factor = usable.astype(jnp.float32)[:, None, :] / (magnitude + 0.5 * (channel_level + 1e-05))
    return jnp.stack([real_part * factor, imag_part * factor]).astype(jnp.bfloat16)


def cross_parts(own_real, own_imag, far_real, far_imag):
    own_real = own_real.astype(jnp.float32)
    own_imag = own_imag.astype(jnp.float32)
    far_real = far_real.astype(jnp.float32)
    far_imag = far_imag.astype(jnp.float32)
    return jnp.stack(
        [own_real * far_real + own_imag * far_imag, own_imag * far_real - own_real * far_imag]
    ).astype(jnp.bfloat16)


def pair_terms(corr_all):
    lag_count = corr_all.shape[-1] // 2
    real_corr = corr_all[..., :lag_count]
    imag_corr = corr_all[..., lag_count:]
    power = real_corr * real_corr + imag_corr * imag_corr
    mean_power = jnp.mean(power, axis=-1, keepdims=True)
    denominator = jnp.sqrt(power + 0.25 * (mean_power + 1e-06))
    return (
        jnp.sum(real_corr, axis=-3),
        jnp.sum(real_corr / denominator, axis=-3),
        jnp.sum(imag_corr / denominator, axis=-3),
    )


def shards(spectra, quality, offsets):
    chan_count = lax.axis_size("chan")
    tm_count = lax.axis_size("tm")
    levels = chan_count.bit_length() - 1
    table_bf = lag_table(F, LAGS)
    inv_root = 1.0 / math.sqrt(F)
    real_part = spectra[0].astype(jnp.float32)
    imag_part = spectra[1].astype(jnp.float32)
    magnitude = jnp.sqrt(real_part * real_part + imag_part * imag_part)
    band_total = lax.psum(jnp.sum(magnitude, axis=1), "chan")
    channel_level = (band_total / F)[:, None, :]
    whitened = whiten_parts(real_part, imag_part, magnitude, channel_level, quality)
    width_all = whitened.shape[3]
    padded = jnp.pad(whitened, ((0, 0), (0, 0), (0, 0), (0, width_all)))
    crossed_list = []
    for offset_index in range(NOFF):
        partner = lax.dynamic_slice_in_dim(padded, offsets[offset_index] * CH_DEV, width_all, 3)
        crossed_list.append(cross_parts(whitened[0], whitened[1], partner[0], partner[1]))
    crossed = jnp.stack(crossed_list, axis=1)
    corr_all = jnp.einsum(
        "cnwfh,cfl->nwhl",
        lax.all_to_all(crossed, "chan", split_axis=4, concat_axis=3, tiled=True),
        table_bf,
        preferred_element_type=jnp.float32,
    )
    linear_sum, real_sum, imag_sum = pair_terms(corr_all * inv_root)
    totals = lax.psum((linear_sum, real_sum, imag_sum), "tm")
    window_count = W_DEV * tm_count
    linear = totals[0] / window_count
    real_phase = totals[1] / window_count
    imag_phase = totals[2] / window_count
    stacks = jnp.transpose(linear * (real_phase * real_phase + imag_phase * imag_phase), (1, 0, 2))
    reverse_part = stacks
    for bit_index in range(levels):
        step_size = 1 << bit_index
        arrived = shifted(reverse_part, "chan", step_size)
        chosen = offsets // step_size % 2 == 1
        reverse_part = jnp.where(chosen[None, :, None], arrived, reverse_part)
    return stacks + jnp.flip(reverse_part, axis=2)


def solution(mesh):
    chan_count, tm_count = mesh.shape["chan"], mesh.shape["tm"]
    by_window = chan_count == W_DEV and tm_count == NOFF
    return jax.shard_map(
        window_shards if by_window else shards,
        mesh=mesh,
        in_specs=(P(None, "tm", "chan", None), P("tm", None), P()),
        out_specs=P("chan", None, None),
        check_vma=False,
    )
```

```python
import functools
import math

import jax
import jax.numpy as jnp
import numpy as np
from jax import lax
from jax.experimental import pallas as pl
from jax.experimental.pallas import tpu as pltpu
from jax.sharding import PartitionSpec as P

F = 2048
LAGS = 256
NOFF = 4
CH_DEV = 16
W_DEV = 8
VMEM_LIMIT = 48 * 1024 * 1024
CODE_TOP = 32767.0
OCTAVE = 256.0
LOWEST = -110.0


def encode(value):
    return jnp.round(value).astype(jnp.int32).astype(jnp.int16)


def decode(code):
    return code.astype(jnp.int32).astype(jnp.float32)


def level_code(peak):
    return jnp.ceil(jnp.maximum(jnp.log2(jnp.maximum(peak, 1e-30)), LOWEST) * OCTAVE) + 1.0


def level_of(code):
    return jnp.exp2(code * (1.0 / OCTAVE))


def half_table(freq_count, lag_count):
    freq_index = np.arange(freq_count, dtype=np.int64)[None, :]
    double_lag = (2 * np.arange(lag_count // 2, lag_count, dtype=np.int64) - lag_count + 1)[:, None]
    turns = np.mod(freq_index * double_lag, 4 * freq_count).astype(np.float32)
    angles = turns * np.float32(2.0 * math.pi / (4 * freq_count))
    return np.concatenate([np.cos(angles), np.sin(angles)]).astype(jnp.bfloat16)


def widest(offs_ref, reach):
    last = offs_ref.shape[0] - 1
    found = last
    for number in reversed(range(last)):
        found = jnp.where(offs_ref[number] == reach, number, found)
    return found


def offset_of(slot, offs_ref, reach):
    last, wide = offs_ref.shape[0] - 1, widest(offs_ref, reach)
    return offs_ref[jnp.where(slot == wide, last, jnp.where(slot == last, wide, slot))]


def window_kernel(order, offs_hbm_ref, where_ref, *refs):
    chan_count = len(order)
    spec_refs, (qual_ref, table_ref) = refs[:chan_count], refs[chan_count : chan_count + 2]
    out_refs = refs[chan_count + 2 : chan_count + 4]
    mag_ref, white_ref, cross_ref, offs_ref, offs_sem = refs[chan_count + 4 :]
    fetch = pltpu.make_async_copy(offs_hbm_ref, offs_ref, offs_sem)
    fetch.start()
    me = where_ref[0]
    _, band, chans = spec_refs[0].shape
    freqs = chan_count * band
    chip_count, blocks, lag_rows, _ = out_refs[0].shape
    offset_count = offs_ref.shape[0]
    half = chan_count * lag_rows
    step = 64

    total = jnp.zeros((8, chans), jnp.float32)
    for number, spec_ref in enumerate(spec_refs):
        for row in range(0, band, step):
            real, imag = (spec_ref[part, row : row + step, :].astype(jnp.float32) for part in range(2))
            square = real * real + imag * imag
            magnitude = square * lax.rsqrt(jnp.maximum(square, 1e-30))
            held = slice(number * band + row, number * band + row + step)
            mag_ref[held, :] = magnitude
            total += jnp.sum(magnitude.reshape(step // 8, 8, chans), axis=0)
    level = jnp.sum(total, axis=0, keepdims=True) * (1.0 / freqs)
    floor = 0.5 * (level + 1e-05)

    for number, spec_ref in enumerate(spec_refs):
        for row in range(0, band, step):
            held = slice(number * band + row, number * band + row + step)
            factor = pl.reciprocal(mag_ref[held, :] + floor, approx=True)
            for part in range(2):
                value = spec_ref[part, row : row + step, :].astype(jnp.float32) * factor
                white_ref[part, held, :] = value.astype(jnp.bfloat16)

    lane = lax.broadcasted_iota(jnp.int32, (1, chans), 1)
    line = lax.broadcasted_iota(jnp.int32, (lag_rows, chans), 0)
    usable = qual_ref[pl.ds(me, 1), :].astype(jnp.float32)
    levels = jnp.zeros((lag_rows, chans), jnp.float32)
    groups = [k ^ core for core in range(2) for k in chips(chan_count)]
    fetch.wait()
    bands = [pl.ds(pl.multiple_of((me ^ k) * band, band), band) for k in order]
    table = jnp.concatenate(
        [
            jnp.concatenate([table_ref[side, me ^ group, :, taken] for taken in bands], axis=1)
            for side in range(2)
            for group in groups
        ],
        axis=0,
    )
    for number in range(offset_count):
        turn = chans - offset_of(number, offs_ref, chan_count // 2) * (chans // chan_count)
        slot = number % 2
        for row in range(0, freqs, step):
            own = [white_ref[part, row : row + step, :] for part in range(2)]
            far_real, far_imag = (pltpu.roll(value, turn, 1).astype(jnp.float32) for value in own)
            own_real, own_imag = (value.astype(jnp.float32) for value in own)
            real = own_real * far_real + own_imag * far_imag
            imag = own_imag * far_real - own_real * far_imag
            cross_ref[slot, row : row + step, 0:chans] = real.astype(jnp.bfloat16)
            cross_ref[slot, row : row + step, chans : 2 * chans] = imag.astype(jnp.bfloat16)
        sums = jnp.dot(table, cross_ref[slot], preferred_element_type=jnp.float32)
        cos_real, sin_real = sums[:half, :chans], sums[half:, :chans]
        cos_imag, sin_imag = sums[:half, chans:], sums[half:, chans:]
        corr = (
            (cos_real - sin_imag, sin_real + cos_imag),
            (cos_real + sin_imag, cos_imag - sin_real),
        )
        power = [real * real + imag * imag for real, imag in corr]
        mean_power = jnp.sum(power[0] + power[1], axis=0, keepdims=True) * (1.0 / (2 * half))
        extra = 0.25 * (mean_power + 1e-06 * freqs)
        peak = jnp.max(jnp.maximum(jnp.abs(corr[0][0]), jnp.abs(corr[1][0])), axis=0, keepdims=True)
        code = level_code(peak)
        keep = jnp.where(lane < turn, usable * pltpu.roll(usable, turn, 1), 0.0) * CODE_TOP
        upscale = keep / level_of(code)
        inverse = [lax.rsqrt(side + extra) * keep for side in power]
        kinds = [
            [real * upscale for real, _ in corr],
            [real * scale for (real, _), scale in zip(corr, inverse)],
            [imag * scale for (_, imag), scale in zip(corr, inverse)],
        ]
        if number == offset_count - 1:
            code = jnp.where(lane < chans // 2, code, pltpu.roll(code, chans // 2, 1))
            kinds = [[jnp.where(lane < chans // 2, ahead, pltpu.roll(back, chans // 2, 1))] for ahead, back in kinds]
        levels = jnp.where(line == number, code, levels)
        for place, value in enumerate(value for kind in kinds for value in kind):
            coded = encode(value).reshape(chan_count, lag_rows, chans)
            for core in range(2):
                rows = slice(core * chip_count, (core + 1) * chip_count)
                out_refs[core][:, 6 * number + place, :, :] = coded[rows]
    for number in range(offset_count):
        levels = jnp.where(line == offset_count + number, offs_ref[number].astype(jnp.float32), levels)
    wide = widest(offs_ref, chan_count // 2).astype(jnp.float32)
    levels = jnp.where(line == 2 * offset_count, wide, levels)
    for out_ref in out_refs:
        for chip in range(chip_count):
            out_ref[chip, blocks - 1, :, :] = encode(levels)


def merge_kernel(slots, own_ref, far_ref, *out_refs):
    blocks = own_ref.shape[1]
    for chip, out_ref in enumerate(out_refs):
        codes = [decode(ref[chip, blocks - 1]) for ref in (own_ref, far_ref)]
        levels = [level_of(code) for code in codes]
        code = level_code(levels[0] + levels[1])
        shares = [level / level_of(code) for level in levels]
        line = lax.broadcasted_iota(jnp.int32, code.shape, 0)
        out_ref[blocks - 1, :, :] = encode(jnp.where(line < slots, code, codes[0]))
        for block in range(blocks - 1):
            number, part = divmod(block, 6)
            linear = part < (2 if blocks - 1 - 6 * number > 3 else 1)
            own, far = decode(own_ref[chip, block]), decode(far_ref[chip, block])
            if linear:
                total = own * shares[0][number : number + 1, :] + far * shares[1][number : number + 1, :]
            else:
                total = (own + far) * 0.5
            out_ref[block, :, :] = encode(total)


def sum_kernel(order, scale, where_ref, *refs):
    code_refs, out_refs, held_ref = refs[: -len(order) - 1], refs[-len(order) - 1 : -1], refs[-1]
    blocks, _, chans = code_refs[0].shape
    slots = held_ref.shape[0]
    heads = [decode(codes_ref[blocks - 1]) for codes_ref in code_refs]
    levels = [level_of(head) * scale for head in heads]
    offsets = [heads[0][slots + number : slots + number + 1, :] for number in range(slots)]
    wide = heads[0][2 * slots : 2 * slots + 1, :]
    low = lax.broadcasted_iota(jnp.int32, (1, chans), 1) < chans // 2
    all_sums = []
    for number in range(slots):
        sides = 2 if number < slots - 1 else 1
        own = [level[number : number + 1, :] for level in levels]
        sums = []
        for place in range(3 * sides):
            codes = [decode(codes_ref[6 * number + place]) for codes_ref in code_refs]
            if place < sides:
                sums.append(sum(code * level for code, level in zip(codes, own)))
            else:
                sums.append(sum(codes) * (1.0 / len(code_refs)))
        if sides == 1:
            sums = [
                jnp.where(low, side, 0.0) for value in sums for side in (value, pltpu.roll(value, chans // 2, 1))
            ]
        all_sums.append(sums)
    line = lax.broadcasted_iota(jnp.int32, levels[0].shape, 0)
    last = slots - 1
    for number in range(slots):
        sums = all_sums[number]
        for other in range(last) if number == last else [last]:
            swap = wide == min(number, other)
            sums = [jnp.where(swap, value, kept) for value, kept in zip(all_sums[other], sums)]
        peak = jnp.max(jnp.maximum(jnp.abs(sums[0]), jnp.abs(sums[1])), axis=0, keepdims=True)
        code = level_code(peak)
        upscale = CODE_TOP / level_of(code)
        head = jnp.where(line == 0, code, offsets[number])
        for part, value in enumerate([sums[0] * upscale, sums[1] * upscale, *sums[2:], head]):
            held_ref[number, part, :, :] = encode(value)
    for k, out_ref in zip(order, out_refs):
        out_ref[...] = held_ref[where_ref[0] ^ k]


def partners(count):
    return sorted(range(1, count), key=lambda k: (-(k >> 1).bit_count(), k & 1, k)) + [0]


def chips(count):
    return [k for k in partners(count) if k % 2 == 0]


def exchange(pieces, axis, order):
    count = lax.axis_size(axis)
    return [
        lax.ppermute(piece, axis, [(source, source ^ k) for source in range(count)]) if k else piece
        for k, piece in zip(order, pieces)
    ]


def split_kernel(order, where_ref, spec_ref, *refs):
    out_refs, sems = refs[:-1], refs[-1]
    copies = [
        pltpu.make_async_copy(spec_ref.at[:, where_ref[0] ^ k], out_ref, sems.at[number])
        for number, (k, out_ref) in enumerate(zip(order, out_refs))
    ]
    for copy in copies:
        copy.start()
    for copy in copies:
        copy.wait()


def stack_kernel(windows, *refs):
    sums_refs, out_ref = refs[:-1], refs[-1]
    blocks, copies, rows, _ = out_ref.shape
    _, lag_rows, chans = sums_refs[0].shape
    per_sum = windows // len(sums_refs)
    heads = [decode(sums_ref[6]) for sums_ref in sums_refs]
    levels = [level_of(head[0:1, :]) * (1.0 / (CODE_TOP * windows)) for head in heads]
    stacks = []
    for side in range(2):
        linear = sum(decode(sums_ref[side]) * level for sums_ref, level in zip(sums_refs, levels))
        real, imag = (
            sum(decode(sums_ref[part + side]) for sums_ref in sums_refs) * (per_sum / (CODE_TOP * windows))
            for part in (2, 4)
        )
        stacks.append(linear * (real * real + imag * imag))
    offset = heads[0][1:2, :]
    lane = lax.broadcasted_iota(jnp.int32, (1, chans), 1)
    behind = [jnp.zeros_like(stack) for stack in stacks]
    for steps in range(1, blocks // 2 + 1):
        ahead = steps * (chans // blocks)
        chosen = (offset == steps) & (lane >= ahead)
        behind = [jnp.where(chosen, pltpu.roll(stack, ahead, 1), kept) for stack, kept in zip(stacks, behind)]
    back = stacks[1] + behind[0]
    both = jnp.concatenate(
        [stacks[0] + behind[1]] + [back[row : row + 1, :] for row in reversed(range(lag_rows))], axis=0
    )
    wide = 2 * lag_rows
    parts = chans // wide
    turned = jnp.concatenate([both] * parts, axis=0).T
    per_block = chans // blocks
    for block in range(blocks):
        piece = jnp.zeros((rows, chans), jnp.float32)
        for part in range(parts):
            begin = block * per_block + part * rows
            piece = jnp.where(lane // wide == part, turned[begin : begin + rows, :], piece)
        for copy in range(copies):
            out_ref[block, copy, :, :] = piece


def place_kernel(parts_ref, out_ref):
    groups, offset_count, rows, lanes = parts_ref.shape
    half = out_ref.shape[2] // 2
    lag_rows = half // groups
    parts = out_ref.shape[0] // rows
    lane = lax.broadcasted_iota(jnp.int32, (1, lanes), 1)
    for number in range(offset_count):
        for part in range(parts):
            ahead = jnp.zeros((rows, lanes), jnp.float32)
            back = jnp.zeros((rows, lanes), jnp.float32)
            begin = part * 2 * lag_rows
            for group in range(groups):
                piece = parts_ref[group, number]
                first, last = group * lag_rows, half - (group + 1) * lag_rows
                ahead = jnp.where(lane // lag_rows == group, pltpu.roll(piece, (first - begin) % lanes, 1), ahead)
                back = jnp.where(
                    lane // lag_rows == groups - 1 - group, pltpu.roll(piece, (last - begin - lag_rows) % lanes, 1), back
                )
            out_ref[part * rows : (part + 1) * rows, number, 0:half] = back
            out_ref[part * rows : (part + 1) * rows, number, half : 2 * half] = ahead


def window_shards(spectra, quality, offsets):
    chan_count = lax.axis_size("chan")
    tm_count = lax.axis_size("tm")
    _, windows, band, chans = spectra.shape
    freqs = band * chan_count
    half = LAGS // 2
    lag_rows = half // chan_count
    offset_count = offsets.shape[0]
    piece_rows = 2 * lag_rows // chan_count
    smem = pl.BlockSpec(memory_space=pltpu.SMEM)
    vmem = pl.BlockSpec(memory_space=pltpu.VMEM)
    params = pltpu.CompilerParams(vmem_limit_bytes=VMEM_LIMIT)
    table = jnp.asarray(half_table(freqs, LAGS).reshape(2, chan_count, lag_rows, freqs))
    chan_index = lax.axis_index("chan").astype(jnp.int32)
    tm_index = lax.axis_index("tm").astype(jnp.int32)
    chan_where, tm_where = chan_index.reshape(1), tm_index.reshape(1)

    chan_order, tm_order = partners(chan_count), partners(tm_count)
    kept = pl.BlockSpec(memory_space=pltpu.HBM)
    spectra = pltpu.with_memory_space_constraint(spectra, pltpu.HBM)
    pieces = []
    for part in (chan_order[:2], chan_order[2:]):
        pieces += pl.pallas_call(
            functools.partial(split_kernel, part),
            out_shape=[jax.ShapeDtypeStruct((2, band, chans), spectra.dtype)] * len(part),
            in_specs=[smem, kept],
            out_specs=[pl.BlockSpec(memory_space=pl.ANY)] * len(part),
            scratch_shapes=[pltpu.SemaphoreType.DMA((len(part),))],
            compiler_params=params,
            name="split_windows",
        )(chan_where, spectra)
    chip_order = chips(chan_count)
    pair_shape = (6 * offset_count - 2, lag_rows, chans)
    own, far = pl.pallas_call(
        functools.partial(window_kernel, chan_order),
        out_shape=[jax.ShapeDtypeStruct((len(chip_order), *pair_shape), jnp.int16)] * 2,
        in_specs=[kept, smem] + [vmem] * (chan_count + 2),
        out_specs=[vmem] * 2,
        scratch_shapes=[
            pltpu.VMEM((freqs, chans), jnp.float32),
            pltpu.VMEM((2, freqs, chans), jnp.bfloat16),
            pltpu.VMEM((2, freqs, 2 * chans), jnp.bfloat16),
            pltpu.SMEM(offsets.shape, jnp.int32),
            pltpu.SemaphoreType.DMA(()),
        ],
        compiler_params=params,
        name="window_pairs",
    )(pltpu.with_memory_space_constraint(offsets, pltpu.HBM), chan_where, *exchange(pieces, "chan", chan_order), quality, table)
    pairs = pl.pallas_call(
        functools.partial(merge_kernel, offset_count),
        out_shape=[jax.ShapeDtypeStruct(pair_shape, jnp.int16)] * len(chip_order),
        in_specs=[vmem] * 2,
        out_specs=[vmem] * len(chip_order),
        compiler_params=params,
        name="merge_windows",
    )(own, *exchange([far], "chan", [1]))
    sums = pl.pallas_call(
        functools.partial(sum_kernel, tm_order, 1.0 / (CODE_TOP * math.sqrt(freqs))),
        out_shape=[jax.ShapeDtypeStruct((7, lag_rows, chans), jnp.int16)] * tm_count,
        in_specs=[smem] + [vmem] * len(chip_order),
        out_specs=[vmem] * tm_count,
        scratch_shapes=[pltpu.VMEM((offset_count, 7, lag_rows, chans), jnp.int16)],
        compiler_params=params,
        name="sum_windows",
    )(tm_where, *exchange(pairs, "chan", chip_order))
    pieces = pl.pallas_call(
        functools.partial(stack_kernel, windows * tm_count),
        out_shape=jax.ShapeDtypeStruct((chan_count, tm_count, piece_rows, chans), jnp.float32),
        in_specs=[vmem] * tm_count,
        out_specs=vmem,
        compiler_params=params,
        name="stack_pairs",
    )(*exchange(sums, "tm", tm_order))
    shape = (chan_count * tm_count, piece_rows, chans)
    arrived = lax.all_to_all(pieces.reshape(shape), ("chan", "tm"), 0, 0, tiled=True)
    return pl.pallas_call(
        place_kernel,
        out_shape=jax.ShapeDtypeStruct((CH_DEV, offset_count, LAGS), jnp.float32),
        in_specs=[vmem],
        out_specs=vmem,
        compiler_params=params,
        name="place_lags",
    )(arrived.reshape(chan_count, tm_count, piece_rows, chans))


def shifted(value, axis, steps):
    count = lax.axis_size(axis)
    leading, last = (max(0, -steps), min(count, count - steps))
    return lax.ppermute(value, axis, [(source, source + steps) for source in range(leading, last)])


def lag_table(freq_count, lag_count):
    freq_index = jnp.arange(freq_count, dtype=jnp.int32)[:, None]
    double_lag = (2 * jnp.arange(lag_count, dtype=jnp.int32) - lag_count + 1)[None, :]
    turns = jnp.mod(freq_index * double_lag, 4 * freq_count)
    angles = turns.astype(jnp.float32) * (2.0 * math.pi / (4 * freq_count))
    cosine = jnp.cos(angles)
    sine = jnp.sin(angles)
    upper = jnp.concatenate([cosine, sine], axis=1)
    lower = jnp.concatenate([-sine, cosine], axis=1)
    return jnp.stack([upper, lower]).astype(jnp.bfloat16)


def whiten_parts(real_part, imag_part, magnitude, channel_level, usable):
    factor = usable.astype(jnp.float32)[:, None, :] / (magnitude + 0.5 * (channel_level + 1e-05))
    return jnp.stack([real_part * factor, imag_part * factor]).astype(jnp.bfloat16)


def cross_parts(own_real, own_imag, far_real, far_imag):
    own_real = own_real.astype(jnp.float32)
    own_imag = own_imag.astype(jnp.float32)
    far_real = far_real.astype(jnp.float32)
    far_imag = far_imag.astype(jnp.float32)
    return jnp.stack(
        [own_real * far_real + own_imag * far_imag, own_imag * far_real - own_real * far_imag]
    ).astype(jnp.bfloat16)


def pair_terms(corr_all):
    lag_count = corr_all.shape[-1] // 2
    real_corr = corr_all[..., :lag_count]
    imag_corr = corr_all[..., lag_count:]
    power = real_corr * real_corr + imag_corr * imag_corr
    mean_power = jnp.mean(power, axis=-1, keepdims=True)
    denominator = jnp.sqrt(power + 0.25 * (mean_power + 1e-06))
    return (
        jnp.sum(real_corr, axis=-3),
        jnp.sum(real_corr / denominator, axis=-3),
        jnp.sum(imag_corr / denominator, axis=-3),
    )


def shards(spectra, quality, offsets):
    chan_count = lax.axis_size("chan")
    tm_count = lax.axis_size("tm")
    levels = chan_count.bit_length() - 1
    table_bf = lag_table(F, LAGS)
    inv_root = 1.0 / math.sqrt(F)
    real_part = spectra[0].astype(jnp.float32)
    imag_part = spectra[1].astype(jnp.float32)
    magnitude = jnp.sqrt(real_part * real_part + imag_part * imag_part)
    band_total = lax.psum(jnp.sum(magnitude, axis=1), "chan")
    channel_level = (band_total / F)[:, None, :]
    whitened = whiten_parts(real_part, imag_part, magnitude, channel_level, quality)
    width_all = whitened.shape[3]
    padded = jnp.pad(whitened, ((0, 0), (0, 0), (0, 0), (0, width_all)))
    crossed_list = []
    for offset_index in range(NOFF):
        partner = lax.dynamic_slice_in_dim(padded, offsets[offset_index] * CH_DEV, width_all, 3)
        crossed_list.append(cross_parts(whitened[0], whitened[1], partner[0], partner[1]))
    crossed = jnp.stack(crossed_list, axis=1)
    corr_all = jnp.einsum(
        "cnwfh,cfl->nwhl",
        lax.all_to_all(crossed, "chan", split_axis=4, concat_axis=3, tiled=True),
        table_bf,
        preferred_element_type=jnp.float32,
    )
    linear_sum, real_sum, imag_sum = pair_terms(corr_all * inv_root)
    totals = lax.psum((linear_sum, real_sum, imag_sum), "tm")
    window_count = W_DEV * tm_count
    linear = totals[0] / window_count
    real_phase = totals[1] / window_count
    imag_phase = totals[2] / window_count
    stacks = jnp.transpose(linear * (real_phase * real_phase + imag_phase * imag_phase), (1, 0, 2))
    reverse_part = stacks
    for bit_index in range(levels):
        step_size = 1 << bit_index
        arrived = shifted(reverse_part, "chan", step_size)
        chosen = offsets // step_size % 2 == 1
        reverse_part = jnp.where(chosen[None, :, None], arrived, reverse_part)
    return stacks + jnp.flip(reverse_part, axis=2)


def solution(mesh):
    chan_count, tm_count = mesh.shape["chan"], mesh.shape["tm"]
    by_window = chan_count == W_DEV and tm_count == NOFF
    return jax.shard_map(
        window_shards if by_window else shards,
        mesh=mesh,
        in_specs=(P(None, "tm", "chan", None), P("tm", None), P()),
        out_specs=P("chan", None, None),
        check_vma=False,
    )
```

```python
import functools
import math

import jax
import jax.numpy as jnp
import numpy as np
from jax import lax
from jax.experimental import pallas as pl
from jax.experimental.pallas import tpu as pltpu
from jax.sharding import PartitionSpec as P

F = 2048
LAGS = 256
NOFF = 4
CH_DEV = 16
W_DEV = 8
VMEM_LIMIT = 48 * 1024 * 1024
CODE_TOP = 32767.0
OCTAVE = 256.0
LOWEST = -110.0


def encode(value):
    return jnp.round(value).astype(jnp.int32).astype(jnp.int16)


def decode(code):
    return code.astype(jnp.int32).astype(jnp.float32)


def level_code(peak):
    return jnp.ceil(jnp.maximum(jnp.log2(jnp.maximum(peak, 1e-30)), LOWEST) * OCTAVE) + 1.0


def level_of(code):
    return jnp.exp2(code * (1.0 / OCTAVE))


def half_table(freq_count, lag_count):
    freq_index = np.arange(freq_count, dtype=np.int64)[None, :]
    double_lag = (2 * np.arange(lag_count // 2, lag_count, dtype=np.int64) - lag_count + 1)[:, None]
    turns = np.mod(freq_index * double_lag, 4 * freq_count).astype(np.float32)
    angles = turns * np.float32(2.0 * math.pi / (4 * freq_count))
    return np.concatenate([np.cos(angles), np.sin(angles)]).astype(jnp.bfloat16)


def widest(offs_ref, reach):
    last = offs_ref.shape[0] - 1
    found = last
    for number in reversed(range(last)):
        found = jnp.where(offs_ref[number] == reach, number, found)
    return found


def offset_of(slot, offs_ref, reach):
    last, wide = offs_ref.shape[0] - 1, widest(offs_ref, reach)
    return offs_ref[jnp.where(slot == wide, last, jnp.where(slot == last, wide, slot))]


def window_kernel(order, offs_hbm_ref, where_ref, *refs):
    chan_count = len(order)
    spec_refs, (qual_ref, table_ref) = refs[:chan_count], refs[chan_count : chan_count + 2]
    out_refs = refs[chan_count + 2 : chan_count + 4]
    mag_ref, white_ref, cross_ref, offs_ref, offs_sem = refs[chan_count + 4 :]
    fetch = pltpu.make_async_copy(offs_hbm_ref, offs_ref, offs_sem)
    fetch.start()
    me = where_ref[0]
    _, band, chans = spec_refs[0].shape
    freqs = chan_count * band
    chip_count, blocks, lag_rows, _ = out_refs[0].shape
    offset_count = offs_ref.shape[0]
    half = chan_count * lag_rows
    step = 64

    total = jnp.zeros((8, chans), jnp.float32)
    for number, spec_ref in enumerate(spec_refs):
        for row in range(0, band, step):
            real, imag = (spec_ref[part, row : row + step, :].astype(jnp.float32) for part in range(2))
            square = real * real + imag * imag
            magnitude = square * lax.rsqrt(jnp.maximum(square, 1e-30))
            held = slice(number * band + row, number * band + row + step)
            mag_ref[held, :] = magnitude
            total += jnp.sum(magnitude.reshape(step // 8, 8, chans), axis=0)
    level = jnp.sum(total, axis=0, keepdims=True) * (1.0 / freqs)
    floor = 0.5 * (level + 1e-05)

    for number, spec_ref in enumerate(spec_refs):
        for row in range(0, band, step):
            held = slice(number * band + row, number * band + row + step)
            factor = pl.reciprocal(mag_ref[held, :] + floor, approx=True)
            for part in range(2):
                value = spec_ref[part, row : row + step, :].astype(jnp.float32) * factor
                white_ref[part, held, :] = value.astype(jnp.bfloat16)

    lane = lax.broadcasted_iota(jnp.int32, (1, chans), 1)
    line = lax.broadcasted_iota(jnp.int32, (lag_rows, chans), 0)
    usable = qual_ref[pl.ds(me, 1), :].astype(jnp.float32)
    levels = jnp.zeros((lag_rows, chans), jnp.float32)
    groups = [k ^ core for core in range(2) for k in chips(chan_count)]
    fetch.wait()
    bands = [pl.ds(pl.multiple_of((me ^ k) * band, band), band) for k in order]
    table = jnp.concatenate(
        [
            jnp.concatenate([table_ref[side, me ^ group, :, taken] for taken in bands], axis=1)
            for side in range(2)
            for group in groups
        ],
        axis=0,
    )
    turns = [chans - offset_of(number, offs_ref, chan_count // 2) * (chans // chan_count) for number in range(offset_count)]
    for row in range(0, freqs, step):
        own = [white_ref[part, row : row + step, :] for part in range(2)]
        own_real, own_imag = (value.astype(jnp.float32) for value in own)
        for number, turn in enumerate(turns):
            far_real, far_imag = (pltpu.roll(value, turn, 1).astype(jnp.float32) for value in own)
            real = own_real * far_real + own_imag * far_imag
            imag = own_imag * far_real - own_real * far_imag
            cross_ref[number, row : row + step, 0:chans] = real.astype(jnp.bfloat16)
            cross_ref[number, row : row + step, chans : 2 * chans] = imag.astype(jnp.bfloat16)

    for number, turn in enumerate(turns):
        sums = jnp.dot(table, cross_ref[number], preferred_element_type=jnp.float32)
        cos_real, sin_real = sums[:half, :chans], sums[half:, :chans]
        cos_imag, sin_imag = sums[:half, chans:], sums[half:, chans:]
        corr = (
            (cos_real - sin_imag, sin_real + cos_imag),
            (cos_real + sin_imag, cos_imag - sin_real),
        )
        power = [real * real + imag * imag for real, imag in corr]
        mean_power = jnp.sum(power[0] + power[1], axis=0, keepdims=True) * (1.0 / (2 * half))
        extra = 0.25 * (mean_power + 1e-06 * freqs)
        peak = jnp.max(jnp.maximum(jnp.abs(corr[0][0]), jnp.abs(corr[1][0])), axis=0, keepdims=True)
        code = level_code(peak)
        keep = jnp.where(lane < turn, usable * pltpu.roll(usable, turn, 1), 0.0) * CODE_TOP
        upscale = keep / level_of(code)
        inverse = [lax.rsqrt(side + extra) * keep for side in power]
        kinds = [
            [real * upscale for real, _ in corr],
            [real * scale for (real, _), scale in zip(corr, inverse)],
            [imag * scale for (_, imag), scale in zip(corr, inverse)],
        ]
        if number == offset_count - 1:
            code = jnp.where(lane < chans // 2, code, pltpu.roll(code, chans // 2, 1))
            kinds = [[jnp.where(lane < chans // 2, ahead, pltpu.roll(back, chans // 2, 1))] for ahead, back in kinds]
        levels = jnp.where(line == number, code, levels)
        for place, value in enumerate(value for kind in kinds for value in kind):
            coded = encode(value).reshape(chan_count, lag_rows, chans)
            for core in range(2):
                rows = slice(core * chip_count, (core + 1) * chip_count)
                out_refs[core][:, 6 * number + place, :, :] = coded[rows]
    for number in range(offset_count):
        levels = jnp.where(line == offset_count + number, offs_ref[number].astype(jnp.float32), levels)
    wide = widest(offs_ref, chan_count // 2).astype(jnp.float32)
    levels = jnp.where(line == 2 * offset_count, wide, levels)
    for out_ref in out_refs:
        for chip in range(chip_count):
            out_ref[chip, blocks - 1, :, :] = encode(levels)


def merge_kernel(slots, own_ref, far_ref, *out_refs):
    blocks = own_ref.shape[1]
    for chip, out_ref in enumerate(out_refs):
        codes = [decode(ref[chip, blocks - 1]) for ref in (own_ref, far_ref)]
        levels = [level_of(code) for code in codes]
        code = level_code(levels[0] + levels[1])
        shares = [level / level_of(code) for level in levels]
        line = lax.broadcasted_iota(jnp.int32, code.shape, 0)
        out_ref[blocks - 1, :, :] = encode(jnp.where(line < slots, code, codes[0]))
        for block in range(blocks - 1):
            number, part = divmod(block, 6)
            linear = part < (2 if blocks - 1 - 6 * number > 3 else 1)
            own, far = decode(own_ref[chip, block]), decode(far_ref[chip, block])
            if linear:
                total = own * shares[0][number : number + 1, :] + far * shares[1][number : number + 1, :]
            else:
                total = (own + far) * 0.5
            out_ref[block, :, :] = encode(total)


def sum_kernel(order, scale, where_ref, *refs):
    code_refs, out_refs, held_ref = refs[: -len(order) - 1], refs[-len(order) - 1 : -1], refs[-1]
    blocks, _, chans = code_refs[0].shape
    slots = held_ref.shape[0]
    heads = [decode(codes_ref[blocks - 1]) for codes_ref in code_refs]
    levels = [level_of(head) * scale for head in heads]
    offsets = [heads[0][slots + number : slots + number + 1, :] for number in range(slots)]
    wide = heads[0][2 * slots : 2 * slots + 1, :]
    low = lax.broadcasted_iota(jnp.int32, (1, chans), 1) < chans // 2
    all_sums = []
    for number in range(slots):
        sides = 2 if number < slots - 1 else 1
        own = [level[number : number + 1, :] for level in levels]
        sums = []
        for place in range(3 * sides):
            codes = [decode(codes_ref[6 * number + place]) for codes_ref in code_refs]
            if place < sides:
                sums.append(sum(code * level for code, level in zip(codes, own)))
            else:
                sums.append(sum(codes) * (1.0 / len(code_refs)))
        if sides == 1:
            sums = [
                jnp.where(low, side, 0.0) for value in sums for side in (value, pltpu.roll(value, chans // 2, 1))
            ]
        all_sums.append(sums)
    line = lax.broadcasted_iota(jnp.int32, levels[0].shape, 0)
    last = slots - 1
    for number in range(slots):
        sums = all_sums[number]
        for other in range(last) if number == last else [last]:
            swap = wide == min(number, other)
            sums = [jnp.where(swap, value, kept) for value, kept in zip(all_sums[other], sums)]
        peak = jnp.max(jnp.maximum(jnp.abs(sums[0]), jnp.abs(sums[1])), axis=0, keepdims=True)
        code = level_code(peak)
        upscale = CODE_TOP / level_of(code)
        head = jnp.where(line == 0, code, offsets[number])
        for part, value in enumerate([sums[0] * upscale, sums[1] * upscale, *sums[2:], head]):
            held_ref[number, part, :, :] = encode(value)
    for k, out_ref in zip(order, out_refs):
        out_ref[...] = held_ref[where_ref[0] ^ k]


def partners(count):
    return sorted(range(1, count), key=lambda k: (-(k >> 1).bit_count(), k & 1, k)) + [0]


def chips(count):
    return [k for k in partners(count) if k % 2 == 0]


def exchange(pieces, axis, order):
    count = lax.axis_size(axis)
    return [
        lax.ppermute(piece, axis, [(source, source ^ k) for source in range(count)]) if k else piece
        for k, piece in zip(order, pieces)
    ]


def split_kernel(order, where_ref, spec_ref, *refs):
    out_refs, sems = refs[:-1], refs[-1]
    copies = [
        pltpu.make_async_copy(spec_ref.at[:, where_ref[0] ^ k], out_ref, sems.at[number])
        for number, (k, out_ref) in enumerate(zip(order, out_refs))
    ]
    for copy in copies:
        copy.start()
    for copy in copies:
        copy.wait()


def stack_kernel(windows, *refs):
    sums_refs, out_ref = refs[:-1], refs[-1]
    blocks, copies, rows, _ = out_ref.shape
    _, lag_rows, chans = sums_refs[0].shape
    per_sum = windows // len(sums_refs)
    heads = [decode(sums_ref[6]) for sums_ref in sums_refs]
    levels = [level_of(head[0:1, :]) * (1.0 / (CODE_TOP * windows)) for head in heads]
    stacks = []
    for side in range(2):
        linear = sum(decode(sums_ref[side]) * level for sums_ref, level in zip(sums_refs, levels))
        real, imag = (
            sum(decode(sums_ref[part + side]) for sums_ref in sums_refs) * (per_sum / (CODE_TOP * windows))
            for part in (2, 4)
        )
        stacks.append(linear * (real * real + imag * imag))
    offset = heads[0][1:2, :]
    lane = lax.broadcasted_iota(jnp.int32, (1, chans), 1)
    behind = [jnp.zeros_like(stack) for stack in stacks]
    for steps in range(1, blocks // 2 + 1):
        ahead = steps * (chans // blocks)
        chosen = (offset == steps) & (lane >= ahead)
        behind = [jnp.where(chosen, pltpu.roll(stack, ahead, 1), kept) for stack, kept in zip(stacks, behind)]
    back = stacks[1] + behind[0]
    both = jnp.concatenate(
        [stacks[0] + behind[1]] + [back[row : row + 1, :] for row in reversed(range(lag_rows))], axis=0
    )
    wide = 2 * lag_rows
    parts = chans // wide
    turned = jnp.concatenate([both] * parts, axis=0).T
    per_block = chans // blocks
    for block in range(blocks):
        piece = jnp.zeros((rows, chans), jnp.float32)
        for part in range(parts):
            begin = block * per_block + part * rows
            piece = jnp.where(lane // wide == part, turned[begin : begin + rows, :], piece)
        for copy in range(copies):
            out_ref[block, copy, :, :] = piece


def place_kernel(parts_ref, out_ref):
    groups, offset_count, rows, lanes = parts_ref.shape
    half = out_ref.shape[2] // 2
    lag_rows = half // groups
    parts = out_ref.shape[0] // rows
    lane = lax.broadcasted_iota(jnp.int32, (1, lanes), 1)
    for number in range(offset_count):
        for part in range(parts):
            ahead = jnp.zeros((rows, lanes), jnp.float32)
            back = jnp.zeros((rows, lanes), jnp.float32)
            begin = part * 2 * lag_rows
            for group in range(groups):
                piece = parts_ref[group, number]
                first, last = group * lag_rows, half - (group + 1) * lag_rows
                ahead = jnp.where(lane // lag_rows == group, pltpu.roll(piece, (first - begin) % lanes, 1), ahead)
                back = jnp.where(
                    lane // lag_rows == groups - 1 - group, pltpu.roll(piece, (last - begin - lag_rows) % lanes, 1), back
                )
            out_ref[part * rows : (part + 1) * rows, number, 0:half] = back
            out_ref[part * rows : (part + 1) * rows, number, half : 2 * half] = ahead


def window_shards(spectra, quality, offsets):
    chan_count = lax.axis_size("chan")
    tm_count = lax.axis_size("tm")
    _, windows, band, chans = spectra.shape
    freqs = band * chan_count
    half = LAGS // 2
    lag_rows = half // chan_count
    offset_count = offsets.shape[0]
    piece_rows = 2 * lag_rows // chan_count
    smem = pl.BlockSpec(memory_space=pltpu.SMEM)
    vmem = pl.BlockSpec(memory_space=pltpu.VMEM)
    params = pltpu.CompilerParams(vmem_limit_bytes=VMEM_LIMIT)
    table = jnp.asarray(half_table(freqs, LAGS).reshape(2, chan_count, lag_rows, freqs))
    chan_index = lax.axis_index("chan").astype(jnp.int32)
    tm_index = lax.axis_index("tm").astype(jnp.int32)
    chan_where, tm_where = chan_index.reshape(1), tm_index.reshape(1)

    chan_order, tm_order = partners(chan_count), partners(tm_count)
    kept = pl.BlockSpec(memory_space=pltpu.HBM)
    begun, left = chan_order[:2], chan_order[2:]
    pieces = [
        lax.dynamic_index_in_dim(spectra, lax.axis_index("chan").astype(jnp.int32) ^ k, 1, keepdims=False) for k in begun
    ]
    pieces += pl.pallas_call(
        functools.partial(split_kernel, left),
        out_shape=[jax.ShapeDtypeStruct((2, band, chans), spectra.dtype)] * len(left),
        in_specs=[smem, kept],
        out_specs=[pl.BlockSpec(memory_space=pl.ANY)] * len(left),
        scratch_shapes=[pltpu.SemaphoreType.DMA((len(left),))],
        compiler_params=params,
        name="split_windows",
    )(chan_where, pltpu.with_memory_space_constraint(spectra, pltpu.HBM))
    chip_order = chips(chan_count)
    pair_shape = (6 * offset_count - 2, lag_rows, chans)
    own, far = pl.pallas_call(
        functools.partial(window_kernel, chan_order),
        out_shape=[jax.ShapeDtypeStruct((len(chip_order), *pair_shape), jnp.int16)] * 2,
        in_specs=[kept, smem] + [vmem] * (chan_count + 2),
        out_specs=[vmem] * 2,
        scratch_shapes=[
            pltpu.VMEM((freqs, chans), jnp.float32),
            pltpu.VMEM((2, freqs, chans), jnp.bfloat16),
            pltpu.VMEM((offset_count, freqs, 2 * chans), jnp.bfloat16),
            pltpu.SMEM(offsets.shape, jnp.int32),
            pltpu.SemaphoreType.DMA(()),
        ],
        compiler_params=params,
        name="window_pairs",
    )(pltpu.with_memory_space_constraint(offsets, pltpu.HBM), chan_where, *exchange(pieces, "chan", chan_order), quality, table)
    pairs = pl.pallas_call(
        functools.partial(merge_kernel, offset_count),
        out_shape=[jax.ShapeDtypeStruct(pair_shape, jnp.int16)] * len(chip_order),
        in_specs=[vmem] * 2,
        out_specs=[vmem] * len(chip_order),
        compiler_params=params,
        name="merge_windows",
    )(own, *exchange([far], "chan", [1]))
    sums = pl.pallas_call(
        functools.partial(sum_kernel, tm_order, 1.0 / (CODE_TOP * math.sqrt(freqs))),
        out_shape=[jax.ShapeDtypeStruct((7, lag_rows, chans), jnp.int16)] * tm_count,
        in_specs=[smem] + [vmem] * len(chip_order),
        out_specs=[vmem] * tm_count,
        scratch_shapes=[pltpu.VMEM((offset_count, 7, lag_rows, chans), jnp.int16)],
        compiler_params=params,
        name="sum_windows",
    )(tm_where, *exchange(pairs, "chan", chip_order))
    pieces = pl.pallas_call(
        functools.partial(stack_kernel, windows * tm_count),
        out_shape=jax.ShapeDtypeStruct((chan_count, tm_count, piece_rows, chans), jnp.float32),
        in_specs=[vmem] * tm_count,
        out_specs=vmem,
        compiler_params=params,
        name="stack_pairs",
    )(*exchange(sums, "tm", tm_order))
    shape = (chan_count * tm_count, piece_rows, chans)
    arrived = lax.all_to_all(pieces.reshape(shape), ("chan", "tm"), 0, 0, tiled=True)
    return pl.pallas_call(
        place_kernel,
        out_shape=jax.ShapeDtypeStruct((CH_DEV, offset_count, LAGS), jnp.float32),
        in_specs=[vmem],
        out_specs=vmem,
        compiler_params=params,
        name="place_lags",
    )(arrived.reshape(chan_count, tm_count, piece_rows, chans))


def shifted(value, axis, steps):
    count = lax.axis_size(axis)
    leading, last = (max(0, -steps), min(count, count - steps))
    return lax.ppermute(value, axis, [(source, source + steps) for source in range(leading, last)])


def lag_table(freq_count, lag_count):
    freq_index = jnp.arange(freq_count, dtype=jnp.int32)[:, None]
    double_lag = (2 * jnp.arange(lag_count, dtype=jnp.int32) - lag_count + 1)[None, :]
    turns = jnp.mod(freq_index * double_lag, 4 * freq_count)
    angles = turns.astype(jnp.float32) * (2.0 * math.pi / (4 * freq_count))
    cosine = jnp.cos(angles)
    sine = jnp.sin(angles)
    upper = jnp.concatenate([cosine, sine], axis=1)
    lower = jnp.concatenate([-sine, cosine], axis=1)
    return jnp.stack([upper, lower]).astype(jnp.bfloat16)


def whiten_parts(real_part, imag_part, magnitude, channel_level, usable):
    factor = usable.astype(jnp.float32)[:, None, :] / (magnitude + 0.5 * (channel_level + 1e-05))
    return jnp.stack([real_part * factor, imag_part * factor]).astype(jnp.bfloat16)


def cross_parts(own_real, own_imag, far_real, far_imag):
    own_real = own_real.astype(jnp.float32)
    own_imag = own_imag.astype(jnp.float32)
    far_real = far_real.astype(jnp.float32)
    far_imag = far_imag.astype(jnp.float32)
    return jnp.stack(
        [own_real * far_real + own_imag * far_imag, own_imag * far_real - own_real * far_imag]
    ).astype(jnp.bfloat16)


def pair_terms(corr_all):
    lag_count = corr_all.shape[-1] // 2
    real_corr = corr_all[..., :lag_count]
    imag_corr = corr_all[..., lag_count:]
    power = real_corr * real_corr + imag_corr * imag_corr
    mean_power = jnp.mean(power, axis=-1, keepdims=True)
    denominator = jnp.sqrt(power + 0.25 * (mean_power + 1e-06))
    return (
        jnp.sum(real_corr, axis=-3),
        jnp.sum(real_corr / denominator, axis=-3),
        jnp.sum(imag_corr / denominator, axis=-3),
    )


def shards(spectra, quality, offsets):
    chan_count = lax.axis_size("chan")
    tm_count = lax.axis_size("tm")
    levels = chan_count.bit_length() - 1
    table_bf = lag_table(F, LAGS)
    inv_root = 1.0 / math.sqrt(F)
    real_part = spectra[0].astype(jnp.float32)
    imag_part = spectra[1].astype(jnp.float32)
    magnitude = jnp.sqrt(real_part * real_part + imag_part * imag_part)
    band_total = lax.psum(jnp.sum(magnitude, axis=1), "chan")
    channel_level = (band_total / F)[:, None, :]
    whitened = whiten_parts(real_part, imag_part, magnitude, channel_level, quality)
    width_all = whitened.shape[3]
    padded = jnp.pad(whitened, ((0, 0), (0, 0), (0, 0), (0, width_all)))
    crossed_list = []
    for offset_index in range(NOFF):
        partner = lax.dynamic_slice_in_dim(padded, offsets[offset_index] * CH_DEV, width_all, 3)
        crossed_list.append(cross_parts(whitened[0], whitened[1], partner[0], partner[1]))
    crossed = jnp.stack(crossed_list, axis=1)
    corr_all = jnp.einsum(
        "cnwfh,cfl->nwhl",
        lax.all_to_all(crossed, "chan", split_axis=4, concat_axis=3, tiled=True),
        table_bf,
        preferred_element_type=jnp.float32,
    )
    linear_sum, real_sum, imag_sum = pair_terms(corr_all * inv_root)
    totals = lax.psum((linear_sum, real_sum, imag_sum), "tm")
    window_count = W_DEV * tm_count
    linear = totals[0] / window_count
    real_phase = totals[1] / window_count
    imag_phase = totals[2] / window_count
    stacks = jnp.transpose(linear * (real_phase * real_phase + imag_phase * imag_phase), (1, 0, 2))
    reverse_part = stacks
    for bit_index in range(levels):
        step_size = 1 << bit_index
        arrived = shifted(reverse_part, "chan", step_size)
        chosen = offsets // step_size % 2 == 1
        reverse_part = jnp.where(chosen[None, :, None], arrived, reverse_part)
    return stacks + jnp.flip(reverse_part, axis=2)


def solution(mesh):
    chan_count, tm_count = mesh.shape["chan"], mesh.shape["tm"]
    by_window = chan_count == W_DEV and tm_count == NOFF
    return jax.shard_map(
        window_shards if by_window else shards,
        mesh=mesh,
        in_specs=(P(None, "tm", "chan", None), P("tm", None), P()),
        out_specs=P("chan", None, None),
        check_vma=False,
    )
```

```python
import functools
import math

import jax
import jax.numpy as jnp
import numpy as np
from jax import lax
from jax.experimental import pallas as pl
from jax.experimental.pallas import tpu as pltpu
from jax.sharding import PartitionSpec as P

F = 2048
LAGS = 256
NOFF = 4
CH_DEV = 16
W_DEV = 8
VMEM_LIMIT = 48 * 1024 * 1024
CODE_TOP = 32767.0
OCTAVE = 256.0
LOWEST = -110.0


def encode(value):
    return jnp.round(value).astype(jnp.int32).astype(jnp.int16)


def decode(code):
    return code.astype(jnp.int32).astype(jnp.float32)


def level_code(peak):
    return jnp.ceil(jnp.maximum(jnp.log2(jnp.maximum(peak, 1e-30)), LOWEST) * OCTAVE) + 1.0


def level_of(code):
    return jnp.exp2(code * (1.0 / OCTAVE))


def half_table(freq_count, lag_count):
    freq_index = np.arange(freq_count, dtype=np.int64)[None, :]
    double_lag = (2 * np.arange(lag_count // 2, lag_count, dtype=np.int64) - lag_count + 1)[:, None]
    turns = np.mod(freq_index * double_lag, 4 * freq_count).astype(np.float32)
    angles = turns * np.float32(2.0 * math.pi / (4 * freq_count))
    return np.concatenate([np.cos(angles), np.sin(angles)]).astype(jnp.bfloat16)


def widest(offs_ref, reach):
    last = offs_ref.shape[0] - 1
    found = last
    for number in reversed(range(last)):
        found = jnp.where(offs_ref[number] == reach, number, found)
    return found


def offset_of(slot, offs_ref, reach):
    last, wide = offs_ref.shape[0] - 1, widest(offs_ref, reach)
    return offs_ref[jnp.where(slot == wide, last, jnp.where(slot == last, wide, slot))]


def window_kernel(order, offs_hbm_ref, where_ref, *refs):
    chan_count = len(order)
    spec_refs, (qual_ref, table_ref) = refs[:chan_count], refs[chan_count : chan_count + 2]
    out_refs = refs[chan_count + 2 : chan_count + 4]
    mag_ref, white_ref, cross_ref, offs_ref, offs_sem = refs[chan_count + 4 :]
    fetch = pltpu.make_async_copy(offs_hbm_ref, offs_ref, offs_sem)
    fetch.start()
    me = where_ref[0]
    _, band, chans = spec_refs[0].shape
    freqs = chan_count * band
    chip_count, blocks, lag_rows, _ = out_refs[0].shape
    offset_count = offs_ref.shape[0]
    half = chan_count * lag_rows
    step = 64

    total = jnp.zeros((8, chans), jnp.float32)
    for number, spec_ref in enumerate(spec_refs):
        for row in range(0, band, step):
            real, imag = (spec_ref[part, row : row + step, :].astype(jnp.float32) for part in range(2))
            square = real * real + imag * imag
            magnitude = square * lax.rsqrt(jnp.maximum(square, 1e-30))
            held = slice(number * band + row, number * band + row + step)
            mag_ref[held, :] = magnitude
            total += jnp.sum(magnitude.reshape(step // 8, 8, chans), axis=0)
    level = jnp.sum(total, axis=0, keepdims=True) * (1.0 / freqs)
    floor = 0.5 * (level + 1e-05)

    for number, spec_ref in enumerate(spec_refs):
        for row in range(0, band, step):
            held = slice(number * band + row, number * band + row + step)
            factor = pl.reciprocal(mag_ref[held, :] + floor, approx=True)
            for part in range(2):
                value = spec_ref[part, row : row + step, :].astype(jnp.float32) * factor
                white_ref[part, held, :] = value.astype(jnp.bfloat16)

    lane = lax.broadcasted_iota(jnp.int32, (1, chans), 1)
    line = lax.broadcasted_iota(jnp.int32, (lag_rows, chans), 0)
    usable = qual_ref[pl.ds(me, 1), :].astype(jnp.float32)
    levels = jnp.zeros((lag_rows, chans), jnp.float32)
    groups = [k ^ core for core in range(2) for k in chips(chan_count)]
    fetch.wait()
    bands = [pl.ds(pl.multiple_of((me ^ k) * band, band), band) for k in order]
    table = jnp.concatenate(
        [
            jnp.concatenate([table_ref[side, me ^ group, :, taken] for taken in bands], axis=1)
            for side in range(2)
            for group in groups
        ],
        axis=0,
    )
    turns = [chans - offset_of(number, offs_ref, chan_count // 2) * (chans // chan_count) for number in range(offset_count)]
    for row in range(0, freqs, step):
        own = [white_ref[part, row : row + step, :] for part in range(2)]
        own_real, own_imag = (value.astype(jnp.float32) for value in own)
        for number, turn in enumerate(turns):
            far_real, far_imag = (pltpu.roll(value, turn, 1).astype(jnp.float32) for value in own)
            real = own_real * far_real + own_imag * far_imag
            imag = own_imag * far_real - own_real * far_imag
            cross_ref[number, row : row + step, 0:chans] = real.astype(jnp.bfloat16)
            cross_ref[number, row : row + step, chans : 2 * chans] = imag.astype(jnp.bfloat16)

    for number, turn in enumerate(turns):
        sums = jnp.dot(table, cross_ref[number], preferred_element_type=jnp.float32)
        cos_real, sin_real = sums[:half, :chans], sums[half:, :chans]
        cos_imag, sin_imag = sums[:half, chans:], sums[half:, chans:]
        corr = (
            (cos_real - sin_imag, sin_real + cos_imag),
            (cos_real + sin_imag, cos_imag - sin_real),
        )
        power = [real * real + imag * imag for real, imag in corr]
        mean_power = jnp.sum(power[0] + power[1], axis=0, keepdims=True) * (1.0 / (2 * half))
        extra = 0.25 * (mean_power + 1e-06 * freqs)
        peak = jnp.max(jnp.maximum(jnp.abs(corr[0][0]), jnp.abs(corr[1][0])), axis=0, keepdims=True)
        code = level_code(peak)
        keep = jnp.where(lane < turn, usable * pltpu.roll(usable, turn, 1), 0.0) * CODE_TOP
        upscale = keep / level_of(code)
        inverse = [lax.rsqrt(side + extra) * keep for side in power]
        kinds = [
            [real * upscale for real, _ in corr],
            [real * scale for (real, _), scale in zip(corr, inverse)],
            [imag * scale for (_, imag), scale in zip(corr, inverse)],
        ]
        if number == offset_count - 1:
            code = jnp.where(lane < chans // 2, code, pltpu.roll(code, chans // 2, 1))
            kinds = [[jnp.where(lane < chans // 2, ahead, pltpu.roll(back, chans // 2, 1))] for ahead, back in kinds]
        levels = jnp.where(line == number, code, levels)
        for place, value in enumerate(value for kind in kinds for value in kind):
            coded = encode(value).reshape(chan_count, lag_rows, chans)
            for core in range(2):
                rows = slice(core * chip_count, (core + 1) * chip_count)
                out_refs[core][:, 6 * number + place, :, :] = coded[rows]
    for number in range(offset_count):
        levels = jnp.where(line == offset_count + number, offs_ref[number].astype(jnp.float32), levels)
    wide = widest(offs_ref, chan_count // 2).astype(jnp.float32)
    levels = jnp.where(line == 2 * offset_count, wide, levels)
    for out_ref in out_refs:
        for chip in range(chip_count):
            out_ref[chip, blocks - 1, :, :] = encode(levels)


def merge_kernel(slots, own_ref, far_ref, *out_refs):
    blocks = own_ref.shape[1]
    for chip, out_ref in enumerate(out_refs):
        codes = [decode(ref[chip, blocks - 1]) for ref in (own_ref, far_ref)]
        levels = [level_of(code) for code in codes]
        code = level_code(levels[0] + levels[1])
        shares = [level / level_of(code) for level in levels]
        line = lax.broadcasted_iota(jnp.int32, code.shape, 0)
        out_ref[blocks - 1, :, :] = encode(jnp.where(line < slots, code, codes[0]))
        for block in range(blocks - 1):
            number, part = divmod(block, 6)
            linear = part < (2 if blocks - 1 - 6 * number > 3 else 1)
            own, far = decode(own_ref[chip, block]), decode(far_ref[chip, block])
            if linear:
                total = own * shares[0][number : number + 1, :] + far * shares[1][number : number + 1, :]
            else:
                total = (own + far) * 0.5
            out_ref[block, :, :] = encode(total)


def sum_kernel(order, scale, where_ref, *refs):
    code_refs, out_refs, held_ref = refs[: -len(order) - 1], refs[-len(order) - 1 : -1], refs[-1]
    blocks, _, chans = code_refs[0].shape
    slots = held_ref.shape[0]
    heads = [decode(codes_ref[blocks - 1]) for codes_ref in code_refs]
    levels = [level_of(head) * scale for head in heads]
    offsets = [heads[0][slots + number : slots + number + 1, :] for number in range(slots)]
    wide = heads[0][2 * slots : 2 * slots + 1, :]
    low = lax.broadcasted_iota(jnp.int32, (1, chans), 1) < chans // 2
    all_sums = []
    for number in range(slots):
        sides = 2 if number < slots - 1 else 1
        own = [level[number : number + 1, :] for level in levels]
        sums = []
        for place in range(3 * sides):
            codes = [decode(codes_ref[6 * number + place]) for codes_ref in code_refs]
            if place < sides:
                sums.append(sum(code * level for code, level in zip(codes, own)))
            else:
                sums.append(sum(codes) * (1.0 / len(code_refs)))
        if sides == 1:
            sums = [
                jnp.where(low, side, 0.0) for value in sums for side in (value, pltpu.roll(value, chans // 2, 1))
            ]
        all_sums.append(sums)
    line = lax.broadcasted_iota(jnp.int32, levels[0].shape, 0)
    last = slots - 1
    for number in range(slots):
        sums = all_sums[number]
        for other in range(last) if number == last else [last]:
            swap = wide == min(number, other)
            sums = [jnp.where(swap, value, kept) for value, kept in zip(all_sums[other], sums)]
        peak = jnp.max(jnp.maximum(jnp.abs(sums[0]), jnp.abs(sums[1])), axis=0, keepdims=True)
        code = level_code(peak)
        upscale = CODE_TOP / level_of(code)
        head = jnp.where(line == 0, code, offsets[number])
        for part, value in enumerate([sums[0] * upscale, sums[1] * upscale, *sums[2:], head]):
            held_ref[number, part, :, :] = encode(value)
    for k, out_ref in zip(order, out_refs):
        out_ref[...] = held_ref[where_ref[0] ^ k]


def partners(count):
    return sorted(range(1, count), key=lambda k: (-(k >> 1).bit_count(), k & 1, k)) + [0]


def chips(count):
    return sorted(range(2, count, 2), key=lambda k: (k.bit_count(), k)) + [0]


def exchange(pieces, axis, order):
    count = lax.axis_size(axis)
    return [
        lax.ppermute(piece, axis, [(source, source ^ k) for source in range(count)]) if k else piece
        for k, piece in zip(order, pieces)
    ]


def split_kernel(order, where_ref, spec_ref, *refs):
    out_refs, sems = refs[:-1], refs[-1]
    copies = [
        pltpu.make_async_copy(spec_ref.at[:, where_ref[0] ^ k], out_ref, sems.at[number])
        for number, (k, out_ref) in enumerate(zip(order, out_refs))
    ]
    for copy in copies:
        copy.start()
    for copy in copies:
        copy.wait()


def stack_kernel(windows, *refs):
    sums_refs, out_ref = refs[:-1], refs[-1]
    blocks, copies, rows, _ = out_ref.shape
    _, lag_rows, chans = sums_refs[0].shape
    per_sum = windows // len(sums_refs)
    heads = [decode(sums_ref[6]) for sums_ref in sums_refs]
    levels = [level_of(head[0:1, :]) * (1.0 / (CODE_TOP * windows)) for head in heads]
    stacks = []
    for side in range(2):
        linear = sum(decode(sums_ref[side]) * level for sums_ref, level in zip(sums_refs, levels))
        real, imag = (
            sum(decode(sums_ref[part + side]) for sums_ref in sums_refs) * (per_sum / (CODE_TOP * windows))
            for part in (2, 4)
        )
        stacks.append(linear * (real * real + imag * imag))
    offset = heads[0][1:2, :]
    lane = lax.broadcasted_iota(jnp.int32, (1, chans), 1)
    behind = [jnp.zeros_like(stack) for stack in stacks]
    for steps in range(1, blocks // 2 + 1):
        ahead = steps * (chans // blocks)
        chosen = (offset == steps) & (lane >= ahead)
        behind = [jnp.where(chosen, pltpu.roll(stack, ahead, 1), kept) for stack, kept in zip(stacks, behind)]
    back = stacks[1] + behind[0]
    both = jnp.concatenate(
        [stacks[0] + behind[1]] + [back[row : row + 1, :] for row in reversed(range(lag_rows))], axis=0
    )
    wide = 2 * lag_rows
    parts = chans // wide
    turned = jnp.concatenate([both] * parts, axis=0).T
    per_block = chans // blocks
    for block in range(blocks):
        piece = jnp.zeros((rows, chans), jnp.float32)
        for part in range(parts):
            begin = block * per_block + part * rows
            piece = jnp.where(lane // wide == part, turned[begin : begin + rows, :], piece)
        for copy in range(copies):
            out_ref[block, copy, :, :] = piece


def place_kernel(parts_ref, out_ref):
    groups, offset_count, rows, lanes = parts_ref.shape
    half = out_ref.shape[2] // 2
    lag_rows = half // groups
    parts = out_ref.shape[0] // rows
    lane = lax.broadcasted_iota(jnp.int32, (1, lanes), 1)
    for number in range(offset_count):
        for part in range(parts):
            ahead = jnp.zeros((rows, lanes), jnp.float32)
            back = jnp.zeros((rows, lanes), jnp.float32)
            begin = part * 2 * lag_rows
            for group in range(groups):
                piece = parts_ref[group, number]
                first, last = group * lag_rows, half - (group + 1) * lag_rows
                ahead = jnp.where(lane // lag_rows == group, pltpu.roll(piece, (first - begin) % lanes, 1), ahead)
                back = jnp.where(
                    lane // lag_rows == groups - 1 - group, pltpu.roll(piece, (last - begin - lag_rows) % lanes, 1), back
                )
            out_ref[part * rows : (part + 1) * rows, number, 0:half] = back
            out_ref[part * rows : (part + 1) * rows, number, half : 2 * half] = ahead


def window_shards(spectra, quality, offsets):
    chan_count = lax.axis_size("chan")
    tm_count = lax.axis_size("tm")
    _, windows, band, chans = spectra.shape
    freqs = band * chan_count
    half = LAGS // 2
    lag_rows = half // chan_count
    offset_count = offsets.shape[0]
    piece_rows = 2 * lag_rows // chan_count
    smem = pl.BlockSpec(memory_space=pltpu.SMEM)
    vmem = pl.BlockSpec(memory_space=pltpu.VMEM)
    params = pltpu.CompilerParams(vmem_limit_bytes=VMEM_LIMIT)
    table = jnp.asarray(half_table(freqs, LAGS).reshape(2, chan_count, lag_rows, freqs))
    chan_index = lax.axis_index("chan").astype(jnp.int32)
    tm_index = lax.axis_index("tm").astype(jnp.int32)
    chan_where, tm_where = chan_index.reshape(1), tm_index.reshape(1)

    chan_order, tm_order = partners(chan_count), partners(tm_count)
    kept = pl.BlockSpec(memory_space=pltpu.HBM)
    spectra = pltpu.with_memory_space_constraint(spectra, pltpu.HBM)
    pieces = []
    for part in (chan_order[:2], chan_order[2:]):
        pieces += pl.pallas_call(
            functools.partial(split_kernel, part),
            out_shape=[jax.ShapeDtypeStruct((2, band, chans), spectra.dtype)] * len(part),
            in_specs=[smem, kept],
            out_specs=[pl.BlockSpec(memory_space=pl.ANY)] * len(part),
            scratch_shapes=[pltpu.SemaphoreType.DMA((len(part),))],
            compiler_params=params,
            name="split_windows",
        )(chan_where, spectra)
    chip_order = chips(chan_count)
    pair_shape = (6 * offset_count - 2, lag_rows, chans)
    own, far = pl.pallas_call(
        functools.partial(window_kernel, chan_order),
        out_shape=[jax.ShapeDtypeStruct((len(chip_order), *pair_shape), jnp.int16)] * 2,
        in_specs=[kept, smem] + [vmem] * (chan_count + 2),
        out_specs=[vmem] * 2,
        scratch_shapes=[
            pltpu.VMEM((freqs, chans), jnp.float32),
            pltpu.VMEM((2, freqs, chans), jnp.bfloat16),
            pltpu.VMEM((offset_count, freqs, 2 * chans), jnp.bfloat16),
            pltpu.SMEM(offsets.shape, jnp.int32),
            pltpu.SemaphoreType.DMA(()),
        ],
        compiler_params=params,
        name="window_pairs",
    )(pltpu.with_memory_space_constraint(offsets, pltpu.HBM), chan_where, *exchange(pieces, "chan", chan_order), quality, table)
    pairs = pl.pallas_call(
        functools.partial(merge_kernel, offset_count),
        out_shape=[jax.ShapeDtypeStruct(pair_shape, jnp.int16)] * len(chip_order),
        in_specs=[vmem] * 2,
        out_specs=[vmem] * len(chip_order),
        compiler_params=params,
        name="merge_windows",
    )(own, *exchange([far], "chan", [1]))
    sums = pl.pallas_call(
        functools.partial(sum_kernel, tm_order, 1.0 / (CODE_TOP * math.sqrt(freqs))),
        out_shape=[jax.ShapeDtypeStruct((7, lag_rows, chans), jnp.int16)] * tm_count,
        in_specs=[smem] + [vmem] * len(chip_order),
        out_specs=[vmem] * tm_count,
        scratch_shapes=[pltpu.VMEM((offset_count, 7, lag_rows, chans), jnp.int16)],
        compiler_params=params,
        name="sum_windows",
    )(tm_where, *exchange(pairs, "chan", chip_order))
    pieces = pl.pallas_call(
        functools.partial(stack_kernel, windows * tm_count),
        out_shape=jax.ShapeDtypeStruct((chan_count, tm_count, piece_rows, chans), jnp.float32),
        in_specs=[vmem] * tm_count,
        out_specs=vmem,
        compiler_params=params,
        name="stack_pairs",
    )(*exchange(sums, "tm", tm_order))
    shape = (chan_count * tm_count, piece_rows, chans)
    arrived = lax.all_to_all(pieces.reshape(shape), ("chan", "tm"), 0, 0, tiled=True)
    return pl.pallas_call(
        place_kernel,
        out_shape=jax.ShapeDtypeStruct((CH_DEV, offset_count, LAGS), jnp.float32),
        in_specs=[vmem],
        out_specs=vmem,
        compiler_params=params,
        name="place_lags",
    )(arrived.reshape(chan_count, tm_count, piece_rows, chans))


def shifted(value, axis, steps):
    count = lax.axis_size(axis)
    leading, last = (max(0, -steps), min(count, count - steps))
    return lax.ppermute(value, axis, [(source, source + steps) for source in range(leading, last)])


def lag_table(freq_count, lag_count):
    freq_index = jnp.arange(freq_count, dtype=jnp.int32)[:, None]
    double_lag = (2 * jnp.arange(lag_count, dtype=jnp.int32) - lag_count + 1)[None, :]
    turns = jnp.mod(freq_index * double_lag, 4 * freq_count)
    angles = turns.astype(jnp.float32) * (2.0 * math.pi / (4 * freq_count))
    cosine = jnp.cos(angles)
    sine = jnp.sin(angles)
    upper = jnp.concatenate([cosine, sine], axis=1)
    lower = jnp.concatenate([-sine, cosine], axis=1)
    return jnp.stack([upper, lower]).astype(jnp.bfloat16)


def whiten_parts(real_part, imag_part, magnitude, channel_level, usable):
    factor = usable.astype(jnp.float32)[:, None, :] / (magnitude + 0.5 * (channel_level + 1e-05))
    return jnp.stack([real_part * factor, imag_part * factor]).astype(jnp.bfloat16)


def cross_parts(own_real, own_imag, far_real, far_imag):
    own_real = own_real.astype(jnp.float32)
    own_imag = own_imag.astype(jnp.float32)
    far_real = far_real.astype(jnp.float32)
    far_imag = far_imag.astype(jnp.float32)
    return jnp.stack(
        [own_real * far_real + own_imag * far_imag, own_imag * far_real - own_real * far_imag]
    ).astype(jnp.bfloat16)


def pair_terms(corr_all):
    lag_count = corr_all.shape[-1] // 2
    real_corr = corr_all[..., :lag_count]
    imag_corr = corr_all[..., lag_count:]
    power = real_corr * real_corr + imag_corr * imag_corr
    mean_power = jnp.mean(power, axis=-1, keepdims=True)
    denominator = jnp.sqrt(power + 0.25 * (mean_power + 1e-06))
    return (
        jnp.sum(real_corr, axis=-3),
        jnp.sum(real_corr / denominator, axis=-3),
        jnp.sum(imag_corr / denominator, axis=-3),
    )


def shards(spectra, quality, offsets):
    chan_count = lax.axis_size("chan")
    tm_count = lax.axis_size("tm")
    levels = chan_count.bit_length() - 1
    table_bf = lag_table(F, LAGS)
    inv_root = 1.0 / math.sqrt(F)
    real_part = spectra[0].astype(jnp.float32)
    imag_part = spectra[1].astype(jnp.float32)
    magnitude = jnp.sqrt(real_part * real_part + imag_part * imag_part)
    band_total = lax.psum(jnp.sum(magnitude, axis=1), "chan")
    channel_level = (band_total / F)[:, None, :]
    whitened = whiten_parts(real_part, imag_part, magnitude, channel_level, quality)
    width_all = whitened.shape[3]
    padded = jnp.pad(whitened, ((0, 0), (0, 0), (0, 0), (0, width_all)))
    crossed_list = []
    for offset_index in range(NOFF):
        partner = lax.dynamic_slice_in_dim(padded, offsets[offset_index] * CH_DEV, width_all, 3)
        crossed_list.append(cross_parts(whitened[0], whitened[1], partner[0], partner[1]))
    crossed = jnp.stack(crossed_list, axis=1)
    corr_all = jnp.einsum(
        "cnwfh,cfl->nwhl",
        lax.all_to_all(crossed, "chan", split_axis=4, concat_axis=3, tiled=True),
        table_bf,
        preferred_element_type=jnp.float32,
    )
    linear_sum, real_sum, imag_sum = pair_terms(corr_all * inv_root)
    totals = lax.psum((linear_sum, real_sum, imag_sum), "tm")
    window_count = W_DEV * tm_count
    linear = totals[0] / window_count
    real_phase = totals[1] / window_count
    imag_phase = totals[2] / window_count
    stacks = jnp.transpose(linear * (real_phase * real_phase + imag_phase * imag_phase), (1, 0, 2))
    reverse_part = stacks
    for bit_index in range(levels):
        step_size = 1 << bit_index
        arrived = shifted(reverse_part, "chan", step_size)
        chosen = offsets // step_size % 2 == 1
        reverse_part = jnp.where(chosen[None, :, None], arrived, reverse_part)
    return stacks + jnp.flip(reverse_part, axis=2)


def solution(mesh):
    chan_count, tm_count = mesh.shape["chan"], mesh.shape["tm"]
    by_window = chan_count == W_DEV and tm_count == NOFF
    return jax.shard_map(
        window_shards if by_window else shards,
        mesh=mesh,
        in_specs=(P(None, "tm", "chan", None), P("tm", None), P()),
        out_specs=P("chan", None, None),
        check_vma=False,
    )
```

```python
import functools
import math

import jax
import jax.numpy as jnp
import numpy as np
from jax import lax
from jax.experimental import pallas as pl
from jax.experimental.pallas import tpu as pltpu
from jax.sharding import PartitionSpec as P

F = 2048
LAGS = 256
NOFF = 4
CH_DEV = 16
W_DEV = 8
VMEM_LIMIT = 48 * 1024 * 1024
CODE_TOP = 32767.0
OCTAVE = 256.0
LOWEST = -110.0


def encode(value):
    return jnp.round(value).astype(jnp.int32).astype(jnp.int16)


def decode(code):
    return code.astype(jnp.int32).astype(jnp.float32)


def level_code(peak):
    return jnp.ceil(jnp.maximum(jnp.log2(jnp.maximum(peak, 1e-30)), LOWEST) * OCTAVE) + 1.0


def level_of(code):
    return jnp.exp2(code * (1.0 / OCTAVE))


def half_table(freq_count, lag_count):
    freq_index = np.arange(freq_count, dtype=np.int64)[None, :]
    double_lag = (2 * np.arange(lag_count // 2, lag_count, dtype=np.int64) - lag_count + 1)[:, None]
    turns = np.mod(freq_index * double_lag, 4 * freq_count).astype(np.float32)
    angles = turns * np.float32(2.0 * math.pi / (4 * freq_count))
    return np.concatenate([np.cos(angles), np.sin(angles)]).astype(jnp.bfloat16)


def widest(offs_ref, reach):
    last = offs_ref.shape[0] - 1
    found = last
    for number in reversed(range(last)):
        found = jnp.where(offs_ref[number] == reach, number, found)
    return found


def offset_of(slot, offs_ref, reach):
    last, wide = offs_ref.shape[0] - 1, widest(offs_ref, reach)
    return offs_ref[jnp.where(slot == wide, last, jnp.where(slot == last, wide, slot))]


def window_kernel(order, offs_hbm_ref, where_ref, *refs):
    chan_count = len(order)
    spec_refs, (qual_ref, table_ref) = refs[:chan_count], refs[chan_count : chan_count + 2]
    out_refs = refs[chan_count + 2 : chan_count + 4]
    mag_ref, white_ref, cross_ref, offs_ref, offs_sem = refs[chan_count + 4 :]
    fetch = pltpu.make_async_copy(offs_hbm_ref, offs_ref, offs_sem)
    fetch.start()
    me = where_ref[0]
    _, band, chans = spec_refs[0].shape
    freqs = chan_count * band
    chip_count, blocks, lag_rows, _ = out_refs[0].shape
    offset_count = offs_ref.shape[0]
    half = chan_count * lag_rows
    step = 64

    total = jnp.zeros((8, chans), jnp.float32)
    for number, spec_ref in enumerate(spec_refs):
        for row in range(0, band, step):
            real, imag = (spec_ref[part, row : row + step, :].astype(jnp.float32) for part in range(2))
            square = real * real + imag * imag
            magnitude = square * lax.rsqrt(jnp.maximum(square, 1e-30))
            held = slice(number * band + row, number * band + row + step)
            mag_ref[held, :] = magnitude
            total += jnp.sum(magnitude.reshape(step // 8, 8, chans), axis=0)
    level = jnp.sum(total, axis=0, keepdims=True) * (1.0 / freqs)
    floor = 0.5 * (level + 1e-05)

    for number, spec_ref in enumerate(spec_refs):
        for row in range(0, band, step):
            held = slice(number * band + row, number * band + row + step)
            factor = pl.reciprocal(mag_ref[held, :] + floor, approx=True)
            for part in range(2):
                value = spec_ref[part, row : row + step, :].astype(jnp.float32) * factor
                white_ref[part, held, :] = value.astype(jnp.bfloat16)

    lane = lax.broadcasted_iota(jnp.int32, (1, chans), 1)
    line = lax.broadcasted_iota(jnp.int32, (lag_rows, chans), 0)
    usable = qual_ref[pl.ds(me, 1), :].astype(jnp.float32)
    levels = jnp.zeros((lag_rows, chans), jnp.float32)
    groups = [k ^ core for core in range(2) for k in chips(chan_count)]
    fetch.wait()
    bands = [pl.ds(pl.multiple_of((me ^ k) * band, band), band) for k in order]
    table = jnp.concatenate(
        [
            jnp.concatenate([table_ref[side, me ^ group, :, taken] for taken in bands], axis=1)
            for side in range(2)
            for group in groups
        ],
        axis=0,
    )
    turns = [chans - offset_of(number, offs_ref, chan_count // 2) * (chans // chan_count) for number in range(offset_count)]
    for row in range(0, freqs, step):
        own = [white_ref[part, row : row + step, :] for part in range(2)]
        own_real, own_imag = (value.astype(jnp.float32) for value in own)
        for number, turn in enumerate(turns):
            far_real, far_imag = (pltpu.roll(value, turn, 1).astype(jnp.float32) for value in own)
            real = own_real * far_real + own_imag * far_imag
            imag = own_imag * far_real - own_real * far_imag
            cross_ref[number, row : row + step, 0:chans] = real.astype(jnp.bfloat16)
            cross_ref[number, row : row + step, chans : 2 * chans] = imag.astype(jnp.bfloat16)

    for number, turn in enumerate(turns):
        sums = jnp.dot(table, cross_ref[number], preferred_element_type=jnp.float32)
        cos_real, sin_real = sums[:half, :chans], sums[half:, :chans]
        cos_imag, sin_imag = sums[:half, chans:], sums[half:, chans:]
        corr = (
            (cos_real - sin_imag, sin_real + cos_imag),
            (cos_real + sin_imag, cos_imag - sin_real),
        )
        power = [real * real + imag * imag for real, imag in corr]
        mean_power = jnp.sum(power[0] + power[1], axis=0, keepdims=True) * (1.0 / (2 * half))
        extra = 0.25 * (mean_power + 1e-06 * freqs)
        peak = jnp.max(jnp.maximum(jnp.abs(corr[0][0]), jnp.abs(corr[1][0])), axis=0, keepdims=True)
        code = level_code(peak)
        keep = jnp.where(lane < turn, usable * pltpu.roll(usable, turn, 1), 0.0) * CODE_TOP
        upscale = keep / level_of(code)
        inverse = [lax.rsqrt(side + extra) * keep for side in power]
        kinds = [
            [real * upscale for real, _ in corr],
            [real * scale for (real, _), scale in zip(corr, inverse)],
            [imag * scale for (_, imag), scale in zip(corr, inverse)],
        ]
        if number == offset_count - 1:
            code = jnp.where(lane < chans // 2, code, pltpu.roll(code, chans // 2, 1))
            kinds = [[jnp.where(lane < chans // 2, ahead, pltpu.roll(back, chans // 2, 1))] for ahead, back in kinds]
        levels = jnp.where(line == number, code, levels)
        for place, value in enumerate(value for kind in kinds for value in kind):
            coded = encode(value).reshape(chan_count, lag_rows, chans)
            for core in range(2):
                rows = slice(core * chip_count, (core + 1) * chip_count)
                out_refs[core][:, 6 * number + place, :, :] = coded[rows]
    for number in range(offset_count):
        levels = jnp.where(line == offset_count + number, offs_ref[number].astype(jnp.float32), levels)
    wide = widest(offs_ref, chan_count // 2).astype(jnp.float32)
    levels = jnp.where(line == 2 * offset_count, wide, levels)
    for out_ref in out_refs:
        for chip in range(chip_count):
            out_ref[chip, blocks - 1, :, :] = encode(levels)


def merge_kernel(slots, own_ref, far_ref, *out_refs):
    blocks = own_ref.shape[1]
    for chip, out_ref in enumerate(out_refs):
        codes = [decode(ref[chip, blocks - 1]) for ref in (own_ref, far_ref)]
        levels = [level_of(code) for code in codes]
        code = level_code(levels[0] + levels[1])
        shares = [level / level_of(code) for level in levels]
        line = lax.broadcasted_iota(jnp.int32, code.shape, 0)
        out_ref[blocks - 1, :, :] = encode(jnp.where(line < slots, code, codes[0]))
        for block in range(blocks - 1):
            number, part = divmod(block, 6)
            linear = part < (2 if blocks - 1 - 6 * number > 3 else 1)
            own, far = decode(own_ref[chip, block]), decode(far_ref[chip, block])
            if linear:
                total = own * shares[0][number : number + 1, :] + far * shares[1][number : number + 1, :]
            else:
                total = (own + far) * 0.5
            out_ref[block, :, :] = encode(total)


def sum_kernel(order, scale, where_ref, *refs):
    code_refs, out_refs, held_ref = refs[: -len(order) - 1], refs[-len(order) - 1 : -1], refs[-1]
    blocks, _, chans = code_refs[0].shape
    slots = held_ref.shape[0]
    heads = [decode(codes_ref[blocks - 1]) for codes_ref in code_refs]
    levels = [level_of(head) * scale for head in heads]
    offsets = [heads[0][slots + number : slots + number + 1, :] for number in range(slots)]
    wide = heads[0][2 * slots : 2 * slots + 1, :]
    low = lax.broadcasted_iota(jnp.int32, (1, chans), 1) < chans // 2
    all_sums = []
    for number in range(slots):
        sides = 2 if number < slots - 1 else 1
        own = [level[number : number + 1, :] for level in levels]
        sums = []
        for place in range(3 * sides):
            codes = [decode(codes_ref[6 * number + place]) for codes_ref in code_refs]
            if place < sides:
                sums.append(sum(code * level for code, level in zip(codes, own)))
            else:
                sums.append(sum(codes) * (1.0 / len(code_refs)))
        if sides == 1:
            sums = [
                jnp.where(low, side, 0.0) for value in sums for side in (value, pltpu.roll(value, chans // 2, 1))
            ]
        all_sums.append(sums)
    line = lax.broadcasted_iota(jnp.int32, levels[0].shape, 0)
    last = slots - 1
    for number in range(slots):
        sums = all_sums[number]
        for other in range(last) if number == last else [last]:
            swap = wide == min(number, other)
            sums = [jnp.where(swap, value, kept) for value, kept in zip(all_sums[other], sums)]
        peak = jnp.max(jnp.maximum(jnp.abs(sums[0]), jnp.abs(sums[1])), axis=0, keepdims=True)
        code = level_code(peak)
        upscale = CODE_TOP / level_of(code)
        head = jnp.where(line == 0, code, offsets[number])
        for part, value in enumerate([sums[0] * upscale, sums[1] * upscale, *sums[2:], head]):
            held_ref[number, part, :, :] = encode(value)
    for k, out_ref in zip(order, out_refs):
        out_ref[...] = held_ref[where_ref[0] ^ k]


def partners(count):
    near = [k for k in range(2, count) if k.bit_count() == 1]
    far = [k for k in range(2, count) if k >> 1 not in (1, 2)]
    return near + far + [k for k in range(2, count) if k not in near + far] + [1, 0]


def chips(count):
    return sorted(range(2, count, 2), key=lambda k: (k.bit_count(), k)) + [0]


def exchange(pieces, axis, order):
    count = lax.axis_size(axis)
    return [
        lax.ppermute(piece, axis, [(source, source ^ k) for source in range(count)]) if k else piece
        for k, piece in zip(order, pieces)
    ]


def split_kernel(order, where_ref, spec_ref, *refs):
    out_refs, sems = refs[:-1], refs[-1]
    copies = [
        pltpu.make_async_copy(spec_ref.at[:, where_ref[0] ^ k], out_ref, sems.at[number])
        for number, (k, out_ref) in enumerate(zip(order, out_refs))
    ]
    for copy in copies:
        copy.start()
    for copy in copies:
        copy.wait()


def stack_kernel(windows, *refs):
    sums_refs, out_ref = refs[:-1], refs[-1]
    blocks, copies, rows, _ = out_ref.shape
    _, lag_rows, chans = sums_refs[0].shape
    per_sum = windows // len(sums_refs)
    heads = [decode(sums_ref[6]) for sums_ref in sums_refs]
    levels = [level_of(head[0:1, :]) * (1.0 / (CODE_TOP * windows)) for head in heads]
    stacks = []
    for side in range(2):
        linear = sum(decode(sums_ref[side]) * level for sums_ref, level in zip(sums_refs, levels))
        real, imag = (
            sum(decode(sums_ref[part + side]) for sums_ref in sums_refs) * (per_sum / (CODE_TOP * windows))
            for part in (2, 4)
        )
        stacks.append(linear * (real * real + imag * imag))
    offset = heads[0][1:2, :]
    lane = lax.broadcasted_iota(jnp.int32, (1, chans), 1)
    behind = [jnp.zeros_like(stack) for stack in stacks]
    for steps in range(1, blocks // 2 + 1):
        ahead = steps * (chans // blocks)
        chosen = (offset == steps) & (lane >= ahead)
        behind = [jnp.where(chosen, pltpu.roll(stack, ahead, 1), kept) for stack, kept in zip(stacks, behind)]
    back = stacks[1] + behind[0]
    both = jnp.concatenate(
        [stacks[0] + behind[1]] + [back[row : row + 1, :] for row in reversed(range(lag_rows))], axis=0
    )
    wide = 2 * lag_rows
    parts = chans // wide
    turned = jnp.concatenate([both] * parts, axis=0).T
    per_block = chans // blocks
    for block in range(blocks):
        piece = jnp.zeros((rows, chans), jnp.float32)
        for part in range(parts):
            begin = block * per_block + part * rows
            piece = jnp.where(lane // wide == part, turned[begin : begin + rows, :], piece)
        for copy in range(copies):
            out_ref[block, copy, :, :] = piece


def place_kernel(parts_ref, out_ref):
    groups, offset_count, rows, lanes = parts_ref.shape
    half = out_ref.shape[2] // 2
    lag_rows = half // groups
    parts = out_ref.shape[0] // rows
    lane = lax.broadcasted_iota(jnp.int32, (1, lanes), 1)
    for number in range(offset_count):
        for part in range(parts):
            ahead = jnp.zeros((rows, lanes), jnp.float32)
            back = jnp.zeros((rows, lanes), jnp.float32)
            begin = part * 2 * lag_rows
            for group in range(groups):
                piece = parts_ref[group, number]
                first, last = group * lag_rows, half - (group + 1) * lag_rows
                ahead = jnp.where(lane // lag_rows == group, pltpu.roll(piece, (first - begin) % lanes, 1), ahead)
                back = jnp.where(
                    lane // lag_rows == groups - 1 - group, pltpu.roll(piece, (last - begin - lag_rows) % lanes, 1), back
                )
            out_ref[part * rows : (part + 1) * rows, number, 0:half] = back
            out_ref[part * rows : (part + 1) * rows, number, half : 2 * half] = ahead


def window_shards(spectra, quality, offsets):
    chan_count = lax.axis_size("chan")
    tm_count = lax.axis_size("tm")
    _, windows, band, chans = spectra.shape
    freqs = band * chan_count
    half = LAGS // 2
    lag_rows = half // chan_count
    offset_count = offsets.shape[0]
    piece_rows = 2 * lag_rows // chan_count
    smem = pl.BlockSpec(memory_space=pltpu.SMEM)
    vmem = pl.BlockSpec(memory_space=pltpu.VMEM)
    params = pltpu.CompilerParams(vmem_limit_bytes=VMEM_LIMIT)
    table = jnp.asarray(half_table(freqs, LAGS).reshape(2, chan_count, lag_rows, freqs))
    chan_index = lax.axis_index("chan").astype(jnp.int32)
    tm_index = lax.axis_index("tm").astype(jnp.int32)
    chan_where, tm_where = chan_index.reshape(1), tm_index.reshape(1)

    chan_order, tm_order = partners(chan_count), partners(tm_count)
    kept = pl.BlockSpec(memory_space=pltpu.HBM)
    spectra = pltpu.with_memory_space_constraint(spectra, pltpu.HBM)
    pieces = []
    for part in (chan_order[:2], chan_order[2:]):
        pieces += pl.pallas_call(
            functools.partial(split_kernel, part),
            out_shape=[jax.ShapeDtypeStruct((2, band, chans), spectra.dtype)] * len(part),
            in_specs=[smem, kept],
            out_specs=[pl.BlockSpec(memory_space=pl.ANY)] * len(part),
            scratch_shapes=[pltpu.SemaphoreType.DMA((len(part),))],
            compiler_params=params,
            name="split_windows",
        )(chan_where, spectra)
    chip_order = chips(chan_count)
    pair_shape = (6 * offset_count - 2, lag_rows, chans)
    own, far = pl.pallas_call(
        functools.partial(window_kernel, chan_order),
        out_shape=[jax.ShapeDtypeStruct((len(chip_order), *pair_shape), jnp.int16)] * 2,
        in_specs=[kept, smem] + [vmem] * (chan_count + 2),
        out_specs=[vmem] * 2,
        scratch_shapes=[
            pltpu.VMEM((freqs, chans), jnp.float32),
            pltpu.VMEM((2, freqs, chans), jnp.bfloat16),
            pltpu.VMEM((offset_count, freqs, 2 * chans), jnp.bfloat16),
            pltpu.SMEM(offsets.shape, jnp.int32),
            pltpu.SemaphoreType.DMA(()),
        ],
        compiler_params=params,
        name="window_pairs",
    )(pltpu.with_memory_space_constraint(offsets, pltpu.HBM), chan_where, *exchange(pieces, "chan", chan_order), quality, table)
    pairs = pl.pallas_call(
        functools.partial(merge_kernel, offset_count),
        out_shape=[jax.ShapeDtypeStruct(pair_shape, jnp.int16)] * len(chip_order),
        in_specs=[vmem] * 2,
        out_specs=[vmem] * len(chip_order),
        compiler_params=params,
        name="merge_windows",
    )(own, *exchange([far], "chan", [1]))
    sums = pl.pallas_call(
        functools.partial(sum_kernel, tm_order, 1.0 / (CODE_TOP * math.sqrt(freqs))),
        out_shape=[jax.ShapeDtypeStruct((7, lag_rows, chans), jnp.int16)] * tm_count,
        in_specs=[smem] + [vmem] * len(chip_order),
        out_specs=[vmem] * tm_count,
        scratch_shapes=[pltpu.VMEM((offset_count, 7, lag_rows, chans), jnp.int16)],
        compiler_params=params,
        name="sum_windows",
    )(tm_where, *exchange(pairs, "chan", chip_order))
    pieces = pl.pallas_call(
        functools.partial(stack_kernel, windows * tm_count),
        out_shape=jax.ShapeDtypeStruct((chan_count, tm_count, piece_rows, chans), jnp.float32),
        in_specs=[vmem] * tm_count,
        out_specs=vmem,
        compiler_params=params,
        name="stack_pairs",
    )(*exchange(sums, "tm", tm_order))
    shape = (chan_count * tm_count, piece_rows, chans)
    arrived = lax.all_to_all(pieces.reshape(shape), ("chan", "tm"), 0, 0, tiled=True)
    return pl.pallas_call(
        place_kernel,
        out_shape=jax.ShapeDtypeStruct((CH_DEV, offset_count, LAGS), jnp.float32),
        in_specs=[vmem],
        out_specs=vmem,
        compiler_params=params,
        name="place_lags",
    )(arrived.reshape(chan_count, tm_count, piece_rows, chans))


def shifted(value, axis, steps):
    count = lax.axis_size(axis)
    leading, last = (max(0, -steps), min(count, count - steps))
    return lax.ppermute(value, axis, [(source, source + steps) for source in range(leading, last)])


def lag_table(freq_count, lag_count):
    freq_index = jnp.arange(freq_count, dtype=jnp.int32)[:, None]
    double_lag = (2 * jnp.arange(lag_count, dtype=jnp.int32) - lag_count + 1)[None, :]
    turns = jnp.mod(freq_index * double_lag, 4 * freq_count)
    angles = turns.astype(jnp.float32) * (2.0 * math.pi / (4 * freq_count))
    cosine = jnp.cos(angles)
    sine = jnp.sin(angles)
    upper = jnp.concatenate([cosine, sine], axis=1)
    lower = jnp.concatenate([-sine, cosine], axis=1)
    return jnp.stack([upper, lower]).astype(jnp.bfloat16)


def whiten_parts(real_part, imag_part, magnitude, channel_level, usable):
    factor = usable.astype(jnp.float32)[:, None, :] / (magnitude + 0.5 * (channel_level + 1e-05))
    return jnp.stack([real_part * factor, imag_part * factor]).astype(jnp.bfloat16)


def cross_parts(own_real, own_imag, far_real, far_imag):
    own_real = own_real.astype(jnp.float32)
    own_imag = own_imag.astype(jnp.float32)
    far_real = far_real.astype(jnp.float32)
    far_imag = far_imag.astype(jnp.float32)
    return jnp.stack(
        [own_real * far_real + own_imag * far_imag, own_imag * far_real - own_real * far_imag]
    ).astype(jnp.bfloat16)


def pair_terms(corr_all):
    lag_count = corr_all.shape[-1] // 2
    real_corr = corr_all[..., :lag_count]
    imag_corr = corr_all[..., lag_count:]
    power = real_corr * real_corr + imag_corr * imag_corr
    mean_power = jnp.mean(power, axis=-1, keepdims=True)
    denominator = jnp.sqrt(power + 0.25 * (mean_power + 1e-06))
    return (
        jnp.sum(real_corr, axis=-3),
        jnp.sum(real_corr / denominator, axis=-3),
        jnp.sum(imag_corr / denominator, axis=-3),
    )


def shards(spectra, quality, offsets):
    chan_count = lax.axis_size("chan")
    tm_count = lax.axis_size("tm")
    levels = chan_count.bit_length() - 1
    table_bf = lag_table(F, LAGS)
    inv_root = 1.0 / math.sqrt(F)
    real_part = spectra[0].astype(jnp.float32)
    imag_part = spectra[1].astype(jnp.float32)
    magnitude = jnp.sqrt(real_part * real_part + imag_part * imag_part)
    band_total = lax.psum(jnp.sum(magnitude, axis=1), "chan")
    channel_level = (band_total / F)[:, None, :]
    whitened = whiten_parts(real_part, imag_part, magnitude, channel_level, quality)
    width_all = whitened.shape[3]
    padded = jnp.pad(whitened, ((0, 0), (0, 0), (0, 0), (0, width_all)))
    crossed_list = []
    for offset_index in range(NOFF):
        partner = lax.dynamic_slice_in_dim(padded, offsets[offset_index] * CH_DEV, width_all, 3)
        crossed_list.append(cross_parts(whitened[0], whitened[1], partner[0], partner[1]))
    crossed = jnp.stack(crossed_list, axis=1)
    corr_all = jnp.einsum(
        "cnwfh,cfl->nwhl",
        lax.all_to_all(crossed, "chan", split_axis=4, concat_axis=3, tiled=True),
        table_bf,
        preferred_element_type=jnp.float32,
    )
    linear_sum, real_sum, imag_sum = pair_terms(corr_all * inv_root)
    totals = lax.psum((linear_sum, real_sum, imag_sum), "tm")
    window_count = W_DEV * tm_count
    linear = totals[0] / window_count
    real_phase = totals[1] / window_count
    imag_phase = totals[2] / window_count
    stacks = jnp.transpose(linear * (real_phase * real_phase + imag_phase * imag_phase), (1, 0, 2))
    reverse_part = stacks
    for bit_index in range(levels):
        step_size = 1 << bit_index
        arrived = shifted(reverse_part, "chan", step_size)
        chosen = offsets // step_size % 2 == 1
        reverse_part = jnp.where(chosen[None, :, None], arrived, reverse_part)
    return stacks + jnp.flip(reverse_part, axis=2)


def solution(mesh):
    chan_count, tm_count = mesh.shape["chan"], mesh.shape["tm"]
    by_window = chan_count == W_DEV and tm_count == NOFF
    return jax.shard_map(
        window_shards if by_window else shards,
        mesh=mesh,
        in_specs=(P(None, "tm", "chan", None), P("tm", None), P()),
        out_specs=P("chan", None, None),
        check_vma=False,
    )
```

```python
import functools
import math

import jax
import jax.numpy as jnp
import numpy as np
from jax import lax
from jax.experimental import pallas as pl
from jax.experimental.pallas import tpu as pltpu
from jax.sharding import PartitionSpec as P

F = 2048
LAGS = 256
NOFF = 4
CH_DEV = 16
W_DEV = 8
VMEM_LIMIT = 48 * 1024 * 1024
CODE_TOP = 32767.0
OCTAVE = 256.0
LOWEST = -110.0


def encode(value):
    return jnp.round(value).astype(jnp.int32).astype(jnp.int16)


def decode(code):
    return code.astype(jnp.int32).astype(jnp.float32)


def level_code(peak):
    return jnp.ceil(jnp.maximum(jnp.log2(jnp.maximum(peak, 1e-30)), LOWEST) * OCTAVE) + 1.0


def level_of(code):
    return jnp.exp2(code * (1.0 / OCTAVE))


def half_table(freq_count, lag_count):
    freq_index = np.arange(freq_count, dtype=np.int64)[None, :]
    double_lag = (2 * np.arange(lag_count // 2, lag_count, dtype=np.int64) - lag_count + 1)[:, None]
    turns = np.mod(freq_index * double_lag, 4 * freq_count).astype(np.float32)
    angles = turns * np.float32(2.0 * math.pi / (4 * freq_count))
    return np.concatenate([np.cos(angles), np.sin(angles)]).astype(jnp.bfloat16)


def widest(offs_ref, reach):
    last = offs_ref.shape[0] - 1
    found = last
    for number in reversed(range(last)):
        found = jnp.where(offs_ref[number] == reach, number, found)
    return found


def offset_of(slot, offs_ref, reach):
    last, wide = offs_ref.shape[0] - 1, widest(offs_ref, reach)
    return offs_ref[jnp.where(slot == wide, last, jnp.where(slot == last, wide, slot))]


def window_kernel(order, offs_hbm_ref, where_ref, *refs):
    chan_count = len(order)
    spec_refs, (qual_ref, table_ref) = refs[:chan_count], refs[chan_count : chan_count + 2]
    out_refs = refs[chan_count + 2 : chan_count + 4]
    mag_ref, white_ref, cross_ref, offs_ref, offs_sem = refs[chan_count + 4 :]
    fetch = pltpu.make_async_copy(offs_hbm_ref, offs_ref, offs_sem)
    fetch.start()
    me = where_ref[0]
    _, band, chans = spec_refs[0].shape
    freqs = chan_count * band
    chip_count, blocks, lag_rows, _ = out_refs[0].shape
    offset_count = offs_ref.shape[0]
    half = chan_count * lag_rows
    step = 64

    total = jnp.zeros((8, chans), jnp.float32)
    for number, spec_ref in enumerate(spec_refs):
        for row in range(0, band, step):
            real, imag = (spec_ref[part, row : row + step, :].astype(jnp.float32) for part in range(2))
            square = real * real + imag * imag
            magnitude = square * lax.rsqrt(jnp.maximum(square, 1e-30))
            held = slice(number * band + row, number * band + row + step)
            mag_ref[held, :] = magnitude
            total += jnp.sum(magnitude.reshape(step // 8, 8, chans), axis=0)
    level = jnp.sum(total, axis=0, keepdims=True) * (1.0 / freqs)
    floor = 0.5 * (level + 1e-05)

    for number, spec_ref in enumerate(spec_refs):
        for row in range(0, band, step):
            held = slice(number * band + row, number * band + row + step)
            factor = pl.reciprocal(mag_ref[held, :] + floor, approx=True)
            for part in range(2):
                value = spec_ref[part, row : row + step, :].astype(jnp.float32) * factor
                white_ref[part, held, :] = value.astype(jnp.bfloat16)

    lane = lax.broadcasted_iota(jnp.int32, (1, chans), 1)
    line = lax.broadcasted_iota(jnp.int32, (lag_rows, chans), 0)
    usable = qual_ref[pl.ds(me, 1), :].astype(jnp.float32)
    levels = jnp.zeros((lag_rows, chans), jnp.float32)
    groups = [k ^ core for core in range(2) for k in chips(chan_count)]
    fetch.wait()
    bands = [pl.ds(pl.multiple_of((me ^ k) * band, band), band) for k in order]
    table = jnp.concatenate(
        [
            jnp.concatenate([table_ref[side, me ^ group, :, taken] for taken in bands], axis=1)
            for side in range(2)
            for group in groups
        ],
        axis=0,
    )
    turns = [chans - offset_of(number, offs_ref, chan_count // 2) * (chans // chan_count) for number in range(offset_count)]
    for row in range(0, freqs, step):
        own = [white_ref[part, row : row + step, :] for part in range(2)]
        own_real, own_imag = (value.astype(jnp.float32) for value in own)
        for number, turn in enumerate(turns):
            far_real, far_imag = (pltpu.roll(value, turn, 1).astype(jnp.float32) for value in own)
            real = own_real * far_real + own_imag * far_imag
            imag = own_imag * far_real - own_real * far_imag
            cross_ref[number, row : row + step, 0:chans] = real.astype(jnp.bfloat16)
            cross_ref[number, row : row + step, chans : 2 * chans] = imag.astype(jnp.bfloat16)

    for number, turn in enumerate(turns):
        sums = jnp.dot(table, cross_ref[number], preferred_element_type=jnp.float32)
        cos_real, sin_real = sums[:half, :chans], sums[half:, :chans]
        cos_imag, sin_imag = sums[:half, chans:], sums[half:, chans:]
        corr = (
            (cos_real - sin_imag, sin_real + cos_imag),
            (cos_real + sin_imag, cos_imag - sin_real),
        )
        power = [real * real + imag * imag for real, imag in corr]
        mean_power = jnp.sum(power[0] + power[1], axis=0, keepdims=True) * (1.0 / (2 * half))
        extra = 0.25 * (mean_power + 1e-06 * freqs)
        peak = jnp.max(jnp.maximum(jnp.abs(corr[0][0]), jnp.abs(corr[1][0])), axis=0, keepdims=True)
        code = level_code(peak)
        keep = jnp.where(lane < turn, usable * pltpu.roll(usable, turn, 1), 0.0) * CODE_TOP
        upscale = keep / level_of(code)
        inverse = [lax.rsqrt(side + extra) * keep for side in power]
        kinds = [
            [real * upscale for real, _ in corr],
            [real * scale for (real, _), scale in zip(corr, inverse)],
            [imag * scale for (_, imag), scale in zip(corr, inverse)],
        ]
        if number == offset_count - 1:
            code = jnp.where(lane < chans // 2, code, pltpu.roll(code, chans // 2, 1))
            kinds = [[jnp.where(lane < chans // 2, ahead, pltpu.roll(back, chans // 2, 1))] for ahead, back in kinds]
        levels = jnp.where(line == number, code, levels)
        for place, value in enumerate(value for kind in kinds for value in kind):
            coded = encode(value).reshape(chan_count, lag_rows, chans)
            for core in range(2):
                rows = slice(core * chip_count, (core + 1) * chip_count)
                out_refs[core][:, 6 * number + place, :, :] = coded[rows]
    for number in range(offset_count):
        levels = jnp.where(line == offset_count + number, offs_ref[number].astype(jnp.float32), levels)
    wide = widest(offs_ref, chan_count // 2).astype(jnp.float32)
    levels = jnp.where(line == 2 * offset_count, wide, levels)
    for out_ref in out_refs:
        for chip in range(chip_count):
            out_ref[chip, blocks - 1, :, :] = encode(levels)


def merge_kernel(slots, own_ref, far_ref, *out_refs):
    blocks = own_ref.shape[1]
    for chip, out_ref in enumerate(out_refs):
        codes = [decode(ref[chip, blocks - 1]) for ref in (own_ref, far_ref)]
        levels = [level_of(code) for code in codes]
        code = level_code(levels[0] + levels[1])
        shares = [level / level_of(code) for level in levels]
        line = lax.broadcasted_iota(jnp.int32, code.shape, 0)
        out_ref[blocks - 1, :, :] = encode(jnp.where(line < slots, code, codes[0]))
        for block in range(blocks - 1):
            number, part = divmod(block, 6)
            linear = part < (2 if blocks - 1 - 6 * number > 3 else 1)
            own, far = decode(own_ref[chip, block]), decode(far_ref[chip, block])
            if linear:
                total = own * shares[0][number : number + 1, :] + far * shares[1][number : number + 1, :]
            else:
                total = (own + far) * 0.5
            out_ref[block, :, :] = encode(total)


def sum_kernel(order, scale, where_ref, *refs):
    code_refs, out_refs, held_ref = refs[: -len(order) - 1], refs[-len(order) - 1 : -1], refs[-1]
    blocks, _, chans = code_refs[0].shape
    slots = held_ref.shape[0]
    heads = [decode(codes_ref[blocks - 1]) for codes_ref in code_refs]
    levels = [level_of(head) * scale for head in heads]
    offsets = [heads[0][slots + number : slots + number + 1, :] for number in range(slots)]
    wide = heads[0][2 * slots : 2 * slots + 1, :]
    low = lax.broadcasted_iota(jnp.int32, (1, chans), 1) < chans // 2
    all_sums = []
    for number in range(slots):
        sides = 2 if number < slots - 1 else 1
        own = [level[number : number + 1, :] for level in levels]
        sums = []
        for place in range(3 * sides):
            codes = [decode(codes_ref[6 * number + place]) for codes_ref in code_refs]
            if place < sides:
                sums.append(sum(code * level for code, level in zip(codes, own)))
            else:
                sums.append(sum(codes) * (1.0 / len(code_refs)))
        if sides == 1:
            sums = [
                jnp.where(low, side, 0.0) for value in sums for side in (value, pltpu.roll(value, chans // 2, 1))
            ]
        all_sums.append(sums)
    line = lax.broadcasted_iota(jnp.int32, levels[0].shape, 0)
    last = slots - 1
    for number in range(slots):
        sums = all_sums[number]
        for other in range(last) if number == last else [last]:
            swap = wide == min(number, other)
            sums = [jnp.where(swap, value, kept) for value, kept in zip(all_sums[other], sums)]
        peak = jnp.max(jnp.maximum(jnp.abs(sums[0]), jnp.abs(sums[1])), axis=0, keepdims=True)
        code = level_code(peak)
        upscale = CODE_TOP / level_of(code)
        head = jnp.where(line == 0, code, offsets[number])
        for part, value in enumerate([sums[0] * upscale, sums[1] * upscale, *sums[2:], head]):
            held_ref[number, part, :, :] = encode(value)
    for k, out_ref in zip(order, out_refs):
        out_ref[...] = held_ref[where_ref[0] ^ k]


def partners(count):
    return sorted(range(1, count), key=lambda k: (-(k >> 1).bit_count(), k & 1, k)) + [0]


def chips(count):
    return sorted(range(2, count, 2), key=lambda k: (k.bit_count(), k)) + [0]


def exchange(pieces, axis, order):
    count = lax.axis_size(axis)
    return [
        lax.ppermute(piece, axis, [(source, source ^ k) for source in range(count)]) if k else piece
        for k, piece in zip(order, pieces)
    ]


def split_kernel(order, spec_ref, *refs):
    out_refs, sems = refs[:-1], refs[-1]
    me = lax.axis_index("chan").astype(jnp.int32)
    copies = [
        pltpu.make_async_copy(spec_ref.at[:, me ^ k], out_ref, sems.at[number])
        for number, (k, out_ref) in enumerate(zip(order, out_refs))
    ]
    for copy in copies:
        copy.start()
    for copy in copies:
        copy.wait()


def stack_kernel(windows, *refs):
    sums_refs, out_ref = refs[:-1], refs[-1]
    blocks, copies, rows, _ = out_ref.shape
    _, lag_rows, chans = sums_refs[0].shape
    per_sum = windows // len(sums_refs)
    heads = [decode(sums_ref[6]) for sums_ref in sums_refs]
    levels = [level_of(head[0:1, :]) * (1.0 / (CODE_TOP * windows)) for head in heads]
    stacks = []
    for side in range(2):
        linear = sum(decode(sums_ref[side]) * level for sums_ref, level in zip(sums_refs, levels))
        real, imag = (
            sum(decode(sums_ref[part + side]) for sums_ref in sums_refs) * (per_sum / (CODE_TOP * windows))
            for part in (2, 4)
        )
        stacks.append(linear * (real * real + imag * imag))
    offset = heads[0][1:2, :]
    lane = lax.broadcasted_iota(jnp.int32, (1, chans), 1)
    behind = [jnp.zeros_like(stack) for stack in stacks]
    for steps in range(1, blocks // 2 + 1):
        ahead = steps * (chans // blocks)
        chosen = (offset == steps) & (lane >= ahead)
        behind = [jnp.where(chosen, pltpu.roll(stack, ahead, 1), kept) for stack, kept in zip(stacks, behind)]
    back = stacks[1] + behind[0]
    both = jnp.concatenate(
        [stacks[0] + behind[1]] + [back[row : row + 1, :] for row in reversed(range(lag_rows))], axis=0
    )
    wide = 2 * lag_rows
    parts = chans // wide
    turned = jnp.concatenate([both] * parts, axis=0).T
    per_block = chans // blocks
    for block in range(blocks):
        piece = jnp.zeros((rows, chans), jnp.float32)
        for part in range(parts):
            begin = block * per_block + part * rows
            piece = jnp.where(lane // wide == part, turned[begin : begin + rows, :], piece)
        for copy in range(copies):
            out_ref[block, copy, :, :] = piece


def place_kernel(parts_ref, out_ref):
    groups, offset_count, rows, lanes = parts_ref.shape
    half = out_ref.shape[2] // 2
    lag_rows = half // groups
    parts = out_ref.shape[0] // rows
    lane = lax.broadcasted_iota(jnp.int32, (1, lanes), 1)
    for number in range(offset_count):
        for part in range(parts):
            ahead = jnp.zeros((rows, lanes), jnp.float32)
            back = jnp.zeros((rows, lanes), jnp.float32)
            begin = part * 2 * lag_rows
            for group in range(groups):
                piece = parts_ref[group, number]
                first, last = group * lag_rows, half - (group + 1) * lag_rows
                ahead = jnp.where(lane // lag_rows == group, pltpu.roll(piece, (first - begin) % lanes, 1), ahead)
                back = jnp.where(
                    lane // lag_rows == groups - 1 - group, pltpu.roll(piece, (last - begin - lag_rows) % lanes, 1), back
                )
            out_ref[part * rows : (part + 1) * rows, number, 0:half] = back
            out_ref[part * rows : (part + 1) * rows, number, half : 2 * half] = ahead


def window_shards(spectra, quality, offsets):
    chan_count = lax.axis_size("chan")
    tm_count = lax.axis_size("tm")
    _, windows, band, chans = spectra.shape
    freqs = band * chan_count
    half = LAGS // 2
    lag_rows = half // chan_count
    offset_count = offsets.shape[0]
    piece_rows = 2 * lag_rows // chan_count
    smem = pl.BlockSpec(memory_space=pltpu.SMEM)
    vmem = pl.BlockSpec(memory_space=pltpu.VMEM)
    params = pltpu.CompilerParams(vmem_limit_bytes=VMEM_LIMIT)
    table = jnp.asarray(half_table(freqs, LAGS).reshape(2, chan_count, lag_rows, freqs))
    chan_index = lax.axis_index("chan").astype(jnp.int32)
    tm_index = lax.axis_index("tm").astype(jnp.int32)
    chan_where, tm_where = chan_index.reshape(1), tm_index.reshape(1)

    chan_order, tm_order = partners(chan_count), partners(tm_count)
    kept = pl.BlockSpec(memory_space=pltpu.HBM)
    spectra = pltpu.with_memory_space_constraint(spectra, pltpu.HBM)
    pieces = []
    for part in (chan_order[:2], chan_order[2:]):
        pieces += pl.pallas_call(
            functools.partial(split_kernel, part),
            out_shape=[jax.ShapeDtypeStruct((2, band, chans), spectra.dtype)] * len(part),
            in_specs=[kept],
            out_specs=[pl.BlockSpec(memory_space=pl.ANY)] * len(part),
            scratch_shapes=[pltpu.SemaphoreType.DMA((len(part),))],
            compiler_params=params,
            name="split_windows",
        )(spectra)
    chip_order = chips(chan_count)
    pair_shape = (6 * offset_count - 2, lag_rows, chans)
    own, far = pl.pallas_call(
        functools.partial(window_kernel, chan_order),
        out_shape=[jax.ShapeDtypeStruct((len(chip_order), *pair_shape), jnp.int16)] * 2,
        in_specs=[kept, smem] + [vmem] * (chan_count + 2),
        out_specs=[vmem] * 2,
        scratch_shapes=[
            pltpu.VMEM((freqs, chans), jnp.float32),
            pltpu.VMEM((2, freqs, chans), jnp.bfloat16),
            pltpu.VMEM((offset_count, freqs, 2 * chans), jnp.bfloat16),
            pltpu.SMEM(offsets.shape, jnp.int32),
            pltpu.SemaphoreType.DMA(()),
        ],
        compiler_params=params,
        name="window_pairs",
    )(pltpu.with_memory_space_constraint(offsets, pltpu.HBM), chan_where, *exchange(pieces, "chan", chan_order), quality, table)
    pairs = pl.pallas_call(
        functools.partial(merge_kernel, offset_count),
        out_shape=[jax.ShapeDtypeStruct(pair_shape, jnp.int16)] * len(chip_order),
        in_specs=[vmem] * 2,
        out_specs=[vmem] * len(chip_order),
        compiler_params=params,
        name="merge_windows",
    )(own, *exchange([far], "chan", [1]))
    sums = pl.pallas_call(
        functools.partial(sum_kernel, tm_order, 1.0 / (CODE_TOP * math.sqrt(freqs))),
        out_shape=[jax.ShapeDtypeStruct((7, lag_rows, chans), jnp.int16)] * tm_count,
        in_specs=[smem] + [vmem] * len(chip_order),
        out_specs=[vmem] * tm_count,
        scratch_shapes=[pltpu.VMEM((offset_count, 7, lag_rows, chans), jnp.int16)],
        compiler_params=params,
        name="sum_windows",
    )(tm_where, *exchange(pairs, "chan", chip_order))
    pieces = pl.pallas_call(
        functools.partial(stack_kernel, windows * tm_count),
        out_shape=jax.ShapeDtypeStruct((chan_count, tm_count, piece_rows, chans), jnp.float32),
        in_specs=[vmem] * tm_count,
        out_specs=vmem,
        compiler_params=params,
        name="stack_pairs",
    )(*exchange(sums, "tm", tm_order))
    shape = (chan_count * tm_count, piece_rows, chans)
    arrived = lax.all_to_all(pieces.reshape(shape), ("chan", "tm"), 0, 0, tiled=True)
    return pl.pallas_call(
        place_kernel,
        out_shape=jax.ShapeDtypeStruct((CH_DEV, offset_count, LAGS), jnp.float32),
        in_specs=[vmem],
        out_specs=vmem,
        compiler_params=params,
        name="place_lags",
    )(arrived.reshape(chan_count, tm_count, piece_rows, chans))


def shifted(value, axis, steps):
    count = lax.axis_size(axis)
    leading, last = (max(0, -steps), min(count, count - steps))
    return lax.ppermute(value, axis, [(source, source + steps) for source in range(leading, last)])


def lag_table(freq_count, lag_count):
    freq_index = jnp.arange(freq_count, dtype=jnp.int32)[:, None]
    double_lag = (2 * jnp.arange(lag_count, dtype=jnp.int32) - lag_count + 1)[None, :]
    turns = jnp.mod(freq_index * double_lag, 4 * freq_count)
    angles = turns.astype(jnp.float32) * (2.0 * math.pi / (4 * freq_count))
    cosine = jnp.cos(angles)
    sine = jnp.sin(angles)
    upper = jnp.concatenate([cosine, sine], axis=1)
    lower = jnp.concatenate([-sine, cosine], axis=1)
    return jnp.stack([upper, lower]).astype(jnp.bfloat16)


def whiten_parts(real_part, imag_part, magnitude, channel_level, usable):
    factor = usable.astype(jnp.float32)[:, None, :] / (magnitude + 0.5 * (channel_level + 1e-05))
    return jnp.stack([real_part * factor, imag_part * factor]).astype(jnp.bfloat16)


def cross_parts(own_real, own_imag, far_real, far_imag):
    own_real = own_real.astype(jnp.float32)
    own_imag = own_imag.astype(jnp.float32)
    far_real = far_real.astype(jnp.float32)
    far_imag = far_imag.astype(jnp.float32)
    return jnp.stack(
        [own_real * far_real + own_imag * far_imag, own_imag * far_real - own_real * far_imag]
    ).astype(jnp.bfloat16)


def pair_terms(corr_all):
    lag_count = corr_all.shape[-1] // 2
    real_corr = corr_all[..., :lag_count]
    imag_corr = corr_all[..., lag_count:]
    power = real_corr * real_corr + imag_corr * imag_corr
    mean_power = jnp.mean(power, axis=-1, keepdims=True)
    denominator = jnp.sqrt(power + 0.25 * (mean_power + 1e-06))
    return (
        jnp.sum(real_corr, axis=-3),
        jnp.sum(real_corr / denominator, axis=-3),
        jnp.sum(imag_corr / denominator, axis=-3),
    )


def shards(spectra, quality, offsets):
    chan_count = lax.axis_size("chan")
    tm_count = lax.axis_size("tm")
    levels = chan_count.bit_length() - 1
    table_bf = lag_table(F, LAGS)
    inv_root = 1.0 / math.sqrt(F)
    real_part = spectra[0].astype(jnp.float32)
    imag_part = spectra[1].astype(jnp.float32)
    magnitude = jnp.sqrt(real_part * real_part + imag_part * imag_part)
    band_total = lax.psum(jnp.sum(magnitude, axis=1), "chan")
    channel_level = (band_total / F)[:, None, :]
    whitened = whiten_parts(real_part, imag_part, magnitude, channel_level, quality)
    width_all = whitened.shape[3]
    padded = jnp.pad(whitened, ((0, 0), (0, 0), (0, 0), (0, width_all)))
    crossed_list = []
    for offset_index in range(NOFF):
        partner = lax.dynamic_slice_in_dim(padded, offsets[offset_index] * CH_DEV, width_all, 3)
        crossed_list.append(cross_parts(whitened[0], whitened[1], partner[0], partner[1]))
    crossed = jnp.stack(crossed_list, axis=1)
    corr_all = jnp.einsum(
        "cnwfh,cfl->nwhl",
        lax.all_to_all(crossed, "chan", split_axis=4, concat_axis=3, tiled=True),
        table_bf,
        preferred_element_type=jnp.float32,
    )
    linear_sum, real_sum, imag_sum = pair_terms(corr_all * inv_root)
    totals = lax.psum((linear_sum, real_sum, imag_sum), "tm")
    window_count = W_DEV * tm_count
    linear = totals[0] / window_count
    real_phase = totals[1] / window_count
    imag_phase = totals[2] / window_count
    stacks = jnp.transpose(linear * (real_phase * real_phase + imag_phase * imag_phase), (1, 0, 2))
    reverse_part = stacks
    for bit_index in range(levels):
        step_size = 1 << bit_index
        arrived = shifted(reverse_part, "chan", step_size)
        chosen = offsets // step_size % 2 == 1
        reverse_part = jnp.where(chosen[None, :, None], arrived, reverse_part)
    return stacks + jnp.flip(reverse_part, axis=2)


def solution(mesh):
    chan_count, tm_count = mesh.shape["chan"], mesh.shape["tm"]
    by_window = chan_count == W_DEV and tm_count == NOFF
    return jax.shard_map(
        window_shards if by_window else shards,
        mesh=mesh,
        in_specs=(P(None, "tm", "chan", None), P("tm", None), P()),
        out_specs=P("chan", None, None),
        check_vma=False,
    )
```

```python
import functools
import math

import jax
import jax.numpy as jnp
import numpy as np
from jax import lax
from jax.experimental import pallas as pl
from jax.experimental.pallas import tpu as pltpu
from jax.sharding import PartitionSpec as P

F = 2048
LAGS = 256
NOFF = 4
CH_DEV = 16
W_DEV = 8
VMEM_LIMIT = 48 * 1024 * 1024
CODE_TOP = 32767.0
OCTAVE = 256.0
LOWEST = -110.0


def encode(value):
    return jnp.round(value).astype(jnp.int32).astype(jnp.int16)


def decode(code):
    return code.astype(jnp.int32).astype(jnp.float32)


def level_code(peak):
    return jnp.ceil(jnp.maximum(jnp.log2(jnp.maximum(peak, 1e-30)), LOWEST) * OCTAVE) + 1.0


def level_of(code):
    return jnp.exp2(code * (1.0 / OCTAVE))


def half_table(freq_count, lag_count):
    freq_index = np.arange(freq_count, dtype=np.int64)[None, :]
    double_lag = (2 * np.arange(lag_count // 2, lag_count, dtype=np.int64) - lag_count + 1)[:, None]
    turns = np.mod(freq_index * double_lag, 4 * freq_count).astype(np.float32)
    angles = turns * np.float32(2.0 * math.pi / (4 * freq_count))
    return np.concatenate([np.cos(angles), np.sin(angles)]).astype(jnp.bfloat16)


def widest(offs_ref, reach):
    last = offs_ref.shape[0] - 1
    found = last
    for number in reversed(range(last)):
        found = jnp.where(offs_ref[number] == reach, number, found)
    return found


def offset_of(slot, offs_ref, reach):
    last, wide = offs_ref.shape[0] - 1, widest(offs_ref, reach)
    return offs_ref[jnp.where(slot == wide, last, jnp.where(slot == last, wide, slot))]


def window_kernel(order, offs_hbm_ref, where_ref, *refs):
    chan_count = len(order)
    spec_refs, (qual_ref, table_ref) = refs[:chan_count], refs[chan_count : chan_count + 2]
    out_refs = refs[chan_count + 2 : chan_count + 4]
    mag_ref, white_ref, cross_ref, offs_ref, offs_sem = refs[chan_count + 4 :]
    fetch = pltpu.make_async_copy(offs_hbm_ref, offs_ref, offs_sem)
    fetch.start()
    me = where_ref[0]
    _, band, chans = spec_refs[0].shape
    freqs = chan_count * band
    chip_count, blocks, lag_rows, _ = out_refs[0].shape
    offset_count = offs_ref.shape[0]
    half = chan_count * lag_rows
    step = 64

    total = jnp.zeros((8, chans), jnp.float32)
    for number, spec_ref in enumerate(spec_refs):
        for row in range(0, band, step):
            real, imag = (spec_ref[part, row : row + step, :].astype(jnp.float32) for part in range(2))
            square = real * real + imag * imag
            magnitude = square * lax.rsqrt(jnp.maximum(square, 1e-30))
            held = slice(number * band + row, number * band + row + step)
            mag_ref[held, :] = magnitude
            total += jnp.sum(magnitude.reshape(step // 8, 8, chans), axis=0)
    level = jnp.sum(total, axis=0, keepdims=True) * (1.0 / freqs)
    floor = 0.5 * (level + 1e-05)

    for number, spec_ref in enumerate(spec_refs):
        for row in range(0, band, step):
            held = slice(number * band + row, number * band + row + step)
            factor = pl.reciprocal(mag_ref[held, :] + floor, approx=True)
            for part in range(2):
                value = spec_ref[part, row : row + step, :].astype(jnp.float32) * factor
                white_ref[part, held, :] = value.astype(jnp.bfloat16)

    lane = lax.broadcasted_iota(jnp.int32, (1, chans), 1)
    line = lax.broadcasted_iota(jnp.int32, (lag_rows, chans), 0)
    usable = qual_ref[pl.ds(me, 1), :].astype(jnp.float32)
    levels = jnp.zeros((lag_rows, chans), jnp.float32)
    groups = [k ^ core for core in range(2) for k in chips(chan_count)]
    fetch.wait()
    bands = [pl.ds(pl.multiple_of((me ^ k) * band, band), band) for k in order]
    table = jnp.concatenate(
        [
            jnp.concatenate([table_ref[side, me ^ group, :, taken] for taken in bands], axis=1)
            for side in range(2)
            for group in groups
        ],
        axis=0,
    )
    turns = [chans - offset_of(number, offs_ref, chan_count // 2) * (chans // chan_count) for number in range(offset_count)]
    for row in range(0, freqs, step):
        own = [white_ref[part, row : row + step, :] for part in range(2)]
        own_real, own_imag = (value.astype(jnp.float32) for value in own)
        for number, turn in enumerate(turns):
            far_real, far_imag = (pltpu.roll(value, turn, 1).astype(jnp.float32) for value in own)
            real = own_real * far_real + own_imag * far_imag
            imag = own_imag * far_real - own_real * far_imag
            cross_ref[number, row : row + step, 0:chans] = real.astype(jnp.bfloat16)
            cross_ref[number, row : row + step, chans : 2 * chans] = imag.astype(jnp.bfloat16)

    for number, turn in enumerate(turns):
        sums = jnp.dot(table, cross_ref[number], preferred_element_type=jnp.float32)
        cos_real, sin_real = sums[:half, :chans], sums[half:, :chans]
        cos_imag, sin_imag = sums[:half, chans:], sums[half:, chans:]
        corr = (
            (cos_real - sin_imag, sin_real + cos_imag),
            (cos_real + sin_imag, cos_imag - sin_real),
        )
        power = [real * real + imag * imag for real, imag in corr]
        mean_power = jnp.sum(power[0] + power[1], axis=0, keepdims=True) * (1.0 / (2 * half))
        extra = 0.25 * (mean_power + 1e-06 * freqs)
        peak = jnp.max(jnp.maximum(jnp.abs(corr[0][0]), jnp.abs(corr[1][0])), axis=0, keepdims=True)
        code = level_code(peak)
        keep = jnp.where(lane < turn, usable * pltpu.roll(usable, turn, 1), 0.0) * CODE_TOP
        upscale = keep / level_of(code)
        inverse = [lax.rsqrt(side + extra) * keep for side in power]
        kinds = [
            [real * upscale for real, _ in corr],
            [real * scale for (real, _), scale in zip(corr, inverse)],
            [imag * scale for (_, imag), scale in zip(corr, inverse)],
        ]
        if number == offset_count - 1:
            code = jnp.where(lane < chans // 2, code, pltpu.roll(code, chans // 2, 1))
            kinds = [[jnp.where(lane < chans // 2, ahead, pltpu.roll(back, chans // 2, 1))] for ahead, back in kinds]
        levels = jnp.where(line == number, code, levels)
        for place, value in enumerate(value for kind in kinds for value in kind):
            coded = encode(value).reshape(chan_count, lag_rows, chans)
            for core in range(2):
                rows = slice(core * chip_count, (core + 1) * chip_count)
                out_refs[core][:, 6 * number + place, :, :] = coded[rows]
    for number in range(offset_count):
        levels = jnp.where(line == offset_count + number, offs_ref[number].astype(jnp.float32), levels)
    wide = widest(offs_ref, chan_count // 2).astype(jnp.float32)
    levels = jnp.where(line == 2 * offset_count, wide, levels)
    for out_ref in out_refs:
        for chip in range(chip_count):
            out_ref[chip, blocks - 1, :, :] = encode(levels)


def merge_kernel(slots, own_ref, far_ref, *out_refs):
    blocks = own_ref.shape[1]
    for chip, out_ref in enumerate(out_refs):
        codes = [decode(ref[chip, blocks - 1]) for ref in (own_ref, far_ref)]
        levels = [level_of(code) for code in codes]
        code = level_code(levels[0] + levels[1])
        shares = [level / level_of(code) for level in levels]
        line = lax.broadcasted_iota(jnp.int32, code.shape, 0)
        out_ref[blocks - 1, :, :] = encode(jnp.where(line < slots, code, codes[0]))
        for block in range(blocks - 1):
            number, part = divmod(block, 6)
            linear = part < (2 if blocks - 1 - 6 * number > 3 else 1)
            own, far = decode(own_ref[chip, block]), decode(far_ref[chip, block])
            if linear:
                total = own * shares[0][number : number + 1, :] + far * shares[1][number : number + 1, :]
            else:
                total = (own + far) * 0.5
            out_ref[block, :, :] = encode(total)


def sum_kernel(order, scale, where_ref, *refs):
    code_refs, out_refs, held_ref = refs[: -len(order) - 1], refs[-len(order) - 1 : -1], refs[-1]
    blocks, _, chans = code_refs[0].shape
    slots = held_ref.shape[0]
    heads = [decode(codes_ref[blocks - 1]) for codes_ref in code_refs]
    levels = [level_of(head) * scale for head in heads]
    offsets = [heads[0][slots + number : slots + number + 1, :] for number in range(slots)]
    wide = heads[0][2 * slots : 2 * slots + 1, :]
    low = lax.broadcasted_iota(jnp.int32, (1, chans), 1) < chans // 2
    all_sums = []
    for number in range(slots):
        sides = 2 if number < slots - 1 else 1
        own = [level[number : number + 1, :] for level in levels]
        sums = []
        for place in range(3 * sides):
            codes = [decode(codes_ref[6 * number + place]) for codes_ref in code_refs]
            if place < sides:
                sums.append(sum(code * level for code, level in zip(codes, own)))
            else:
                sums.append(sum(codes) * (1.0 / len(code_refs)))
        if sides == 1:
            sums = [
                jnp.where(low, side, 0.0) for value in sums for side in (value, pltpu.roll(value, chans // 2, 1))
            ]
        all_sums.append(sums)
    line = lax.broadcasted_iota(jnp.int32, levels[0].shape, 0)
    last = slots - 1
    for number in range(slots):
        sums = all_sums[number]
        for other in range(last) if number == last else [last]:
            swap = wide == min(number, other)
            sums = [jnp.where(swap, value, kept) for value, kept in zip(all_sums[other], sums)]
        peak = jnp.max(jnp.maximum(jnp.abs(sums[0]), jnp.abs(sums[1])), axis=0, keepdims=True)
        code = level_code(peak)
        upscale = CODE_TOP / level_of(code)
        head = jnp.where(line == 0, code, offsets[number])
        for part, value in enumerate([sums[0] * upscale, sums[1] * upscale, *sums[2:], head]):
            held_ref[number, part, :, :] = encode(value)
    for k, out_ref in zip(order, out_refs):
        out_ref[...] = held_ref[where_ref[0] ^ k]


def partners(count):
    return sorted(range(1, count), key=lambda k: (-(k >> 1).bit_count(), k & 1, k)) + [0]


def chips(count):
    return sorted(range(2, count, 2), key=lambda k: (k.bit_count(), k)) + [0]


def exchange(pieces, axis, order):
    count = lax.axis_size(axis)
    return [
        lax.ppermute(piece, axis, [(source, source ^ k) for source in range(count)]) if k else piece
        for k, piece in zip(order, pieces)
    ]


def split_kernel(order, spec_ref, *refs):
    out_refs, sems = refs[:-1], refs[-1]
    me = lax.axis_index("chan").astype(jnp.int32)
    chunks = sems.shape[2]
    rows = spec_ref.shape[2] // chunks
    copies = [
        pltpu.make_async_copy(
            spec_ref.at[part, me ^ k, pl.ds(chunk * rows, rows)],
            out_ref.at[part, pl.ds(chunk * rows, rows)],
            sems.at[number, part, chunk],
        )
        for number, (k, out_ref) in enumerate(zip(order, out_refs))
        for part in range(2)
        for chunk in range(chunks)
    ]
    for copy in copies:
        copy.start()
    for copy in copies:
        copy.wait()


def stack_kernel(windows, *refs):
    sums_refs, out_ref = refs[:-1], refs[-1]
    blocks, copies, rows, _ = out_ref.shape
    _, lag_rows, chans = sums_refs[0].shape
    per_sum = windows // len(sums_refs)
    heads = [decode(sums_ref[6]) for sums_ref in sums_refs]
    levels = [level_of(head[0:1, :]) * (1.0 / (CODE_TOP * windows)) for head in heads]
    stacks = []
    for side in range(2):
        linear = sum(decode(sums_ref[side]) * level for sums_ref, level in zip(sums_refs, levels))
        real, imag = (
            sum(decode(sums_ref[part + side]) for sums_ref in sums_refs) * (per_sum / (CODE_TOP * windows))
            for part in (2, 4)
        )
        stacks.append(linear * (real * real + imag * imag))
    offset = heads[0][1:2, :]
    lane = lax.broadcasted_iota(jnp.int32, (1, chans), 1)
    behind = [jnp.zeros_like(stack) for stack in stacks]
    for steps in range(1, blocks // 2 + 1):
        ahead = steps * (chans // blocks)
        chosen = (offset == steps) & (lane >= ahead)
        behind = [jnp.where(chosen, pltpu.roll(stack, ahead, 1), kept) for stack, kept in zip(stacks, behind)]
    back = stacks[1] + behind[0]
    both = jnp.concatenate(
        [stacks[0] + behind[1]] + [back[row : row + 1, :] for row in reversed(range(lag_rows))], axis=0
    )
    wide = 2 * lag_rows
    parts = chans // wide
    turned = jnp.concatenate([both] * parts, axis=0).T
    per_block = chans // blocks
    for block in range(blocks):
        piece = jnp.zeros((rows, chans), jnp.float32)
        for part in range(parts):
            begin = block * per_block + part * rows
            piece = jnp.where(lane // wide == part, turned[begin : begin + rows, :], piece)
        for copy in range(copies):
            out_ref[block, copy, :, :] = piece


def place_kernel(parts_ref, out_ref):
    groups, offset_count, rows, lanes = parts_ref.shape
    half = out_ref.shape[2] // 2
    lag_rows = half // groups
    parts = out_ref.shape[0] // rows
    lane = lax.broadcasted_iota(jnp.int32, (1, lanes), 1)
    for number in range(offset_count):
        for part in range(parts):
            ahead = jnp.zeros((rows, lanes), jnp.float32)
            back = jnp.zeros((rows, lanes), jnp.float32)
            begin = part * 2 * lag_rows
            for group in range(groups):
                piece = parts_ref[group, number]
                first, last = group * lag_rows, half - (group + 1) * lag_rows
                ahead = jnp.where(lane // lag_rows == group, pltpu.roll(piece, (first - begin) % lanes, 1), ahead)
                back = jnp.where(
                    lane // lag_rows == groups - 1 - group, pltpu.roll(piece, (last - begin - lag_rows) % lanes, 1), back
                )
            out_ref[part * rows : (part + 1) * rows, number, 0:half] = back
            out_ref[part * rows : (part + 1) * rows, number, half : 2 * half] = ahead


def window_shards(spectra, quality, offsets):
    chan_count = lax.axis_size("chan")
    tm_count = lax.axis_size("tm")
    _, windows, band, chans = spectra.shape
    freqs = band * chan_count
    half = LAGS // 2
    lag_rows = half // chan_count
    offset_count = offsets.shape[0]
    piece_rows = 2 * lag_rows // chan_count
    smem = pl.BlockSpec(memory_space=pltpu.SMEM)
    vmem = pl.BlockSpec(memory_space=pltpu.VMEM)
    params = pltpu.CompilerParams(vmem_limit_bytes=VMEM_LIMIT)
    table = jnp.asarray(half_table(freqs, LAGS).reshape(2, chan_count, lag_rows, freqs))
    chan_index = lax.axis_index("chan").astype(jnp.int32)
    tm_index = lax.axis_index("tm").astype(jnp.int32)
    chan_where, tm_where = chan_index.reshape(1), tm_index.reshape(1)

    chan_order, tm_order = partners(chan_count), partners(tm_count)
    kept = pl.BlockSpec(memory_space=pltpu.HBM)
    spectra = pltpu.with_memory_space_constraint(spectra, pltpu.HBM)
    pieces = []
    for part in (chan_order[:2], chan_order[2:]):
        pieces += pl.pallas_call(
            functools.partial(split_kernel, part),
            out_shape=[jax.ShapeDtypeStruct((2, band, chans), spectra.dtype)] * len(part),
            in_specs=[kept],
            out_specs=[pl.BlockSpec(memory_space=pl.ANY)] * len(part),
            scratch_shapes=[pltpu.SemaphoreType.DMA((len(part), 2, 4))],
            compiler_params=params,
            name="split_windows",
        )(spectra)
    chip_order = chips(chan_count)
    pair_shape = (6 * offset_count - 2, lag_rows, chans)
    own, far = pl.pallas_call(
        functools.partial(window_kernel, chan_order),
        out_shape=[jax.ShapeDtypeStruct((len(chip_order), *pair_shape), jnp.int16)] * 2,
        in_specs=[kept, smem] + [vmem] * (chan_count + 2),
        out_specs=[vmem] * 2,
        scratch_shapes=[
            pltpu.VMEM((freqs, chans), jnp.float32),
            pltpu.VMEM((2, freqs, chans), jnp.bfloat16),
            pltpu.VMEM((offset_count, freqs, 2 * chans), jnp.bfloat16),
            pltpu.SMEM(offsets.shape, jnp.int32),
            pltpu.SemaphoreType.DMA(()),
        ],
        compiler_params=params,
        name="window_pairs",
    )(pltpu.with_memory_space_constraint(offsets, pltpu.HBM), chan_where, *exchange(pieces, "chan", chan_order), quality, table)
    pairs = pl.pallas_call(
        functools.partial(merge_kernel, offset_count),
        out_shape=[jax.ShapeDtypeStruct(pair_shape, jnp.int16)] * len(chip_order),
        in_specs=[vmem] * 2,
        out_specs=[vmem] * len(chip_order),
        compiler_params=params,
        name="merge_windows",
    )(own, *exchange([far], "chan", [1]))
    sums = pl.pallas_call(
        functools.partial(sum_kernel, tm_order, 1.0 / (CODE_TOP * math.sqrt(freqs))),
        out_shape=[jax.ShapeDtypeStruct((7, lag_rows, chans), jnp.int16)] * tm_count,
        in_specs=[smem] + [vmem] * len(chip_order),
        out_specs=[vmem] * tm_count,
        scratch_shapes=[pltpu.VMEM((offset_count, 7, lag_rows, chans), jnp.int16)],
        compiler_params=params,
        name="sum_windows",
    )(tm_where, *exchange(pairs, "chan", chip_order))
    pieces = pl.pallas_call(
        functools.partial(stack_kernel, windows * tm_count),
        out_shape=jax.ShapeDtypeStruct((chan_count, tm_count, piece_rows, chans), jnp.float32),
        in_specs=[vmem] * tm_count,
        out_specs=vmem,
        compiler_params=params,
        name="stack_pairs",
    )(*exchange(sums, "tm", tm_order))
    shape = (chan_count * tm_count, piece_rows, chans)
    arrived = lax.all_to_all(pieces.reshape(shape), ("chan", "tm"), 0, 0, tiled=True)
    return pl.pallas_call(
        place_kernel,
        out_shape=jax.ShapeDtypeStruct((CH_DEV, offset_count, LAGS), jnp.float32),
        in_specs=[vmem],
        out_specs=vmem,
        compiler_params=params,
        name="place_lags",
    )(arrived.reshape(chan_count, tm_count, piece_rows, chans))


def shifted(value, axis, steps):
    count = lax.axis_size(axis)
    leading, last = (max(0, -steps), min(count, count - steps))
    return lax.ppermute(value, axis, [(source, source + steps) for source in range(leading, last)])


def lag_table(freq_count, lag_count):
    freq_index = jnp.arange(freq_count, dtype=jnp.int32)[:, None]
    double_lag = (2 * jnp.arange(lag_count, dtype=jnp.int32) - lag_count + 1)[None, :]
    turns = jnp.mod(freq_index * double_lag, 4 * freq_count)
    angles = turns.astype(jnp.float32) * (2.0 * math.pi / (4 * freq_count))
    cosine = jnp.cos(angles)
    sine = jnp.sin(angles)
    upper = jnp.concatenate([cosine, sine], axis=1)
    lower = jnp.concatenate([-sine, cosine], axis=1)
    return jnp.stack([upper, lower]).astype(jnp.bfloat16)


def whiten_parts(real_part, imag_part, magnitude, channel_level, usable):
    factor = usable.astype(jnp.float32)[:, None, :] / (magnitude + 0.5 * (channel_level + 1e-05))
    return jnp.stack([real_part * factor, imag_part * factor]).astype(jnp.bfloat16)


def cross_parts(own_real, own_imag, far_real, far_imag):
    own_real = own_real.astype(jnp.float32)
    own_imag = own_imag.astype(jnp.float32)
    far_real = far_real.astype(jnp.float32)
    far_imag = far_imag.astype(jnp.float32)
    return jnp.stack(
        [own_real * far_real + own_imag * far_imag, own_imag * far_real - own_real * far_imag]
    ).astype(jnp.bfloat16)


def pair_terms(corr_all):
    lag_count = corr_all.shape[-1] // 2
    real_corr = corr_all[..., :lag_count]
    imag_corr = corr_all[..., lag_count:]
    power = real_corr * real_corr + imag_corr * imag_corr
    mean_power = jnp.mean(power, axis=-1, keepdims=True)
    denominator = jnp.sqrt(power + 0.25 * (mean_power + 1e-06))
    return (
        jnp.sum(real_corr, axis=-3),
        jnp.sum(real_corr / denominator, axis=-3),
        jnp.sum(imag_corr / denominator, axis=-3),
    )


def shards(spectra, quality, offsets):
    chan_count = lax.axis_size("chan")
    tm_count = lax.axis_size("tm")
    levels = chan_count.bit_length() - 1
    table_bf = lag_table(F, LAGS)
    inv_root = 1.0 / math.sqrt(F)
    real_part = spectra[0].astype(jnp.float32)
    imag_part = spectra[1].astype(jnp.float32)
    magnitude = jnp.sqrt(real_part * real_part + imag_part * imag_part)
    band_total = lax.psum(jnp.sum(magnitude, axis=1), "chan")
    channel_level = (band_total / F)[:, None, :]
    whitened = whiten_parts(real_part, imag_part, magnitude, channel_level, quality)
    width_all = whitened.shape[3]
    padded = jnp.pad(whitened, ((0, 0), (0, 0), (0, 0), (0, width_all)))
    crossed_list = []
    for offset_index in range(NOFF):
        partner = lax.dynamic_slice_in_dim(padded, offsets[offset_index] * CH_DEV, width_all, 3)
        crossed_list.append(cross_parts(whitened[0], whitened[1], partner[0], partner[1]))
    crossed = jnp.stack(crossed_list, axis=1)
    corr_all = jnp.einsum(
        "cnwfh,cfl->nwhl",
        lax.all_to_all(crossed, "chan", split_axis=4, concat_axis=3, tiled=True),
        table_bf,
        preferred_element_type=jnp.float32,
    )
    linear_sum, real_sum, imag_sum = pair_terms(corr_all * inv_root)
    totals = lax.psum((linear_sum, real_sum, imag_sum), "tm")
    window_count = W_DEV * tm_count
    linear = totals[0] / window_count
    real_phase = totals[1] / window_count
    imag_phase = totals[2] / window_count
    stacks = jnp.transpose(linear * (real_phase * real_phase + imag_phase * imag_phase), (1, 0, 2))
    reverse_part = stacks
    for bit_index in range(levels):
        step_size = 1 << bit_index
        arrived = shifted(reverse_part, "chan", step_size)
        chosen = offsets // step_size % 2 == 1
        reverse_part = jnp.where(chosen[None, :, None], arrived, reverse_part)
    return stacks + jnp.flip(reverse_part, axis=2)


def solution(mesh):
    chan_count, tm_count = mesh.shape["chan"], mesh.shape["tm"]
    by_window = chan_count == W_DEV and tm_count == NOFF
    return jax.shard_map(
        window_shards if by_window else shards,
        mesh=mesh,
        in_specs=(P(None, "tm", "chan", None), P("tm", None), P()),
        out_specs=P("chan", None, None),
        check_vma=False,
    )
```

```python
import functools
import math

import jax
import jax.numpy as jnp
import numpy as np
from jax import lax
from jax.experimental import pallas as pl
from jax.experimental.pallas import tpu as pltpu
from jax.sharding import PartitionSpec as P

F = 2048
LAGS = 256
NOFF = 4
CH_DEV = 16
W_DEV = 8
VMEM_LIMIT = 48 * 1024 * 1024
CODE_TOP = 32767.0
OCTAVE = 256.0
LOWEST = -110.0


def encode(value):
    return jnp.round(value).astype(jnp.int32).astype(jnp.int16)


def decode(code):
    return code.astype(jnp.int32).astype(jnp.float32)


def level_code(peak):
    return jnp.ceil(jnp.maximum(jnp.log2(jnp.maximum(peak, 1e-30)), LOWEST) * OCTAVE) + 1.0


def level_of(code):
    return jnp.exp2(code * (1.0 / OCTAVE))


def half_table(freq_count, lag_count):
    freq_index = np.arange(freq_count, dtype=np.int64)[None, :]
    double_lag = (2 * np.arange(lag_count // 2, lag_count, dtype=np.int64) - lag_count + 1)[:, None]
    turns = np.mod(freq_index * double_lag, 4 * freq_count).astype(np.float32)
    angles = turns * np.float32(2.0 * math.pi / (4 * freq_count))
    return np.concatenate([np.cos(angles), np.sin(angles)]).astype(jnp.bfloat16)


def widest(offs_ref, reach):
    last = offs_ref.shape[0] - 1
    found = last
    for number in reversed(range(last)):
        found = jnp.where(offs_ref[number] == reach, number, found)
    return found


def offset_of(slot, offs_ref, reach):
    last, wide = offs_ref.shape[0] - 1, widest(offs_ref, reach)
    return offs_ref[jnp.where(slot == wide, last, jnp.where(slot == last, wide, slot))]


def window_kernel(order, offs_hbm_ref, where_ref, *refs):
    chan_count = len(order)
    spec_refs, (qual_ref, table_ref) = refs[:chan_count], refs[chan_count : chan_count + 2]
    out_refs = refs[chan_count + 2 : chan_count + 4]
    mag_ref, white_ref, cross_ref, offs_ref, offs_sem = refs[chan_count + 4 :]
    fetch = pltpu.make_async_copy(offs_hbm_ref, offs_ref, offs_sem)
    fetch.start()
    me = where_ref[0]
    _, band, chans = spec_refs[0].shape
    freqs = chan_count * band
    chip_count, blocks, lag_rows, _ = out_refs[0].shape
    offset_count = offs_ref.shape[0]
    half = chan_count * lag_rows
    step = 64

    total = jnp.zeros((8, chans), jnp.float32)
    for number, spec_ref in enumerate(spec_refs):
        for row in range(0, band, step):
            real, imag = (spec_ref[part, row : row + step, :].astype(jnp.float32) for part in range(2))
            square = real * real + imag * imag
            magnitude = square * lax.rsqrt(jnp.maximum(square, 1e-30))
            held = slice(number * band + row, number * band + row + step)
            mag_ref[held, :] = magnitude
            total += jnp.sum(magnitude.reshape(step // 8, 8, chans), axis=0)
    level = jnp.sum(total, axis=0, keepdims=True) * (1.0 / freqs)
    floor = 0.5 * (level + 1e-05)

    for number, spec_ref in enumerate(spec_refs):
        for row in range(0, band, step):
            held = slice(number * band + row, number * band + row + step)
            factor = pl.reciprocal(mag_ref[held, :] + floor, approx=True)
            for part in range(2):
                value = spec_ref[part, row : row + step, :].astype(jnp.float32) * factor
                white_ref[part, held, :] = value.astype(jnp.bfloat16)

    lane = lax.broadcasted_iota(jnp.int32, (1, chans), 1)
    line = lax.broadcasted_iota(jnp.int32, (lag_rows, chans), 0)
    usable = qual_ref[pl.ds(me, 1), :].astype(jnp.float32)
    levels = jnp.zeros((lag_rows, chans), jnp.float32)
    groups = [k ^ core for core in range(2) for k in chips(chan_count)]
    fetch.wait()
    bands = [pl.ds(pl.multiple_of((me ^ k) * band, band), band) for k in order]
    table = jnp.concatenate(
        [
            jnp.concatenate([table_ref[side, me ^ group, :, taken] for taken in bands], axis=1)
            for side in range(2)
            for group in groups
        ],
        axis=0,
    )
    turns = [chans - offset_of(number, offs_ref, chan_count // 2) * (chans // chan_count) for number in range(offset_count - 1)]
    low = lane < chans // 2
    for row in range(0, freqs, step):
        own = [white_ref[part, row : row + step, :] for part in range(2)]
        own_real, own_imag = (value.astype(jnp.float32) for value in own)
        for number, turn in enumerate(turns):
            far_real, far_imag = (pltpu.roll(value, turn, 1).astype(jnp.float32) for value in own)
            real = own_real * far_real + own_imag * far_imag
            imag = own_imag * far_real - own_real * far_imag
            cross_ref[number, row : row + step, 0:chans] = real.astype(jnp.bfloat16)
            cross_ref[number, row : row + step, chans : 2 * chans] = imag.astype(jnp.bfloat16)
        far_real, far_imag = (pltpu.roll(value, chans // 2, 1).astype(jnp.float32) for value in own)
        both = own_real * jnp.where(low, far_real, far_imag) + own_imag * jnp.where(low, far_imag, -far_real)
        cross_ref[offset_count - 1, row : row + step, 0:chans] = both.astype(jnp.bfloat16)

    def store(block, value):
        coded = encode(value).reshape(chan_count, lag_rows, chans)
        for core in range(2):
            rows = slice(core * chip_count, (core + 1) * chip_count)
            out_refs[core][:, block, :, :] = coded[rows]

    def extra_of(power):
        return 0.25 * (jnp.sum(power[0] + power[1], axis=0, keepdims=True) * (1.0 / (2 * half)) + 1e-06 * freqs)

    for number, turn in enumerate(turns):
        sums = jnp.dot(table, cross_ref[number], preferred_element_type=jnp.float32)
        cos_real, sin_real = sums[:half, :chans], sums[half:, :chans]
        cos_imag, sin_imag = sums[:half, chans:], sums[half:, chans:]
        corr = (
            (cos_real - sin_imag, sin_real + cos_imag),
            (cos_real + sin_imag, cos_imag - sin_real),
        )
        power = [real * real + imag * imag for real, imag in corr]
        extra = extra_of(power)
        peak = jnp.max(jnp.maximum(jnp.abs(corr[0][0]), jnp.abs(corr[1][0])), axis=0, keepdims=True)
        code = level_code(peak)
        levels = jnp.where(line == number, code, levels)
        keep = jnp.where(lane < turn, usable * pltpu.roll(usable, turn, 1), 0.0) * CODE_TOP
        upscale = keep / level_of(code)
        for side in range(2):
            inverse = lax.rsqrt(power[side] + extra) * keep
            real, imag = corr[side]
            for kind, value in enumerate((real * upscale, real * inverse, imag * inverse)):
                store(6 * number + 2 * kind + side, value)

    def swap(value):
        return pltpu.roll(value, chans // 2, 1)

    number = offset_count - 1
    sums = jnp.dot(table, cross_ref[number, :, 0:chans], preferred_element_type=jnp.float32)
    cosine, sine = sums[:half], swap(sums[half:])
    less, more = cosine - sine, cosine + sine
    sides = (jnp.where(low, less, more), jnp.where(low, more, less))
    power = [value * value for value in sides]
    power = [value + swap(value) for value in power]
    extra = extra_of(power)
    linear = jnp.where(low, sides[0], swap(sides[1]))
    code = level_code(jnp.max(jnp.abs(linear), axis=0, keepdims=True))
    levels = jnp.where(line == number, code, levels)
    keep = usable * swap(usable) * CODE_TOP
    store(6 * number, linear * (keep / level_of(code)))
    for side in range(2):
        store(6 * number + 1 + side, sides[side] * (lax.rsqrt(power[side] + extra) * keep))
    for number in range(offset_count):
        levels = jnp.where(line == offset_count + number, offs_ref[number].astype(jnp.float32), levels)
    wide = widest(offs_ref, chan_count // 2).astype(jnp.float32)
    levels = jnp.where(line == 2 * offset_count, wide, levels)
    for out_ref in out_refs:
        for chip in range(chip_count):
            out_ref[chip, blocks - 1, :, :] = encode(levels)


def merge_kernel(slots, own_ref, far_ref, *out_refs):
    blocks = own_ref.shape[1]
    for chip, out_ref in enumerate(out_refs):
        codes = [decode(ref[chip, blocks - 1]) for ref in (own_ref, far_ref)]
        levels = [level_of(code) for code in codes]
        code = level_code(levels[0] + levels[1])
        shares = [level / level_of(code) for level in levels]
        line = lax.broadcasted_iota(jnp.int32, code.shape, 0)
        out_ref[blocks - 1, :, :] = encode(jnp.where(line < slots, code, codes[0]))
        for block in range(blocks - 1):
            number, part = divmod(block, 6)
            linear = part < (2 if blocks - 1 - 6 * number > 3 else 1)
            own, far = decode(own_ref[chip, block]), decode(far_ref[chip, block])
            if linear:
                total = own * shares[0][number : number + 1, :] + far * shares[1][number : number + 1, :]
            else:
                total = (own + far) * 0.5
            out_ref[block, :, :] = encode(total)


def sum_kernel(order, scale, where_ref, *refs):
    code_refs, out_refs, held_ref = refs[: -len(order) - 1], refs[-len(order) - 1 : -1], refs[-1]
    blocks, _, chans = code_refs[0].shape
    slots = held_ref.shape[0]
    heads = [decode(codes_ref[blocks - 1]) for codes_ref in code_refs]
    levels = [level_of(head) * scale for head in heads]
    offsets = [heads[0][slots + number : slots + number + 1, :] for number in range(slots)]
    wide = heads[0][2 * slots : 2 * slots + 1, :]
    low = lax.broadcasted_iota(jnp.int32, (1, chans), 1) < chans // 2

    def swap(value):
        return pltpu.roll(value, chans // 2, 1)

    all_sums = []
    for number in range(slots):
        sides = 2 if number < slots - 1 else 1
        own = [level[number : number + 1, :] for level in levels]
        sums = []
        for place in range(3 * sides):
            codes = [decode(codes_ref[6 * number + place]) for codes_ref in code_refs]
            if place < sides:
                sums.append(sum(code * level for code, level in zip(codes, own)))
            else:
                sums.append(sum(codes) * (1.0 / len(code_refs)))
        if sides == 1:
            linear, ahead, back = sums
            sums = [linear, swap(linear), ahead, back, swap(ahead), swap(back)]
            sums = [jnp.where(low, value, 0.0) for value in sums]
        all_sums.append(sums)
    line = lax.broadcasted_iota(jnp.int32, levels[0].shape, 0)
    last = slots - 1
    for number in range(slots):
        sums = all_sums[number]
        for other in range(last) if number == last else [last]:
            swap = wide == min(number, other)
            sums = [jnp.where(swap, value, kept) for value, kept in zip(all_sums[other], sums)]
        peak = jnp.max(jnp.maximum(jnp.abs(sums[0]), jnp.abs(sums[1])), axis=0, keepdims=True)
        code = level_code(peak)
        upscale = CODE_TOP / level_of(code)
        head = jnp.where(line == 0, code, offsets[number])
        for part, value in enumerate([sums[0] * upscale, sums[1] * upscale, *sums[2:], head]):
            held_ref[number, part, :, :] = encode(value)
    for k, out_ref in zip(order, out_refs):
        out_ref[...] = held_ref[where_ref[0] ^ k]


def partners(count):
    return sorted(range(1, count), key=lambda k: (-(k >> 1).bit_count(), k & 1, k)) + [0]


def chips(count):
    return sorted(range(2, count, 2), key=lambda k: (k.bit_count(), k)) + [0]


def exchange(pieces, axis, order):
    count = lax.axis_size(axis)
    return [
        lax.ppermute(piece, axis, [(source, source ^ k) for source in range(count)]) if k else piece
        for k, piece in zip(order, pieces)
    ]


def split_kernel(order, spec_ref, *refs):
    out_refs, sems = refs[:-1], refs[-1]
    me = lax.axis_index("chan").astype(jnp.int32)
    copies = [
        pltpu.make_async_copy(spec_ref.at[:, me ^ k], out_ref, sems.at[number])
        for number, (k, out_ref) in enumerate(zip(order, out_refs))
    ]
    for copy in copies:
        copy.start()
    for copy in copies:
        copy.wait()


def stack_kernel(windows, where_ref, *refs):
    sums_refs, out_ref = refs[:-1], refs[-1]
    blocks, copies, rows, _ = out_ref.shape
    _, lag_rows, chans = sums_refs[0].shape
    per_sum = windows // len(sums_refs)
    heads = [decode(sums_ref[6]) for sums_ref in sums_refs]
    levels = [level_of(head[0:1, :]) * (1.0 / (CODE_TOP * windows)) for head in heads]
    stacks = []
    for side in range(2):
        linear = sum(decode(sums_ref[side]) * level for sums_ref, level in zip(sums_refs, levels))
        real, imag = (
            sum(decode(sums_ref[part + side]) for sums_ref in sums_refs) * (per_sum / (CODE_TOP * windows))
            for part in (2, 4)
        )
        stacks.append(linear * (real * real + imag * imag))
    offset = heads[0][1:2, :]
    lane = lax.broadcasted_iota(jnp.int32, (1, chans), 1)
    behind = [jnp.zeros_like(stack) for stack in stacks]
    for steps in range(1, blocks // 2 + 1):
        ahead = steps * (chans // blocks)
        chosen = (offset == steps) & (lane >= ahead)
        behind = [jnp.where(chosen, pltpu.roll(stack, ahead, 1), kept) for stack, kept in zip(stacks, behind)]
    back = stacks[1] + behind[0]
    back = jnp.concatenate([back[row : row + 1, :] for row in reversed(range(lag_rows))], axis=0)
    me = where_ref[0]
    even = (me & 1) == 0
    ahead = stacks[0] + behind[1]
    both = jnp.concatenate([jnp.where(even, ahead, back), jnp.where(even, back, ahead)], axis=0)
    parts = chans // (2 * lag_rows)
    turned = jnp.concatenate([both] * parts, axis=0).T
    unit = lane // lag_rows
    part_of = jnp.where(((unit ^ me) & 1) == 0, unit - me, unit + me + 1) % blocks // 2
    per_block = chans // blocks
    for block in range(blocks):
        piece = jnp.zeros((rows, chans), jnp.float32)
        for part in range(parts):
            begin = block * per_block + part * rows
            piece = jnp.where(part_of == part, turned[begin : begin + rows, :], piece)
        for copy in range(copies):
            out_ref[block, copy, :, :] = piece


def place_kernel(parts_ref, out_ref):
    groups, offset_count, rows, lanes = parts_ref.shape
    half = out_ref.shape[2] // 2
    lag_rows = half // groups
    parts = out_ref.shape[0] // rows
    unit = lax.broadcasted_iota(jnp.int32, (1, lanes), 1) // lag_rows
    for number in range(offset_count):
        pieces = [parts_ref[group, number] for group in range(groups)]
        for part in range(parts):
            sides = [jnp.zeros((rows, lanes), jnp.float32)] * 2
            for group, piece in enumerate(pieces):
                places = ((groups - 1 - group + 2 * part) % groups, (group + 2 * part) % groups)
                sides = [jnp.where(unit == place, piece, side) for place, side in zip(places, sides)]
            for side, value in enumerate(sides):
                value = pltpu.roll(value, (lanes - 2 * part * lag_rows) % lanes, 1) if part else value
                out_ref[part * rows : (part + 1) * rows, number, side * half : (side + 1) * half] = value


def window_shards(spectra, quality, offsets):
    chan_count = lax.axis_size("chan")
    tm_count = lax.axis_size("tm")
    _, windows, band, chans = spectra.shape
    freqs = band * chan_count
    half = LAGS // 2
    lag_rows = half // chan_count
    offset_count = offsets.shape[0]
    piece_rows = 2 * lag_rows // chan_count
    smem = pl.BlockSpec(memory_space=pltpu.SMEM)
    vmem = pl.BlockSpec(memory_space=pltpu.VMEM)
    params = pltpu.CompilerParams(vmem_limit_bytes=VMEM_LIMIT)
    table = jnp.asarray(half_table(freqs, LAGS).reshape(2, chan_count, lag_rows, freqs))
    chan_index = lax.axis_index("chan").astype(jnp.int32)
    tm_index = lax.axis_index("tm").astype(jnp.int32)
    chan_where, tm_where = chan_index.reshape(1), tm_index.reshape(1)

    chan_order, tm_order = partners(chan_count), partners(tm_count)
    kept = pl.BlockSpec(memory_space=pltpu.HBM)
    spectra = pltpu.with_memory_space_constraint(spectra, pltpu.HBM)
    pieces = []
    for part in (chan_order[:2], chan_order[2:]):
        pieces += pl.pallas_call(
            functools.partial(split_kernel, part),
            out_shape=[jax.ShapeDtypeStruct((2, band, chans), spectra.dtype)] * len(part),
            in_specs=[kept],
            out_specs=[pl.BlockSpec(memory_space=pl.ANY)] * len(part),
            scratch_shapes=[pltpu.SemaphoreType.DMA((len(part),))],
            compiler_params=params,
            name="split_windows",
        )(spectra)
    chip_order = chips(chan_count)
    pair_shape = (6 * offset_count - 2, lag_rows, chans)
    own, far = pl.pallas_call(
        functools.partial(window_kernel, chan_order),
        out_shape=[jax.ShapeDtypeStruct((len(chip_order), *pair_shape), jnp.int16)] * 2,
        in_specs=[kept, smem] + [vmem] * (chan_count + 2),
        out_specs=[vmem] * 2,
        scratch_shapes=[
            pltpu.VMEM((freqs, chans), jnp.float32),
            pltpu.VMEM((2, freqs, chans), jnp.bfloat16),
            pltpu.VMEM((offset_count, freqs, 2 * chans), jnp.bfloat16),
            pltpu.SMEM(offsets.shape, jnp.int32),
            pltpu.SemaphoreType.DMA(()),
        ],
        compiler_params=params,
        name="window_pairs",
    )(pltpu.with_memory_space_constraint(offsets, pltpu.HBM), chan_where, *exchange(pieces, "chan", chan_order), quality, table)
    pairs = pl.pallas_call(
        functools.partial(merge_kernel, offset_count),
        out_shape=[jax.ShapeDtypeStruct(pair_shape, jnp.int16)] * len(chip_order),
        in_specs=[vmem] * 2,
        out_specs=[vmem] * len(chip_order),
        compiler_params=params,
        name="merge_windows",
    )(own, *exchange([far], "chan", [1]))
    sums = pl.pallas_call(
        functools.partial(sum_kernel, tm_order, 1.0 / (CODE_TOP * math.sqrt(freqs))),
        out_shape=[jax.ShapeDtypeStruct((7, lag_rows, chans), jnp.int16)] * tm_count,
        in_specs=[smem] + [vmem] * len(chip_order),
        out_specs=[vmem] * tm_count,
        scratch_shapes=[pltpu.VMEM((offset_count, 7, lag_rows, chans), jnp.int16)],
        compiler_params=params,
        name="sum_windows",
    )(tm_where, *exchange(pairs, "chan", chip_order))
    pieces = pl.pallas_call(
        functools.partial(stack_kernel, windows * tm_count),
        out_shape=jax.ShapeDtypeStruct((chan_count, tm_count, piece_rows, chans), jnp.float32),
        in_specs=[smem] + [vmem] * tm_count,
        out_specs=vmem,
        compiler_params=params,
        name="stack_pairs",
    )(chan_where, *exchange(sums, "tm", tm_order))
    shape = (chan_count * tm_count, piece_rows, chans)
    arrived = lax.all_to_all(pieces.reshape(shape), ("chan", "tm"), 0, 0, tiled=True)
    return pl.pallas_call(
        place_kernel,
        out_shape=jax.ShapeDtypeStruct((CH_DEV, offset_count, LAGS), jnp.float32),
        in_specs=[vmem],
        out_specs=vmem,
        compiler_params=params,
        name="place_lags",
    )(arrived.reshape(chan_count, tm_count, piece_rows, chans))


def shifted(value, axis, steps):
    count = lax.axis_size(axis)
    leading, last = (max(0, -steps), min(count, count - steps))
    return lax.ppermute(value, axis, [(source, source + steps) for source in range(leading, last)])


def lag_table(freq_count, lag_count):
    freq_index = jnp.arange(freq_count, dtype=jnp.int32)[:, None]
    double_lag = (2 * jnp.arange(lag_count, dtype=jnp.int32) - lag_count + 1)[None, :]
    turns = jnp.mod(freq_index * double_lag, 4 * freq_count)
    angles = turns.astype(jnp.float32) * (2.0 * math.pi / (4 * freq_count))
    cosine = jnp.cos(angles)
    sine = jnp.sin(angles)
    upper = jnp.concatenate([cosine, sine], axis=1)
    lower = jnp.concatenate([-sine, cosine], axis=1)
    return jnp.stack([upper, lower]).astype(jnp.bfloat16)


def whiten_parts(real_part, imag_part, magnitude, channel_level, usable):
    factor = usable.astype(jnp.float32)[:, None, :] / (magnitude + 0.5 * (channel_level + 1e-05))
    return jnp.stack([real_part * factor, imag_part * factor]).astype(jnp.bfloat16)


def cross_parts(own_real, own_imag, far_real, far_imag):
    own_real = own_real.astype(jnp.float32)
    own_imag = own_imag.astype(jnp.float32)
    far_real = far_real.astype(jnp.float32)
    far_imag = far_imag.astype(jnp.float32)
    return jnp.stack(
        [own_real * far_real + own_imag * far_imag, own_imag * far_real - own_real * far_imag]
    ).astype(jnp.bfloat16)


def pair_terms(corr_all):
    lag_count = corr_all.shape[-1] // 2
    real_corr = corr_all[..., :lag_count]
    imag_corr = corr_all[..., lag_count:]
    power = real_corr * real_corr + imag_corr * imag_corr
    mean_power = jnp.mean(power, axis=-1, keepdims=True)
    denominator = jnp.sqrt(power + 0.25 * (mean_power + 1e-06))
    return (
        jnp.sum(real_corr, axis=-3),
        jnp.sum(real_corr / denominator, axis=-3),
        jnp.sum(imag_corr / denominator, axis=-3),
    )


def shards(spectra, quality, offsets):
    chan_count = lax.axis_size("chan")
    tm_count = lax.axis_size("tm")
    levels = chan_count.bit_length() - 1
    table_bf = lag_table(F, LAGS)
    inv_root = 1.0 / math.sqrt(F)
    real_part = spectra[0].astype(jnp.float32)
    imag_part = spectra[1].astype(jnp.float32)
    magnitude = jnp.sqrt(real_part * real_part + imag_part * imag_part)
    band_total = lax.psum(jnp.sum(magnitude, axis=1), "chan")
    channel_level = (band_total / F)[:, None, :]
    whitened = whiten_parts(real_part, imag_part, magnitude, channel_level, quality)
    width_all = whitened.shape[3]
    padded = jnp.pad(whitened, ((0, 0), (0, 0), (0, 0), (0, width_all)))
    crossed_list = []
    for offset_index in range(NOFF):
        partner = lax.dynamic_slice_in_dim(padded, offsets[offset_index] * CH_DEV, width_all, 3)
        crossed_list.append(cross_parts(whitened[0], whitened[1], partner[0], partner[1]))
    crossed = jnp.stack(crossed_list, axis=1)
    corr_all = jnp.einsum(
        "cnwfh,cfl->nwhl",
        lax.all_to_all(crossed, "chan", split_axis=4, concat_axis=3, tiled=True),
        table_bf,
        preferred_element_type=jnp.float32,
    )
    linear_sum, real_sum, imag_sum = pair_terms(corr_all * inv_root)
    totals = lax.psum((linear_sum, real_sum, imag_sum), "tm")
    window_count = W_DEV * tm_count
    linear = totals[0] / window_count
    real_phase = totals[1] / window_count
    imag_phase = totals[2] / window_count
    stacks = jnp.transpose(linear * (real_phase * real_phase + imag_phase * imag_phase), (1, 0, 2))
    reverse_part = stacks
    for bit_index in range(levels):
        step_size = 1 << bit_index
        arrived = shifted(reverse_part, "chan", step_size)
        chosen = offsets // step_size % 2 == 1
        reverse_part = jnp.where(chosen[None, :, None], arrived, reverse_part)
    return stacks + jnp.flip(reverse_part, axis=2)


def solution(mesh):
    chan_count, tm_count = mesh.shape["chan"], mesh.shape["tm"]
    by_window = chan_count == W_DEV and tm_count == NOFF
    return jax.shard_map(
        window_shards if by_window else shards,
        mesh=mesh,
        in_specs=(P(None, "tm", "chan", None), P("tm", None), P()),
        out_specs=P("chan", None, None),
        check_vma=False,
    )
```

```python
import functools
import math

import jax
import jax.numpy as jnp
import numpy as np
from jax import lax
from jax.experimental import pallas as pl
from jax.experimental.pallas import tpu as pltpu
from jax.sharding import PartitionSpec as P

F = 2048
LAGS = 256
NOFF = 4
CH_DEV = 16
W_DEV = 8
VMEM_LIMIT = 48 * 1024 * 1024
CODE_TOP = 32767.0
OCTAVE = 256.0
LOWEST = -110.0


def encode(value):
    return jnp.round(value).astype(jnp.int32).astype(jnp.int16)


def decode(code):
    return code.astype(jnp.int32).astype(jnp.float32)


def level_code(peak):
    return jnp.ceil(jnp.maximum(jnp.log2(jnp.maximum(peak, 1e-30)), LOWEST) * OCTAVE) + 1.0


def level_of(code):
    return jnp.exp2(code * (1.0 / OCTAVE))


def half_table(freq_count, lag_count):
    freq_index = np.arange(freq_count, dtype=np.int64)[None, :]
    double_lag = (2 * np.arange(lag_count // 2, lag_count, dtype=np.int64) - lag_count + 1)[:, None]
    turns = np.mod(freq_index * double_lag, 4 * freq_count).astype(np.float32)
    angles = turns * np.float32(2.0 * math.pi / (4 * freq_count))
    return np.concatenate([np.cos(angles), np.sin(angles)]).astype(jnp.bfloat16)


def widest(offs_ref, reach):
    last = offs_ref.shape[0] - 1
    found = last
    for number in reversed(range(last)):
        found = jnp.where(offs_ref[number] == reach, number, found)
    return found


def offset_of(slot, offs_ref, reach):
    last, wide = offs_ref.shape[0] - 1, widest(offs_ref, reach)
    return offs_ref[jnp.where(slot == wide, last, jnp.where(slot == last, wide, slot))]


def window_kernel(order, offs_hbm_ref, where_ref, *refs):
    chan_count = len(order)
    spec_refs, (qual_ref, table_ref) = refs[:chan_count], refs[chan_count : chan_count + 2]
    out_refs = refs[chan_count + 2 : chan_count + 4]
    mag_ref, white_ref, cross_ref, offs_ref, offs_sem = refs[chan_count + 4 :]
    fetch = pltpu.make_async_copy(offs_hbm_ref, offs_ref, offs_sem)
    fetch.start()
    me = where_ref[0]
    _, band, chans = spec_refs[0].shape
    freqs = chan_count * band
    chip_count, blocks, lag_rows, _ = out_refs[0].shape
    offset_count = offs_ref.shape[0]
    half = chan_count * lag_rows
    step = 64

    total = jnp.zeros((8, chans), jnp.float32)
    for number, spec_ref in enumerate(spec_refs):
        for row in range(0, band, step):
            real, imag = (spec_ref[part, row : row + step, :].astype(jnp.float32) for part in range(2))
            square = real * real + imag * imag
            magnitude = square * lax.rsqrt(jnp.maximum(square, 1e-30))
            held = slice(number * band + row, number * band + row + step)
            mag_ref[held, :] = magnitude
            total += jnp.sum(magnitude.reshape(step // 8, 8, chans), axis=0)
    level = jnp.sum(total, axis=0, keepdims=True) * (1.0 / freqs)
    floor = 0.5 * (level + 1e-05)

    for number, spec_ref in enumerate(spec_refs):
        for row in range(0, band, step):
            held = slice(number * band + row, number * band + row + step)
            factor = pl.reciprocal(mag_ref[held, :] + floor, approx=True)
            for part in range(2):
                value = spec_ref[part, row : row + step, :].astype(jnp.float32) * factor
                white_ref[part, held, :] = value.astype(jnp.bfloat16)

    lane = lax.broadcasted_iota(jnp.int32, (1, chans), 1)
    line = lax.broadcasted_iota(jnp.int32, (lag_rows, chans), 0)
    usable = qual_ref[pl.ds(me, 1), :].astype(jnp.float32)
    levels = jnp.zeros((lag_rows, chans), jnp.float32)
    groups = [k ^ core for core in range(2) for k in chips(chan_count)]
    fetch.wait()
    bands = [pl.ds(pl.multiple_of((me ^ k) * band, band), band) for k in order]
    table = jnp.concatenate(
        [
            jnp.concatenate([table_ref[side, me ^ group, :, taken] for taken in bands], axis=1)
            for side in range(2)
            for group in groups
        ],
        axis=0,
    )
    turns = [chans - offset_of(number, offs_ref, chan_count // 2) * (chans // chan_count) for number in range(offset_count - 1)]
    low = lane < chans // 2
    for row in range(0, freqs, step):
        own = [white_ref[part, row : row + step, :] for part in range(2)]
        own_real, own_imag = (value.astype(jnp.float32) for value in own)
        for number, turn in enumerate(turns):
            far_real, far_imag = (pltpu.roll(value, turn, 1).astype(jnp.float32) for value in own)
            real = own_real * far_real + own_imag * far_imag
            imag = own_imag * far_real - own_real * far_imag
            begin = 2 * number * chans
            cross_ref[row : row + step, begin : begin + chans] = real.astype(jnp.bfloat16)
            cross_ref[row : row + step, begin + chans : begin + 2 * chans] = imag.astype(jnp.bfloat16)
        far_real, far_imag = (pltpu.roll(value, chans // 2, 1).astype(jnp.float32) for value in own)
        both = own_real * jnp.where(low, far_real, far_imag) + own_imag * jnp.where(low, far_imag, -far_real)
        cross_ref[row : row + step, 2 * (offset_count - 1) * chans :] = both.astype(jnp.bfloat16)
    all_sums = jnp.dot(table, cross_ref[...], preferred_element_type=jnp.float32)

    def store(block, value):
        coded = encode(value).reshape(chan_count, lag_rows, chans)
        for core in range(2):
            rows = slice(core * chip_count, (core + 1) * chip_count)
            out_refs[core][:, block, :, :] = coded[rows]

    def extra_of(power):
        return 0.25 * (jnp.sum(power[0] + power[1], axis=0, keepdims=True) * (1.0 / (2 * half)) + 1e-06 * freqs)

    for number, turn in enumerate(turns):
        sums = all_sums[:, 2 * number * chans : 2 * (number + 1) * chans]
        cos_real, sin_real = sums[:half, :chans], sums[half:, :chans]
        cos_imag, sin_imag = sums[:half, chans:], sums[half:, chans:]
        corr = (
            (cos_real - sin_imag, sin_real + cos_imag),
            (cos_real + sin_imag, cos_imag - sin_real),
        )
        power = [real * real + imag * imag for real, imag in corr]
        extra = extra_of(power)
        peak = jnp.max(jnp.maximum(jnp.abs(corr[0][0]), jnp.abs(corr[1][0])), axis=0, keepdims=True)
        code = level_code(peak)
        levels = jnp.where(line == number, code, levels)
        keep = jnp.where(lane < turn, usable * pltpu.roll(usable, turn, 1), 0.0) * CODE_TOP
        upscale = keep / level_of(code)
        for side in range(2):
            inverse = lax.rsqrt(power[side] + extra) * keep
            real, imag = corr[side]
            for kind, value in enumerate((real * upscale, real * inverse, imag * inverse)):
                store(6 * number + 2 * kind + side, value)

    def swap(value):
        return pltpu.roll(value, chans // 2, 1)

    number = offset_count - 1
    sums = all_sums[:, 2 * number * chans :]
    cosine, sine = sums[:half], swap(sums[half:])
    less, more = cosine - sine, cosine + sine
    sides = (jnp.where(low, less, more), jnp.where(low, more, less))
    power = [value * value for value in sides]
    power = [value + swap(value) for value in power]
    extra = extra_of(power)
    linear = jnp.where(low, sides[0], swap(sides[1]))
    code = level_code(jnp.max(jnp.abs(linear), axis=0, keepdims=True))
    levels = jnp.where(line == number, code, levels)
    keep = usable * swap(usable) * CODE_TOP
    store(6 * number, linear * (keep / level_of(code)))
    for side in range(2):
        store(6 * number + 1 + side, sides[side] * (lax.rsqrt(power[side] + extra) * keep))
    for number in range(offset_count):
        levels = jnp.where(line == offset_count + number, offs_ref[number].astype(jnp.float32), levels)
    wide = widest(offs_ref, chan_count // 2).astype(jnp.float32)
    levels = jnp.where(line == 2 * offset_count, wide, levels)
    for out_ref in out_refs:
        for chip in range(chip_count):
            out_ref[chip, blocks - 1, :, :] = encode(levels)


def merge_kernel(slots, own_ref, far_ref, *out_refs):
    blocks = own_ref.shape[1]
    for chip, out_ref in enumerate(out_refs):
        codes = [decode(ref[chip, blocks - 1]) for ref in (own_ref, far_ref)]
        levels = [level_of(code) for code in codes]
        code = level_code(levels[0] + levels[1])
        shares = [level / level_of(code) for level in levels]
        line = lax.broadcasted_iota(jnp.int32, code.shape, 0)
        out_ref[blocks - 1, :, :] = encode(jnp.where(line < slots, code, codes[0]))
        for block in range(blocks - 1):
            number, part = divmod(block, 6)
            linear = part < (2 if blocks - 1 - 6 * number > 3 else 1)
            own, far = decode(own_ref[chip, block]), decode(far_ref[chip, block])
            if linear:
                total = own * shares[0][number : number + 1, :] + far * shares[1][number : number + 1, :]
            else:
                total = (own + far) * 0.5
            out_ref[block, :, :] = encode(total)


def sum_kernel(order, scale, where_ref, *refs):
    code_refs, out_refs, held_ref = refs[: -len(order) - 1], refs[-len(order) - 1 : -1], refs[-1]
    blocks, _, chans = code_refs[0].shape
    slots = held_ref.shape[0]
    heads = [decode(codes_ref[blocks - 1]) for codes_ref in code_refs]
    levels = [level_of(head) * scale for head in heads]
    offsets = [heads[0][slots + number : slots + number + 1, :] for number in range(slots)]
    wide = heads[0][2 * slots : 2 * slots + 1, :]
    low = lax.broadcasted_iota(jnp.int32, (1, chans), 1) < chans // 2

    def swap(value):
        return pltpu.roll(value, chans // 2, 1)

    all_sums = []
    for number in range(slots):
        sides = 2 if number < slots - 1 else 1
        own = [level[number : number + 1, :] for level in levels]
        sums = []
        for place in range(3 * sides):
            codes = [decode(codes_ref[6 * number + place]) for codes_ref in code_refs]
            if place < sides:
                sums.append(sum(code * level for code, level in zip(codes, own)))
            else:
                sums.append(sum(codes) * (1.0 / len(code_refs)))
        if sides == 1:
            linear, ahead, back = sums
            sums = [linear, swap(linear), ahead, back, swap(ahead), swap(back)]
            sums = [jnp.where(low, value, 0.0) for value in sums]
        all_sums.append(sums)
    line = lax.broadcasted_iota(jnp.int32, levels[0].shape, 0)
    last = slots - 1
    for number in range(slots):
        sums = all_sums[number]
        for other in range(last) if number == last else [last]:
            swap = wide == min(number, other)
            sums = [jnp.where(swap, value, kept) for value, kept in zip(all_sums[other], sums)]
        peak = jnp.max(jnp.maximum(jnp.abs(sums[0]), jnp.abs(sums[1])), axis=0, keepdims=True)
        code = level_code(peak)
        upscale = CODE_TOP / level_of(code)
        head = jnp.where(line == 0, code, offsets[number])
        for part, value in enumerate([sums[0] * upscale, sums[1] * upscale, *sums[2:], head]):
            held_ref[number, part, :, :] = encode(value)
    for k, out_ref in zip(order, out_refs):
        out_ref[...] = held_ref[where_ref[0] ^ k]


def partners(count):
    return sorted(range(1, count), key=lambda k: (-(k >> 1).bit_count(), k & 1, k)) + [0]


def chips(count):
    return sorted(range(2, count, 2), key=lambda k: (k.bit_count(), k)) + [0]


def exchange(pieces, axis, order):
    count = lax.axis_size(axis)
    return [
        lax.ppermute(piece, axis, [(source, source ^ k) for source in range(count)]) if k else piece
        for k, piece in zip(order, pieces)
    ]


def split_kernel(order, spec_ref, *refs):
    out_refs, sems = refs[:-1], refs[-1]
    me = lax.axis_index("chan").astype(jnp.int32)
    copies = [
        pltpu.make_async_copy(spec_ref.at[:, me ^ k], out_ref, sems.at[number])
        for number, (k, out_ref) in enumerate(zip(order, out_refs))
    ]
    for copy in copies:
        copy.start()
    for copy in copies:
        copy.wait()


def stack_kernel(windows, where_ref, *refs):
    sums_refs, out_ref = refs[:-1], refs[-1]
    blocks, copies, rows, _ = out_ref.shape
    _, lag_rows, chans = sums_refs[0].shape
    per_sum = windows // len(sums_refs)
    heads = [decode(sums_ref[6]) for sums_ref in sums_refs]
    levels = [level_of(head[0:1, :]) * (1.0 / (CODE_TOP * windows)) for head in heads]
    stacks = []
    for side in range(2):
        linear = sum(decode(sums_ref[side]) * level for sums_ref, level in zip(sums_refs, levels))
        real, imag = (
            sum(decode(sums_ref[part + side]) for sums_ref in sums_refs) * (per_sum / (CODE_TOP * windows))
            for part in (2, 4)
        )
        stacks.append(linear * (real * real + imag * imag))
    offset = heads[0][1:2, :]
    lane = lax.broadcasted_iota(jnp.int32, (1, chans), 1)
    behind = [jnp.zeros_like(stack) for stack in stacks]
    for steps in range(1, blocks // 2 + 1):
        ahead = steps * (chans // blocks)
        chosen = (offset == steps) & (lane >= ahead)
        behind = [jnp.where(chosen, pltpu.roll(stack, ahead, 1), kept) for stack, kept in zip(stacks, behind)]
    back = stacks[1] + behind[0]
    back = jnp.concatenate([back[row : row + 1, :] for row in reversed(range(lag_rows))], axis=0)
    me = where_ref[0]
    even = (me & 1) == 0
    ahead = stacks[0] + behind[1]
    both = jnp.concatenate([jnp.where(even, ahead, back), jnp.where(even, back, ahead)], axis=0)
    parts = chans // (2 * lag_rows)
    turned = jnp.concatenate([both] * parts, axis=0).T
    unit = lane // lag_rows
    part_of = jnp.where(((unit ^ me) & 1) == 0, unit - me, unit + me + 1) % blocks // 2
    per_block = chans // blocks
    for block in range(blocks):
        piece = jnp.zeros((rows, chans), jnp.float32)
        for part in range(parts):
            begin = block * per_block + part * rows
            piece = jnp.where(part_of == part, turned[begin : begin + rows, :], piece)
        for copy in range(copies):
            out_ref[block, copy, :, :] = piece


def place_kernel(parts_ref, out_ref):
    groups, offset_count, rows, lanes = parts_ref.shape
    half = out_ref.shape[2] // 2
    lag_rows = half // groups
    parts = out_ref.shape[0] // rows
    unit = lax.broadcasted_iota(jnp.int32, (1, lanes), 1) // lag_rows
    for number in range(offset_count):
        pieces = [parts_ref[group, number] for group in range(groups)]
        for part in range(parts):
            sides = [jnp.zeros((rows, lanes), jnp.float32)] * 2
            for group, piece in enumerate(pieces):
                places = ((groups - 1 - group + 2 * part) % groups, (group + 2 * part) % groups)
                sides = [jnp.where(unit == place, piece, side) for place, side in zip(places, sides)]
            for side, value in enumerate(sides):
                value = pltpu.roll(value, (lanes - 2 * part * lag_rows) % lanes, 1) if part else value
                out_ref[part * rows : (part + 1) * rows, number, side * half : (side + 1) * half] = value


def window_shards(spectra, quality, offsets):
    chan_count = lax.axis_size("chan")
    tm_count = lax.axis_size("tm")
    _, windows, band, chans = spectra.shape
    freqs = band * chan_count
    half = LAGS // 2
    lag_rows = half // chan_count
    offset_count = offsets.shape[0]
    piece_rows = 2 * lag_rows // chan_count
    smem = pl.BlockSpec(memory_space=pltpu.SMEM)
    vmem = pl.BlockSpec(memory_space=pltpu.VMEM)
    params = pltpu.CompilerParams(vmem_limit_bytes=VMEM_LIMIT)
    table = jnp.asarray(half_table(freqs, LAGS).reshape(2, chan_count, lag_rows, freqs))
    chan_index = lax.axis_index("chan").astype(jnp.int32)
    tm_index = lax.axis_index("tm").astype(jnp.int32)
    chan_where, tm_where = chan_index.reshape(1), tm_index.reshape(1)

    chan_order, tm_order = partners(chan_count), partners(tm_count)
    kept = pl.BlockSpec(memory_space=pltpu.HBM)
    spectra = pltpu.with_memory_space_constraint(spectra, pltpu.HBM)
    pieces = []
    for part in (chan_order[:2], chan_order[2:]):
        pieces += pl.pallas_call(
            functools.partial(split_kernel, part),
            out_shape=[jax.ShapeDtypeStruct((2, band, chans), spectra.dtype)] * len(part),
            in_specs=[kept],
            out_specs=[pl.BlockSpec(memory_space=pl.ANY)] * len(part),
            scratch_shapes=[pltpu.SemaphoreType.DMA((len(part),))],
            compiler_params=params,
            name="split_windows",
        )(spectra)
    chip_order = chips(chan_count)
    pair_shape = (6 * offset_count - 2, lag_rows, chans)
    own, far = pl.pallas_call(
        functools.partial(window_kernel, chan_order),
        out_shape=[jax.ShapeDtypeStruct((len(chip_order), *pair_shape), jnp.int16)] * 2,
        in_specs=[kept, smem] + [vmem] * (chan_count + 2),
        out_specs=[vmem] * 2,
        scratch_shapes=[
            pltpu.VMEM((freqs, chans), jnp.float32),
            pltpu.VMEM((2, freqs, chans), jnp.bfloat16),
            pltpu.VMEM((freqs, (2 * offset_count - 1) * chans), jnp.bfloat16),
            pltpu.SMEM(offsets.shape, jnp.int32),
            pltpu.SemaphoreType.DMA(()),
        ],
        compiler_params=params,
        name="window_pairs",
    )(pltpu.with_memory_space_constraint(offsets, pltpu.HBM), chan_where, *exchange(pieces, "chan", chan_order), quality, table)
    pairs = pl.pallas_call(
        functools.partial(merge_kernel, offset_count),
        out_shape=[jax.ShapeDtypeStruct(pair_shape, jnp.int16)] * len(chip_order),
        in_specs=[vmem] * 2,
        out_specs=[vmem] * len(chip_order),
        compiler_params=params,
        name="merge_windows",
    )(own, *exchange([far], "chan", [1]))
    sums = pl.pallas_call(
        functools.partial(sum_kernel, tm_order, 1.0 / (CODE_TOP * math.sqrt(freqs))),
        out_shape=[jax.ShapeDtypeStruct((7, lag_rows, chans), jnp.int16)] * tm_count,
        in_specs=[smem] + [vmem] * len(chip_order),
        out_specs=[vmem] * tm_count,
        scratch_shapes=[pltpu.VMEM((offset_count, 7, lag_rows, chans), jnp.int16)],
        compiler_params=params,
        name="sum_windows",
    )(tm_where, *exchange(pairs, "chan", chip_order))
    pieces = pl.pallas_call(
        functools.partial(stack_kernel, windows * tm_count),
        out_shape=jax.ShapeDtypeStruct((chan_count, tm_count, piece_rows, chans), jnp.float32),
        in_specs=[smem] + [vmem] * tm_count,
        out_specs=vmem,
        compiler_params=params,
        name="stack_pairs",
    )(chan_where, *exchange(sums, "tm", tm_order))
    shape = (chan_count * tm_count, piece_rows, chans)
    arrived = lax.all_to_all(pieces.reshape(shape), ("chan", "tm"), 0, 0, tiled=True)
    return pl.pallas_call(
        place_kernel,
        out_shape=jax.ShapeDtypeStruct((CH_DEV, offset_count, LAGS), jnp.float32),
        in_specs=[vmem],
        out_specs=vmem,
        compiler_params=params,
        name="place_lags",
    )(arrived.reshape(chan_count, tm_count, piece_rows, chans))


def shifted(value, axis, steps):
    count = lax.axis_size(axis)
    leading, last = (max(0, -steps), min(count, count - steps))
    return lax.ppermute(value, axis, [(source, source + steps) for source in range(leading, last)])


def lag_table(freq_count, lag_count):
    freq_index = jnp.arange(freq_count, dtype=jnp.int32)[:, None]
    double_lag = (2 * jnp.arange(lag_count, dtype=jnp.int32) - lag_count + 1)[None, :]
    turns = jnp.mod(freq_index * double_lag, 4 * freq_count)
    angles = turns.astype(jnp.float32) * (2.0 * math.pi / (4 * freq_count))
    cosine = jnp.cos(angles)
    sine = jnp.sin(angles)
    upper = jnp.concatenate([cosine, sine], axis=1)
    lower = jnp.concatenate([-sine, cosine], axis=1)
    return jnp.stack([upper, lower]).astype(jnp.bfloat16)


def whiten_parts(real_part, imag_part, magnitude, channel_level, usable):
    factor = usable.astype(jnp.float32)[:, None, :] / (magnitude + 0.5 * (channel_level + 1e-05))
    return jnp.stack([real_part * factor, imag_part * factor]).astype(jnp.bfloat16)


def cross_parts(own_real, own_imag, far_real, far_imag):
    own_real = own_real.astype(jnp.float32)
    own_imag = own_imag.astype(jnp.float32)
    far_real = far_real.astype(jnp.float32)
    far_imag = far_imag.astype(jnp.float32)
    return jnp.stack(
        [own_real * far_real + own_imag * far_imag, own_imag * far_real - own_real * far_imag]
    ).astype(jnp.bfloat16)


def pair_terms(corr_all):
    lag_count = corr_all.shape[-1] // 2
    real_corr = corr_all[..., :lag_count]
    imag_corr = corr_all[..., lag_count:]
    power = real_corr * real_corr + imag_corr * imag_corr
    mean_power = jnp.mean(power, axis=-1, keepdims=True)
    denominator = jnp.sqrt(power + 0.25 * (mean_power + 1e-06))
    return (
        jnp.sum(real_corr, axis=-3),
        jnp.sum(real_corr / denominator, axis=-3),
        jnp.sum(imag_corr / denominator, axis=-3),
    )


def shards(spectra, quality, offsets):
    chan_count = lax.axis_size("chan")
    tm_count = lax.axis_size("tm")
    levels = chan_count.bit_length() - 1
    table_bf = lag_table(F, LAGS)
    inv_root = 1.0 / math.sqrt(F)
    real_part = spectra[0].astype(jnp.float32)
    imag_part = spectra[1].astype(jnp.float32)
    magnitude = jnp.sqrt(real_part * real_part + imag_part * imag_part)
    band_total = lax.psum(jnp.sum(magnitude, axis=1), "chan")
    channel_level = (band_total / F)[:, None, :]
    whitened = whiten_parts(real_part, imag_part, magnitude, channel_level, quality)
    width_all = whitened.shape[3]
    padded = jnp.pad(whitened, ((0, 0), (0, 0), (0, 0), (0, width_all)))
    crossed_list = []
    for offset_index in range(NOFF):
        partner = lax.dynamic_slice_in_dim(padded, offsets[offset_index] * CH_DEV, width_all, 3)
        crossed_list.append(cross_parts(whitened[0], whitened[1], partner[0], partner[1]))
    crossed = jnp.stack(crossed_list, axis=1)
    corr_all = jnp.einsum(
        "cnwfh,cfl->nwhl",
        lax.all_to_all(crossed, "chan", split_axis=4, concat_axis=3, tiled=True),
        table_bf,
        preferred_element_type=jnp.float32,
    )
    linear_sum, real_sum, imag_sum = pair_terms(corr_all * inv_root)
    totals = lax.psum((linear_sum, real_sum, imag_sum), "tm")
    window_count = W_DEV * tm_count
    linear = totals[0] / window_count
    real_phase = totals[1] / window_count
    imag_phase = totals[2] / window_count
    stacks = jnp.transpose(linear * (real_phase * real_phase + imag_phase * imag_phase), (1, 0, 2))
    reverse_part = stacks
    for bit_index in range(levels):
        step_size = 1 << bit_index
        arrived = shifted(reverse_part, "chan", step_size)
        chosen = offsets // step_size % 2 == 1
        reverse_part = jnp.where(chosen[None, :, None], arrived, reverse_part)
    return stacks + jnp.flip(reverse_part, axis=2)


def solution(mesh):
    chan_count, tm_count = mesh.shape["chan"], mesh.shape["tm"]
    by_window = chan_count == W_DEV and tm_count == NOFF
    return jax.shard_map(
        window_shards if by_window else shards,
        mesh=mesh,
        in_specs=(P(None, "tm", "chan", None), P("tm", None), P()),
        out_specs=P("chan", None, None),
        check_vma=False,
    )
```

```python
import functools
import math

import jax
import jax.numpy as jnp
import numpy as np
from jax import lax
from jax.experimental import pallas as pl
from jax.experimental.pallas import tpu as pltpu
from jax.sharding import PartitionSpec as P

F = 2048
LAGS = 256
NOFF = 4
CH_DEV = 16
W_DEV = 8
VMEM_LIMIT = 48 * 1024 * 1024
CODE_TOP = 32767.0
OCTAVE = 256.0
LOWEST = -110.0


def encode(value):
    return jnp.round(value).astype(jnp.int32).astype(jnp.int16)


def decode(code):
    return code.astype(jnp.int32).astype(jnp.float32)


def level_code(peak):
    return jnp.ceil(jnp.maximum(jnp.log2(jnp.maximum(peak, 1e-30)), LOWEST) * OCTAVE) + 1.0


def level_of(code):
    return jnp.exp2(code * (1.0 / OCTAVE))


def half_table(freq_count, lag_count):
    freq_index = np.arange(freq_count, dtype=np.int64)[None, :]
    double_lag = (2 * np.arange(lag_count // 2, lag_count, dtype=np.int64) - lag_count + 1)[:, None]
    turns = np.mod(freq_index * double_lag, 4 * freq_count).astype(np.float32)
    angles = turns * np.float32(2.0 * math.pi / (4 * freq_count))
    return np.concatenate([np.cos(angles), np.sin(angles)]).astype(jnp.bfloat16)


def widest(offs_ref, reach):
    last = offs_ref.shape[0] - 1
    found = last
    for number in reversed(range(last)):
        found = jnp.where(offs_ref[number] == reach, number, found)
    return found


def offset_of(slot, offs_ref, reach):
    last, wide = offs_ref.shape[0] - 1, widest(offs_ref, reach)
    return offs_ref[jnp.where(slot == wide, last, jnp.where(slot == last, wide, slot))]


def window_kernel(order, offs_hbm_ref, where_ref, *refs):
    chan_count = len(order)
    spec_refs, (qual_ref, table_ref) = refs[:chan_count], refs[chan_count : chan_count + 2]
    out_refs = refs[chan_count + 2 : chan_count + 4]
    mag_ref, white_ref, cross_ref, offs_ref, offs_sem = refs[chan_count + 4 :]
    fetch = pltpu.make_async_copy(offs_hbm_ref, offs_ref, offs_sem)
    fetch.start()
    me = where_ref[0]
    _, band, chans = spec_refs[0].shape
    freqs = chan_count * band
    chip_count, blocks, lag_rows, _ = out_refs[0].shape
    offset_count = offs_ref.shape[0]
    half = chan_count * lag_rows
    step = 64

    total = jnp.zeros((8, chans), jnp.float32)
    for number, spec_ref in enumerate(spec_refs):
        for row in range(0, band, step):
            real, imag = (spec_ref[part, row : row + step, :].astype(jnp.float32) for part in range(2))
            square = real * real + imag * imag
            magnitude = square * lax.rsqrt(jnp.maximum(square, 1e-30))
            held = slice(number * band + row, number * band + row + step)
            mag_ref[held, :] = magnitude
            total += jnp.sum(magnitude.reshape(step // 8, 8, chans), axis=0)
    level = jnp.sum(total, axis=0, keepdims=True) * (1.0 / freqs)
    floor = 0.5 * (level + 1e-05)

    for number, spec_ref in enumerate(spec_refs):
        for row in range(0, band, step):
            held = slice(number * band + row, number * band + row + step)
            factor = pl.reciprocal(mag_ref[held, :] + floor, approx=True)
            for part in range(2):
                value = spec_ref[part, row : row + step, :].astype(jnp.float32) * factor
                white_ref[part, held, :] = value.astype(jnp.bfloat16)

    lane = lax.broadcasted_iota(jnp.int32, (1, chans), 1)
    line = lax.broadcasted_iota(jnp.int32, (lag_rows, chans), 0)
    usable = qual_ref[pl.ds(me, 1), :].astype(jnp.float32)
    levels = jnp.zeros((lag_rows, chans), jnp.float32)
    groups = [k ^ core for core in range(2) for k in chips(chan_count)]
    fetch.wait()
    per_band = table_ref.shape[0] // chan_count
    chunks = [(me ^ k) * per_band + chunk for k in order for chunk in range(per_band)]
    table = jnp.concatenate(
        [
            jnp.concatenate([table_ref[chunk, side, me ^ group] for side in range(2) for group in groups], axis=0)
            for chunk in chunks
        ],
        axis=1,
    )
    turns = [chans - offset_of(number, offs_ref, chan_count // 2) * (chans // chan_count) for number in range(offset_count)]
    for row in range(0, freqs, step):
        own = [white_ref[part, row : row + step, :] for part in range(2)]
        own_real, own_imag = (value.astype(jnp.float32) for value in own)
        for number, turn in enumerate(turns):
            far_real, far_imag = (pltpu.roll(value, turn, 1).astype(jnp.float32) for value in own)
            real = own_real * far_real + own_imag * far_imag
            imag = own_imag * far_real - own_real * far_imag
            cross_ref[number, 0, row : row + step, :] = real.astype(jnp.bfloat16)
            cross_ref[number, 1, row : row + step, :] = imag.astype(jnp.bfloat16)

    for number, turn in enumerate(turns):
        both = jnp.concatenate([cross_ref[number, 0], cross_ref[number, 1]], axis=1)
        sums = jnp.dot(table, both, preferred_element_type=jnp.float32)
        cos_real, sin_real = sums[:half, :chans], sums[half:, :chans]
        cos_imag, sin_imag = sums[:half, chans:], sums[half:, chans:]
        corr = (
            (cos_real - sin_imag, sin_real + cos_imag),
            (cos_real + sin_imag, cos_imag - sin_real),
        )
        power = [real * real + imag * imag for real, imag in corr]
        mean_power = jnp.sum(power[0] + power[1], axis=0, keepdims=True) * (1.0 / (2 * half))
        extra = 0.25 * (mean_power + 1e-06 * freqs)
        peak = jnp.max(jnp.maximum(jnp.abs(corr[0][0]), jnp.abs(corr[1][0])), axis=0, keepdims=True)
        code = level_code(peak)
        keep = jnp.where(lane < turn, usable * pltpu.roll(usable, turn, 1), 0.0) * CODE_TOP
        upscale = keep / level_of(code)
        inverse = [lax.rsqrt(side + extra) * keep for side in power]
        kinds = [
            [real * upscale for real, _ in corr],
            [real * scale for (real, _), scale in zip(corr, inverse)],
            [imag * scale for (_, imag), scale in zip(corr, inverse)],
        ]
        if number == offset_count - 1:
            code = jnp.where(lane < chans // 2, code, pltpu.roll(code, chans // 2, 1))
            kinds = [[jnp.where(lane < chans // 2, ahead, pltpu.roll(back, chans // 2, 1))] for ahead, back in kinds]
        levels = jnp.where(line == number, code, levels)
        for place, value in enumerate(value for kind in kinds for value in kind):
            coded = encode(value).reshape(chan_count, lag_rows, chans)
            for core in range(2):
                rows = slice(core * chip_count, (core + 1) * chip_count)
                out_refs[core][:, 6 * number + place, :, :] = coded[rows]
    for number in range(offset_count):
        levels = jnp.where(line == offset_count + number, offs_ref[number].astype(jnp.float32), levels)
    wide = widest(offs_ref, chan_count // 2).astype(jnp.float32)
    levels = jnp.where(line == 2 * offset_count, wide, levels)
    for out_ref in out_refs:
        for chip in range(chip_count):
            out_ref[chip, blocks - 1, :, :] = encode(levels)


def merge_kernel(slots, own_ref, far_ref, *out_refs):
    blocks = own_ref.shape[1]
    for chip, out_ref in enumerate(out_refs):
        codes = [decode(ref[chip, blocks - 1]) for ref in (own_ref, far_ref)]
        levels = [level_of(code) for code in codes]
        code = level_code(levels[0] + levels[1])
        shares = [level / level_of(code) for level in levels]
        line = lax.broadcasted_iota(jnp.int32, code.shape, 0)
        out_ref[blocks - 1, :, :] = encode(jnp.where(line < slots, code, codes[0]))
        for block in range(blocks - 1):
            number, part = divmod(block, 6)
            linear = part < (2 if blocks - 1 - 6 * number > 3 else 1)
            own, far = decode(own_ref[chip, block]), decode(far_ref[chip, block])
            if linear:
                total = own * shares[0][number : number + 1, :] + far * shares[1][number : number + 1, :]
            else:
                total = (own + far) * 0.5
            out_ref[block, :, :] = encode(total)


def sum_kernel(order, scale, where_ref, *refs):
    code_refs, out_refs, held_ref = refs[: -len(order) - 1], refs[-len(order) - 1 : -1], refs[-1]
    blocks, _, chans = code_refs[0].shape
    slots = held_ref.shape[0]
    heads = [decode(codes_ref[blocks - 1]) for codes_ref in code_refs]
    levels = [level_of(head) * scale for head in heads]
    offsets = [heads[0][slots + number : slots + number + 1, :] for number in range(slots)]
    wide = heads[0][2 * slots : 2 * slots + 1, :]
    low = lax.broadcasted_iota(jnp.int32, (1, chans), 1) < chans // 2
    all_sums = []
    for number in range(slots):
        sides = 2 if number < slots - 1 else 1
        own = [level[number : number + 1, :] for level in levels]
        sums = []
        for place in range(3 * sides):
            codes = [decode(codes_ref[6 * number + place]) for codes_ref in code_refs]
            if place < sides:
                sums.append(sum(code * level for code, level in zip(codes, own)))
            else:
                sums.append(sum(codes) * (1.0 / len(code_refs)))
        if sides == 1:
            sums = [
                jnp.where(low, side, 0.0) for value in sums for side in (value, pltpu.roll(value, chans // 2, 1))
            ]
        all_sums.append(sums)
    line = lax.broadcasted_iota(jnp.int32, levels[0].shape, 0)
    last = slots - 1
    for number in range(slots):
        sums = all_sums[number]
        for other in range(last) if number == last else [last]:
            swap = wide == min(number, other)
            sums = [jnp.where(swap, value, kept) for value, kept in zip(all_sums[other], sums)]
        peak = jnp.max(jnp.maximum(jnp.abs(sums[0]), jnp.abs(sums[1])), axis=0, keepdims=True)
        code = level_code(peak)
        upscale = CODE_TOP / level_of(code)
        head = jnp.where(line == 0, code, offsets[number])
        for part, value in enumerate([sums[0] * upscale, sums[1] * upscale, *sums[2:], head]):
            held_ref[number, part, :, :] = encode(value)
    for k, out_ref in zip(order, out_refs):
        out_ref[...] = held_ref[where_ref[0] ^ k]


def partners(count):
    return sorted(range(1, count), key=lambda k: (-(k >> 1).bit_count(), k & 1, k)) + [0]


def chips(count):
    return sorted(range(2, count, 2), key=lambda k: (k.bit_count(), k)) + [0]


def exchange(pieces, axis, order):
    count = lax.axis_size(axis)
    return [
        lax.ppermute(piece, axis, [(source, source ^ k) for source in range(count)]) if k else piece
        for k, piece in zip(order, pieces)
    ]


def split_kernel(order, spec_ref, *refs):
    out_refs, sems = refs[:-1], refs[-1]
    me = lax.axis_index("chan").astype(jnp.int32)
    copies = [
        pltpu.make_async_copy(spec_ref.at[:, me ^ k], out_ref, sems.at[number])
        for number, (k, out_ref) in enumerate(zip(order, out_refs))
    ]
    for copy in copies:
        copy.start()
    for copy in copies:
        copy.wait()


def stack_kernel(windows, where_ref, *refs):
    sums_refs, out_ref = refs[:-1], refs[-1]
    blocks, copies, rows, _ = out_ref.shape
    _, lag_rows, chans = sums_refs[0].shape
    per_sum = windows // len(sums_refs)
    heads = [decode(sums_ref[6]) for sums_ref in sums_refs]
    levels = [level_of(head[0:1, :]) * (1.0 / (CODE_TOP * windows)) for head in heads]
    stacks = []
    for side in range(2):
        linear = sum(decode(sums_ref[side]) * level for sums_ref, level in zip(sums_refs, levels))
        real, imag = (
            sum(decode(sums_ref[part + side]) for sums_ref in sums_refs) * (per_sum / (CODE_TOP * windows))
            for part in (2, 4)
        )
        stacks.append(linear * (real * real + imag * imag))
    offset = heads[0][1:2, :]
    lane = lax.broadcasted_iota(jnp.int32, (1, chans), 1)
    behind = [jnp.zeros_like(stack) for stack in stacks]
    for steps in range(1, blocks // 2 + 1):
        ahead = steps * (chans // blocks)
        chosen = (offset == steps) & (lane >= ahead)
        behind = [jnp.where(chosen, pltpu.roll(stack, ahead, 1), kept) for stack, kept in zip(stacks, behind)]
    back = stacks[1] + behind[0]
    back = jnp.concatenate([back[row : row + 1, :] for row in reversed(range(lag_rows))], axis=0)
    me = where_ref[0]
    even = (me & 1) == 0
    ahead = stacks[0] + behind[1]
    both = jnp.concatenate([jnp.where(even, ahead, back), jnp.where(even, back, ahead)], axis=0)
    parts = chans // (2 * lag_rows)
    turned = jnp.concatenate([both] * parts, axis=0).T
    unit = lane // lag_rows
    part_of = jnp.where(((unit ^ me) & 1) == 0, unit - me, unit + me + 1) % blocks // 2
    per_block = chans // blocks
    for block in range(blocks):
        piece = jnp.zeros((rows, chans), jnp.float32)
        for part in range(parts):
            begin = block * per_block + part * rows
            piece = jnp.where(part_of == part, turned[begin : begin + rows, :], piece)
        for copy in range(copies):
            out_ref[block, copy, :, :] = piece


def place_kernel(parts_ref, out_ref):
    groups, offset_count, rows, lanes = parts_ref.shape
    half = out_ref.shape[2] // 2
    lag_rows = half // groups
    parts = out_ref.shape[0] // rows
    unit = lax.broadcasted_iota(jnp.int32, (1, lanes), 1) // lag_rows
    for number in range(offset_count):
        pieces = [parts_ref[group, number] for group in range(groups)]
        for part in range(parts):
            sides = [jnp.zeros((rows, lanes), jnp.float32)] * 2
            for group, piece in enumerate(pieces):
                places = ((groups - 1 - group + 2 * part) % groups, (group + 2 * part) % groups)
                sides = [jnp.where(unit == place, piece, side) for place, side in zip(places, sides)]
            for side, value in enumerate(sides):
                value = pltpu.roll(value, (lanes - 2 * part * lag_rows) % lanes, 1) if part else value
                out_ref[part * rows : (part + 1) * rows, number, side * half : (side + 1) * half] = value


def window_shards(spectra, quality, offsets):
    chan_count = lax.axis_size("chan")
    tm_count = lax.axis_size("tm")
    _, windows, band, chans = spectra.shape
    freqs = band * chan_count
    half = LAGS // 2
    lag_rows = half // chan_count
    offset_count = offsets.shape[0]
    piece_rows = 2 * lag_rows // chan_count
    smem = pl.BlockSpec(memory_space=pltpu.SMEM)
    vmem = pl.BlockSpec(memory_space=pltpu.VMEM)
    params = pltpu.CompilerParams(vmem_limit_bytes=VMEM_LIMIT)
    table = half_table(freqs, LAGS).reshape(2, chan_count, lag_rows, freqs // 128, 128)
    table = jnp.asarray(np.ascontiguousarray(table.transpose(3, 0, 1, 2, 4)))
    chan_index = lax.axis_index("chan").astype(jnp.int32)
    tm_index = lax.axis_index("tm").astype(jnp.int32)
    chan_where, tm_where = chan_index.reshape(1), tm_index.reshape(1)

    chan_order, tm_order = partners(chan_count), partners(tm_count)
    kept = pl.BlockSpec(memory_space=pltpu.HBM)
    spectra = pltpu.with_memory_space_constraint(spectra, pltpu.HBM)
    pieces = []
    for part in (chan_order[:2], chan_order[2:]):
        pieces += pl.pallas_call(
            functools.partial(split_kernel, part),
            out_shape=[jax.ShapeDtypeStruct((2, band, chans), spectra.dtype)] * len(part),
            in_specs=[kept],
            out_specs=[pl.BlockSpec(memory_space=pl.ANY)] * len(part),
            scratch_shapes=[pltpu.SemaphoreType.DMA((len(part),))],
            compiler_params=params,
            name="split_windows",
        )(spectra)
    chip_order = chips(chan_count)
    pair_shape = (6 * offset_count - 2, lag_rows, chans)
    own, far = pl.pallas_call(
        functools.partial(window_kernel, chan_order),
        out_shape=[jax.ShapeDtypeStruct((len(chip_order), *pair_shape), jnp.int16)] * 2,
        in_specs=[kept, smem] + [vmem] * (chan_count + 2),
        out_specs=[vmem] * 2,
        scratch_shapes=[
            pltpu.VMEM((freqs, chans), jnp.float32),
            pltpu.VMEM((2, freqs, chans), jnp.bfloat16),
            pltpu.VMEM((offset_count, 2, freqs, chans), jnp.bfloat16),
            pltpu.SMEM(offsets.shape, jnp.int32),
            pltpu.SemaphoreType.DMA(()),
        ],
        compiler_params=params,
        name="window_pairs",
    )(pltpu.with_memory_space_constraint(offsets, pltpu.HBM), chan_where, *exchange(pieces, "chan", chan_order), quality, table)
    pairs = pl.pallas_call(
        functools.partial(merge_kernel, offset_count),
        out_shape=[jax.ShapeDtypeStruct(pair_shape, jnp.int16)] * len(chip_order),
        in_specs=[vmem] * 2,
        out_specs=[vmem] * len(chip_order),
        compiler_params=params,
        name="merge_windows",
    )(own, *exchange([far], "chan", [1]))
    sums = pl.pallas_call(
        functools.partial(sum_kernel, tm_order, 1.0 / (CODE_TOP * math.sqrt(freqs))),
        out_shape=[jax.ShapeDtypeStruct((7, lag_rows, chans), jnp.int16)] * tm_count,
        in_specs=[smem] + [vmem] * len(chip_order),
        out_specs=[vmem] * tm_count,
        scratch_shapes=[pltpu.VMEM((offset_count, 7, lag_rows, chans), jnp.int16)],
        compiler_params=params,
        name="sum_windows",
    )(tm_where, *exchange(pairs, "chan", chip_order))
    pieces = pl.pallas_call(
        functools.partial(stack_kernel, windows * tm_count),
        out_shape=jax.ShapeDtypeStruct((chan_count, tm_count, piece_rows, chans), jnp.float32),
        in_specs=[smem] + [vmem] * tm_count,
        out_specs=vmem,
        compiler_params=params,
        name="stack_pairs",
    )(chan_where, *exchange(sums, "tm", tm_order))
    shape = (chan_count * tm_count, piece_rows, chans)
    arrived = lax.all_to_all(pieces.reshape(shape), ("chan", "tm"), 0, 0, tiled=True)
    return pl.pallas_call(
        place_kernel,
        out_shape=jax.ShapeDtypeStruct((CH_DEV, offset_count, LAGS), jnp.float32),
        in_specs=[vmem],
        out_specs=vmem,
        compiler_params=params,
        name="place_lags",
    )(arrived.reshape(chan_count, tm_count, piece_rows, chans))


def shifted(value, axis, steps):
    count = lax.axis_size(axis)
    leading, last = (max(0, -steps), min(count, count - steps))
    return lax.ppermute(value, axis, [(source, source + steps) for source in range(leading, last)])


def lag_table(freq_count, lag_count):
    freq_index = jnp.arange(freq_count, dtype=jnp.int32)[:, None]
    double_lag = (2 * jnp.arange(lag_count, dtype=jnp.int32) - lag_count + 1)[None, :]
    turns = jnp.mod(freq_index * double_lag, 4 * freq_count)
    angles = turns.astype(jnp.float32) * (2.0 * math.pi / (4 * freq_count))
    cosine = jnp.cos(angles)
    sine = jnp.sin(angles)
    upper = jnp.concatenate([cosine, sine], axis=1)
    lower = jnp.concatenate([-sine, cosine], axis=1)
    return jnp.stack([upper, lower]).astype(jnp.bfloat16)


def whiten_parts(real_part, imag_part, magnitude, channel_level, usable):
    factor = usable.astype(jnp.float32)[:, None, :] / (magnitude + 0.5 * (channel_level + 1e-05))
    return jnp.stack([real_part * factor, imag_part * factor]).astype(jnp.bfloat16)


def cross_parts(own_real, own_imag, far_real, far_imag):
    own_real = own_real.astype(jnp.float32)
    own_imag = own_imag.astype(jnp.float32)
    far_real = far_real.astype(jnp.float32)
    far_imag = far_imag.astype(jnp.float32)
    return jnp.stack(
        [own_real * far_real + own_imag * far_imag, own_imag * far_real - own_real * far_imag]
    ).astype(jnp.bfloat16)


def pair_terms(corr_all):
    lag_count = corr_all.shape[-1] // 2
    real_corr = corr_all[..., :lag_count]
    imag_corr = corr_all[..., lag_count:]
    power = real_corr * real_corr + imag_corr * imag_corr
    mean_power = jnp.mean(power, axis=-1, keepdims=True)
    denominator = jnp.sqrt(power + 0.25 * (mean_power + 1e-06))
    return (
        jnp.sum(real_corr, axis=-3),
        jnp.sum(real_corr / denominator, axis=-3),
        jnp.sum(imag_corr / denominator, axis=-3),
    )


def shards(spectra, quality, offsets):
    chan_count = lax.axis_size("chan")
    tm_count = lax.axis_size("tm")
    levels = chan_count.bit_length() - 1
    table_bf = lag_table(F, LAGS)
    inv_root = 1.0 / math.sqrt(F)
    real_part = spectra[0].astype(jnp.float32)
    imag_part = spectra[1].astype(jnp.float32)
    magnitude = jnp.sqrt(real_part * real_part + imag_part * imag_part)
    band_total = lax.psum(jnp.sum(magnitude, axis=1), "chan")
    channel_level = (band_total / F)[:, None, :]
    whitened = whiten_parts(real_part, imag_part, magnitude, channel_level, quality)
    width_all = whitened.shape[3]
    padded = jnp.pad(whitened, ((0, 0), (0, 0), (0, 0), (0, width_all)))
    crossed_list = []
    for offset_index in range(NOFF):
        partner = lax.dynamic_slice_in_dim(padded, offsets[offset_index] * CH_DEV, width_all, 3)
        crossed_list.append(cross_parts(whitened[0], whitened[1], partner[0], partner[1]))
    crossed = jnp.stack(crossed_list, axis=1)
    corr_all = jnp.einsum(
        "cnwfh,cfl->nwhl",
        lax.all_to_all(crossed, "chan", split_axis=4, concat_axis=3, tiled=True),
        table_bf,
        preferred_element_type=jnp.float32,
    )
    linear_sum, real_sum, imag_sum = pair_terms(corr_all * inv_root)
    totals = lax.psum((linear_sum, real_sum, imag_sum), "tm")
    window_count = W_DEV * tm_count
    linear = totals[0] / window_count
    real_phase = totals[1] / window_count
    imag_phase = totals[2] / window_count
    stacks = jnp.transpose(linear * (real_phase * real_phase + imag_phase * imag_phase), (1, 0, 2))
    reverse_part = stacks
    for bit_index in range(levels):
        step_size = 1 << bit_index
        arrived = shifted(reverse_part, "chan", step_size)
        chosen = offsets // step_size % 2 == 1
        reverse_part = jnp.where(chosen[None, :, None], arrived, reverse_part)
    return stacks + jnp.flip(reverse_part, axis=2)


def solution(mesh):
    chan_count, tm_count = mesh.shape["chan"], mesh.shape["tm"]
    by_window = chan_count == W_DEV and tm_count == NOFF
    return jax.shard_map(
        window_shards if by_window else shards,
        mesh=mesh,
        in_specs=(P(None, "tm", "chan", None), P("tm", None), P()),
        out_specs=P("chan", None, None),
        check_vma=False,
    )
```

```python
import functools
import math

import jax
import jax.numpy as jnp
import numpy as np
from jax import lax
from jax.experimental import pallas as pl
from jax.experimental.pallas import tpu as pltpu
from jax.sharding import PartitionSpec as P

F = 2048
LAGS = 256
NOFF = 4
CH_DEV = 16
W_DEV = 8
VMEM_LIMIT = 48 * 1024 * 1024
CODE_TOP = 32767.0
OCTAVE = 256.0
LOWEST = -110.0


def encode(value):
    return jnp.round(value).astype(jnp.int32).astype(jnp.int16)


def decode(code):
    return code.astype(jnp.int32).astype(jnp.float32)


def level_code(peak):
    return jnp.ceil(jnp.maximum(jnp.log2(jnp.maximum(peak, 1e-30)), LOWEST) * OCTAVE) + 1.0


def level_of(code):
    return jnp.exp2(code * (1.0 / OCTAVE))


def half_table(freq_count, lag_count):
    freq_index = np.arange(freq_count, dtype=np.int64)[None, :]
    double_lag = (2 * np.arange(lag_count // 2, lag_count, dtype=np.int64) - lag_count + 1)[:, None]
    turns = np.mod(freq_index * double_lag, 4 * freq_count).astype(np.float32)
    angles = turns * np.float32(2.0 * math.pi / (4 * freq_count))
    return np.concatenate([np.cos(angles), np.sin(angles)]).astype(jnp.bfloat16)


def widest(offs_ref, reach):
    last = offs_ref.shape[0] - 1
    found = last
    for number in reversed(range(last)):
        found = jnp.where(offs_ref[number] == reach, number, found)
    return found


def offset_of(slot, offs_ref, reach):
    last, wide = offs_ref.shape[0] - 1, widest(offs_ref, reach)
    return offs_ref[jnp.where(slot == wide, last, jnp.where(slot == last, wide, slot))]


def window_kernel(order, offs_hbm_ref, where_ref, *refs):
    chan_count = len(order)
    spec_refs, (qual_ref, table_ref) = refs[:chan_count], refs[chan_count : chan_count + 2]
    out_refs = refs[chan_count + 2 : chan_count + 4]
    mag_ref, white_ref, cross_ref, offs_ref, offs_sem = refs[chan_count + 4 :]
    fetch = pltpu.make_async_copy(offs_hbm_ref, offs_ref, offs_sem)
    fetch.start()
    me = where_ref[0]
    _, band, chans = spec_refs[0].shape
    freqs = chan_count * band
    chip_count, blocks, lag_rows, _ = out_refs[0].shape
    offset_count = offs_ref.shape[0]
    half = chan_count * lag_rows
    step = 64

    total = jnp.zeros((8, chans), jnp.float32)
    for number, spec_ref in enumerate(spec_refs):
        for row in range(0, band, step):
            real, imag = (spec_ref[part, row : row + step, :].astype(jnp.float32) for part in range(2))
            square = real * real + imag * imag
            magnitude = square * lax.rsqrt(jnp.maximum(square, 1e-30))
            held = slice(number * band + row, number * band + row + step)
            mag_ref[held, :] = magnitude
            total += jnp.sum(magnitude.reshape(step // 8, 8, chans), axis=0)
    level = jnp.sum(total, axis=0, keepdims=True) * (1.0 / freqs)
    floor = 0.5 * (level + 1e-05)

    for number, spec_ref in enumerate(spec_refs):
        for row in range(0, band, step):
            held = slice(number * band + row, number * band + row + step)
            factor = pl.reciprocal(mag_ref[held, :] + floor, approx=True)
            for part in range(2):
                value = spec_ref[part, row : row + step, :].astype(jnp.float32) * factor
                white_ref[part, held, :] = value.astype(jnp.bfloat16)

    lane = lax.broadcasted_iota(jnp.int32, (1, chans), 1)
    line = lax.broadcasted_iota(jnp.int32, (lag_rows, chans), 0)
    usable = qual_ref[pl.ds(me, 1), :].astype(jnp.float32)
    levels = jnp.zeros((lag_rows, chans), jnp.float32)
    groups = [k ^ core for core in range(2) for k in chips(chan_count)]
    fetch.wait()
    per_band = table_ref.shape[0] // chan_count
    chunks = [(me ^ k) * per_band + chunk for k in order for chunk in range(per_band)]
    table = jnp.concatenate(
        [
            jnp.concatenate([table_ref[chunk, side, me ^ group] for side in range(2) for group in groups], axis=0)
            for chunk in chunks
        ],
        axis=1,
    )
    turns = [chans - offset_of(number, offs_ref, chan_count // 2) * (chans // chan_count) for number in range(offset_count)]
    for row in range(0, freqs, step):
        own = [white_ref[part, row : row + step, :] for part in range(2)]
        own_real, own_imag = (value.astype(jnp.float32) for value in own)
        for number, turn in enumerate(turns):
            far_real, far_imag = (pltpu.roll(value, turn, 1).astype(jnp.float32) for value in own)
            real = own_real * far_real + own_imag * far_imag
            imag = own_imag * far_real - own_real * far_imag
            cross_ref[number, 0, row : row + step, :] = real.astype(jnp.bfloat16)
            cross_ref[number, 1, row : row + step, :] = imag.astype(jnp.bfloat16)

    for number, turn in enumerate(turns):
        both = jnp.concatenate([cross_ref[number, 0], cross_ref[number, 1]], axis=1)
        sums = jnp.dot(table, both, preferred_element_type=jnp.float32)
        cos_real, sin_real = sums[:half, :chans], sums[half:, :chans]
        cos_imag, sin_imag = sums[:half, chans:], sums[half:, chans:]
        corr = (
            (cos_real - sin_imag, sin_real + cos_imag),
            (cos_real + sin_imag, cos_imag - sin_real),
        )
        power = [real * real + imag * imag for real, imag in corr]
        mean_power = jnp.sum(power[0] + power[1], axis=0, keepdims=True) * (1.0 / (2 * half))
        extra = 0.25 * (mean_power + 1e-06 * freqs)
        peak = jnp.max(jnp.maximum(jnp.abs(corr[0][0]), jnp.abs(corr[1][0])), axis=0, keepdims=True)
        code = level_code(peak)
        keep = jnp.where(lane < turn, usable * pltpu.roll(usable, turn, 1), 0.0) * CODE_TOP
        upscale = keep / level_of(code)
        inverse = [lax.rsqrt(side + extra) * keep for side in power]
        kinds = [
            [real * upscale for real, _ in corr],
            [real * scale for (real, _), scale in zip(corr, inverse)],
            [imag * scale for (_, imag), scale in zip(corr, inverse)],
        ]
        if number == offset_count - 1:
            code = jnp.where(lane < chans // 2, code, pltpu.roll(code, chans // 2, 1))
            kinds = [[jnp.where(lane < chans // 2, ahead, pltpu.roll(back, chans // 2, 1))] for ahead, back in kinds]
        levels = jnp.where(line == number, code, levels)
        for place, value in enumerate(value for kind in kinds for value in kind):
            coded = encode(value).reshape(chan_count, lag_rows, chans)
            for core in range(2):
                rows = slice(core * chip_count, (core + 1) * chip_count)
                out_refs[core][:, 6 * number + place, :, :] = coded[rows]
    for number in range(offset_count):
        levels = jnp.where(line == offset_count + number, offs_ref[number].astype(jnp.float32), levels)
    wide = widest(offs_ref, chan_count // 2).astype(jnp.float32)
    levels = jnp.where(line == 2 * offset_count, wide, levels)
    for out_ref in out_refs:
        for chip in range(chip_count):
            out_ref[chip, blocks - 1, :, :] = encode(levels)


def merge_kernel(slots, own_ref, far_ref, *out_refs):
    blocks = own_ref.shape[1]
    for chip, out_ref in enumerate(out_refs):
        codes = [decode(ref[chip, blocks - 1]) for ref in (own_ref, far_ref)]
        levels = [level_of(code) for code in codes]
        code = level_code(levels[0] + levels[1])
        shares = [level / level_of(code) for level in levels]
        line = lax.broadcasted_iota(jnp.int32, code.shape, 0)
        out_ref[blocks - 1, :, :] = encode(jnp.where(line < slots, code, codes[0]))
        for block in range(blocks - 1):
            number, part = divmod(block, 6)
            linear = part < (2 if blocks - 1 - 6 * number > 3 else 1)
            own, far = decode(own_ref[chip, block]), decode(far_ref[chip, block])
            if linear:
                total = own * shares[0][number : number + 1, :] + far * shares[1][number : number + 1, :]
            else:
                total = (own + far) * 0.5
            out_ref[block, :, :] = encode(total)


def sum_kernel(order, scale, where_ref, *refs):
    code_refs, out_refs, held_ref = refs[: -len(order) - 1], refs[-len(order) - 1 : -1], refs[-1]
    blocks, _, chans = code_refs[0].shape
    slots = held_ref.shape[0]
    heads = [decode(codes_ref[blocks - 1]) for codes_ref in code_refs]
    levels = [level_of(head) * scale for head in heads]
    offsets = [heads[0][slots + number : slots + number + 1, :] for number in range(slots)]
    wide = heads[0][2 * slots : 2 * slots + 1, :]
    low = lax.broadcasted_iota(jnp.int32, (1, chans), 1) < chans // 2
    all_sums = []
    for number in range(slots):
        sides = 2 if number < slots - 1 else 1
        own = [level[number : number + 1, :] for level in levels]
        sums = []
        for place in range(3 * sides):
            codes = [decode(codes_ref[6 * number + place]) for codes_ref in code_refs]
            if place < sides:
                sums.append(sum(code * level for code, level in zip(codes, own)))
            else:
                sums.append(sum(codes) * (1.0 / len(code_refs)))
        if sides == 1:
            sums = [
                jnp.where(low, side, 0.0) for value in sums for side in (value, pltpu.roll(value, chans // 2, 1))
            ]
        all_sums.append(sums)
    line = lax.broadcasted_iota(jnp.int32, levels[0].shape, 0)
    last = slots - 1
    for number in range(slots):
        sums = all_sums[number]
        for other in range(last) if number == last else [last]:
            swap = wide == min(number, other)
            sums = [jnp.where(swap, value, kept) for value, kept in zip(all_sums[other], sums)]
        peak = jnp.max(jnp.maximum(jnp.abs(sums[0]), jnp.abs(sums[1])), axis=0, keepdims=True)
        code = level_code(peak)
        upscale = CODE_TOP / level_of(code)
        head = jnp.where(line == 0, code, offsets[number])
        for part, value in enumerate([sums[0] * upscale, sums[1] * upscale, *sums[2:], head]):
            held_ref[number, part, :, :] = encode(value)
    for k, out_ref in zip(order, out_refs):
        out_ref[...] = held_ref[where_ref[0] ^ k]


def partners(count):
    return sorted(range(1, count), key=lambda k: (-(k >> 1).bit_count(), k & 1, k)) + [0]


def chips(count):
    return sorted(range(2, count, 2), key=lambda k: (k.bit_count(), k)) + [0]


def exchange(pieces, axis, order):
    count = lax.axis_size(axis)
    return [
        lax.ppermute(piece, axis, [(source, source ^ k) for source in range(count)]) if k else piece
        for k, piece in zip(order, pieces)
    ]


def split_kernel(order, spec_ref, *refs):
    out_refs, sems = refs[:-1], refs[-1]
    me = lax.axis_index("chan").astype(jnp.int32)
    copies = [
        pltpu.make_async_copy(spec_ref.at[:, me ^ k], out_ref, sems.at[number])
        for number, (k, out_ref) in enumerate(zip(order, out_refs))
    ]
    for copy in copies:
        copy.start()
    for copy in copies:
        copy.wait()


def stack_kernel(windows, where_ref, *refs):
    sums_refs, out_ref = refs[:-1], refs[-1]
    copies, blocks, rows, _ = out_ref.shape
    _, lag_rows, chans = sums_refs[0].shape
    per_sum = windows // len(sums_refs)
    heads = [decode(sums_ref[6]) for sums_ref in sums_refs]
    levels = [level_of(head[0:1, :]) * (1.0 / (CODE_TOP * windows)) for head in heads]
    stacks = []
    for side in range(2):
        linear = sum(decode(sums_ref[side]) * level for sums_ref, level in zip(sums_refs, levels))
        real, imag = (
            sum(decode(sums_ref[part + side]) for sums_ref in sums_refs) * (per_sum / (CODE_TOP * windows))
            for part in (2, 4)
        )
        stacks.append(linear * (real * real + imag * imag))
    offset = heads[0][1:2, :]
    lane = lax.broadcasted_iota(jnp.int32, (1, chans), 1)
    behind = [jnp.zeros_like(stack) for stack in stacks]
    for steps in range(1, blocks // 2 + 1):
        ahead = steps * (chans // blocks)
        chosen = (offset == steps) & (lane >= ahead)
        behind = [jnp.where(chosen, pltpu.roll(stack, ahead, 1), kept) for stack, kept in zip(stacks, behind)]
    back = stacks[1] + behind[0]
    back = jnp.concatenate([back[row : row + 1, :] for row in reversed(range(lag_rows))], axis=0)
    me = where_ref[0]
    even = (me & 1) == 0
    ahead = stacks[0] + behind[1]
    both = jnp.concatenate([jnp.where(even, ahead, back), jnp.where(even, back, ahead)], axis=0)
    parts = chans // (2 * lag_rows)
    turned = jnp.concatenate([both] * parts, axis=0).T
    unit = lane // lag_rows
    part_of = jnp.where(((unit ^ me) & 1) == 0, unit - me, unit + me + 1) % blocks // 2
    per_block = chans // blocks
    for block in range(blocks):
        piece = jnp.zeros((rows, chans), jnp.float32)
        for part in range(parts):
            begin = block * per_block + part * rows
            piece = jnp.where(part_of == part, turned[begin : begin + rows, :], piece)
        for copy in range(copies):
            out_ref[copy, block, :, :] = piece


def place_kernel(parts_ref, out_ref):
    offset_count, groups, rows, lanes = parts_ref.shape
    half = out_ref.shape[2] // 2
    lag_rows = half // groups
    parts = out_ref.shape[0] // rows
    unit = lax.broadcasted_iota(jnp.int32, (1, lanes), 1) // lag_rows
    for number in range(offset_count):
        pieces = [parts_ref[number, group] for group in range(groups)]
        for part in range(parts):
            sides = [jnp.zeros((rows, lanes), jnp.float32)] * 2
            for group, piece in enumerate(pieces):
                places = ((groups - 1 - group + 2 * part) % groups, (group + 2 * part) % groups)
                sides = [jnp.where(unit == place, piece, side) for place, side in zip(places, sides)]
            for side, value in enumerate(sides):
                value = pltpu.roll(value, (lanes - 2 * part * lag_rows) % lanes, 1) if part else value
                out_ref[part * rows : (part + 1) * rows, number, side * half : (side + 1) * half] = value


def window_shards(spectra, quality, offsets):
    chan_count = lax.axis_size("chan")
    tm_count = lax.axis_size("tm")
    _, windows, band, chans = spectra.shape
    freqs = band * chan_count
    half = LAGS // 2
    lag_rows = half // chan_count
    offset_count = offsets.shape[0]
    piece_rows = 2 * lag_rows // chan_count
    smem = pl.BlockSpec(memory_space=pltpu.SMEM)
    vmem = pl.BlockSpec(memory_space=pltpu.VMEM)
    params = pltpu.CompilerParams(vmem_limit_bytes=VMEM_LIMIT)
    table = half_table(freqs, LAGS).reshape(2, chan_count, lag_rows, freqs // 128, 128)
    table = jnp.asarray(np.ascontiguousarray(table.transpose(3, 0, 1, 2, 4)))
    chan_index = lax.axis_index("chan").astype(jnp.int32)
    tm_index = lax.axis_index("tm").astype(jnp.int32)
    chan_where, tm_where = chan_index.reshape(1), tm_index.reshape(1)

    chan_order, tm_order = partners(chan_count), partners(tm_count)
    kept = pl.BlockSpec(memory_space=pltpu.HBM)
    spectra = pltpu.with_memory_space_constraint(spectra, pltpu.HBM)
    pieces = []
    for part in (chan_order[:2], chan_order[2:]):
        pieces += pl.pallas_call(
            functools.partial(split_kernel, part),
            out_shape=[jax.ShapeDtypeStruct((2, band, chans), spectra.dtype)] * len(part),
            in_specs=[kept],
            out_specs=[pl.BlockSpec(memory_space=pl.ANY)] * len(part),
            scratch_shapes=[pltpu.SemaphoreType.DMA((len(part),))],
            compiler_params=params,
            name="split_windows",
        )(spectra)
    chip_order = chips(chan_count)
    pair_shape = (6 * offset_count - 2, lag_rows, chans)
    own, far = pl.pallas_call(
        functools.partial(window_kernel, chan_order),
        out_shape=[jax.ShapeDtypeStruct((len(chip_order), *pair_shape), jnp.int16)] * 2,
        in_specs=[kept, smem] + [vmem] * (chan_count + 2),
        out_specs=[vmem] * 2,
        scratch_shapes=[
            pltpu.VMEM((freqs, chans), jnp.float32),
            pltpu.VMEM((2, freqs, chans), jnp.bfloat16),
            pltpu.VMEM((offset_count, 2, freqs, chans), jnp.bfloat16),
            pltpu.SMEM(offsets.shape, jnp.int32),
            pltpu.SemaphoreType.DMA(()),
        ],
        compiler_params=params,
        name="window_pairs",
    )(pltpu.with_memory_space_constraint(offsets, pltpu.HBM), chan_where, *exchange(pieces, "chan", chan_order), quality, table)
    pairs = pl.pallas_call(
        functools.partial(merge_kernel, offset_count),
        out_shape=[jax.ShapeDtypeStruct(pair_shape, jnp.int16)] * len(chip_order),
        in_specs=[vmem] * 2,
        out_specs=[vmem] * len(chip_order),
        compiler_params=params,
        name="merge_windows",
    )(own, *exchange([far], "chan", [1]))
    sums = pl.pallas_call(
        functools.partial(sum_kernel, tm_order, 1.0 / (CODE_TOP * math.sqrt(freqs))),
        out_shape=[jax.ShapeDtypeStruct((7, lag_rows, chans), jnp.int16)] * tm_count,
        in_specs=[smem] + [vmem] * len(chip_order),
        out_specs=[vmem] * tm_count,
        scratch_shapes=[pltpu.VMEM((offset_count, 7, lag_rows, chans), jnp.int16)],
        compiler_params=params,
        name="sum_windows",
    )(tm_where, *exchange(pairs, "chan", chip_order))
    pieces = pl.pallas_call(
        functools.partial(stack_kernel, windows * tm_count),
        out_shape=jax.ShapeDtypeStruct((tm_count, chan_count, piece_rows, chans), jnp.float32),
        in_specs=[smem] + [vmem] * tm_count,
        out_specs=vmem,
        compiler_params=params,
        name="stack_pairs",
    )(chan_where, *exchange(sums, "tm", tm_order))
    shape = (chan_count * tm_count, piece_rows, chans)
    arrived = lax.all_to_all(pieces.reshape(shape), ("tm", "chan"), 0, 0, tiled=True)
    return pl.pallas_call(
        place_kernel,
        out_shape=jax.ShapeDtypeStruct((CH_DEV, offset_count, LAGS), jnp.float32),
        in_specs=[vmem],
        out_specs=vmem,
        compiler_params=params,
        name="place_lags",
    )(arrived.reshape(tm_count, chan_count, piece_rows, chans))


def shifted(value, axis, steps):
    count = lax.axis_size(axis)
    leading, last = (max(0, -steps), min(count, count - steps))
    return lax.ppermute(value, axis, [(source, source + steps) for source in range(leading, last)])


def lag_table(freq_count, lag_count):
    freq_index = jnp.arange(freq_count, dtype=jnp.int32)[:, None]
    double_lag = (2 * jnp.arange(lag_count, dtype=jnp.int32) - lag_count + 1)[None, :]
    turns = jnp.mod(freq_index * double_lag, 4 * freq_count)
    angles = turns.astype(jnp.float32) * (2.0 * math.pi / (4 * freq_count))
    cosine = jnp.cos(angles)
    sine = jnp.sin(angles)
    upper = jnp.concatenate([cosine, sine], axis=1)
    lower = jnp.concatenate([-sine, cosine], axis=1)
    return jnp.stack([upper, lower]).astype(jnp.bfloat16)


def whiten_parts(real_part, imag_part, magnitude, channel_level, usable):
    factor = usable.astype(jnp.float32)[:, None, :] / (magnitude + 0.5 * (channel_level + 1e-05))
    return jnp.stack([real_part * factor, imag_part * factor]).astype(jnp.bfloat16)


def cross_parts(own_real, own_imag, far_real, far_imag):
    own_real = own_real.astype(jnp.float32)
    own_imag = own_imag.astype(jnp.float32)
    far_real = far_real.astype(jnp.float32)
    far_imag = far_imag.astype(jnp.float32)
    return jnp.stack(
        [own_real * far_real + own_imag * far_imag, own_imag * far_real - own_real * far_imag]
    ).astype(jnp.bfloat16)


def pair_terms(corr_all):
    lag_count = corr_all.shape[-1] // 2
    real_corr = corr_all[..., :lag_count]
    imag_corr = corr_all[..., lag_count:]
    power = real_corr * real_corr + imag_corr * imag_corr
    mean_power = jnp.mean(power, axis=-1, keepdims=True)
    denominator = jnp.sqrt(power + 0.25 * (mean_power + 1e-06))
    return (
        jnp.sum(real_corr, axis=-3),
        jnp.sum(real_corr / denominator, axis=-3),
        jnp.sum(imag_corr / denominator, axis=-3),
    )


def shards(spectra, quality, offsets):
    chan_count = lax.axis_size("chan")
    tm_count = lax.axis_size("tm")
    levels = chan_count.bit_length() - 1
    table_bf = lag_table(F, LAGS)
    inv_root = 1.0 / math.sqrt(F)
    real_part = spectra[0].astype(jnp.float32)
    imag_part = spectra[1].astype(jnp.float32)
    magnitude = jnp.sqrt(real_part * real_part + imag_part * imag_part)
    band_total = lax.psum(jnp.sum(magnitude, axis=1), "chan")
    channel_level = (band_total / F)[:, None, :]
    whitened = whiten_parts(real_part, imag_part, magnitude, channel_level, quality)
    width_all = whitened.shape[3]
    padded = jnp.pad(whitened, ((0, 0), (0, 0), (0, 0), (0, width_all)))
    crossed_list = []
    for offset_index in range(NOFF):
        partner = lax.dynamic_slice_in_dim(padded, offsets[offset_index] * CH_DEV, width_all, 3)
        crossed_list.append(cross_parts(whitened[0], whitened[1], partner[0], partner[1]))
    crossed = jnp.stack(crossed_list, axis=1)
    corr_all = jnp.einsum(
        "cnwfh,cfl->nwhl",
        lax.all_to_all(crossed, "chan", split_axis=4, concat_axis=3, tiled=True),
        table_bf,
        preferred_element_type=jnp.float32,
    )
    linear_sum, real_sum, imag_sum = pair_terms(corr_all * inv_root)
    totals = lax.psum((linear_sum, real_sum, imag_sum), "tm")
    window_count = W_DEV * tm_count
    linear = totals[0] / window_count
    real_phase = totals[1] / window_count
    imag_phase = totals[2] / window_count
    stacks = jnp.transpose(linear * (real_phase * real_phase + imag_phase * imag_phase), (1, 0, 2))
    reverse_part = stacks
    for bit_index in range(levels):
        step_size = 1 << bit_index
        arrived = shifted(reverse_part, "chan", step_size)
        chosen = offsets // step_size % 2 == 1
        reverse_part = jnp.where(chosen[None, :, None], arrived, reverse_part)
    return stacks + jnp.flip(reverse_part, axis=2)


def solution(mesh):
    chan_count, tm_count = mesh.shape["chan"], mesh.shape["tm"]
    by_window = chan_count == W_DEV and tm_count == NOFF
    return jax.shard_map(
        window_shards if by_window else shards,
        mesh=mesh,
        in_specs=(P(None, "tm", "chan", None), P("tm", None), P()),
        out_specs=P("chan", None, None),
        check_vma=False,
    )
```

```python
import functools
import math

import jax
import jax.numpy as jnp
import numpy as np
from jax import lax
from jax.experimental import pallas as pl
from jax.experimental.pallas import tpu as pltpu
from jax.sharding import PartitionSpec as P

F = 2048
LAGS = 256
NOFF = 4
CH_DEV = 16
W_DEV = 8
VMEM_LIMIT = 48 * 1024 * 1024
CODE_TOP = 32767.0
OCTAVE = 256.0
LOWEST = -110.0


def encode(value):
    return jnp.round(value).astype(jnp.int32).astype(jnp.int16)


def decode(code):
    return code.astype(jnp.int32).astype(jnp.float32)


def level_code(peak):
    return jnp.ceil(jnp.maximum(jnp.log2(jnp.maximum(peak, 1e-30)), LOWEST) * OCTAVE) + 1.0


def level_of(code):
    return jnp.exp2(code * (1.0 / OCTAVE))


def half_table(freq_count, lag_count):
    freq_index = np.arange(freq_count, dtype=np.int64)[None, :]
    double_lag = (2 * np.arange(lag_count // 2, lag_count, dtype=np.int64) - lag_count + 1)[:, None]
    turns = np.mod(freq_index * double_lag, 4 * freq_count).astype(np.float32)
    angles = turns * np.float32(2.0 * math.pi / (4 * freq_count))
    return np.concatenate([np.cos(angles), np.sin(angles)]).astype(jnp.bfloat16)


def widest(offs_ref, reach):
    last = offs_ref.shape[0] - 1
    found = last
    for number in reversed(range(last)):
        found = jnp.where(offs_ref[number] == reach, number, found)
    return found


def offset_of(slot, offs_ref, reach):
    last, wide = offs_ref.shape[0] - 1, widest(offs_ref, reach)
    return offs_ref[jnp.where(slot == wide, last, jnp.where(slot == last, wide, slot))]


def window_kernel(order, offs_hbm_ref, where_ref, *refs):
    chan_count = len(order)
    spec_refs, (qual_ref, table_ref) = refs[:chan_count], refs[chan_count : chan_count + 2]
    out_refs = refs[chan_count + 2 : chan_count + 4]
    mag_ref, white_ref, cross_ref, offs_ref, offs_sem = refs[chan_count + 4 :]
    fetch = pltpu.make_async_copy(offs_hbm_ref, offs_ref, offs_sem)
    fetch.start()
    me = where_ref[0]
    _, band, chans = spec_refs[0].shape
    freqs = chan_count * band
    chip_count, blocks, lag_rows, _ = out_refs[0].shape
    offset_count = offs_ref.shape[0]
    half = chan_count * lag_rows
    step = 64

    total = jnp.zeros((8, chans), jnp.float32)
    for number, spec_ref in enumerate(spec_refs):
        for row in range(0, band, step):
            real, imag = (spec_ref[part, row : row + step, :].astype(jnp.float32) for part in range(2))
            square = real * real + imag * imag
            magnitude = square * lax.rsqrt(jnp.maximum(square, 1e-30))
            held = slice(number * band + row, number * band + row + step)
            mag_ref[held, :] = magnitude
            total += jnp.sum(magnitude.reshape(step // 8, 8, chans), axis=0)
    level = jnp.sum(total, axis=0, keepdims=True) * (1.0 / freqs)
    floor = 0.5 * (level + 1e-05)

    for number, spec_ref in enumerate(spec_refs):
        for row in range(0, band, step):
            held = slice(number * band + row, number * band + row + step)
            factor = pl.reciprocal(mag_ref[held, :] + floor, approx=True)
            for part in range(2):
                value = spec_ref[part, row : row + step, :].astype(jnp.float32) * factor
                white_ref[part, held, :] = value.astype(jnp.bfloat16)

    lane = lax.broadcasted_iota(jnp.int32, (1, chans), 1)
    line = lax.broadcasted_iota(jnp.int32, (lag_rows, chans), 0)
    usable = qual_ref[pl.ds(me, 1), :].astype(jnp.float32)
    levels = jnp.zeros((lag_rows, chans), jnp.float32)
    core = me & 1
    orders = chips(chan_count)
    groups = [partner(orders, place, core) for place in range(chip_count)]
    groups += [partner(orders, place, 1 - core) ^ 1 for place in range(chip_count)]
    fetch.wait()
    per_band = table_ref.shape[0] // chan_count
    chunks = [(me ^ k) * per_band + chunk for k in order for chunk in range(per_band)]
    table = jnp.concatenate(
        [
            jnp.concatenate([table_ref[chunk, side, me ^ group] for side in range(2) for group in groups], axis=0)
            for chunk in chunks
        ],
        axis=1,
    )
    turns = [chans - offset_of(number, offs_ref, chan_count // 2) * (chans // chan_count) for number in range(offset_count)]
    for row in range(0, freqs, step):
        own = [white_ref[part, row : row + step, :] for part in range(2)]
        own_real, own_imag = (value.astype(jnp.float32) for value in own)
        for number, turn in enumerate(turns):
            far_real, far_imag = (pltpu.roll(value, turn, 1).astype(jnp.float32) for value in own)
            real = own_real * far_real + own_imag * far_imag
            imag = own_imag * far_real - own_real * far_imag
            cross_ref[number, 0, row : row + step, :] = real.astype(jnp.bfloat16)
            cross_ref[number, 1, row : row + step, :] = imag.astype(jnp.bfloat16)

    for number, turn in enumerate(turns):
        both = jnp.concatenate([cross_ref[number, 0], cross_ref[number, 1]], axis=1)
        sums = jnp.dot(table, both, preferred_element_type=jnp.float32)
        cos_real, sin_real = sums[:half, :chans], sums[half:, :chans]
        cos_imag, sin_imag = sums[:half, chans:], sums[half:, chans:]
        corr = (
            (cos_real - sin_imag, sin_real + cos_imag),
            (cos_real + sin_imag, cos_imag - sin_real),
        )
        power = [real * real + imag * imag for real, imag in corr]
        mean_power = jnp.sum(power[0] + power[1], axis=0, keepdims=True) * (1.0 / (2 * half))
        extra = 0.25 * (mean_power + 1e-06 * freqs)
        peak = jnp.max(jnp.maximum(jnp.abs(corr[0][0]), jnp.abs(corr[1][0])), axis=0, keepdims=True)
        code = level_code(peak)
        keep = jnp.where(lane < turn, usable * pltpu.roll(usable, turn, 1), 0.0) * CODE_TOP
        upscale = keep / level_of(code)
        inverse = [lax.rsqrt(side + extra) * keep for side in power]
        kinds = [
            [real * upscale for real, _ in corr],
            [real * scale for (real, _), scale in zip(corr, inverse)],
            [imag * scale for (_, imag), scale in zip(corr, inverse)],
        ]
        if number == offset_count - 1:
            code = jnp.where(lane < chans // 2, code, pltpu.roll(code, chans // 2, 1))
            kinds = [[jnp.where(lane < chans // 2, ahead, pltpu.roll(back, chans // 2, 1))] for ahead, back in kinds]
        levels = jnp.where(line == number, code, levels)
        for place, value in enumerate(value for kind in kinds for value in kind):
            coded = encode(value).reshape(chan_count, lag_rows, chans)
            for core in range(2):
                rows = slice(core * chip_count, (core + 1) * chip_count)
                out_refs[core][:, 6 * number + place, :, :] = coded[rows]
    for number in range(offset_count):
        levels = jnp.where(line == offset_count + number, offs_ref[number].astype(jnp.float32), levels)
    wide = widest(offs_ref, chan_count // 2).astype(jnp.float32)
    levels = jnp.where(line == 2 * offset_count, wide, levels)
    for out_ref in out_refs:
        for chip in range(chip_count):
            out_ref[chip, blocks - 1, :, :] = encode(levels)


def merge_kernel(slots, own_ref, far_ref, *out_refs):
    blocks = own_ref.shape[1]
    for chip, out_ref in enumerate(out_refs):
        codes = [decode(ref[chip, blocks - 1]) for ref in (own_ref, far_ref)]
        levels = [level_of(code) for code in codes]
        code = level_code(levels[0] + levels[1])
        shares = [level / level_of(code) for level in levels]
        line = lax.broadcasted_iota(jnp.int32, code.shape, 0)
        out_ref[blocks - 1, :, :] = encode(jnp.where(line < slots, code, codes[0]))
        for block in range(blocks - 1):
            number, part = divmod(block, 6)
            linear = part < (2 if blocks - 1 - 6 * number > 3 else 1)
            own, far = decode(own_ref[chip, block]), decode(far_ref[chip, block])
            if linear:
                total = own * shares[0][number : number + 1, :] + far * shares[1][number : number + 1, :]
            else:
                total = (own + far) * 0.5
            out_ref[block, :, :] = encode(total)


def sum_kernel(orders, scale, where_ref, core_ref, *refs):
    count = len(orders[0])
    code_refs, out_refs, held_ref = refs[: -count - 1], refs[-count - 1 : -1], refs[-1]
    blocks, _, chans = code_refs[0].shape
    slots = held_ref.shape[0]
    heads = [decode(codes_ref[blocks - 1]) for codes_ref in code_refs]
    levels = [level_of(head) * scale for head in heads]
    offsets = [heads[0][slots + number : slots + number + 1, :] for number in range(slots)]
    wide = heads[0][2 * slots : 2 * slots + 1, :]
    low = lax.broadcasted_iota(jnp.int32, (1, chans), 1) < chans // 2
    all_sums = []
    for number in range(slots):
        sides = 2 if number < slots - 1 else 1
        own = [level[number : number + 1, :] for level in levels]
        sums = []
        for place in range(3 * sides):
            codes = [decode(codes_ref[6 * number + place]) for codes_ref in code_refs]
            if place < sides:
                sums.append(sum(code * level for code, level in zip(codes, own)))
            else:
                sums.append(sum(codes) * (1.0 / len(code_refs)))
        if sides == 1:
            sums = [
                jnp.where(low, side, 0.0) for value in sums for side in (value, pltpu.roll(value, chans // 2, 1))
            ]
        all_sums.append(sums)
    line = lax.broadcasted_iota(jnp.int32, levels[0].shape, 0)
    last = slots - 1
    for number in range(slots):
        sums = all_sums[number]
        for other in range(last) if number == last else [last]:
            swap = wide == min(number, other)
            sums = [jnp.where(swap, value, kept) for value, kept in zip(all_sums[other], sums)]
        peak = jnp.max(jnp.maximum(jnp.abs(sums[0]), jnp.abs(sums[1])), axis=0, keepdims=True)
        code = level_code(peak)
        upscale = CODE_TOP / level_of(code)
        head = jnp.where(line == 0, code, offsets[number])
        for part, value in enumerate([sums[0] * upscale, sums[1] * upscale, *sums[2:], head]):
            held_ref[number, part, :, :] = encode(value)
    for place, out_ref in enumerate(out_refs):
        out_ref[...] = held_ref[where_ref[0] ^ partner(orders, place, core_ref[0] & 1)]


def partners(count):
    return sorted(range(1, count), key=lambda k: (-(k >> 1).bit_count(), k & 1, k)) + [0]


def chips(count):
    near = [k for k in range(2, count, 2) if k.bit_count() == 1]
    far = [k for k in range(2, count, 2) if k.bit_count() > 1]
    return near[::-1] + far + [0], near + far + [0]


def planes(count):
    others = partners(count)[:-1]
    return others + [0], others[1:] + others[:1] + [0]


def partner(orders, place, core):
    return jnp.where(core == 0, orders[0][place], orders[1][place])


def exchange(pieces, orders, over_tm=False):
    chan_count, tm_count = lax.axis_size("chan"), lax.axis_size("tm")
    arrived = []
    for place, piece in enumerate(pieces):
        pairs = []
        for source in range(chan_count * tm_count):
            k = orders[source // tm_count % 2][place]
            pairs.append((source, source ^ k if over_tm else source ^ (k * tm_count)))
        moved = any(source != target for source, target in pairs)
        arrived.append(lax.ppermute(piece, ("chan", "tm"), pairs) if moved else piece)
    return arrived


def split_kernel(order, spec_ref, *refs):
    out_refs, sems = refs[:-1], refs[-1]
    me = lax.axis_index("chan").astype(jnp.int32)
    copies = [
        pltpu.make_async_copy(spec_ref.at[:, me ^ k], out_ref, sems.at[number])
        for number, (k, out_ref) in enumerate(zip(order, out_refs))
    ]
    for copy in copies:
        copy.start()
    for copy in copies:
        copy.wait()


def stack_kernel(windows, where_ref, *refs):
    sums_refs, out_ref = refs[:-1], refs[-1]
    blocks, copies, rows, _ = out_ref.shape
    _, lag_rows, chans = sums_refs[0].shape
    per_sum = windows // len(sums_refs)
    heads = [decode(sums_ref[6]) for sums_ref in sums_refs]
    levels = [level_of(head[0:1, :]) * (1.0 / (CODE_TOP * windows)) for head in heads]
    stacks = []
    for side in range(2):
        linear = sum(decode(sums_ref[side]) * level for sums_ref, level in zip(sums_refs, levels))
        real, imag = (
            sum(decode(sums_ref[part + side]) for sums_ref in sums_refs) * (per_sum / (CODE_TOP * windows))
            for part in (2, 4)
        )
        stacks.append(linear * (real * real + imag * imag))
    offset = heads[0][1:2, :]
    lane = lax.broadcasted_iota(jnp.int32, (1, chans), 1)
    behind = [jnp.zeros_like(stack) for stack in stacks]
    for steps in range(1, blocks // 2 + 1):
        ahead = steps * (chans // blocks)
        chosen = (offset == steps) & (lane >= ahead)
        behind = [jnp.where(chosen, pltpu.roll(stack, ahead, 1), kept) for stack, kept in zip(stacks, behind)]
    back = stacks[1] + behind[0]
    back = jnp.concatenate([back[row : row + 1, :] for row in reversed(range(lag_rows))], axis=0)
    me = where_ref[0]
    even = (me & 1) == 0
    ahead = stacks[0] + behind[1]
    both = jnp.concatenate([jnp.where(even, ahead, back), jnp.where(even, back, ahead)], axis=0)
    parts = chans // (2 * lag_rows)
    turned = jnp.concatenate([both] * parts, axis=0).T
    unit = lane // lag_rows
    part_of = jnp.where(((unit ^ me) & 1) == 0, unit - me, unit + me + 1) % blocks // 2
    per_block = chans // blocks
    for block in range(blocks):
        piece = jnp.zeros((rows, chans), jnp.float32)
        for part in range(parts):
            begin = block * per_block + part * rows
            piece = jnp.where(part_of == part, turned[begin : begin + rows, :], piece)
        for copy in range(copies):
            out_ref[block, copy, :, :] = piece


def place_kernel(parts_ref, out_ref):
    groups, offset_count, rows, lanes = parts_ref.shape
    half = out_ref.shape[2] // 2
    lag_rows = half // groups
    parts = out_ref.shape[0] // rows
    unit = lax.broadcasted_iota(jnp.int32, (1, lanes), 1) // lag_rows
    for number in range(offset_count):
        pieces = [parts_ref[group, number] for group in range(groups)]
        for part in range(parts):
            sides = [jnp.zeros((rows, lanes), jnp.float32)] * 2
            for group, piece in enumerate(pieces):
                places = ((groups - 1 - group + 2 * part) % groups, (group + 2 * part) % groups)
                sides = [jnp.where(unit == place, piece, side) for place, side in zip(places, sides)]
            for side, value in enumerate(sides):
                value = pltpu.roll(value, (lanes - 2 * part * lag_rows) % lanes, 1) if part else value
                out_ref[part * rows : (part + 1) * rows, number, side * half : (side + 1) * half] = value


def window_shards(spectra, quality, offsets):
    chan_count = lax.axis_size("chan")
    tm_count = lax.axis_size("tm")
    _, windows, band, chans = spectra.shape
    freqs = band * chan_count
    half = LAGS // 2
    lag_rows = half // chan_count
    offset_count = offsets.shape[0]
    piece_rows = 2 * lag_rows // chan_count
    smem = pl.BlockSpec(memory_space=pltpu.SMEM)
    vmem = pl.BlockSpec(memory_space=pltpu.VMEM)
    params = pltpu.CompilerParams(vmem_limit_bytes=VMEM_LIMIT)
    table = half_table(freqs, LAGS).reshape(2, chan_count, lag_rows, freqs // 128, 128)
    table = jnp.asarray(np.ascontiguousarray(table.transpose(3, 0, 1, 2, 4)))
    chan_index = lax.axis_index("chan").astype(jnp.int32)
    tm_index = lax.axis_index("tm").astype(jnp.int32)
    chan_where, tm_where = chan_index.reshape(1), tm_index.reshape(1)

    chan_order, tm_orders = partners(chan_count), planes(tm_count)
    kept = pl.BlockSpec(memory_space=pltpu.HBM)
    spectra = pltpu.with_memory_space_constraint(spectra, pltpu.HBM)
    pieces = []
    for part in (chan_order[:2], chan_order[2:]):
        pieces += pl.pallas_call(
            functools.partial(split_kernel, part),
            out_shape=[jax.ShapeDtypeStruct((2, band, chans), spectra.dtype)] * len(part),
            in_specs=[kept],
            out_specs=[pl.BlockSpec(memory_space=pl.ANY)] * len(part),
            scratch_shapes=[pltpu.SemaphoreType.DMA((len(part),))],
            compiler_params=params,
            name="split_windows",
        )(spectra)
    chip_count = chan_count // 2
    pair_shape = (6 * offset_count - 2, lag_rows, chans)
    own, far = pl.pallas_call(
        functools.partial(window_kernel, chan_order),
        out_shape=[jax.ShapeDtypeStruct((chip_count, *pair_shape), jnp.int16)] * 2,
        in_specs=[kept, smem] + [vmem] * (chan_count + 2),
        out_specs=[vmem] * 2,
        scratch_shapes=[
            pltpu.VMEM((freqs, chans), jnp.float32),
            pltpu.VMEM((2, freqs, chans), jnp.bfloat16),
            pltpu.VMEM((offset_count, 2, freqs, chans), jnp.bfloat16),
            pltpu.SMEM(offsets.shape, jnp.int32),
            pltpu.SemaphoreType.DMA(()),
        ],
        compiler_params=params,
        name="window_pairs",
    )(pltpu.with_memory_space_constraint(offsets, pltpu.HBM), chan_where, *exchange(pieces, (chan_order, chan_order)), quality, table)
    pairs = pl.pallas_call(
        functools.partial(merge_kernel, offset_count),
        out_shape=[jax.ShapeDtypeStruct(pair_shape, jnp.int16)] * chip_count,
        in_specs=[vmem] * 2,
        out_specs=[vmem] * chip_count,
        compiler_params=params,
        name="merge_windows",
    )(own, *exchange([far], ([1], [1])))
    sums = pl.pallas_call(
        functools.partial(sum_kernel, tm_orders, 1.0 / (CODE_TOP * math.sqrt(freqs))),
        out_shape=[jax.ShapeDtypeStruct((7, lag_rows, chans), jnp.int16)] * tm_count,
        in_specs=[smem, smem] + [vmem] * chip_count,
        out_specs=[vmem] * tm_count,
        scratch_shapes=[pltpu.VMEM((offset_count, 7, lag_rows, chans), jnp.int16)],
        compiler_params=params,
        name="sum_windows",
    )(tm_where, chan_where, *exchange(pairs, chips(chan_count)))
    pieces = pl.pallas_call(
        functools.partial(stack_kernel, windows * tm_count),
        out_shape=jax.ShapeDtypeStruct((chan_count, tm_count, piece_rows, chans), jnp.float32),
        in_specs=[smem] + [vmem] * tm_count,
        out_specs=vmem,
        compiler_params=params,
        name="stack_pairs",
    )(chan_where, *exchange(sums, tm_orders, over_tm=True))
    shape = (chan_count * tm_count, piece_rows, chans)
    arrived = lax.all_to_all(pieces.reshape(shape), ("chan", "tm"), 0, 0, tiled=True)
    return pl.pallas_call(
        place_kernel,
        out_shape=jax.ShapeDtypeStruct((CH_DEV, offset_count, LAGS), jnp.float32),
        in_specs=[vmem],
        out_specs=vmem,
        compiler_params=params,
        name="place_lags",
    )(arrived.reshape(chan_count, tm_count, piece_rows, chans))


def shifted(value, axis, steps):
    count = lax.axis_size(axis)
    leading, last = (max(0, -steps), min(count, count - steps))
    return lax.ppermute(value, axis, [(source, source + steps) for source in range(leading, last)])


def lag_table(freq_count, lag_count):
    freq_index = jnp.arange(freq_count, dtype=jnp.int32)[:, None]
    double_lag = (2 * jnp.arange(lag_count, dtype=jnp.int32) - lag_count + 1)[None, :]
    turns = jnp.mod(freq_index * double_lag, 4 * freq_count)
    angles = turns.astype(jnp.float32) * (2.0 * math.pi / (4 * freq_count))
    cosine = jnp.cos(angles)
    sine = jnp.sin(angles)
    upper = jnp.concatenate([cosine, sine], axis=1)
    lower = jnp.concatenate([-sine, cosine], axis=1)
    return jnp.stack([upper, lower]).astype(jnp.bfloat16)


def whiten_parts(real_part, imag_part, magnitude, channel_level, usable):
    factor = usable.astype(jnp.float32)[:, None, :] / (magnitude + 0.5 * (channel_level + 1e-05))
    return jnp.stack([real_part * factor, imag_part * factor]).astype(jnp.bfloat16)


def cross_parts(own_real, own_imag, far_real, far_imag):
    own_real = own_real.astype(jnp.float32)
    own_imag = own_imag.astype(jnp.float32)
    far_real = far_real.astype(jnp.float32)
    far_imag = far_imag.astype(jnp.float32)
    return jnp.stack(
        [own_real * far_real + own_imag * far_imag, own_imag * far_real - own_real * far_imag]
    ).astype(jnp.bfloat16)


def pair_terms(corr_all):
    lag_count = corr_all.shape[-1] // 2
    real_corr = corr_all[..., :lag_count]
    imag_corr = corr_all[..., lag_count:]
    power = real_corr * real_corr + imag_corr * imag_corr
    mean_power = jnp.mean(power, axis=-1, keepdims=True)
    denominator = jnp.sqrt(power + 0.25 * (mean_power + 1e-06))
    return (
        jnp.sum(real_corr, axis=-3),
        jnp.sum(real_corr / denominator, axis=-3),
        jnp.sum(imag_corr / denominator, axis=-3),
    )


def shards(spectra, quality, offsets):
    chan_count = lax.axis_size("chan")
    tm_count = lax.axis_size("tm")
    levels = chan_count.bit_length() - 1
    table_bf = lag_table(F, LAGS)
    inv_root = 1.0 / math.sqrt(F)
    real_part = spectra[0].astype(jnp.float32)
    imag_part = spectra[1].astype(jnp.float32)
    magnitude = jnp.sqrt(real_part * real_part + imag_part * imag_part)
    band_total = lax.psum(jnp.sum(magnitude, axis=1), "chan")
    channel_level = (band_total / F)[:, None, :]
    whitened = whiten_parts(real_part, imag_part, magnitude, channel_level, quality)
    width_all = whitened.shape[3]
    padded = jnp.pad(whitened, ((0, 0), (0, 0), (0, 0), (0, width_all)))
    crossed_list = []
    for offset_index in range(NOFF):
        partner = lax.dynamic_slice_in_dim(padded, offsets[offset_index] * CH_DEV, width_all, 3)
        crossed_list.append(cross_parts(whitened[0], whitened[1], partner[0], partner[1]))
    crossed = jnp.stack(crossed_list, axis=1)
    corr_all = jnp.einsum(
        "cnwfh,cfl->nwhl",
        lax.all_to_all(crossed, "chan", split_axis=4, concat_axis=3, tiled=True),
        table_bf,
        preferred_element_type=jnp.float32,
    )
    linear_sum, real_sum, imag_sum = pair_terms(corr_all * inv_root)
    totals = lax.psum((linear_sum, real_sum, imag_sum), "tm")
    window_count = W_DEV * tm_count
    linear = totals[0] / window_count
    real_phase = totals[1] / window_count
    imag_phase = totals[2] / window_count
    stacks = jnp.transpose(linear * (real_phase * real_phase + imag_phase * imag_phase), (1, 0, 2))
    reverse_part = stacks
    for bit_index in range(levels):
        step_size = 1 << bit_index
        arrived = shifted(reverse_part, "chan", step_size)
        chosen = offsets // step_size % 2 == 1
        reverse_part = jnp.where(chosen[None, :, None], arrived, reverse_part)
    return stacks + jnp.flip(reverse_part, axis=2)


def solution(mesh):
    chan_count, tm_count = mesh.shape["chan"], mesh.shape["tm"]
    by_window = chan_count == W_DEV and tm_count == NOFF
    return jax.shard_map(
        window_shards if by_window else shards,
        mesh=mesh,
        in_specs=(P(None, "tm", "chan", None), P("tm", None), P()),
        out_specs=P("chan", None, None),
        check_vma=False,
    )
```

```python
import functools
import math

import jax
import jax.numpy as jnp
import numpy as np
from jax import lax
from jax.experimental import pallas as pl
from jax.experimental.pallas import tpu as pltpu
from jax.sharding import PartitionSpec as P

F = 2048
LAGS = 256
NOFF = 4
CH_DEV = 16
W_DEV = 8
VMEM_LIMIT = 48 * 1024 * 1024
CODE_TOP = 32767.0
OCTAVE = 256.0
LOWEST = -110.0


def encode(value):
    return jnp.round(value).astype(jnp.int32).astype(jnp.int16)


def decode(code):
    return code.astype(jnp.int32).astype(jnp.float32)


def level_code(peak):
    return jnp.ceil(jnp.maximum(jnp.log2(jnp.maximum(peak, 1e-30)), LOWEST) * OCTAVE) + 1.0


def level_of(code):
    return jnp.exp2(code * (1.0 / OCTAVE))


def half_table(freq_count, lag_count):
    freq_index = np.arange(freq_count, dtype=np.int64)[None, :]
    double_lag = (2 * np.arange(lag_count // 2, lag_count, dtype=np.int64) - lag_count + 1)[:, None]
    turns = np.mod(freq_index * double_lag, 4 * freq_count).astype(np.float32)
    angles = turns * np.float32(2.0 * math.pi / (4 * freq_count))
    return np.concatenate([np.cos(angles), np.sin(angles)]).astype(jnp.bfloat16)


def widest(offs_ref, reach):
    last = offs_ref.shape[0] - 1
    found = last
    for number in reversed(range(last)):
        found = jnp.where(offs_ref[number] == reach, number, found)
    return found


def offset_of(slot, offs_ref, reach):
    last, wide = offs_ref.shape[0] - 1, widest(offs_ref, reach)
    return offs_ref[jnp.where(slot == wide, last, jnp.where(slot == last, wide, slot))]


def window_kernel(order, offs_hbm_ref, where_ref, *refs):
    chan_count = len(order)
    spec_refs, (qual_ref, table_ref) = refs[:chan_count], refs[chan_count : chan_count + 2]
    out_refs = refs[chan_count + 2 : chan_count + 4]
    mag_ref, white_ref, cross_ref, offs_ref, offs_sem = refs[chan_count + 4 :]
    fetch = pltpu.make_async_copy(offs_hbm_ref, offs_ref, offs_sem)
    fetch.start()
    me = where_ref[0]
    _, band, chans = spec_refs[0].shape
    freqs = chan_count * band
    chip_count, blocks, lag_rows, _ = out_refs[0].shape
    offset_count = offs_ref.shape[0]
    half = chan_count * lag_rows
    step = 64

    total = jnp.zeros((8, chans), jnp.float32)
    for number, spec_ref in enumerate(spec_refs):
        for row in range(0, band, step):
            real, imag = (spec_ref[part, row : row + step, :].astype(jnp.float32) for part in range(2))
            square = real * real + imag * imag
            magnitude = square * lax.rsqrt(jnp.maximum(square, 1e-30))
            held = slice(number * band + row, number * band + row + step)
            mag_ref[held, :] = magnitude
            total += jnp.sum(magnitude.reshape(step // 8, 8, chans), axis=0)
    level = jnp.sum(total, axis=0, keepdims=True) * (1.0 / freqs)
    floor = 0.5 * (level + 1e-05)

    for number, spec_ref in enumerate(spec_refs):
        for row in range(0, band, step):
            held = slice(number * band + row, number * band + row + step)
            factor = pl.reciprocal(mag_ref[held, :] + floor, approx=True)
            for part in range(2):
                value = spec_ref[part, row : row + step, :].astype(jnp.float32) * factor
                white_ref[part, held, :] = value.astype(jnp.bfloat16)

    lane = lax.broadcasted_iota(jnp.int32, (1, chans), 1)
    line = lax.broadcasted_iota(jnp.int32, (lag_rows, chans), 0)
    usable = qual_ref[pl.ds(me, 1), :].astype(jnp.float32)
    levels = jnp.zeros((lag_rows, chans), jnp.float32)
    core = me & 1
    orders = chips(chan_count)
    groups = [partner(orders, place, core) for place in range(chip_count)]
    groups += [partner(orders, place, 1 - core) ^ 1 for place in range(chip_count)]
    fetch.wait()
    per_band = table_ref.shape[0] // chan_count
    chunks = [(me ^ k) * per_band + chunk for k in order for chunk in range(per_band)]
    table = jnp.concatenate(
        [
            jnp.concatenate([table_ref[chunk, side, me ^ group] for side in range(2) for group in groups], axis=0)
            for chunk in chunks
        ],
        axis=1,
    )
    turns = [chans - offset_of(number, offs_ref, chan_count // 2) * (chans // chan_count) for number in range(offset_count)]
    for row in range(0, freqs, step):
        own = [white_ref[part, row : row + step, :] for part in range(2)]
        own_real, own_imag = (value.astype(jnp.float32) for value in own)
        for number, turn in enumerate(turns):
            far_real, far_imag = (pltpu.roll(value, turn, 1).astype(jnp.float32) for value in own)
            real = own_real * far_real + own_imag * far_imag
            imag = own_imag * far_real - own_real * far_imag
            cross_ref[number, 0, row : row + step, :] = real.astype(jnp.bfloat16)
            cross_ref[number, 1, row : row + step, :] = imag.astype(jnp.bfloat16)

    for number, turn in enumerate(turns):
        both = jnp.concatenate([cross_ref[number, 0], cross_ref[number, 1]], axis=1)
        sums = jnp.dot(table, both, preferred_element_type=jnp.float32)
        cos_real, sin_real = sums[:half, :chans], sums[half:, :chans]
        cos_imag, sin_imag = sums[:half, chans:], sums[half:, chans:]
        corr = (
            (cos_real - sin_imag, sin_real + cos_imag),
            (cos_real + sin_imag, cos_imag - sin_real),
        )
        power = [real * real + imag * imag for real, imag in corr]
        mean_power = jnp.sum(power[0] + power[1], axis=0, keepdims=True) * (1.0 / (2 * half))
        extra = 0.25 * (mean_power + 1e-06 * freqs)
        peak = jnp.max(jnp.maximum(jnp.abs(corr[0][0]), jnp.abs(corr[1][0])), axis=0, keepdims=True)
        code = level_code(peak)
        keep = jnp.where(lane < turn, usable * pltpu.roll(usable, turn, 1), 0.0) * CODE_TOP
        upscale = keep / level_of(code)
        inverse = [lax.rsqrt(side + extra) * keep for side in power]
        kinds = [
            [real * upscale for real, _ in corr],
            [real * scale for (real, _), scale in zip(corr, inverse)],
            [imag * scale for (_, imag), scale in zip(corr, inverse)],
        ]
        if number == offset_count - 1:
            code = jnp.where(lane < chans // 2, code, pltpu.roll(code, chans // 2, 1))
            kinds = [[jnp.where(lane < chans // 2, ahead, pltpu.roll(back, chans // 2, 1))] for ahead, back in kinds]
        levels = jnp.where(line == number, code, levels)
        for place, value in enumerate(value for kind in kinds for value in kind):
            coded = encode(value).reshape(chan_count, lag_rows, chans)
            for core in range(2):
                rows = slice(core * chip_count, (core + 1) * chip_count)
                out_refs[core][:, 6 * number + place, :, :] = coded[rows]
    for number in range(offset_count):
        levels = jnp.where(line == offset_count + number, offs_ref[number].astype(jnp.float32), levels)
    wide = widest(offs_ref, chan_count // 2).astype(jnp.float32)
    levels = jnp.where(line == 2 * offset_count, wide, levels)
    for out_ref in out_refs:
        for chip in range(chip_count):
            out_ref[chip, blocks - 1, :, :] = encode(levels)


def merge_kernel(slots, own_ref, far_ref, *out_refs):
    blocks = own_ref.shape[1]
    for chip, out_ref in enumerate(out_refs):
        codes = [decode(ref[chip, blocks - 1]) for ref in (own_ref, far_ref)]
        levels = [level_of(code) for code in codes]
        code = level_code(levels[0] + levels[1])
        shares = [level / level_of(code) for level in levels]
        line = lax.broadcasted_iota(jnp.int32, code.shape, 0)
        out_ref[blocks - 1, :, :] = encode(jnp.where(line < slots, code, codes[0]))
        for block in range(blocks - 1):
            number, part = divmod(block, 6)
            linear = part < (2 if blocks - 1 - 6 * number > 3 else 1)
            own, far = decode(own_ref[chip, block]), decode(far_ref[chip, block])
            if linear:
                total = own * shares[0][number : number + 1, :] + far * shares[1][number : number + 1, :]
            else:
                total = (own + far) * 0.5
            out_ref[block, :, :] = encode(total)


def sum_kernel(orders, scale, where_ref, core_ref, *refs):
    count = len(orders[0])
    code_refs, out_refs, held_ref = refs[: -count - 1], refs[-count - 1 : -1], refs[-1]
    blocks, _, chans = code_refs[0].shape
    slots = held_ref.shape[0]
    heads = [decode(codes_ref[blocks - 1]) for codes_ref in code_refs]
    levels = [level_of(head) * scale for head in heads]
    offsets = [heads[0][slots + number : slots + number + 1, :] for number in range(slots)]
    wide = heads[0][2 * slots : 2 * slots + 1, :]
    low = lax.broadcasted_iota(jnp.int32, (1, chans), 1) < chans // 2
    all_sums = []
    for number in range(slots):
        sides = 2 if number < slots - 1 else 1
        own = [level[number : number + 1, :] for level in levels]
        sums = []
        for place in range(3 * sides):
            codes = [decode(codes_ref[6 * number + place]) for codes_ref in code_refs]
            if place < sides:
                sums.append(sum(code * level for code, level in zip(codes, own)))
            else:
                sums.append(sum(codes) * (1.0 / len(code_refs)))
        if sides == 1:
            sums = [
                jnp.where(low, side, 0.0) for value in sums for side in (value, pltpu.roll(value, chans // 2, 1))
            ]
        all_sums.append(sums)
    line = lax.broadcasted_iota(jnp.int32, levels[0].shape, 0)
    last = slots - 1
    for number in range(slots):
        sums = all_sums[number]
        for other in range(last) if number == last else [last]:
            swap = wide == min(number, other)
            sums = [jnp.where(swap, value, kept) for value, kept in zip(all_sums[other], sums)]
        peak = jnp.max(jnp.maximum(jnp.abs(sums[0]), jnp.abs(sums[1])), axis=0, keepdims=True)
        code = level_code(peak)
        upscale = CODE_TOP / level_of(code)
        head = jnp.where(line == 0, code, offsets[number])
        for part, value in enumerate([sums[0] * upscale, sums[1] * upscale, *sums[2:], head]):
            held_ref[number, part, :, :] = encode(value)
    for place, out_ref in enumerate(out_refs):
        out_ref[...] = held_ref[where_ref[0] ^ partner(orders, place, core_ref[0] & 1)]


def partners(count):
    return sorted(range(1, count), key=lambda k: (-(k >> 1).bit_count(), k & 1, k)) + [0]


def chips(count):
    near = [k for k in range(2, count, 2) if k.bit_count() == 1]
    far = [k for k in range(2, count, 2) if k.bit_count() > 1]
    return far + near + [0], near + far + [0]


def planes(count):
    others = partners(count)[:-1]
    return others + [0], others[1:] + others[:1] + [0]


def partner(orders, place, core):
    return jnp.where(core == 0, orders[0][place], orders[1][place])


def exchange(pieces, orders, over_tm=False):
    chan_count, tm_count = lax.axis_size("chan"), lax.axis_size("tm")
    arrived = []
    for place, piece in enumerate(pieces):
        pairs = []
        for source in range(chan_count * tm_count):
            k = orders[source // tm_count % 2][place]
            pairs.append((source, source ^ k if over_tm else source ^ (k * tm_count)))
        moved = any(source != target for source, target in pairs)
        arrived.append(lax.ppermute(piece, ("chan", "tm"), pairs) if moved else piece)
    return arrived


def split_kernel(order, spec_ref, *refs):
    out_refs, sems = refs[:-1], refs[-1]
    me = lax.axis_index("chan").astype(jnp.int32)
    copies = [
        pltpu.make_async_copy(spec_ref.at[:, me ^ k], out_ref, sems.at[number])
        for number, (k, out_ref) in enumerate(zip(order, out_refs))
    ]
    for copy in copies:
        copy.start()
    for copy in copies:
        copy.wait()


def stack_kernel(windows, where_ref, *refs):
    sums_refs, out_ref = refs[:-1], refs[-1]
    blocks, copies, rows, _ = out_ref.shape
    _, lag_rows, chans = sums_refs[0].shape
    per_sum = windows // len(sums_refs)
    heads = [decode(sums_ref[6]) for sums_ref in sums_refs]
    levels = [level_of(head[0:1, :]) * (1.0 / (CODE_TOP * windows)) for head in heads]
    stacks = []
    for side in range(2):
        linear = sum(decode(sums_ref[side]) * level for sums_ref, level in zip(sums_refs, levels))
        real, imag = (
            sum(decode(sums_ref[part + side]) for sums_ref in sums_refs) * (per_sum / (CODE_TOP * windows))
            for part in (2, 4)
        )
        stacks.append(linear * (real * real + imag * imag))
    offset = heads[0][1:2, :]
    lane = lax.broadcasted_iota(jnp.int32, (1, chans), 1)
    behind = [jnp.zeros_like(stack) for stack in stacks]
    for steps in range(1, blocks // 2 + 1):
        ahead = steps * (chans // blocks)
        chosen = (offset == steps) & (lane >= ahead)
        behind = [jnp.where(chosen, pltpu.roll(stack, ahead, 1), kept) for stack, kept in zip(stacks, behind)]
    back = stacks[1] + behind[0]
    back = jnp.concatenate([back[row : row + 1, :] for row in reversed(range(lag_rows))], axis=0)
    me = where_ref[0]
    even = (me & 1) == 0
    ahead = stacks[0] + behind[1]
    both = jnp.concatenate([jnp.where(even, ahead, back), jnp.where(even, back, ahead)], axis=0)
    parts = chans // (2 * lag_rows)
    turned = jnp.concatenate([both] * parts, axis=0).T
    unit = lane // lag_rows
    part_of = jnp.where(((unit ^ me) & 1) == 0, unit - me, unit + me + 1) % blocks // 2
    per_block = chans // blocks
    for block in range(blocks):
        piece = jnp.zeros((rows, chans), jnp.float32)
        for part in range(parts):
            begin = block * per_block + part * rows
            piece = jnp.where(part_of == part, turned[begin : begin + rows, :], piece)
        for copy in range(copies):
            out_ref[block, copy, :, :] = piece


def place_kernel(parts_ref, out_ref):
    groups, offset_count, rows, lanes = parts_ref.shape
    half = out_ref.shape[2] // 2
    lag_rows = half // groups
    parts = out_ref.shape[0] // rows
    unit = lax.broadcasted_iota(jnp.int32, (1, lanes), 1) // lag_rows
    for number in range(offset_count):
        pieces = [parts_ref[group, number] for group in range(groups)]
        for part in range(parts):
            sides = [jnp.zeros((rows, lanes), jnp.float32)] * 2
            for group, piece in enumerate(pieces):
                places = ((groups - 1 - group + 2 * part) % groups, (group + 2 * part) % groups)
                sides = [jnp.where(unit == place, piece, side) for place, side in zip(places, sides)]
            for side, value in enumerate(sides):
                value = pltpu.roll(value, (lanes - 2 * part * lag_rows) % lanes, 1) if part else value
                out_ref[part * rows : (part + 1) * rows, number, side * half : (side + 1) * half] = value


def window_shards(spectra, quality, offsets):
    chan_count = lax.axis_size("chan")
    tm_count = lax.axis_size("tm")
    _, windows, band, chans = spectra.shape
    freqs = band * chan_count
    half = LAGS // 2
    lag_rows = half // chan_count
    offset_count = offsets.shape[0]
    piece_rows = 2 * lag_rows // chan_count
    smem = pl.BlockSpec(memory_space=pltpu.SMEM)
    vmem = pl.BlockSpec(memory_space=pltpu.VMEM)
    params = pltpu.CompilerParams(vmem_limit_bytes=VMEM_LIMIT)
    table = half_table(freqs, LAGS).reshape(2, chan_count, lag_rows, freqs // 128, 128)
    table = jnp.asarray(np.ascontiguousarray(table.transpose(3, 0, 1, 2, 4)))
    chan_index = lax.axis_index("chan").astype(jnp.int32)
    tm_index = lax.axis_index("tm").astype(jnp.int32)
    chan_where, tm_where = chan_index.reshape(1), tm_index.reshape(1)

    chan_order, tm_orders = partners(chan_count), planes(tm_count)
    kept = pl.BlockSpec(memory_space=pltpu.HBM)
    spectra = pltpu.with_memory_space_constraint(spectra, pltpu.HBM)
    pieces = []
    for part in (chan_order[:2], chan_order[2:]):
        pieces += pl.pallas_call(
            functools.partial(split_kernel, part),
            out_shape=[jax.ShapeDtypeStruct((2, band, chans), spectra.dtype)] * len(part),
            in_specs=[kept],
            out_specs=[pl.BlockSpec(memory_space=pl.ANY)] * len(part),
            scratch_shapes=[pltpu.SemaphoreType.DMA((len(part),))],
            compiler_params=params,
            name="split_windows",
        )(spectra)
    chip_count = chan_count // 2
    pair_shape = (6 * offset_count - 2, lag_rows, chans)
    own, far = pl.pallas_call(
        functools.partial(window_kernel, chan_order),
        out_shape=[jax.ShapeDtypeStruct((chip_count, *pair_shape), jnp.int16)] * 2,
        in_specs=[kept, smem] + [vmem] * (chan_count + 2),
        out_specs=[vmem] * 2,
        scratch_shapes=[
            pltpu.VMEM((freqs, chans), jnp.float32),
            pltpu.VMEM((2, freqs, chans), jnp.bfloat16),
            pltpu.VMEM((offset_count, 2, freqs, chans), jnp.bfloat16),
            pltpu.SMEM(offsets.shape, jnp.int32),
            pltpu.SemaphoreType.DMA(()),
        ],
        compiler_params=params,
        name="window_pairs",
    )(pltpu.with_memory_space_constraint(offsets, pltpu.HBM), chan_where, *exchange(pieces, (chan_order, chan_order)), quality, table)
    pairs = pl.pallas_call(
        functools.partial(merge_kernel, offset_count),
        out_shape=[jax.ShapeDtypeStruct(pair_shape, jnp.int16)] * chip_count,
        in_specs=[vmem] * 2,
        out_specs=[vmem] * chip_count,
        compiler_params=params,
        name="merge_windows",
    )(own, *exchange([far], ([1], [1])))
    sums = pl.pallas_call(
        functools.partial(sum_kernel, tm_orders, 1.0 / (CODE_TOP * math.sqrt(freqs))),
        out_shape=[jax.ShapeDtypeStruct((7, lag_rows, chans), jnp.int16)] * tm_count,
        in_specs=[smem, smem] + [vmem] * chip_count,
        out_specs=[vmem] * tm_count,
        scratch_shapes=[pltpu.VMEM((offset_count, 7, lag_rows, chans), jnp.int16)],
        compiler_params=params,
        name="sum_windows",
    )(tm_where, chan_where, *exchange(pairs, chips(chan_count)))
    pieces = pl.pallas_call(
        functools.partial(stack_kernel, windows * tm_count),
        out_shape=jax.ShapeDtypeStruct((chan_count, tm_count, piece_rows, chans), jnp.float32),
        in_specs=[smem] + [vmem] * tm_count,
        out_specs=vmem,
        compiler_params=params,
        name="stack_pairs",
    )(chan_where, *exchange(sums, tm_orders, over_tm=True))
    shape = (chan_count * tm_count, piece_rows, chans)
    arrived = lax.all_to_all(pieces.reshape(shape), ("chan", "tm"), 0, 0, tiled=True)
    return pl.pallas_call(
        place_kernel,
        out_shape=jax.ShapeDtypeStruct((CH_DEV, offset_count, LAGS), jnp.float32),
        in_specs=[vmem],
        out_specs=vmem,
        compiler_params=params,
        name="place_lags",
    )(arrived.reshape(chan_count, tm_count, piece_rows, chans))


def shifted(value, axis, steps):
    count = lax.axis_size(axis)
    leading, last = (max(0, -steps), min(count, count - steps))
    return lax.ppermute(value, axis, [(source, source + steps) for source in range(leading, last)])


def lag_table(freq_count, lag_count):
    freq_index = jnp.arange(freq_count, dtype=jnp.int32)[:, None]
    double_lag = (2 * jnp.arange(lag_count, dtype=jnp.int32) - lag_count + 1)[None, :]
    turns = jnp.mod(freq_index * double_lag, 4 * freq_count)
    angles = turns.astype(jnp.float32) * (2.0 * math.pi / (4 * freq_count))
    cosine = jnp.cos(angles)
    sine = jnp.sin(angles)
    upper = jnp.concatenate([cosine, sine], axis=1)
    lower = jnp.concatenate([-sine, cosine], axis=1)
    return jnp.stack([upper, lower]).astype(jnp.bfloat16)


def whiten_parts(real_part, imag_part, magnitude, channel_level, usable):
    factor = usable.astype(jnp.float32)[:, None, :] / (magnitude + 0.5 * (channel_level + 1e-05))
    return jnp.stack([real_part * factor, imag_part * factor]).astype(jnp.bfloat16)


def cross_parts(own_real, own_imag, far_real, far_imag):
    own_real = own_real.astype(jnp.float32)
    own_imag = own_imag.astype(jnp.float32)
    far_real = far_real.astype(jnp.float32)
    far_imag = far_imag.astype(jnp.float32)
    return jnp.stack(
        [own_real * far_real + own_imag * far_imag, own_imag * far_real - own_real * far_imag]
    ).astype(jnp.bfloat16)


def pair_terms(corr_all):
    lag_count = corr_all.shape[-1] // 2
    real_corr = corr_all[..., :lag_count]
    imag_corr = corr_all[..., lag_count:]
    power = real_corr * real_corr + imag_corr * imag_corr
    mean_power = jnp.mean(power, axis=-1, keepdims=True)
    denominator = jnp.sqrt(power + 0.25 * (mean_power + 1e-06))
    return (
        jnp.sum(real_corr, axis=-3),
        jnp.sum(real_corr / denominator, axis=-3),
        jnp.sum(imag_corr / denominator, axis=-3),
    )


def shards(spectra, quality, offsets):
    chan_count = lax.axis_size("chan")
    tm_count = lax.axis_size("tm")
    levels = chan_count.bit_length() - 1
    table_bf = lag_table(F, LAGS)
    inv_root = 1.0 / math.sqrt(F)
    real_part = spectra[0].astype(jnp.float32)
    imag_part = spectra[1].astype(jnp.float32)
    magnitude = jnp.sqrt(real_part * real_part + imag_part * imag_part)
    band_total = lax.psum(jnp.sum(magnitude, axis=1), "chan")
    channel_level = (band_total / F)[:, None, :]
    whitened = whiten_parts(real_part, imag_part, magnitude, channel_level, quality)
    width_all = whitened.shape[3]
    padded = jnp.pad(whitened, ((0, 0), (0, 0), (0, 0), (0, width_all)))
    crossed_list = []
    for offset_index in range(NOFF):
        partner = lax.dynamic_slice_in_dim(padded, offsets[offset_index] * CH_DEV, width_all, 3)
        crossed_list.append(cross_parts(whitened[0], whitened[1], partner[0], partner[1]))
    crossed = jnp.stack(crossed_list, axis=1)
    corr_all = jnp.einsum(
        "cnwfh,cfl->nwhl",
        lax.all_to_all(crossed, "chan", split_axis=4, concat_axis=3, tiled=True),
        table_bf,
        preferred_element_type=jnp.float32,
    )
    linear_sum, real_sum, imag_sum = pair_terms(corr_all * inv_root)
    totals = lax.psum((linear_sum, real_sum, imag_sum), "tm")
    window_count = W_DEV * tm_count
    linear = totals[0] / window_count
    real_phase = totals[1] / window_count
    imag_phase = totals[2] / window_count
    stacks = jnp.transpose(linear * (real_phase * real_phase + imag_phase * imag_phase), (1, 0, 2))
    reverse_part = stacks
    for bit_index in range(levels):
        step_size = 1 << bit_index
        arrived = shifted(reverse_part, "chan", step_size)
        chosen = offsets // step_size % 2 == 1
        reverse_part = jnp.where(chosen[None, :, None], arrived, reverse_part)
    return stacks + jnp.flip(reverse_part, axis=2)


def solution(mesh):
    chan_count, tm_count = mesh.shape["chan"], mesh.shape["tm"]
    by_window = chan_count == W_DEV and tm_count == NOFF
    return jax.shard_map(
        window_shards if by_window else shards,
        mesh=mesh,
        in_specs=(P(None, "tm", "chan", None), P("tm", None), P()),
        out_specs=P("chan", None, None),
        check_vma=False,
    )
```

```python
import functools
import math

import jax
import jax.numpy as jnp
import numpy as np
from jax import lax
from jax.experimental import pallas as pl
from jax.experimental.pallas import tpu as pltpu
from jax.sharding import PartitionSpec as P

F = 2048
LAGS = 256
NOFF = 4
CH_DEV = 16
W_DEV = 8
VMEM_LIMIT = 48 * 1024 * 1024
CODE_TOP = 32767.0
OCTAVE = 256.0
LOWEST = -110.0


def encode(value):
    return jnp.round(value).astype(jnp.int32).astype(jnp.int16)


def decode(code):
    return code.astype(jnp.int32).astype(jnp.float32)


def level_code(peak):
    return jnp.ceil(jnp.maximum(jnp.log2(jnp.maximum(peak, 1e-30)), LOWEST) * OCTAVE) + 1.0


def level_of(code):
    return jnp.exp2(code * (1.0 / OCTAVE))


def half_table(freq_count, lag_count):
    freq_index = np.arange(freq_count, dtype=np.int64)[None, :]
    double_lag = (2 * np.arange(lag_count // 2, lag_count, dtype=np.int64) - lag_count + 1)[:, None]
    turns = np.mod(freq_index * double_lag, 4 * freq_count).astype(np.float32)
    angles = turns * np.float32(2.0 * math.pi / (4 * freq_count))
    return np.concatenate([np.cos(angles), np.sin(angles)]).astype(jnp.bfloat16)


def widest(offs_ref, reach):
    last = offs_ref.shape[0] - 1
    found = last
    for number in reversed(range(last)):
        found = jnp.where(offs_ref[number] == reach, number, found)
    return found


def offset_of(slot, offs_ref, reach):
    last, wide = offs_ref.shape[0] - 1, widest(offs_ref, reach)
    return offs_ref[jnp.where(slot == wide, last, jnp.where(slot == last, wide, slot))]


def window_kernel(order, offs_hbm_ref, where_ref, *refs):
    chan_count = len(order)
    spec_refs, (qual_ref, table_ref) = refs[:chan_count], refs[chan_count : chan_count + 2]
    out_refs = refs[chan_count + 2 : chan_count + 5]
    mag_ref, white_ref, cross_ref, offs_ref, offs_sem = refs[chan_count + 5 :]
    fetch = pltpu.make_async_copy(offs_hbm_ref, offs_ref, offs_sem)
    fetch.start()
    me = where_ref[0]
    _, band, chans = spec_refs[0].shape
    freqs = chan_count * band
    chip_count, blocks, lag_rows, _ = out_refs[0].shape
    offset_count = offs_ref.shape[0]
    half = chan_count * lag_rows
    step = 64

    total = jnp.zeros((8, chans), jnp.float32)
    for number, spec_ref in enumerate(spec_refs):
        for row in range(0, band, step):
            real, imag = (spec_ref[part, row : row + step, :].astype(jnp.float32) for part in range(2))
            square = real * real + imag * imag
            magnitude = square * lax.rsqrt(jnp.maximum(square, 1e-30))
            held = slice(number * band + row, number * band + row + step)
            mag_ref[held, :] = magnitude
            total += jnp.sum(magnitude.reshape(step // 8, 8, chans), axis=0)
    level = jnp.sum(total, axis=0, keepdims=True) * (1.0 / freqs)
    floor = 0.5 * (level + 1e-05)

    for number, spec_ref in enumerate(spec_refs):
        for row in range(0, band, step):
            held = slice(number * band + row, number * band + row + step)
            factor = pl.reciprocal(mag_ref[held, :] + floor, approx=True)
            for part in range(2):
                value = spec_ref[part, row : row + step, :].astype(jnp.float32) * factor
                white_ref[part, held, :] = value.astype(jnp.bfloat16)

    lane = lax.broadcasted_iota(jnp.int32, (1, chans), 1)
    line = lax.broadcasted_iota(jnp.int32, (lag_rows, chans), 0)
    usable = qual_ref[pl.ds(me, 1), :].astype(jnp.float32)
    levels = jnp.zeros((lag_rows, chans), jnp.float32)
    core = me & 1
    orders = chips(chan_count)
    groups = [partner(orders, place, core) for place in range(chip_count)]
    groups += [partner(orders, place, 1 - core) ^ 1 for place in range(chip_count)]
    fetch.wait()
    per_band = table_ref.shape[0] // chan_count
    chunks = [(me ^ k) * per_band + chunk for k in order for chunk in range(per_band)]
    table = jnp.concatenate(
        [
            jnp.concatenate([table_ref[chunk, side, me ^ group] for side in range(2) for group in groups], axis=0)
            for chunk in chunks
        ],
        axis=1,
    )
    turns = [chans - offset_of(number, offs_ref, chan_count // 2) * (chans // chan_count) for number in range(offset_count)]
    for row in range(0, freqs, step):
        own = [white_ref[part, row : row + step, :] for part in range(2)]
        own_real, own_imag = (value.astype(jnp.float32) for value in own)
        for number, turn in enumerate(turns):
            far_real, far_imag = (pltpu.roll(value, turn, 1).astype(jnp.float32) for value in own)
            real = own_real * far_real + own_imag * far_imag
            imag = own_imag * far_real - own_real * far_imag
            cross_ref[number, 0, row : row + step, :] = real.astype(jnp.bfloat16)
            cross_ref[number, 1, row : row + step, :] = imag.astype(jnp.bfloat16)

    for number, turn in enumerate(turns):
        both = jnp.concatenate([cross_ref[number, 0], cross_ref[number, 1]], axis=1)
        sums = jnp.dot(table, both, preferred_element_type=jnp.float32)
        cos_real, sin_real = sums[:half, :chans], sums[half:, :chans]
        cos_imag, sin_imag = sums[:half, chans:], sums[half:, chans:]
        corr = (
            (cos_real - sin_imag, sin_real + cos_imag),
            (cos_real + sin_imag, cos_imag - sin_real),
        )
        power = [real * real + imag * imag for real, imag in corr]
        mean_power = jnp.sum(power[0] + power[1], axis=0, keepdims=True) * (1.0 / (2 * half))
        extra = 0.25 * (mean_power + 1e-06 * freqs)
        peak = jnp.max(jnp.maximum(jnp.abs(corr[0][0]), jnp.abs(corr[1][0])), axis=0, keepdims=True)
        code = level_code(peak)
        keep = jnp.where(lane < turn, usable * pltpu.roll(usable, turn, 1), 0.0) * CODE_TOP
        upscale = keep / level_of(code)
        inverse = [lax.rsqrt(side + extra) * keep for side in power]
        kinds = [
            [real * upscale for real, _ in corr],
            [real * scale for (real, _), scale in zip(corr, inverse)],
            [imag * scale for (_, imag), scale in zip(corr, inverse)],
        ]
        if number == offset_count - 1:
            code = jnp.where(lane < chans // 2, code, pltpu.roll(code, chans // 2, 1))
            kinds = [[jnp.where(lane < chans // 2, ahead, pltpu.roll(back, chans // 2, 1))] for ahead, back in kinds]
        levels = jnp.where(line == number, code, levels)
        for place, value in enumerate(value for kind in kinds for value in kind):
            coded = encode(value).reshape(chan_count, lag_rows, chans)
            begin = 0
            for out_ref in out_refs:
                out_ref[:, 6 * number + place, :, :] = coded[begin : begin + out_ref.shape[0]]
                begin += out_ref.shape[0]
    for number in range(offset_count):
        levels = jnp.where(line == offset_count + number, offs_ref[number].astype(jnp.float32), levels)
    wide = widest(offs_ref, chan_count // 2).astype(jnp.float32)
    levels = jnp.where(line == 2 * offset_count, wide, levels)
    for out_ref in out_refs:
        for chip in range(out_ref.shape[0]):
            out_ref[chip, blocks - 1, :, :] = encode(levels)


def merge_kernel(slots, own_ref, far_ref, more_ref, *out_refs):
    blocks = own_ref.shape[1]
    for chip, out_ref in enumerate(out_refs):
        far, from_far = (far_ref, chip) if chip < far_ref.shape[0] else (more_ref, chip - far_ref.shape[0])
        codes = [decode(own_ref[chip, blocks - 1]), decode(far[from_far, blocks - 1])]
        levels = [level_of(code) for code in codes]
        code = level_code(levels[0] + levels[1])
        shares = [level / level_of(code) for level in levels]
        line = lax.broadcasted_iota(jnp.int32, code.shape, 0)
        out_ref[blocks - 1, :, :] = encode(jnp.where(line < slots, code, codes[0]))
        for block in range(blocks - 1):
            number, part = divmod(block, 6)
            linear = part < (2 if blocks - 1 - 6 * number > 3 else 1)
            own, other = decode(own_ref[chip, block]), decode(far[from_far, block])
            if linear:
                total = own * shares[0][number : number + 1, :] + other * shares[1][number : number + 1, :]
            else:
                total = (own + other) * 0.5
            out_ref[block, :, :] = encode(total)


def sum_kernel(orders, scale, where_ref, core_ref, *refs):
    count = len(orders[0])
    code_refs, out_refs, held_ref = refs[: -count - 1], refs[-count - 1 : -1], refs[-1]
    blocks, _, chans = code_refs[0].shape
    slots = held_ref.shape[0]
    heads = [decode(codes_ref[blocks - 1]) for codes_ref in code_refs]
    levels = [level_of(head) * scale for head in heads]
    offsets = [heads[0][slots + number : slots + number + 1, :] for number in range(slots)]
    wide = heads[0][2 * slots : 2 * slots + 1, :]
    low = lax.broadcasted_iota(jnp.int32, (1, chans), 1) < chans // 2
    all_sums = []
    for number in range(slots):
        sides = 2 if number < slots - 1 else 1
        own = [level[number : number + 1, :] for level in levels]
        sums = []
        for place in range(3 * sides):
            codes = [decode(codes_ref[6 * number + place]) for codes_ref in code_refs]
            if place < sides:
                sums.append(sum(code * level for code, level in zip(codes, own)))
            else:
                sums.append(sum(codes) * (1.0 / len(code_refs)))
        if sides == 1:
            sums = [
                jnp.where(low, side, 0.0) for value in sums for side in (value, pltpu.roll(value, chans // 2, 1))
            ]
        all_sums.append(sums)
    line = lax.broadcasted_iota(jnp.int32, levels[0].shape, 0)
    last = slots - 1
    for number in range(slots):
        sums = all_sums[number]
        for other in range(last) if number == last else [last]:
            swap = wide == min(number, other)
            sums = [jnp.where(swap, value, kept) for value, kept in zip(all_sums[other], sums)]
        peak = jnp.max(jnp.maximum(jnp.abs(sums[0]), jnp.abs(sums[1])), axis=0, keepdims=True)
        code = level_code(peak)
        upscale = CODE_TOP / level_of(code)
        head = jnp.where(line == 0, code, offsets[number])
        for part, value in enumerate([sums[0] * upscale, sums[1] * upscale, *sums[2:], head]):
            held_ref[number, part, :, :] = encode(value)
    for place, out_ref in enumerate(out_refs):
        out_ref[...] = held_ref[where_ref[0] ^ partner(orders, place, core_ref[0] & 1)]


def partners(count):
    return sorted(range(1, count), key=lambda k: (-(k >> 1).bit_count(), k & 1, k)) + [0]


def chips(count):
    near = [k for k in range(2, count, 2) if k.bit_count() == 1]
    far = [k for k in range(2, count, 2) if k.bit_count() > 1]
    return near[::-1] + far + [0], near + far + [0]


def planes(count):
    others = partners(count)[:-1]
    return others + [0], others[1:] + others[:1] + [0]


def partner(orders, place, core):
    return jnp.where(core == 0, orders[0][place], orders[1][place])


def exchange(pieces, orders, over_tm=False):
    chan_count, tm_count = lax.axis_size("chan"), lax.axis_size("tm")
    arrived = []
    for place, piece in enumerate(pieces):
        pairs = []
        for source in range(chan_count * tm_count):
            k = orders[source // tm_count % 2][place]
            pairs.append((source, source ^ k if over_tm else source ^ (k * tm_count)))
        moved = any(source != target for source, target in pairs)
        arrived.append(lax.ppermute(piece, ("chan", "tm"), pairs) if moved else piece)
    return arrived


def split_kernel(order, spec_ref, *refs):
    out_refs, sems = refs[:-1], refs[-1]
    me = lax.axis_index("chan").astype(jnp.int32)
    copies = [
        pltpu.make_async_copy(spec_ref.at[:, me ^ k], out_ref, sems.at[number])
        for number, (k, out_ref) in enumerate(zip(order, out_refs))
    ]
    for copy in copies:
        copy.start()
    for copy in copies:
        copy.wait()


def stack_kernel(windows, where_ref, *refs):
    sums_refs, out_ref = refs[:-1], refs[-1]
    blocks, copies, rows, _ = out_ref.shape
    _, lag_rows, chans = sums_refs[0].shape
    per_sum = windows // len(sums_refs)
    heads = [decode(sums_ref[6]) for sums_ref in sums_refs]
    levels = [level_of(head[0:1, :]) * (1.0 / (CODE_TOP * windows)) for head in heads]
    stacks = []
    for side in range(2):
        linear = sum(decode(sums_ref[side]) * level for sums_ref, level in zip(sums_refs, levels))
        real, imag = (
            sum(decode(sums_ref[part + side]) for sums_ref in sums_refs) * (per_sum / (CODE_TOP * windows))
            for part in (2, 4)
        )
        stacks.append(linear * (real * real + imag * imag))
    offset = heads[0][1:2, :]
    lane = lax.broadcasted_iota(jnp.int32, (1, chans), 1)
    behind = [jnp.zeros_like(stack) for stack in stacks]
    for steps in range(1, blocks // 2 + 1):
        ahead = steps * (chans // blocks)
        chosen = (offset == steps) & (lane >= ahead)
        behind = [jnp.where(chosen, pltpu.roll(stack, ahead, 1), kept) for stack, kept in zip(stacks, behind)]
    back = stacks[1] + behind[0]
    back = jnp.concatenate([back[row : row + 1, :] for row in reversed(range(lag_rows))], axis=0)
    me = where_ref[0]
    even = (me & 1) == 0
    ahead = stacks[0] + behind[1]
    both = jnp.concatenate([jnp.where(even, ahead, back), jnp.where(even, back, ahead)], axis=0)
    parts = chans // (2 * lag_rows)
    turned = jnp.concatenate([both] * parts, axis=0).T
    unit = lane // lag_rows
    part_of = jnp.where(((unit ^ me) & 1) == 0, unit - me, unit + me + 1) % blocks // 2
    per_block = chans // blocks
    for block in range(blocks):
        piece = jnp.zeros((rows, chans), jnp.float32)
        for part in range(parts):
            begin = block * per_block + part * rows
            piece = jnp.where(part_of == part, turned[begin : begin + rows, :], piece)
        for copy in range(copies):
            out_ref[block, copy, :, :] = piece


def place_kernel(parts_ref, out_ref):
    groups, offset_count, rows, lanes = parts_ref.shape
    half = out_ref.shape[2] // 2
    lag_rows = half // groups
    parts = out_ref.shape[0] // rows
    unit = lax.broadcasted_iota(jnp.int32, (1, lanes), 1) // lag_rows
    for number in range(offset_count):
        pieces = [parts_ref[group, number] for group in range(groups)]
        for part in range(parts):
            sides = [jnp.zeros((rows, lanes), jnp.float32)] * 2
            for group, piece in enumerate(pieces):
                places = ((groups - 1 - group + 2 * part) % groups, (group + 2 * part) % groups)
                sides = [jnp.where(unit == place, piece, side) for place, side in zip(places, sides)]
            for side, value in enumerate(sides):
                value = pltpu.roll(value, (lanes - 2 * part * lag_rows) % lanes, 1) if part else value
                out_ref[part * rows : (part + 1) * rows, number, side * half : (side + 1) * half] = value


def window_shards(spectra, quality, offsets):
    chan_count = lax.axis_size("chan")
    tm_count = lax.axis_size("tm")
    _, windows, band, chans = spectra.shape
    freqs = band * chan_count
    half = LAGS // 2
    lag_rows = half // chan_count
    offset_count = offsets.shape[0]
    piece_rows = 2 * lag_rows // chan_count
    smem = pl.BlockSpec(memory_space=pltpu.SMEM)
    vmem = pl.BlockSpec(memory_space=pltpu.VMEM)
    params = pltpu.CompilerParams(vmem_limit_bytes=VMEM_LIMIT)
    table = half_table(freqs, LAGS).reshape(2, chan_count, lag_rows, freqs // 128, 128)
    table = jnp.asarray(np.ascontiguousarray(table.transpose(3, 0, 1, 2, 4)))
    chan_index = lax.axis_index("chan").astype(jnp.int32)
    tm_index = lax.axis_index("tm").astype(jnp.int32)
    chan_where, tm_where = chan_index.reshape(1), tm_index.reshape(1)

    chan_order, tm_orders = partners(chan_count), planes(tm_count)
    kept = pl.BlockSpec(memory_space=pltpu.HBM)
    spectra = pltpu.with_memory_space_constraint(spectra, pltpu.HBM)
    pieces = []
    for part in (chan_order[:2], chan_order[2:]):
        pieces += pl.pallas_call(
            functools.partial(split_kernel, part),
            out_shape=[jax.ShapeDtypeStruct((2, band, chans), spectra.dtype)] * len(part),
            in_specs=[kept],
            out_specs=[pl.BlockSpec(memory_space=pl.ANY)] * len(part),
            scratch_shapes=[pltpu.SemaphoreType.DMA((len(part),))],
            compiler_params=params,
            name="split_windows",
        )(spectra)
    chip_count = chan_count // 2
    pair_shape = (6 * offset_count - 2, lag_rows, chans)
    own, *far = pl.pallas_call(
        functools.partial(window_kernel, chan_order),
        out_shape=[
            jax.ShapeDtypeStruct((chips_in, *pair_shape), jnp.int16) for chips_in in (chip_count, chip_count // 2, chip_count // 2)
        ],
        in_specs=[kept, smem] + [vmem] * (chan_count + 2),
        out_specs=[vmem] * 3,
        scratch_shapes=[
            pltpu.VMEM((freqs, chans), jnp.float32),
            pltpu.VMEM((2, freqs, chans), jnp.bfloat16),
            pltpu.VMEM((offset_count, 2, freqs, chans), jnp.bfloat16),
            pltpu.SMEM(offsets.shape, jnp.int32),
            pltpu.SemaphoreType.DMA(()),
        ],
        compiler_params=params,
        name="window_pairs",
    )(pltpu.with_memory_space_constraint(offsets, pltpu.HBM), chan_where, *exchange(pieces, (chan_order, chan_order)), quality, table)
    pairs = pl.pallas_call(
        functools.partial(merge_kernel, offset_count),
        out_shape=[jax.ShapeDtypeStruct(pair_shape, jnp.int16)] * chip_count,
        in_specs=[vmem] * 3,
        out_specs=[vmem] * chip_count,
        compiler_params=params,
        name="merge_windows",
    )(own, *exchange(far, ([1, 1], [1, 1])))
    sums = pl.pallas_call(
        functools.partial(sum_kernel, tm_orders, 1.0 / (CODE_TOP * math.sqrt(freqs))),
        out_shape=[jax.ShapeDtypeStruct((7, lag_rows, chans), jnp.int16)] * tm_count,
        in_specs=[smem, smem] + [vmem] * chip_count,
        out_specs=[vmem] * tm_count,
        scratch_shapes=[pltpu.VMEM((offset_count, 7, lag_rows, chans), jnp.int16)],
        compiler_params=params,
        name="sum_windows",
    )(tm_where, chan_where, *exchange(pairs, chips(chan_count)))
    pieces = pl.pallas_call(
        functools.partial(stack_kernel, windows * tm_count),
        out_shape=jax.ShapeDtypeStruct((chan_count, tm_count, piece_rows, chans), jnp.float32),
        in_specs=[smem] + [vmem] * tm_count,
        out_specs=vmem,
        compiler_params=params,
        name="stack_pairs",
    )(chan_where, *exchange(sums, tm_orders, over_tm=True))
    shape = (chan_count * tm_count, piece_rows, chans)
    arrived = lax.all_to_all(pieces.reshape(shape), ("chan", "tm"), 0, 0, tiled=True)
    return pl.pallas_call(
        place_kernel,
        out_shape=jax.ShapeDtypeStruct((CH_DEV, offset_count, LAGS), jnp.float32),
        in_specs=[vmem],
        out_specs=vmem,
        compiler_params=params,
        name="place_lags",
    )(arrived.reshape(chan_count, tm_count, piece_rows, chans))


def shifted(value, axis, steps):
    count = lax.axis_size(axis)
    leading, last = (max(0, -steps), min(count, count - steps))
    return lax.ppermute(value, axis, [(source, source + steps) for source in range(leading, last)])


def lag_table(freq_count, lag_count):
    freq_index = jnp.arange(freq_count, dtype=jnp.int32)[:, None]
    double_lag = (2 * jnp.arange(lag_count, dtype=jnp.int32) - lag_count + 1)[None, :]
    turns = jnp.mod(freq_index * double_lag, 4 * freq_count)
    angles = turns.astype(jnp.float32) * (2.0 * math.pi / (4 * freq_count))
    cosine = jnp.cos(angles)
    sine = jnp.sin(angles)
    upper = jnp.concatenate([cosine, sine], axis=1)
    lower = jnp.concatenate([-sine, cosine], axis=1)
    return jnp.stack([upper, lower]).astype(jnp.bfloat16)


def whiten_parts(real_part, imag_part, magnitude, channel_level, usable):
    factor = usable.astype(jnp.float32)[:, None, :] / (magnitude + 0.5 * (channel_level + 1e-05))
    return jnp.stack([real_part * factor, imag_part * factor]).astype(jnp.bfloat16)


def cross_parts(own_real, own_imag, far_real, far_imag):
    own_real = own_real.astype(jnp.float32)
    own_imag = own_imag.astype(jnp.float32)
    far_real = far_real.astype(jnp.float32)
    far_imag = far_imag.astype(jnp.float32)
    return jnp.stack(
        [own_real * far_real + own_imag * far_imag, own_imag * far_real - own_real * far_imag]
    ).astype(jnp.bfloat16)


def pair_terms(corr_all):
    lag_count = corr_all.shape[-1] // 2
    real_corr = corr_all[..., :lag_count]
    imag_corr = corr_all[..., lag_count:]
    power = real_corr * real_corr + imag_corr * imag_corr
    mean_power = jnp.mean(power, axis=-1, keepdims=True)
    denominator = jnp.sqrt(power + 0.25 * (mean_power + 1e-06))
    return (
        jnp.sum(real_corr, axis=-3),
        jnp.sum(real_corr / denominator, axis=-3),
        jnp.sum(imag_corr / denominator, axis=-3),
    )


def shards(spectra, quality, offsets):
    chan_count = lax.axis_size("chan")
    tm_count = lax.axis_size("tm")
    levels = chan_count.bit_length() - 1
    table_bf = lag_table(F, LAGS)
    inv_root = 1.0 / math.sqrt(F)
    real_part = spectra[0].astype(jnp.float32)
    imag_part = spectra[1].astype(jnp.float32)
    magnitude = jnp.sqrt(real_part * real_part + imag_part * imag_part)
    band_total = lax.psum(jnp.sum(magnitude, axis=1), "chan")
    channel_level = (band_total / F)[:, None, :]
    whitened = whiten_parts(real_part, imag_part, magnitude, channel_level, quality)
    width_all = whitened.shape[3]
    padded = jnp.pad(whitened, ((0, 0), (0, 0), (0, 0), (0, width_all)))
    crossed_list = []
    for offset_index in range(NOFF):
        partner = lax.dynamic_slice_in_dim(padded, offsets[offset_index] * CH_DEV, width_all, 3)
        crossed_list.append(cross_parts(whitened[0], whitened[1], partner[0], partner[1]))
    crossed = jnp.stack(crossed_list, axis=1)
    corr_all = jnp.einsum(
        "cnwfh,cfl->nwhl",
        lax.all_to_all(crossed, "chan", split_axis=4, concat_axis=3, tiled=True),
        table_bf,
        preferred_element_type=jnp.float32,
    )
    linear_sum, real_sum, imag_sum = pair_terms(corr_all * inv_root)
    totals = lax.psum((linear_sum, real_sum, imag_sum), "tm")
    window_count = W_DEV * tm_count
    linear = totals[0] / window_count
    real_phase = totals[1] / window_count
    imag_phase = totals[2] / window_count
    stacks = jnp.transpose(linear * (real_phase * real_phase + imag_phase * imag_phase), (1, 0, 2))
    reverse_part = stacks
    for bit_index in range(levels):
        step_size = 1 << bit_index
        arrived = shifted(reverse_part, "chan", step_size)
        chosen = offsets // step_size % 2 == 1
        reverse_part = jnp.where(chosen[None, :, None], arrived, reverse_part)
    return stacks + jnp.flip(reverse_part, axis=2)


def solution(mesh):
    chan_count, tm_count = mesh.shape["chan"], mesh.shape["tm"]
    by_window = chan_count == W_DEV and tm_count == NOFF
    return jax.shard_map(
        window_shards if by_window else shards,
        mesh=mesh,
        in_specs=(P(None, "tm", "chan", None), P("tm", None), P()),
        out_specs=P("chan", None, None),
        check_vma=False,
    )
```

```python
import functools
import math

import jax
import jax.numpy as jnp
import numpy as np
from jax import lax
from jax.experimental import pallas as pl
from jax.experimental.pallas import tpu as pltpu
from jax.sharding import PartitionSpec as P

F = 2048
LAGS = 256
NOFF = 4
CH_DEV = 16
W_DEV = 8
VMEM_LIMIT = 48 * 1024 * 1024
CODE_TOP = 32767.0
OCTAVE = 256.0
LOWEST = -110.0


def encode(value):
    return jnp.round(value).astype(jnp.int32).astype(jnp.int16)


def decode(code):
    return code.astype(jnp.int32).astype(jnp.float32)


def level_code(peak):
    return jnp.ceil(jnp.maximum(jnp.log2(jnp.maximum(peak, 1e-30)), LOWEST) * OCTAVE) + 1.0


def level_of(code):
    return jnp.exp2(code * (1.0 / OCTAVE))


def half_table(freq_count, lag_count):
    freq_index = np.arange(freq_count, dtype=np.int64)[None, :]
    double_lag = (2 * np.arange(lag_count // 2, lag_count, dtype=np.int64) - lag_count + 1)[:, None]
    turns = np.mod(freq_index * double_lag, 4 * freq_count).astype(np.float32)
    angles = turns * np.float32(2.0 * math.pi / (4 * freq_count))
    return np.concatenate([np.cos(angles), np.sin(angles)]).astype(jnp.bfloat16)


def widest(offs_ref, reach):
    last = offs_ref.shape[0] - 1
    found = last
    for number in reversed(range(last)):
        found = jnp.where(offs_ref[number] == reach, number, found)
    return found


def offset_of(slot, offs_ref, reach):
    last, wide = offs_ref.shape[0] - 1, widest(offs_ref, reach)
    return offs_ref[jnp.where(slot == wide, last, jnp.where(slot == last, wide, slot))]


def window_kernel(order, offs_hbm_ref, where_ref, *refs):
    chan_count = len(order)
    spec_refs, (qual_ref, table_ref) = refs[:chan_count], refs[chan_count : chan_count + 2]
    out_refs = refs[chan_count + 2 : chan_count + 6]
    mag_ref, white_ref, cross_ref, offs_ref, offs_sem = refs[chan_count + 6 :]
    fetch = pltpu.make_async_copy(offs_hbm_ref, offs_ref, offs_sem)
    fetch.start()
    me = where_ref[0]
    _, band, chans = spec_refs[0].shape
    freqs = chan_count * band
    chip_count = chan_count // 2
    _, blocks, lag_rows, _ = out_refs[0].shape
    offset_count = offs_ref.shape[0]
    half = chan_count * lag_rows
    step = 64

    total = jnp.zeros((8, chans), jnp.float32)
    for number, spec_ref in enumerate(spec_refs):
        for row in range(0, band, step):
            real, imag = (spec_ref[part, row : row + step, :].astype(jnp.float32) for part in range(2))
            square = real * real + imag * imag
            magnitude = square * lax.rsqrt(jnp.maximum(square, 1e-30))
            held = slice(number * band + row, number * band + row + step)
            mag_ref[held, :] = magnitude
            total += jnp.sum(magnitude.reshape(step // 8, 8, chans), axis=0)
    level = jnp.sum(total, axis=0, keepdims=True) * (1.0 / freqs)
    floor = 0.5 * (level + 1e-05)

    for number, spec_ref in enumerate(spec_refs):
        for row in range(0, band, step):
            held = slice(number * band + row, number * band + row + step)
            factor = pl.reciprocal(mag_ref[held, :] + floor, approx=True)
            for part in range(2):
                value = spec_ref[part, row : row + step, :].astype(jnp.float32) * factor
                white_ref[part, held, :] = value.astype(jnp.bfloat16)

    lane = lax.broadcasted_iota(jnp.int32, (1, chans), 1)
    line = lax.broadcasted_iota(jnp.int32, (lag_rows, chans), 0)
    usable = qual_ref[pl.ds(me, 1), :].astype(jnp.float32)
    levels = jnp.zeros((lag_rows, chans), jnp.float32)
    core = me & 1
    orders = chips(chan_count)
    groups = [partner(orders, place, core) for place in range(chip_count)]
    groups += [partner(orders, place, 1 - core) ^ 1 for place in range(chip_count)]
    fetch.wait()
    per_band = table_ref.shape[0] // chan_count
    chunks = [(me ^ k) * per_band + chunk for k in order for chunk in range(per_band)]
    table = jnp.concatenate(
        [
            jnp.concatenate([table_ref[chunk, side, me ^ group] for side in range(2) for group in groups], axis=0)
            for chunk in chunks
        ],
        axis=1,
    )
    turns = [chans - offset_of(number, offs_ref, chan_count // 2) * (chans // chan_count) for number in range(offset_count)]
    for row in range(0, freqs, step):
        own = [white_ref[part, row : row + step, :] for part in range(2)]
        own_real, own_imag = (value.astype(jnp.float32) for value in own)
        for number, turn in enumerate(turns):
            far_real, far_imag = (pltpu.roll(value, turn, 1).astype(jnp.float32) for value in own)
            real = own_real * far_real + own_imag * far_imag
            imag = own_imag * far_real - own_real * far_imag
            cross_ref[number, 0, row : row + step, :] = real.astype(jnp.bfloat16)
            cross_ref[number, 1, row : row + step, :] = imag.astype(jnp.bfloat16)

    for number, turn in enumerate(turns):
        both = jnp.concatenate([cross_ref[number, 0], cross_ref[number, 1]], axis=1)
        sums = jnp.dot(table, both, preferred_element_type=jnp.float32)
        cos_real, sin_real = sums[:half, :chans], sums[half:, :chans]
        cos_imag, sin_imag = sums[:half, chans:], sums[half:, chans:]
        corr = (
            (cos_real - sin_imag, sin_real + cos_imag),
            (cos_real + sin_imag, cos_imag - sin_real),
        )
        power = [real * real + imag * imag for real, imag in corr]
        mean_power = jnp.sum(power[0] + power[1], axis=0, keepdims=True) * (1.0 / (2 * half))
        extra = 0.25 * (mean_power + 1e-06 * freqs)
        peak = jnp.max(jnp.maximum(jnp.abs(corr[0][0]), jnp.abs(corr[1][0])), axis=0, keepdims=True)
        code = level_code(peak)
        keep = jnp.where(lane < turn, usable * pltpu.roll(usable, turn, 1), 0.0) * CODE_TOP
        upscale = keep / level_of(code)
        inverse = [lax.rsqrt(side + extra) * keep for side in power]
        kinds = [
            [real * upscale for real, _ in corr],
            [real * scale for (real, _), scale in zip(corr, inverse)],
            [imag * scale for (_, imag), scale in zip(corr, inverse)],
        ]
        if number == offset_count - 1:
            code = jnp.where(lane < chans // 2, code, pltpu.roll(code, chans // 2, 1))
            kinds = [[jnp.where(lane < chans // 2, ahead, pltpu.roll(back, chans // 2, 1))] for ahead, back in kinds]
        levels = jnp.where(line == number, code, levels)
        for place, value in enumerate(value for kind in kinds for value in kind):
            coded = encode(value).reshape(chan_count, lag_rows, chans)
            begin = 0
            for out_ref in out_refs:
                out_ref[:, 6 * number + place, :, :] = coded[begin : begin + out_ref.shape[0]]
                begin += out_ref.shape[0]
    for number in range(offset_count):
        levels = jnp.where(line == offset_count + number, offs_ref[number].astype(jnp.float32), levels)
    wide = widest(offs_ref, chan_count // 2).astype(jnp.float32)
    levels = jnp.where(line == 2 * offset_count, wide, levels)
    for out_ref in out_refs:
        for chip in range(out_ref.shape[0]):
            out_ref[chip, blocks - 1, :, :] = encode(levels)


def merge_kernel(slots, own_ref, far_ref, *out_refs):
    blocks = own_ref.shape[1]
    for chip, out_ref in enumerate(out_refs):
        codes = [decode(ref[chip, blocks - 1]) for ref in (own_ref, far_ref)]
        levels = [level_of(code) for code in codes]
        code = level_code(levels[0] + levels[1])
        shares = [level / level_of(code) for level in levels]
        line = lax.broadcasted_iota(jnp.int32, code.shape, 0)
        out_ref[blocks - 1, :, :] = encode(jnp.where(line < slots, code, codes[0]))
        for block in range(blocks - 1):
            number, part = divmod(block, 6)
            linear = part < (2 if blocks - 1 - 6 * number > 3 else 1)
            own, far = decode(own_ref[chip, block]), decode(far_ref[chip, block])
            if linear:
                total = own * shares[0][number : number + 1, :] + far * shares[1][number : number + 1, :]
            else:
                total = (own + far) * 0.5
            out_ref[block, :, :] = encode(total)


def sum_kernel(orders, scale, where_ref, core_ref, *refs):
    count = len(orders[0])
    code_refs, out_refs, held_ref = refs[: -count - 1], refs[-count - 1 : -1], refs[-1]
    blocks, _, chans = code_refs[0].shape
    slots = held_ref.shape[0]
    heads = [decode(codes_ref[blocks - 1]) for codes_ref in code_refs]
    levels = [level_of(head) * scale for head in heads]
    offsets = [heads[0][slots + number : slots + number + 1, :] for number in range(slots)]
    wide = heads[0][2 * slots : 2 * slots + 1, :]
    low = lax.broadcasted_iota(jnp.int32, (1, chans), 1) < chans // 2
    all_sums = []
    for number in range(slots):
        sides = 2 if number < slots - 1 else 1
        own = [level[number : number + 1, :] for level in levels]
        sums = []
        for place in range(3 * sides):
            codes = [decode(codes_ref[6 * number + place]) for codes_ref in code_refs]
            if place < sides:
                sums.append(sum(code * level for code, level in zip(codes, own)))
            else:
                sums.append(sum(codes) * (1.0 / len(code_refs)))
        if sides == 1:
            sums = [
                jnp.where(low, side, 0.0) for value in sums for side in (value, pltpu.roll(value, chans // 2, 1))
            ]
        all_sums.append(sums)
    line = lax.broadcasted_iota(jnp.int32, levels[0].shape, 0)
    last = slots - 1
    for number in range(slots):
        sums = all_sums[number]
        for other in range(last) if number == last else [last]:
            swap = wide == min(number, other)
            sums = [jnp.where(swap, value, kept) for value, kept in zip(all_sums[other], sums)]
        peak = jnp.max(jnp.maximum(jnp.abs(sums[0]), jnp.abs(sums[1])), axis=0, keepdims=True)
        code = level_code(peak)
        upscale = CODE_TOP / level_of(code)
        head = jnp.where(line == 0, code, offsets[number])
        for part, value in enumerate([sums[0] * upscale, sums[1] * upscale, *sums[2:], head]):
            held_ref[number, part, :, :] = encode(value)
    for place, out_ref in enumerate(out_refs):
        out_ref[...] = held_ref[where_ref[0] ^ partner(orders, place, core_ref[0] & 1)]


def partners(count):
    return sorted(range(1, count), key=lambda k: (-(k >> 1).bit_count(), k & 1, k)) + [0]


def chips(count):
    near = [k for k in range(2, count, 2) if k.bit_count() == 1]
    far = [k for k in range(2, count, 2) if k.bit_count() > 1]
    return near[::-1] + far + [0], near + far + [0]


def planes(count):
    others = partners(count)[:-1]
    return others + [0], others[1:] + others[:1] + [0]


def partner(orders, place, core):
    return jnp.where(core == 0, orders[0][place], orders[1][place])


def exchange(pieces, orders, over_tm=False):
    chan_count, tm_count = lax.axis_size("chan"), lax.axis_size("tm")
    arrived = []
    for place, piece in enumerate(pieces):
        pairs = []
        for source in range(chan_count * tm_count):
            k = orders[source // tm_count % 2][place]
            pairs.append((source, source ^ k if over_tm else source ^ (k * tm_count)))
        moved = any(source != target for source, target in pairs)
        arrived.append(lax.ppermute(piece, ("chan", "tm"), pairs) if moved else piece)
    return arrived


def split_kernel(order, spec_ref, *refs):
    out_refs, sems = refs[:-1], refs[-1]
    me = lax.axis_index("chan").astype(jnp.int32)
    copies = [
        pltpu.make_async_copy(spec_ref.at[:, me ^ k], out_ref, sems.at[number])
        for number, (k, out_ref) in enumerate(zip(order, out_refs))
    ]
    for copy in copies:
        copy.start()
    for copy in copies:
        copy.wait()


def stack_kernel(windows, where_ref, *refs):
    sums_refs, out_ref = refs[:-1], refs[-1]
    blocks, copies, rows, _ = out_ref.shape
    _, lag_rows, chans = sums_refs[0].shape
    per_sum = windows // len(sums_refs)
    heads = [decode(sums_ref[6]) for sums_ref in sums_refs]
    levels = [level_of(head[0:1, :]) * (1.0 / (CODE_TOP * windows)) for head in heads]
    stacks = []
    for side in range(2):
        linear = sum(decode(sums_ref[side]) * level for sums_ref, level in zip(sums_refs, levels))
        real, imag = (
            sum(decode(sums_ref[part + side]) for sums_ref in sums_refs) * (per_sum / (CODE_TOP * windows))
            for part in (2, 4)
        )
        stacks.append(linear * (real * real + imag * imag))
    offset = heads[0][1:2, :]
    lane = lax.broadcasted_iota(jnp.int32, (1, chans), 1)
    behind = [jnp.zeros_like(stack) for stack in stacks]
    for steps in range(1, blocks // 2 + 1):
        ahead = steps * (chans // blocks)
        chosen = (offset == steps) & (lane >= ahead)
        behind = [jnp.where(chosen, pltpu.roll(stack, ahead, 1), kept) for stack, kept in zip(stacks, behind)]
    back = stacks[1] + behind[0]
    back = jnp.concatenate([back[row : row + 1, :] for row in reversed(range(lag_rows))], axis=0)
    me = where_ref[0]
    even = (me & 1) == 0
    ahead = stacks[0] + behind[1]
    both = jnp.concatenate([jnp.where(even, ahead, back), jnp.where(even, back, ahead)], axis=0)
    parts = chans // (2 * lag_rows)
    turned = jnp.concatenate([both] * parts, axis=0).T
    unit = lane // lag_rows
    part_of = jnp.where(((unit ^ me) & 1) == 0, unit - me, unit + me + 1) % blocks // 2
    per_block = chans // blocks
    for block in range(blocks):
        piece = jnp.zeros((rows, chans), jnp.float32)
        for part in range(parts):
            begin = block * per_block + part * rows
            piece = jnp.where(part_of == part, turned[begin : begin + rows, :], piece)
        for copy in range(copies):
            out_ref[block, copy, :, :] = piece


def place_kernel(parts_ref, out_ref):
    groups, offset_count, rows, lanes = parts_ref.shape
    half = out_ref.shape[2] // 2
    lag_rows = half // groups
    parts = out_ref.shape[0] // rows
    unit = lax.broadcasted_iota(jnp.int32, (1, lanes), 1) // lag_rows
    for number in range(offset_count):
        pieces = [parts_ref[group, number] for group in range(groups)]
        for part in range(parts):
            sides = [jnp.zeros((rows, lanes), jnp.float32)] * 2
            for group, piece in enumerate(pieces):
                places = ((groups - 1 - group + 2 * part) % groups, (group + 2 * part) % groups)
                sides = [jnp.where(unit == place, piece, side) for place, side in zip(places, sides)]
            for side, value in enumerate(sides):
                value = pltpu.roll(value, (lanes - 2 * part * lag_rows) % lanes, 1) if part else value
                out_ref[part * rows : (part + 1) * rows, number, side * half : (side + 1) * half] = value


def window_shards(spectra, quality, offsets):
    chan_count = lax.axis_size("chan")
    tm_count = lax.axis_size("tm")
    _, windows, band, chans = spectra.shape
    freqs = band * chan_count
    half = LAGS // 2
    lag_rows = half // chan_count
    offset_count = offsets.shape[0]
    piece_rows = 2 * lag_rows // chan_count
    smem = pl.BlockSpec(memory_space=pltpu.SMEM)
    vmem = pl.BlockSpec(memory_space=pltpu.VMEM)
    params = pltpu.CompilerParams(vmem_limit_bytes=VMEM_LIMIT)
    table = half_table(freqs, LAGS).reshape(2, chan_count, lag_rows, freqs // 128, 128)
    table = jnp.asarray(np.ascontiguousarray(table.transpose(3, 0, 1, 2, 4)))
    chan_index = lax.axis_index("chan").astype(jnp.int32)
    tm_index = lax.axis_index("tm").astype(jnp.int32)
    chan_where, tm_where = chan_index.reshape(1), tm_index.reshape(1)

    chan_order, tm_orders = partners(chan_count), planes(tm_count)
    kept = pl.BlockSpec(memory_space=pltpu.HBM)
    spectra = pltpu.with_memory_space_constraint(spectra, pltpu.HBM)
    pieces = []
    for part in (chan_order[:2], chan_order[2:]):
        pieces += pl.pallas_call(
            functools.partial(split_kernel, part),
            out_shape=[jax.ShapeDtypeStruct((2, band, chans), spectra.dtype)] * len(part),
            in_specs=[kept],
            out_specs=[pl.BlockSpec(memory_space=pl.ANY)] * len(part),
            scratch_shapes=[pltpu.SemaphoreType.DMA((len(part),))],
            compiler_params=params,
            name="split_windows",
        )(spectra)
    chip_count = chan_count // 2
    pair_shape = (6 * offset_count - 2, lag_rows, chans)
    first_half, second_half, *far = pl.pallas_call(
        functools.partial(window_kernel, chan_order),
        out_shape=[jax.ShapeDtypeStruct((chip_count // 2, *pair_shape), jnp.int16)] * 4,
        in_specs=[kept, smem] + [vmem] * (chan_count + 2),
        out_specs=[vmem] * 4,
        scratch_shapes=[
            pltpu.VMEM((freqs, chans), jnp.float32),
            pltpu.VMEM((2, freqs, chans), jnp.bfloat16),
            pltpu.VMEM((offset_count, 2, freqs, chans), jnp.bfloat16),
            pltpu.SMEM(offsets.shape, jnp.int32),
            pltpu.SemaphoreType.DMA(()),
        ],
        compiler_params=params,
        name="window_pairs",
    )(pltpu.with_memory_space_constraint(offsets, pltpu.HBM), chan_where, *exchange(pieces, (chan_order, chan_order)), quality, table)
    pairs = []
    for own, other in zip((first_half, second_half), exchange(far, ([1, 1], [1, 1]))):
        pairs += pl.pallas_call(
            functools.partial(merge_kernel, offset_count),
            out_shape=[jax.ShapeDtypeStruct(pair_shape, jnp.int16)] * (chip_count // 2),
            in_specs=[vmem] * 2,
            out_specs=[vmem] * (chip_count // 2),
            compiler_params=params,
            name="merge_windows",
        )(own, other)
    sums = pl.pallas_call(
        functools.partial(sum_kernel, tm_orders, 1.0 / (CODE_TOP * math.sqrt(freqs))),
        out_shape=[jax.ShapeDtypeStruct((7, lag_rows, chans), jnp.int16)] * tm_count,
        in_specs=[smem, smem] + [vmem] * chip_count,
        out_specs=[vmem] * tm_count,
        scratch_shapes=[pltpu.VMEM((offset_count, 7, lag_rows, chans), jnp.int16)],
        compiler_params=params,
        name="sum_windows",
    )(tm_where, chan_where, *exchange(pairs, chips(chan_count)))
    pieces = pl.pallas_call(
        functools.partial(stack_kernel, windows * tm_count),
        out_shape=jax.ShapeDtypeStruct((chan_count, tm_count, piece_rows, chans), jnp.float32),
        in_specs=[smem] + [vmem] * tm_count,
        out_specs=vmem,
        compiler_params=params,
        name="stack_pairs",
    )(chan_where, *exchange(sums, tm_orders, over_tm=True))
    shape = (chan_count * tm_count, piece_rows, chans)
    arrived = lax.all_to_all(pieces.reshape(shape), ("chan", "tm"), 0, 0, tiled=True)
    return pl.pallas_call(
        place_kernel,
        out_shape=jax.ShapeDtypeStruct((CH_DEV, offset_count, LAGS), jnp.float32),
        in_specs=[vmem],
        out_specs=vmem,
        compiler_params=params,
        name="place_lags",
    )(arrived.reshape(chan_count, tm_count, piece_rows, chans))


def shifted(value, axis, steps):
    count = lax.axis_size(axis)
    leading, last = (max(0, -steps), min(count, count - steps))
    return lax.ppermute(value, axis, [(source, source + steps) for source in range(leading, last)])


def lag_table(freq_count, lag_count):
    freq_index = jnp.arange(freq_count, dtype=jnp.int32)[:, None]
    double_lag = (2 * jnp.arange(lag_count, dtype=jnp.int32) - lag_count + 1)[None, :]
    turns = jnp.mod(freq_index * double_lag, 4 * freq_count)
    angles = turns.astype(jnp.float32) * (2.0 * math.pi / (4 * freq_count))
    cosine = jnp.cos(angles)
    sine = jnp.sin(angles)
    upper = jnp.concatenate([cosine, sine], axis=1)
    lower = jnp.concatenate([-sine, cosine], axis=1)
    return jnp.stack([upper, lower]).astype(jnp.bfloat16)


def whiten_parts(real_part, imag_part, magnitude, channel_level, usable):
    factor = usable.astype(jnp.float32)[:, None, :] / (magnitude + 0.5 * (channel_level + 1e-05))
    return jnp.stack([real_part * factor, imag_part * factor]).astype(jnp.bfloat16)


def cross_parts(own_real, own_imag, far_real, far_imag):
    own_real = own_real.astype(jnp.float32)
    own_imag = own_imag.astype(jnp.float32)
    far_real = far_real.astype(jnp.float32)
    far_imag = far_imag.astype(jnp.float32)
    return jnp.stack(
        [own_real * far_real + own_imag * far_imag, own_imag * far_real - own_real * far_imag]
    ).astype(jnp.bfloat16)


def pair_terms(corr_all):
    lag_count = corr_all.shape[-1] // 2
    real_corr = corr_all[..., :lag_count]
    imag_corr = corr_all[..., lag_count:]
    power = real_corr * real_corr + imag_corr * imag_corr
    mean_power = jnp.mean(power, axis=-1, keepdims=True)
    denominator = jnp.sqrt(power + 0.25 * (mean_power + 1e-06))
    return (
        jnp.sum(real_corr, axis=-3),
        jnp.sum(real_corr / denominator, axis=-3),
        jnp.sum(imag_corr / denominator, axis=-3),
    )


def shards(spectra, quality, offsets):
    chan_count = lax.axis_size("chan")
    tm_count = lax.axis_size("tm")
    levels = chan_count.bit_length() - 1
    table_bf = lag_table(F, LAGS)
    inv_root = 1.0 / math.sqrt(F)
    real_part = spectra[0].astype(jnp.float32)
    imag_part = spectra[1].astype(jnp.float32)
    magnitude = jnp.sqrt(real_part * real_part + imag_part * imag_part)
    band_total = lax.psum(jnp.sum(magnitude, axis=1), "chan")
    channel_level = (band_total / F)[:, None, :]
    whitened = whiten_parts(real_part, imag_part, magnitude, channel_level, quality)
    width_all = whitened.shape[3]
    padded = jnp.pad(whitened, ((0, 0), (0, 0), (0, 0), (0, width_all)))
    crossed_list = []
    for offset_index in range(NOFF):
        partner = lax.dynamic_slice_in_dim(padded, offsets[offset_index] * CH_DEV, width_all, 3)
        crossed_list.append(cross_parts(whitened[0], whitened[1], partner[0], partner[1]))
    crossed = jnp.stack(crossed_list, axis=1)
    corr_all = jnp.einsum(
        "cnwfh,cfl->nwhl",
        lax.all_to_all(crossed, "chan", split_axis=4, concat_axis=3, tiled=True),
        table_bf,
        preferred_element_type=jnp.float32,
    )
    linear_sum, real_sum, imag_sum = pair_terms(corr_all * inv_root)
    totals = lax.psum((linear_sum, real_sum, imag_sum), "tm")
    window_count = W_DEV * tm_count
    linear = totals[0] / window_count
    real_phase = totals[1] / window_count
    imag_phase = totals[2] / window_count
    stacks = jnp.transpose(linear * (real_phase * real_phase + imag_phase * imag_phase), (1, 0, 2))
    reverse_part = stacks
    for bit_index in range(levels):
        step_size = 1 << bit_index
        arrived = shifted(reverse_part, "chan", step_size)
        chosen = offsets // step_size % 2 == 1
        reverse_part = jnp.where(chosen[None, :, None], arrived, reverse_part)
    return stacks + jnp.flip(reverse_part, axis=2)


def solution(mesh):
    chan_count, tm_count = mesh.shape["chan"], mesh.shape["tm"]
    by_window = chan_count == W_DEV and tm_count == NOFF
    return jax.shard_map(
        window_shards if by_window else shards,
        mesh=mesh,
        in_specs=(P(None, "tm", "chan", None), P("tm", None), P()),
        out_specs=P("chan", None, None),
        check_vma=False,
    )
```

```python
import functools
import math

import jax
import jax.numpy as jnp
import numpy as np
from jax import lax
from jax.experimental import pallas as pl
from jax.experimental.pallas import tpu as pltpu
from jax.sharding import PartitionSpec as P

F = 2048
LAGS = 256
NOFF = 4
CH_DEV = 16
W_DEV = 8
VMEM_LIMIT = 48 * 1024 * 1024
CODE_TOP = 32767.0
OCTAVE = 256.0
LOWEST = -110.0


def encode(value):
    return jnp.round(value).astype(jnp.int32).astype(jnp.int16)


def decode(code):
    return code.astype(jnp.int32).astype(jnp.float32)


def level_code(peak):
    return jnp.ceil(jnp.maximum(jnp.log2(jnp.maximum(peak, 1e-30)), LOWEST) * OCTAVE) + 1.0


def level_of(code):
    return jnp.exp2(code * (1.0 / OCTAVE))


def half_table(freq_count, lag_count):
    freq_index = np.arange(freq_count, dtype=np.int64)[None, :]
    double_lag = (2 * np.arange(lag_count // 2, lag_count, dtype=np.int64) - lag_count + 1)[:, None]
    turns = np.mod(freq_index * double_lag, 4 * freq_count).astype(np.float32)
    angles = turns * np.float32(2.0 * math.pi / (4 * freq_count))
    return np.concatenate([np.cos(angles), np.sin(angles)]).astype(jnp.bfloat16)


def widest(offs_ref, reach):
    last = offs_ref.shape[0] - 1
    found = last
    for number in reversed(range(last)):
        found = jnp.where(offs_ref[number] == reach, number, found)
    return found


def offset_of(slot, offs_ref, reach):
    last, wide = offs_ref.shape[0] - 1, widest(offs_ref, reach)
    return offs_ref[jnp.where(slot == wide, last, jnp.where(slot == last, wide, slot))]


def window_kernel(order, offs_hbm_ref, where_ref, *refs):
    chan_count = len(order)
    spec_refs, (qual_ref, table_ref) = refs[:chan_count], refs[chan_count : chan_count + 2]
    out_refs = refs[chan_count + 2 : chan_count + 6]
    mag_ref, white_ref, cross_ref, offs_ref, offs_sem = refs[chan_count + 6 :]
    fetch = pltpu.make_async_copy(offs_hbm_ref, offs_ref, offs_sem)
    fetch.start()
    me = where_ref[0]
    _, band, chans = spec_refs[0].shape
    freqs = chan_count * band
    chip_count = chan_count // 2
    _, blocks, lag_rows, _ = out_refs[0].shape
    offset_count = offs_ref.shape[0]
    half = chan_count * lag_rows
    step = 64

    total = jnp.zeros((8, chans), jnp.float32)
    for number, spec_ref in enumerate(spec_refs):
        for row in range(0, band, step):
            real, imag = (spec_ref[part, row : row + step, :].astype(jnp.float32) for part in range(2))
            square = real * real + imag * imag
            magnitude = square * lax.rsqrt(jnp.maximum(square, 1e-30))
            held = slice(number * band + row, number * band + row + step)
            mag_ref[held, :] = magnitude
            total += jnp.sum(magnitude.reshape(step // 8, 8, chans), axis=0)
    level = jnp.sum(total, axis=0, keepdims=True) * (1.0 / freqs)
    floor = 0.5 * (level + 1e-05)

    for number, spec_ref in enumerate(spec_refs):
        for row in range(0, band, step):
            held = slice(number * band + row, number * band + row + step)
            factor = pl.reciprocal(mag_ref[held, :] + floor, approx=True)
            for part in range(2):
                value = spec_ref[part, row : row + step, :].astype(jnp.float32) * factor
                white_ref[part, held, :] = value.astype(jnp.bfloat16)

    lane = lax.broadcasted_iota(jnp.int32, (1, chans), 1)
    line = lax.broadcasted_iota(jnp.int32, (lag_rows, chans), 0)
    usable = qual_ref[pl.ds(me, 1), :].astype(jnp.float32)
    levels = jnp.zeros((lag_rows, chans), jnp.float32)
    core = me & 1
    orders = chips(chan_count)
    groups = [partner(orders, place, core) for place in range(chip_count)]
    groups += [partner(orders, place, 1 - core) ^ 1 for place in range(chip_count)]
    fetch.wait()
    per_band = table_ref.shape[0] // chan_count
    chunks = [(me ^ k) * per_band + chunk for k in order for chunk in range(per_band)]
    table = jnp.concatenate(
        [
            jnp.concatenate([table_ref[chunk, side, me ^ group] for side in range(2) for group in groups], axis=0)
            for chunk in chunks
        ],
        axis=1,
    )
    turns = [chans - offset_of(number, offs_ref, chan_count // 2) * (chans // chan_count) for number in range(offset_count)]
    for row in range(0, freqs, step):
        own = [white_ref[part, row : row + step, :] for part in range(2)]
        own_real, own_imag = (value.astype(jnp.float32) for value in own)
        for number, turn in enumerate(turns):
            far_real, far_imag = (pltpu.roll(value, turn, 1).astype(jnp.float32) for value in own)
            real = own_real * far_real + own_imag * far_imag
            imag = own_imag * far_real - own_real * far_imag
            cross_ref[number, 0, row : row + step, :] = real.astype(jnp.bfloat16)
            cross_ref[number, 1, row : row + step, :] = imag.astype(jnp.bfloat16)

    for number, turn in enumerate(turns):
        both = jnp.concatenate([cross_ref[number, 0], cross_ref[number, 1]], axis=1)
        sums = jnp.dot(table, both, preferred_element_type=jnp.float32)
        cos_real, sin_real = sums[:half, :chans], sums[half:, :chans]
        cos_imag, sin_imag = sums[:half, chans:], sums[half:, chans:]
        corr = (
            (cos_real - sin_imag, sin_real + cos_imag),
            (cos_real + sin_imag, cos_imag - sin_real),
        )
        power = [real * real + imag * imag for real, imag in corr]
        mean_power = jnp.sum(power[0] + power[1], axis=0, keepdims=True) * (1.0 / (2 * half))
        extra = 0.25 * (mean_power + 1e-06 * freqs)
        peak = jnp.max(jnp.maximum(jnp.abs(corr[0][0]), jnp.abs(corr[1][0])), axis=0, keepdims=True)
        code = level_code(peak)
        keep = jnp.where(lane < turn, usable * pltpu.roll(usable, turn, 1), 0.0) * CODE_TOP
        upscale = keep / level_of(code)
        inverse = [lax.rsqrt(side + extra) * keep for side in power]
        kinds = [
            [real * upscale for real, _ in corr],
            [real * scale for (real, _), scale in zip(corr, inverse)],
            [imag * scale for (_, imag), scale in zip(corr, inverse)],
        ]
        if number == offset_count - 1:
            code = jnp.where(lane < chans // 2, code, pltpu.roll(code, chans // 2, 1))
            kinds = [[jnp.where(lane < chans // 2, ahead, pltpu.roll(back, chans // 2, 1))] for ahead, back in kinds]
        levels = jnp.where(line == number, code, levels)
        for place, value in enumerate(value for kind in kinds for value in kind):
            coded = encode(value).reshape(chan_count, lag_rows, chans)
            begin = 0
            for out_ref in out_refs:
                out_ref[:, 6 * number + place, :, :] = coded[begin : begin + out_ref.shape[0]]
                begin += out_ref.shape[0]
    for number in range(offset_count):
        levels = jnp.where(line == offset_count + number, offs_ref[number].astype(jnp.float32), levels)
    wide = widest(offs_ref, chan_count // 2).astype(jnp.float32)
    levels = jnp.where(line == 2 * offset_count, wide, levels)
    for out_ref in out_refs:
        for chip in range(out_ref.shape[0]):
            out_ref[chip, blocks - 1, :, :] = encode(levels)


def merge_kernel(slots, own_ref, far_ref, *out_refs):
    blocks = own_ref.shape[1]
    for chip, out_ref in enumerate(out_refs):
        codes = [decode(ref[chip, blocks - 1]) for ref in (own_ref, far_ref)]
        levels = [level_of(code) for code in codes]
        code = level_code(levels[0] + levels[1])
        shares = [level / level_of(code) for level in levels]
        line = lax.broadcasted_iota(jnp.int32, code.shape, 0)
        out_ref[blocks - 1, :, :] = encode(jnp.where(line < slots, code, codes[0]))
        for block in range(blocks - 1):
            number, part = divmod(block, 6)
            linear = part < (2 if blocks - 1 - 6 * number > 3 else 1)
            own, far = decode(own_ref[chip, block]), decode(far_ref[chip, block])
            if linear:
                total = own * shares[0][number : number + 1, :] + far * shares[1][number : number + 1, :]
            else:
                total = (own + far) * 0.5
            out_ref[block, :, :] = encode(total)


def sum_kernel(orders, scale, where_ref, core_ref, *refs):
    count = len(orders[0])
    code_refs, out_refs, held_ref = refs[: -count - 1], refs[-count - 1 : -1], refs[-1]
    blocks, _, chans = code_refs[0].shape
    slots = held_ref.shape[0]
    heads = [decode(codes_ref[blocks - 1]) for codes_ref in code_refs]
    levels = [level_of(head) * scale for head in heads]
    offsets = [heads[0][slots + number : slots + number + 1, :] for number in range(slots)]
    wide = heads[0][2 * slots : 2 * slots + 1, :]
    low = lax.broadcasted_iota(jnp.int32, (1, chans), 1) < chans // 2
    all_sums = []
    for number in range(slots):
        sides = 2 if number < slots - 1 else 1
        own = [level[number : number + 1, :] for level in levels]
        sums = []
        for place in range(3 * sides):
            codes = [decode(codes_ref[6 * number + place]) for codes_ref in code_refs]
            if place < sides:
                sums.append(sum(code * level for code, level in zip(codes, own)))
            else:
                sums.append(sum(codes) * (1.0 / len(code_refs)))
        if sides == 1:
            sums = [
                jnp.where(low, side, 0.0) for value in sums for side in (value, pltpu.roll(value, chans // 2, 1))
            ]
        all_sums.append(sums)
    line = lax.broadcasted_iota(jnp.int32, levels[0].shape, 0)
    last = slots - 1
    for number in range(slots):
        sums = all_sums[number]
        for other in range(last) if number == last else [last]:
            swap = wide == min(number, other)
            sums = [jnp.where(swap, value, kept) for value, kept in zip(all_sums[other], sums)]
        peak = jnp.max(jnp.maximum(jnp.abs(sums[0]), jnp.abs(sums[1])), axis=0, keepdims=True)
        code = level_code(peak)
        upscale = CODE_TOP / level_of(code)
        head = jnp.where(line == 0, code, offsets[number])
        for part, value in enumerate([sums[0] * upscale, sums[1] * upscale, *sums[2:], head]):
            held_ref[number, part, :, :] = encode(value)
    for place, out_ref in enumerate(out_refs):
        out_ref[...] = held_ref[where_ref[0] ^ partner(orders, place, core_ref[0] & 1)]


def partners(count):
    return sorted(range(1, count), key=lambda k: (-(k >> 1).bit_count(), k & 1, k)) + [0]


def chips(count):
    near = [k for k in range(2, count, 2) if k.bit_count() == 1]
    far = [k for k in range(2, count, 2) if k.bit_count() > 1]
    return near[::-1] + far + [0], near + far + [0]


def planes(count):
    order = list(range(1, count)) + [0]
    return order, order


def partner(orders, place, core):
    return jnp.where(core == 0, orders[0][place], orders[1][place])


def exchange(pieces, orders, over_tm=False):
    chan_count, tm_count = lax.axis_size("chan"), lax.axis_size("tm")
    arrived = []
    for place, piece in enumerate(pieces):
        pairs = []
        for source in range(chan_count * tm_count):
            k = orders[source // tm_count % 2][place]
            pairs.append((source, source ^ k if over_tm else source ^ (k * tm_count)))
        moved = any(source != target for source, target in pairs)
        arrived.append(lax.ppermute(piece, ("chan", "tm"), pairs) if moved else piece)
    return arrived


def split_kernel(order, spec_ref, *refs):
    out_refs, sems = refs[:-1], refs[-1]
    me = lax.axis_index("chan").astype(jnp.int32)
    copies = [
        pltpu.make_async_copy(spec_ref.at[:, me ^ k], out_ref, sems.at[number])
        for number, (k, out_ref) in enumerate(zip(order, out_refs))
    ]
    for copy in copies:
        copy.start()
    for copy in copies:
        copy.wait()


def stack_kernel(windows, where_ref, *refs):
    sums_refs, out_ref = refs[:-1], refs[-1]
    blocks, copies, rows, _ = out_ref.shape
    _, lag_rows, chans = sums_refs[0].shape
    per_sum = windows // len(sums_refs)
    heads = [decode(sums_ref[6]) for sums_ref in sums_refs]
    levels = [level_of(head[0:1, :]) * (1.0 / (CODE_TOP * windows)) for head in heads]
    stacks = []
    for side in range(2):
        linear = sum(decode(sums_ref[side]) * level for sums_ref, level in zip(sums_refs, levels))
        real, imag = (
            sum(decode(sums_ref[part + side]) for sums_ref in sums_refs) * (per_sum / (CODE_TOP * windows))
            for part in (2, 4)
        )
        stacks.append(linear * (real * real + imag * imag))
    offset = heads[0][1:2, :]
    lane = lax.broadcasted_iota(jnp.int32, (1, chans), 1)
    behind = [jnp.zeros_like(stack) for stack in stacks]
    for steps in range(1, blocks // 2 + 1):
        ahead = steps * (chans // blocks)
        chosen = (offset == steps) & (lane >= ahead)
        behind = [jnp.where(chosen, pltpu.roll(stack, ahead, 1), kept) for stack, kept in zip(stacks, behind)]
    back = stacks[1] + behind[0]
    back = jnp.concatenate([back[row : row + 1, :] for row in reversed(range(lag_rows))], axis=0)
    me = where_ref[0]
    even = (me & 1) == 0
    ahead = stacks[0] + behind[1]
    both = jnp.concatenate([jnp.where(even, ahead, back), jnp.where(even, back, ahead)], axis=0)
    parts = chans // (2 * lag_rows)
    turned = jnp.concatenate([both] * parts, axis=0).T
    unit = lane // lag_rows
    part_of = jnp.where(((unit ^ me) & 1) == 0, unit - me, unit + me + 1) % blocks // 2
    per_block = chans // blocks
    for block in range(blocks):
        piece = jnp.zeros((rows, chans), jnp.float32)
        for part in range(parts):
            begin = block * per_block + part * rows
            piece = jnp.where(part_of == part, turned[begin : begin + rows, :], piece)
        for copy in range(copies):
            out_ref[block, copy, :, :] = piece


def place_kernel(parts_ref, out_ref):
    groups, offset_count, rows, lanes = parts_ref.shape
    half = out_ref.shape[2] // 2
    lag_rows = half // groups
    parts = out_ref.shape[0] // rows
    unit = lax.broadcasted_iota(jnp.int32, (1, lanes), 1) // lag_rows
    for number in range(offset_count):
        pieces = [parts_ref[group, number] for group in range(groups)]
        for part in range(parts):
            sides = [jnp.zeros((rows, lanes), jnp.float32)] * 2
            for group, piece in enumerate(pieces):
                places = ((groups - 1 - group + 2 * part) % groups, (group + 2 * part) % groups)
                sides = [jnp.where(unit == place, piece, side) for place, side in zip(places, sides)]
            for side, value in enumerate(sides):
                value = pltpu.roll(value, (lanes - 2 * part * lag_rows) % lanes, 1) if part else value
                out_ref[part * rows : (part + 1) * rows, number, side * half : (side + 1) * half] = value


def window_shards(spectra, quality, offsets):
    chan_count = lax.axis_size("chan")
    tm_count = lax.axis_size("tm")
    _, windows, band, chans = spectra.shape
    freqs = band * chan_count
    half = LAGS // 2
    lag_rows = half // chan_count
    offset_count = offsets.shape[0]
    piece_rows = 2 * lag_rows // chan_count
    smem = pl.BlockSpec(memory_space=pltpu.SMEM)
    vmem = pl.BlockSpec(memory_space=pltpu.VMEM)
    params = pltpu.CompilerParams(vmem_limit_bytes=VMEM_LIMIT)
    table = half_table(freqs, LAGS).reshape(2, chan_count, lag_rows, freqs // 128, 128)
    table = jnp.asarray(np.ascontiguousarray(table.transpose(3, 0, 1, 2, 4)))
    chan_index = lax.axis_index("chan").astype(jnp.int32)
    tm_index = lax.axis_index("tm").astype(jnp.int32)
    chan_where, tm_where = chan_index.reshape(1), tm_index.reshape(1)

    chan_order, tm_orders = partners(chan_count), planes(tm_count)
    kept = pl.BlockSpec(memory_space=pltpu.HBM)
    spectra = pltpu.with_memory_space_constraint(spectra, pltpu.HBM)
    pieces = []
    for part in (chan_order[:2], chan_order[2:]):
        pieces += pl.pallas_call(
            functools.partial(split_kernel, part),
            out_shape=[jax.ShapeDtypeStruct((2, band, chans), spectra.dtype)] * len(part),
            in_specs=[kept],
            out_specs=[pl.BlockSpec(memory_space=pl.ANY)] * len(part),
            scratch_shapes=[pltpu.SemaphoreType.DMA((len(part),))],
            compiler_params=params,
            name="split_windows",
        )(spectra)
    chip_count = chan_count // 2
    pair_shape = (6 * offset_count - 2, lag_rows, chans)
    first_half, second_half, *far = pl.pallas_call(
        functools.partial(window_kernel, chan_order),
        out_shape=[jax.ShapeDtypeStruct((chip_count // 2, *pair_shape), jnp.int16)] * 4,
        in_specs=[kept, smem] + [vmem] * (chan_count + 2),
        out_specs=[vmem] * 4,
        scratch_shapes=[
            pltpu.VMEM((freqs, chans), jnp.float32),
            pltpu.VMEM((2, freqs, chans), jnp.bfloat16),
            pltpu.VMEM((offset_count, 2, freqs, chans), jnp.bfloat16),
            pltpu.SMEM(offsets.shape, jnp.int32),
            pltpu.SemaphoreType.DMA(()),
        ],
        compiler_params=params,
        name="window_pairs",
    )(pltpu.with_memory_space_constraint(offsets, pltpu.HBM), chan_where, *exchange(pieces, (chan_order, chan_order)), quality, table)
    pairs = []
    for own, other in zip((first_half, second_half), exchange(far, ([1, 1], [1, 1]))):
        pairs += pl.pallas_call(
            functools.partial(merge_kernel, offset_count),
            out_shape=[jax.ShapeDtypeStruct(pair_shape, jnp.int16)] * (chip_count // 2),
            in_specs=[vmem] * 2,
            out_specs=[vmem] * (chip_count // 2),
            compiler_params=params,
            name="merge_windows",
        )(own, other)
    sums = pl.pallas_call(
        functools.partial(sum_kernel, tm_orders, 1.0 / (CODE_TOP * math.sqrt(freqs))),
        out_shape=[jax.ShapeDtypeStruct((7, lag_rows, chans), jnp.int16)] * tm_count,
        in_specs=[smem, smem] + [vmem] * chip_count,
        out_specs=[vmem] * tm_count,
        scratch_shapes=[pltpu.VMEM((offset_count, 7, lag_rows, chans), jnp.int16)],
        compiler_params=params,
        name="sum_windows",
    )(tm_where, chan_where, *exchange(pairs, chips(chan_count)))
    pieces = pl.pallas_call(
        functools.partial(stack_kernel, windows * tm_count),
        out_shape=jax.ShapeDtypeStruct((chan_count, tm_count, piece_rows, chans), jnp.float32),
        in_specs=[smem] + [vmem] * tm_count,
        out_specs=vmem,
        compiler_params=params,
        name="stack_pairs",
    )(chan_where, *exchange(sums, tm_orders, over_tm=True))
    shape = (chan_count * tm_count, piece_rows, chans)
    arrived = lax.all_to_all(pieces.reshape(shape), ("chan", "tm"), 0, 0, tiled=True)
    return pl.pallas_call(
        place_kernel,
        out_shape=jax.ShapeDtypeStruct((CH_DEV, offset_count, LAGS), jnp.float32),
        in_specs=[vmem],
        out_specs=vmem,
        compiler_params=params,
        name="place_lags",
    )(arrived.reshape(chan_count, tm_count, piece_rows, chans))


def shifted(value, axis, steps):
    count = lax.axis_size(axis)
    leading, last = (max(0, -steps), min(count, count - steps))
    return lax.ppermute(value, axis, [(source, source + steps) for source in range(leading, last)])


def lag_table(freq_count, lag_count):
    freq_index = jnp.arange(freq_count, dtype=jnp.int32)[:, None]
    double_lag = (2 * jnp.arange(lag_count, dtype=jnp.int32) - lag_count + 1)[None, :]
    turns = jnp.mod(freq_index * double_lag, 4 * freq_count)
    angles = turns.astype(jnp.float32) * (2.0 * math.pi / (4 * freq_count))
    cosine = jnp.cos(angles)
    sine = jnp.sin(angles)
    upper = jnp.concatenate([cosine, sine], axis=1)
    lower = jnp.concatenate([-sine, cosine], axis=1)
    return jnp.stack([upper, lower]).astype(jnp.bfloat16)


def whiten_parts(real_part, imag_part, magnitude, channel_level, usable):
    factor = usable.astype(jnp.float32)[:, None, :] / (magnitude + 0.5 * (channel_level + 1e-05))
    return jnp.stack([real_part * factor, imag_part * factor]).astype(jnp.bfloat16)


def cross_parts(own_real, own_imag, far_real, far_imag):
    own_real = own_real.astype(jnp.float32)
    own_imag = own_imag.astype(jnp.float32)
    far_real = far_real.astype(jnp.float32)
    far_imag = far_imag.astype(jnp.float32)
    return jnp.stack(
        [own_real * far_real + own_imag * far_imag, own_imag * far_real - own_real * far_imag]
    ).astype(jnp.bfloat16)


def pair_terms(corr_all):
    lag_count = corr_all.shape[-1] // 2
    real_corr = corr_all[..., :lag_count]
    imag_corr = corr_all[..., lag_count:]
    power = real_corr * real_corr + imag_corr * imag_corr
    mean_power = jnp.mean(power, axis=-1, keepdims=True)
    denominator = jnp.sqrt(power + 0.25 * (mean_power + 1e-06))
    return (
        jnp.sum(real_corr, axis=-3),
        jnp.sum(real_corr / denominator, axis=-3),
        jnp.sum(imag_corr / denominator, axis=-3),
    )


def shards(spectra, quality, offsets):
    chan_count = lax.axis_size("chan")
    tm_count = lax.axis_size("tm")
    levels = chan_count.bit_length() - 1
    table_bf = lag_table(F, LAGS)
    inv_root = 1.0 / math.sqrt(F)
    real_part = spectra[0].astype(jnp.float32)
    imag_part = spectra[1].astype(jnp.float32)
    magnitude = jnp.sqrt(real_part * real_part + imag_part * imag_part)
    band_total = lax.psum(jnp.sum(magnitude, axis=1), "chan")
    channel_level = (band_total / F)[:, None, :]
    whitened = whiten_parts(real_part, imag_part, magnitude, channel_level, quality)
    width_all = whitened.shape[3]
    padded = jnp.pad(whitened, ((0, 0), (0, 0), (0, 0), (0, width_all)))
    crossed_list = []
    for offset_index in range(NOFF):
        partner = lax.dynamic_slice_in_dim(padded, offsets[offset_index] * CH_DEV, width_all, 3)
        crossed_list.append(cross_parts(whitened[0], whitened[1], partner[0], partner[1]))
    crossed = jnp.stack(crossed_list, axis=1)
    corr_all = jnp.einsum(
        "cnwfh,cfl->nwhl",
        lax.all_to_all(crossed, "chan", split_axis=4, concat_axis=3, tiled=True),
        table_bf,
        preferred_element_type=jnp.float32,
    )
    linear_sum, real_sum, imag_sum = pair_terms(corr_all * inv_root)
    totals = lax.psum((linear_sum, real_sum, imag_sum), "tm")
    window_count = W_DEV * tm_count
    linear = totals[0] / window_count
    real_phase = totals[1] / window_count
    imag_phase = totals[2] / window_count
    stacks = jnp.transpose(linear * (real_phase * real_phase + imag_phase * imag_phase), (1, 0, 2))
    reverse_part = stacks
    for bit_index in range(levels):
        step_size = 1 << bit_index
        arrived = shifted(reverse_part, "chan", step_size)
        chosen = offsets // step_size % 2 == 1
        reverse_part = jnp.where(chosen[None, :, None], arrived, reverse_part)
    return stacks + jnp.flip(reverse_part, axis=2)


def solution(mesh):
    chan_count, tm_count = mesh.shape["chan"], mesh.shape["tm"]
    by_window = chan_count == W_DEV and tm_count == NOFF
    return jax.shard_map(
        window_shards if by_window else shards,
        mesh=mesh,
        in_specs=(P(None, "tm", "chan", None), P("tm", None), P()),
        out_specs=P("chan", None, None),
        check_vma=False,
    )
```

```python
import functools
import math

import jax
import jax.numpy as jnp
import numpy as np
from jax import lax
from jax.experimental import pallas as pl
from jax.experimental.pallas import tpu as pltpu
from jax.sharding import PartitionSpec as P

F = 2048
LAGS = 256
NOFF = 4
CH_DEV = 16
W_DEV = 8
VMEM_LIMIT = 48 * 1024 * 1024
CODE_TOP = 32767.0
OCTAVE = 256.0
LOWEST = -110.0


def encode(value):
    return jnp.round(value).astype(jnp.int32).astype(jnp.int16)


def decode(code):
    return code.astype(jnp.int32).astype(jnp.float32)


def level_code(peak):
    return jnp.ceil(jnp.maximum(jnp.log2(jnp.maximum(peak, 1e-30)), LOWEST) * OCTAVE) + 1.0


def level_of(code):
    return jnp.exp2(code * (1.0 / OCTAVE))


def half_table(freq_count, lag_count):
    freq_index = np.arange(freq_count, dtype=np.int64)[None, :]
    double_lag = (2 * np.arange(lag_count // 2, lag_count, dtype=np.int64) - lag_count + 1)[:, None]
    turns = np.mod(freq_index * double_lag, 4 * freq_count).astype(np.float32)
    angles = turns * np.float32(2.0 * math.pi / (4 * freq_count))
    return np.concatenate([np.cos(angles), np.sin(angles)]).astype(jnp.bfloat16)


def widest(offs_ref, reach):
    last = offs_ref.shape[0] - 1
    found = last
    for number in reversed(range(last)):
        found = jnp.where(offs_ref[number] == reach, number, found)
    return found


def offset_of(slot, offs_ref, reach):
    last, wide = offs_ref.shape[0] - 1, widest(offs_ref, reach)
    return offs_ref[jnp.where(slot == wide, last, jnp.where(slot == last, wide, slot))]


def window_kernel(order, offs_hbm_ref, where_ref, *refs):
    chan_count = len(order)
    spec_refs, (qual_ref, table_ref) = refs[:chan_count], refs[chan_count : chan_count + 2]
    out_refs = refs[chan_count + 2 : chan_count + 4]
    mag_ref, white_ref, cross_ref, offs_ref, offs_sem = refs[chan_count + 4 :]
    fetch = pltpu.make_async_copy(offs_hbm_ref, offs_ref, offs_sem)
    fetch.start()
    me = where_ref[0]
    _, band, chans = spec_refs[0].shape
    freqs = chan_count * band
    chip_count, blocks, lag_rows, _ = out_refs[0].shape
    offset_count = offs_ref.shape[0]
    half = chan_count * lag_rows
    step = 64

    total = jnp.zeros((8, chans), jnp.float32)
    for number, spec_ref in enumerate(spec_refs):
        for row in range(0, band, step):
            real, imag = (spec_ref[part, row : row + step, :].astype(jnp.float32) for part in range(2))
            square = real * real + imag * imag
            magnitude = square * lax.rsqrt(jnp.maximum(square, 1e-30))
            held = slice(number * band + row, number * band + row + step)
            mag_ref[held, :] = magnitude
            total += jnp.sum(magnitude.reshape(step // 8, 8, chans), axis=0)
    level = jnp.sum(total, axis=0, keepdims=True) * (1.0 / freqs)
    floor = 0.5 * (level + 1e-05)

    for number, spec_ref in enumerate(spec_refs):
        for row in range(0, band, step):
            held = slice(number * band + row, number * band + row + step)
            factor = pl.reciprocal(mag_ref[held, :] + floor, approx=True)
            for part in range(2):
                value = spec_ref[part, row : row + step, :].astype(jnp.float32) * factor
                white_ref[part, held, :] = value.astype(jnp.bfloat16)

    lane = lax.broadcasted_iota(jnp.int32, (1, chans), 1)
    line = lax.broadcasted_iota(jnp.int32, (lag_rows, chans), 0)
    usable = qual_ref[pl.ds(me, 1), :].astype(jnp.float32)
    levels = jnp.zeros((lag_rows, chans), jnp.float32)
    core = me & 1
    orders = chips(chan_count)
    groups = [partner(orders, place, core) for place in range(chip_count)]
    groups += [partner(orders, place, 1 - core) ^ 1 for place in range(chip_count)]
    fetch.wait()
    per_band = table_ref.shape[0] // chan_count
    chunks = [(me ^ k) * per_band + chunk for k in order for chunk in range(per_band)]
    table = jnp.concatenate(
        [
            jnp.concatenate([table_ref[chunk, side, me ^ group] for side in range(2) for group in groups], axis=0)
            for chunk in chunks
        ],
        axis=1,
    )
    turns = [chans - offset_of(number, offs_ref, chan_count // 2) * (chans // chan_count) for number in range(offset_count)]
    for row in range(0, freqs, step):
        own = [white_ref[part, row : row + step, :] for part in range(2)]
        own_real, own_imag = (value.astype(jnp.float32) for value in own)
        for number, turn in enumerate(turns):
            far_real, far_imag = (pltpu.roll(value, turn, 1).astype(jnp.float32) for value in own)
            real = own_real * far_real + own_imag * far_imag
            imag = own_imag * far_real - own_real * far_imag
            cross_ref[number, 0, row : row + step, :] = real.astype(jnp.bfloat16)
            cross_ref[number, 1, row : row + step, :] = imag.astype(jnp.bfloat16)

    for number, turn in enumerate(turns):
        if number % 2 == 0:
            taken = range(number, min(number + 2, offset_count))
            wide = jnp.concatenate([cross_ref[each, part] for each in taken for part in range(2)], axis=1)
            pair_sums = jnp.dot(table, wide, preferred_element_type=jnp.float32)
        sums = pair_sums[:, number % 2 * 2 * chans : (number % 2 + 1) * 2 * chans]
        cos_real, sin_real = sums[:half, :chans], sums[half:, :chans]
        cos_imag, sin_imag = sums[:half, chans:], sums[half:, chans:]
        corr = (
            (cos_real - sin_imag, sin_real + cos_imag),
            (cos_real + sin_imag, cos_imag - sin_real),
        )
        power = [real * real + imag * imag for real, imag in corr]
        mean_power = jnp.sum(power[0] + power[1], axis=0, keepdims=True) * (1.0 / (2 * half))
        extra = 0.25 * (mean_power + 1e-06 * freqs)
        peak = jnp.max(jnp.maximum(jnp.abs(corr[0][0]), jnp.abs(corr[1][0])), axis=0, keepdims=True)
        code = level_code(peak)
        keep = jnp.where(lane < turn, usable * pltpu.roll(usable, turn, 1), 0.0) * CODE_TOP
        upscale = keep / level_of(code)
        inverse = [lax.rsqrt(side + extra) * keep for side in power]
        kinds = [
            [real * upscale for real, _ in corr],
            [real * scale for (real, _), scale in zip(corr, inverse)],
            [imag * scale for (_, imag), scale in zip(corr, inverse)],
        ]
        if number == offset_count - 1:
            code = jnp.where(lane < chans // 2, code, pltpu.roll(code, chans // 2, 1))
            kinds = [[jnp.where(lane < chans // 2, ahead, pltpu.roll(back, chans // 2, 1))] for ahead, back in kinds]
        levels = jnp.where(line == number, code, levels)
        for place, value in enumerate(value for kind in kinds for value in kind):
            coded = encode(value).reshape(chan_count, lag_rows, chans)
            for core in range(2):
                rows = slice(core * chip_count, (core + 1) * chip_count)
                out_refs[core][:, 6 * number + place, :, :] = coded[rows]
    for number in range(offset_count):
        levels = jnp.where(line == offset_count + number, offs_ref[number].astype(jnp.float32), levels)
    wide = widest(offs_ref, chan_count // 2).astype(jnp.float32)
    levels = jnp.where(line == 2 * offset_count, wide, levels)
    for out_ref in out_refs:
        for chip in range(chip_count):
            out_ref[chip, blocks - 1, :, :] = encode(levels)


def merge_kernel(slots, own_ref, far_ref, *out_refs):
    blocks = own_ref.shape[1]
    for chip, out_ref in enumerate(out_refs):
        codes = [decode(ref[chip, blocks - 1]) for ref in (own_ref, far_ref)]
        levels = [level_of(code) for code in codes]
        code = level_code(levels[0] + levels[1])
        shares = [level / level_of(code) for level in levels]
        line = lax.broadcasted_iota(jnp.int32, code.shape, 0)
        out_ref[blocks - 1, :, :] = encode(jnp.where(line < slots, code, codes[0]))
        for block in range(blocks - 1):
            number, part = divmod(block, 6)
            linear = part < (2 if blocks - 1 - 6 * number > 3 else 1)
            own, far = decode(own_ref[chip, block]), decode(far_ref[chip, block])
            if linear:
                total = own * shares[0][number : number + 1, :] + far * shares[1][number : number + 1, :]
            else:
                total = (own + far) * 0.5
            out_ref[block, :, :] = encode(total)


def sum_kernel(orders, scale, where_ref, core_ref, *refs):
    count = len(orders[0])
    code_refs, out_refs, held_ref = refs[: -count - 1], refs[-count - 1 : -1], refs[-1]
    blocks, _, chans = code_refs[0].shape
    slots = held_ref.shape[0]
    heads = [decode(codes_ref[blocks - 1]) for codes_ref in code_refs]
    levels = [level_of(head) * scale for head in heads]
    offsets = [heads[0][slots + number : slots + number + 1, :] for number in range(slots)]
    wide = heads[0][2 * slots : 2 * slots + 1, :]
    low = lax.broadcasted_iota(jnp.int32, (1, chans), 1) < chans // 2
    all_sums = []
    for number in range(slots):
        sides = 2 if number < slots - 1 else 1
        own = [level[number : number + 1, :] for level in levels]
        sums = []
        for place in range(3 * sides):
            codes = [decode(codes_ref[6 * number + place]) for codes_ref in code_refs]
            if place < sides:
                sums.append(sum(code * level for code, level in zip(codes, own)))
            else:
                sums.append(sum(codes) * (1.0 / len(code_refs)))
        if sides == 1:
            sums = [
                jnp.where(low, side, 0.0) for value in sums for side in (value, pltpu.roll(value, chans // 2, 1))
            ]
        all_sums.append(sums)
    line = lax.broadcasted_iota(jnp.int32, levels[0].shape, 0)
    last = slots - 1
    for number in range(slots):
        sums = all_sums[number]
        for other in range(last) if number == last else [last]:
            swap = wide == min(number, other)
            sums = [jnp.where(swap, value, kept) for value, kept in zip(all_sums[other], sums)]
        peak = jnp.max(jnp.maximum(jnp.abs(sums[0]), jnp.abs(sums[1])), axis=0, keepdims=True)
        code = level_code(peak)
        upscale = CODE_TOP / level_of(code)
        head = jnp.where(line == 0, code, offsets[number])
        for part, value in enumerate([sums[0] * upscale, sums[1] * upscale, *sums[2:], head]):
            held_ref[number, part, :, :] = encode(value)
    for place, out_ref in enumerate(out_refs):
        out_ref[...] = held_ref[where_ref[0] ^ partner(orders, place, core_ref[0] & 1)]


def partners(count):
    return sorted(range(1, count), key=lambda k: (-(k >> 1).bit_count(), k & 1, k)) + [0]


def chips(count):
    near = [k for k in range(2, count, 2) if k.bit_count() == 1]
    far = [k for k in range(2, count, 2) if k.bit_count() > 1]
    return near[::-1] + far + [0], near + far + [0]


def planes(count):
    others = partners(count)[:-1]
    return others + [0], others[1:] + others[:1] + [0]


def partner(orders, place, core):
    return jnp.where(core == 0, orders[0][place], orders[1][place])


def exchange(pieces, orders, over_tm=False):
    chan_count, tm_count = lax.axis_size("chan"), lax.axis_size("tm")
    arrived = []
    for place, piece in enumerate(pieces):
        pairs = []
        for source in range(chan_count * tm_count):
            k = orders[source // tm_count % 2][place]
            pairs.append((source, source ^ k if over_tm else source ^ (k * tm_count)))
        moved = any(source != target for source, target in pairs)
        arrived.append(lax.ppermute(piece, ("chan", "tm"), pairs) if moved else piece)
    return arrived


def split_kernel(order, spec_ref, *refs):
    out_refs, sems = refs[:-1], refs[-1]
    me = lax.axis_index("chan").astype(jnp.int32)
    copies = [
        pltpu.make_async_copy(spec_ref.at[:, me ^ k], out_ref, sems.at[number])
        for number, (k, out_ref) in enumerate(zip(order, out_refs))
    ]
    for copy in copies:
        copy.start()
    for copy in copies:
        copy.wait()


def stack_kernel(windows, where_ref, *refs):
    sums_refs, out_ref = refs[:-1], refs[-1]
    blocks, copies, rows, _ = out_ref.shape
    _, lag_rows, chans = sums_refs[0].shape
    per_sum = windows // len(sums_refs)
    heads = [decode(sums_ref[6]) for sums_ref in sums_refs]
    levels = [level_of(head[0:1, :]) * (1.0 / (CODE_TOP * windows)) for head in heads]
    stacks = []
    for side in range(2):
        linear = sum(decode(sums_ref[side]) * level for sums_ref, level in zip(sums_refs, levels))
        real, imag = (
            sum(decode(sums_ref[part + side]) for sums_ref in sums_refs) * (per_sum / (CODE_TOP * windows))
            for part in (2, 4)
        )
        stacks.append(linear * (real * real + imag * imag))
    offset = heads[0][1:2, :]
    lane = lax.broadcasted_iota(jnp.int32, (1, chans), 1)
    behind = [jnp.zeros_like(stack) for stack in stacks]
    for steps in range(1, blocks // 2 + 1):
        ahead = steps * (chans // blocks)
        chosen = (offset == steps) & (lane >= ahead)
        behind = [jnp.where(chosen, pltpu.roll(stack, ahead, 1), kept) for stack, kept in zip(stacks, behind)]
    back = stacks[1] + behind[0]
    back = jnp.concatenate([back[row : row + 1, :] for row in reversed(range(lag_rows))], axis=0)
    me = where_ref[0]
    even = (me & 1) == 0
    ahead = stacks[0] + behind[1]
    both = jnp.concatenate([jnp.where(even, ahead, back), jnp.where(even, back, ahead)], axis=0)
    parts = chans // (2 * lag_rows)
    turned = jnp.concatenate([both] * parts, axis=0).T
    unit = lane // lag_rows
    part_of = jnp.where(((unit ^ me) & 1) == 0, unit - me, unit + me + 1) % blocks // 2
    per_block = chans // blocks
    for block in range(blocks):
        piece = jnp.zeros((rows, chans), jnp.float32)
        for part in range(parts):
            begin = block * per_block + part * rows
            piece = jnp.where(part_of == part, turned[begin : begin + rows, :], piece)
        for copy in range(copies):
            out_ref[block, copy, :, :] = piece


def place_kernel(parts_ref, out_ref):
    groups, offset_count, rows, lanes = parts_ref.shape
    half = out_ref.shape[2] // 2
    lag_rows = half // groups
    parts = out_ref.shape[0] // rows
    unit = lax.broadcasted_iota(jnp.int32, (1, lanes), 1) // lag_rows
    for number in range(offset_count):
        pieces = [parts_ref[group, number] for group in range(groups)]
        for part in range(parts):
            sides = [jnp.zeros((rows, lanes), jnp.float32)] * 2
            for group, piece in enumerate(pieces):
                places = ((groups - 1 - group + 2 * part) % groups, (group + 2 * part) % groups)
                sides = [jnp.where(unit == place, piece, side) for place, side in zip(places, sides)]
            for side, value in enumerate(sides):
                value = pltpu.roll(value, (lanes - 2 * part * lag_rows) % lanes, 1) if part else value
                out_ref[part * rows : (part + 1) * rows, number, side * half : (side + 1) * half] = value


def window_shards(spectra, quality, offsets):
    chan_count = lax.axis_size("chan")
    tm_count = lax.axis_size("tm")
    _, windows, band, chans = spectra.shape
    freqs = band * chan_count
    half = LAGS // 2
    lag_rows = half // chan_count
    offset_count = offsets.shape[0]
    piece_rows = 2 * lag_rows // chan_count
    smem = pl.BlockSpec(memory_space=pltpu.SMEM)
    vmem = pl.BlockSpec(memory_space=pltpu.VMEM)
    params = pltpu.CompilerParams(vmem_limit_bytes=VMEM_LIMIT)
    table = half_table(freqs, LAGS).reshape(2, chan_count, lag_rows, freqs // 128, 128)
    table = jnp.asarray(np.ascontiguousarray(table.transpose(3, 0, 1, 2, 4)))
    chan_index = lax.axis_index("chan").astype(jnp.int32)
    tm_index = lax.axis_index("tm").astype(jnp.int32)
    chan_where, tm_where = chan_index.reshape(1), tm_index.reshape(1)

    chan_order, tm_orders = partners(chan_count), planes(tm_count)
    kept = pl.BlockSpec(memory_space=pltpu.HBM)
    spectra = pltpu.with_memory_space_constraint(spectra, pltpu.HBM)
    pieces = []
    for part in (chan_order[:2], chan_order[2:]):
        pieces += pl.pallas_call(
            functools.partial(split_kernel, part),
            out_shape=[jax.ShapeDtypeStruct((2, band, chans), spectra.dtype)] * len(part),
            in_specs=[kept],
            out_specs=[pl.BlockSpec(memory_space=pl.ANY)] * len(part),
            scratch_shapes=[pltpu.SemaphoreType.DMA((len(part),))],
            compiler_params=params,
            name="split_windows",
        )(spectra)
    chip_count = chan_count // 2
    pair_shape = (6 * offset_count - 2, lag_rows, chans)
    own, far = pl.pallas_call(
        functools.partial(window_kernel, chan_order),
        out_shape=[jax.ShapeDtypeStruct((chip_count, *pair_shape), jnp.int16)] * 2,
        in_specs=[kept, smem] + [vmem] * (chan_count + 2),
        out_specs=[vmem] * 2,
        scratch_shapes=[
            pltpu.VMEM((freqs, chans), jnp.float32),
            pltpu.VMEM((2, freqs, chans), jnp.bfloat16),
            pltpu.VMEM((offset_count, 2, freqs, chans), jnp.bfloat16),
            pltpu.SMEM(offsets.shape, jnp.int32),
            pltpu.SemaphoreType.DMA(()),
        ],
        compiler_params=params,
        name="window_pairs",
    )(pltpu.with_memory_space_constraint(offsets, pltpu.HBM), chan_where, *exchange(pieces, (chan_order, chan_order)), quality, table)
    pairs = pl.pallas_call(
        functools.partial(merge_kernel, offset_count),
        out_shape=[jax.ShapeDtypeStruct(pair_shape, jnp.int16)] * chip_count,
        in_specs=[vmem] * 2,
        out_specs=[vmem] * chip_count,
        compiler_params=params,
        name="merge_windows",
    )(own, *exchange([far], ([1], [1])))
    sums = pl.pallas_call(
        functools.partial(sum_kernel, tm_orders, 1.0 / (CODE_TOP * math.sqrt(freqs))),
        out_shape=[jax.ShapeDtypeStruct((7, lag_rows, chans), jnp.int16)] * tm_count,
        in_specs=[smem, smem] + [vmem] * chip_count,
        out_specs=[vmem] * tm_count,
        scratch_shapes=[pltpu.VMEM((offset_count, 7, lag_rows, chans), jnp.int16)],
        compiler_params=params,
        name="sum_windows",
    )(tm_where, chan_where, *exchange(pairs, chips(chan_count)))
    pieces = pl.pallas_call(
        functools.partial(stack_kernel, windows * tm_count),
        out_shape=jax.ShapeDtypeStruct((chan_count, tm_count, piece_rows, chans), jnp.float32),
        in_specs=[smem] + [vmem] * tm_count,
        out_specs=vmem,
        compiler_params=params,
        name="stack_pairs",
    )(chan_where, *exchange(sums, tm_orders, over_tm=True))
    shape = (chan_count * tm_count, piece_rows, chans)
    arrived = lax.all_to_all(pieces.reshape(shape), ("chan", "tm"), 0, 0, tiled=True)
    return pl.pallas_call(
        place_kernel,
        out_shape=jax.ShapeDtypeStruct((CH_DEV, offset_count, LAGS), jnp.float32),
        in_specs=[vmem],
        out_specs=vmem,
        compiler_params=params,
        name="place_lags",
    )(arrived.reshape(chan_count, tm_count, piece_rows, chans))


def shifted(value, axis, steps):
    count = lax.axis_size(axis)
    leading, last = (max(0, -steps), min(count, count - steps))
    return lax.ppermute(value, axis, [(source, source + steps) for source in range(leading, last)])


def lag_table(freq_count, lag_count):
    freq_index = jnp.arange(freq_count, dtype=jnp.int32)[:, None]
    double_lag = (2 * jnp.arange(lag_count, dtype=jnp.int32) - lag_count + 1)[None, :]
    turns = jnp.mod(freq_index * double_lag, 4 * freq_count)
    angles = turns.astype(jnp.float32) * (2.0 * math.pi / (4 * freq_count))
    cosine = jnp.cos(angles)
    sine = jnp.sin(angles)
    upper = jnp.concatenate([cosine, sine], axis=1)
    lower = jnp.concatenate([-sine, cosine], axis=1)
    return jnp.stack([upper, lower]).astype(jnp.bfloat16)


def whiten_parts(real_part, imag_part, magnitude, channel_level, usable):
    factor = usable.astype(jnp.float32)[:, None, :] / (magnitude + 0.5 * (channel_level + 1e-05))
    return jnp.stack([real_part * factor, imag_part * factor]).astype(jnp.bfloat16)


def cross_parts(own_real, own_imag, far_real, far_imag):
    own_real = own_real.astype(jnp.float32)
    own_imag = own_imag.astype(jnp.float32)
    far_real = far_real.astype(jnp.float32)
    far_imag = far_imag.astype(jnp.float32)
    return jnp.stack(
        [own_real * far_real + own_imag * far_imag, own_imag * far_real - own_real * far_imag]
    ).astype(jnp.bfloat16)


def pair_terms(corr_all):
    lag_count = corr_all.shape[-1] // 2
    real_corr = corr_all[..., :lag_count]
    imag_corr = corr_all[..., lag_count:]
    power = real_corr * real_corr + imag_corr * imag_corr
    mean_power = jnp.mean(power, axis=-1, keepdims=True)
    denominator = jnp.sqrt(power + 0.25 * (mean_power + 1e-06))
    return (
        jnp.sum(real_corr, axis=-3),
        jnp.sum(real_corr / denominator, axis=-3),
        jnp.sum(imag_corr / denominator, axis=-3),
    )


def shards(spectra, quality, offsets):
    chan_count = lax.axis_size("chan")
    tm_count = lax.axis_size("tm")
    levels = chan_count.bit_length() - 1
    table_bf = lag_table(F, LAGS)
    inv_root = 1.0 / math.sqrt(F)
    real_part = spectra[0].astype(jnp.float32)
    imag_part = spectra[1].astype(jnp.float32)
    magnitude = jnp.sqrt(real_part * real_part + imag_part * imag_part)
    band_total = lax.psum(jnp.sum(magnitude, axis=1), "chan")
    channel_level = (band_total / F)[:, None, :]
    whitened = whiten_parts(real_part, imag_part, magnitude, channel_level, quality)
    width_all = whitened.shape[3]
    padded = jnp.pad(whitened, ((0, 0), (0, 0), (0, 0), (0, width_all)))
    crossed_list = []
    for offset_index in range(NOFF):
        partner = lax.dynamic_slice_in_dim(padded, offsets[offset_index] * CH_DEV, width_all, 3)
        crossed_list.append(cross_parts(whitened[0], whitened[1], partner[0], partner[1]))
    crossed = jnp.stack(crossed_list, axis=1)
    corr_all = jnp.einsum(
        "cnwfh,cfl->nwhl",
        lax.all_to_all(crossed, "chan", split_axis=4, concat_axis=3, tiled=True),
        table_bf,
        preferred_element_type=jnp.float32,
    )
    linear_sum, real_sum, imag_sum = pair_terms(corr_all * inv_root)
    totals = lax.psum((linear_sum, real_sum, imag_sum), "tm")
    window_count = W_DEV * tm_count
    linear = totals[0] / window_count
    real_phase = totals[1] / window_count
    imag_phase = totals[2] / window_count
    stacks = jnp.transpose(linear * (real_phase * real_phase + imag_phase * imag_phase), (1, 0, 2))
    reverse_part = stacks
    for bit_index in range(levels):
        step_size = 1 << bit_index
        arrived = shifted(reverse_part, "chan", step_size)
        chosen = offsets // step_size % 2 == 1
        reverse_part = jnp.where(chosen[None, :, None], arrived, reverse_part)
    return stacks + jnp.flip(reverse_part, axis=2)


def solution(mesh):
    chan_count, tm_count = mesh.shape["chan"], mesh.shape["tm"]
    by_window = chan_count == W_DEV and tm_count == NOFF
    return jax.shard_map(
        window_shards if by_window else shards,
        mesh=mesh,
        in_specs=(P(None, "tm", "chan", None), P("tm", None), P()),
        out_specs=P("chan", None, None),
        check_vma=False,
    )
```

```python
import functools
import math

import jax
import jax.numpy as jnp
import numpy as np
from jax import lax
from jax.experimental import pallas as pl
from jax.experimental.pallas import tpu as pltpu
from jax.sharding import PartitionSpec as P

F = 2048
LAGS = 256
NOFF = 4
CH_DEV = 16
W_DEV = 8
VMEM_LIMIT = 48 * 1024 * 1024
CODE_TOP = 32767.0
OCTAVE = 256.0
LOWEST = -110.0


def encode(value):
    return jnp.round(value).astype(jnp.int32).astype(jnp.int16)


def decode(code):
    return code.astype(jnp.int32).astype(jnp.float32)


def level_code(peak):
    return jnp.ceil(jnp.maximum(jnp.log2(jnp.maximum(peak, 1e-30)), LOWEST) * OCTAVE) + 1.0


def level_of(code):
    return jnp.exp2(code * (1.0 / OCTAVE))


def half_table(freq_count, lag_count):
    freq_index = np.arange(freq_count, dtype=np.int64)[None, :]
    double_lag = (2 * np.arange(lag_count // 2, lag_count, dtype=np.int64) - lag_count + 1)[:, None]
    turns = np.mod(freq_index * double_lag, 4 * freq_count).astype(np.float32)
    angles = turns * np.float32(2.0 * math.pi / (4 * freq_count))
    return np.concatenate([np.cos(angles), np.sin(angles)]).astype(jnp.bfloat16)


def magnitude_of(real, imag):
    square = real * real + imag * imag
    return square * lax.rsqrt(jnp.maximum(square, 1e-30))


def widest(offs_ref, reach):
    last = offs_ref.shape[0] - 1
    found = last
    for number in reversed(range(last)):
        found = jnp.where(offs_ref[number] == reach, number, found)
    return found


def offset_of(slot, offs_ref, reach):
    last, wide = offs_ref.shape[0] - 1, widest(offs_ref, reach)
    return offs_ref[jnp.where(slot == wide, last, jnp.where(slot == last, wide, slot))]


def window_kernel(order, offs_hbm_ref, where_ref, *refs):
    chan_count = len(order)
    spec_refs, (qual_ref, table_ref) = refs[:chan_count], refs[chan_count : chan_count + 2]
    out_refs = refs[chan_count + 2 : chan_count + 4]
    white_ref, cross_ref, offs_ref, offs_sem = refs[chan_count + 4 :]
    fetch = pltpu.make_async_copy(offs_hbm_ref, offs_ref, offs_sem)
    fetch.start()
    me = where_ref[0]
    _, band, chans = spec_refs[0].shape
    freqs = chan_count * band
    chip_count, blocks, lag_rows, _ = out_refs[0].shape
    offset_count = offs_ref.shape[0]
    half = chan_count * lag_rows
    step = 64

    total = jnp.zeros((8, chans), jnp.float32)
    for number, spec_ref in enumerate(spec_refs):
        for row in range(0, band, step):
            real, imag = (spec_ref[part, row : row + step, :].astype(jnp.float32) for part in range(2))
            total += jnp.sum(magnitude_of(real, imag).reshape(step // 8, 8, chans), axis=0)
    level = jnp.sum(total, axis=0, keepdims=True) * (1.0 / freqs)
    floor = 0.5 * (level + 1e-05)

    for number, spec_ref in enumerate(spec_refs):
        for row in range(0, band, step):
            held = slice(number * band + row, number * band + row + step)
            values = [spec_ref[part, row : row + step, :].astype(jnp.float32) for part in range(2)]
            factor = pl.reciprocal(magnitude_of(*values) + floor, approx=True)
            for part, value in enumerate(values):
                white_ref[part, held, :] = (value * factor).astype(jnp.bfloat16)

    lane = lax.broadcasted_iota(jnp.int32, (1, chans), 1)
    line = lax.broadcasted_iota(jnp.int32, (lag_rows, chans), 0)
    usable = qual_ref[pl.ds(me, 1), :].astype(jnp.float32)
    levels = jnp.zeros((lag_rows, chans), jnp.float32)
    core = me & 1
    orders = chips(chan_count)
    groups = [partner(orders, place, core) for place in range(chip_count)]
    groups += [partner(orders, place, 1 - core) ^ 1 for place in range(chip_count)]
    fetch.wait()
    per_band = table_ref.shape[0] // chan_count
    chunks = [(me ^ k) * per_band + chunk for k in order for chunk in range(per_band)]
    table = jnp.concatenate(
        [
            jnp.concatenate([table_ref[chunk, side, me ^ group] for side in range(2) for group in groups], axis=0)
            for chunk in chunks
        ],
        axis=1,
    )
    turns = [chans - offset_of(number, offs_ref, chan_count // 2) * (chans // chan_count) for number in range(offset_count)]
    for row in range(0, freqs, step):
        own = [white_ref[part, row : row + step, :] for part in range(2)]
        own_real, own_imag = (value.astype(jnp.float32) for value in own)
        for number, turn in enumerate(turns):
            far_real, far_imag = (pltpu.roll(value, turn, 1).astype(jnp.float32) for value in own)
            real = own_real * far_real + own_imag * far_imag
            imag = own_imag * far_real - own_real * far_imag
            cross_ref[number, 0, row : row + step, :] = real.astype(jnp.bfloat16)
            cross_ref[number, 1, row : row + step, :] = imag.astype(jnp.bfloat16)

    for number, turn in enumerate(turns):
        if number % 2 == 0:
            taken = range(number, min(number + 2, offset_count))
            wide = jnp.concatenate([cross_ref[each, part] for each in taken for part in range(2)], axis=1)
            pair_sums = jnp.dot(table, wide, preferred_element_type=jnp.float32)
        sums = pair_sums[:, number % 2 * 2 * chans : (number % 2 + 1) * 2 * chans]
        cos_real, sin_real = sums[:half, :chans], sums[half:, :chans]
        cos_imag, sin_imag = sums[:half, chans:], sums[half:, chans:]
        corr = (
            (cos_real - sin_imag, sin_real + cos_imag),
            (cos_real + sin_imag, cos_imag - sin_real),
        )
        power = [real * real + imag * imag for real, imag in corr]
        mean_power = jnp.sum(power[0] + power[1], axis=0, keepdims=True) * (1.0 / (2 * half))
        extra = 0.25 * (mean_power + 1e-06 * freqs)
        peak = jnp.max(jnp.maximum(jnp.abs(corr[0][0]), jnp.abs(corr[1][0])), axis=0, keepdims=True)
        code = level_code(peak)
        keep = jnp.where(lane < turn, usable * pltpu.roll(usable, turn, 1), 0.0) * CODE_TOP
        upscale = keep / level_of(code)
        inverse = [lax.rsqrt(side + extra) * keep for side in power]
        kinds = [
            [real * upscale for real, _ in corr],
            [real * scale for (real, _), scale in zip(corr, inverse)],
            [imag * scale for (_, imag), scale in zip(corr, inverse)],
        ]
        if number == offset_count - 1:
            code = jnp.where(lane < chans // 2, code, pltpu.roll(code, chans // 2, 1))
            kinds = [[jnp.where(lane < chans // 2, ahead, pltpu.roll(back, chans // 2, 1))] for ahead, back in kinds]
        levels = jnp.where(line == number, code, levels)
        for place, value in enumerate(value for kind in kinds for value in kind):
            coded = encode(value).reshape(chan_count, lag_rows, chans)
            for core in range(2):
                rows = slice(core * chip_count, (core + 1) * chip_count)
                out_refs[core][:, 6 * number + place, :, :] = coded[rows]
    for number in range(offset_count):
        levels = jnp.where(line == offset_count + number, offs_ref[number].astype(jnp.float32), levels)
    wide = widest(offs_ref, chan_count // 2).astype(jnp.float32)
    levels = jnp.where(line == 2 * offset_count, wide, levels)
    for out_ref in out_refs:
        for chip in range(chip_count):
            out_ref[chip, blocks - 1, :, :] = encode(levels)


def merge_kernel(slots, own_ref, far_ref, *out_refs):
    blocks = own_ref.shape[1]
    for chip, out_ref in enumerate(out_refs):
        codes = [decode(ref[chip, blocks - 1]) for ref in (own_ref, far_ref)]
        levels = [level_of(code) for code in codes]
        code = level_code(levels[0] + levels[1])
        shares = [level / level_of(code) for level in levels]
        line = lax.broadcasted_iota(jnp.int32, code.shape, 0)
        out_ref[blocks - 1, :, :] = encode(jnp.where(line < slots, code, codes[0]))
        for block in range(blocks - 1):
            number, part = divmod(block, 6)
            linear = part < (2 if blocks - 1 - 6 * number > 3 else 1)
            own, far = decode(own_ref[chip, block]), decode(far_ref[chip, block])
            if linear:
                total = own * shares[0][number : number + 1, :] + far * shares[1][number : number + 1, :]
            else:
                total = (own + far) * 0.5
            out_ref[block, :, :] = encode(total)


def sum_kernel(orders, scale, where_ref, core_ref, *refs):
    count = len(orders[0])
    code_refs, out_refs, held_ref = refs[: -count - 1], refs[-count - 1 : -1], refs[-1]
    blocks, _, chans = code_refs[0].shape
    slots = held_ref.shape[0]
    heads = [decode(codes_ref[blocks - 1]) for codes_ref in code_refs]
    levels = [level_of(head) * scale for head in heads]
    offsets = [heads[0][slots + number : slots + number + 1, :] for number in range(slots)]
    wide = heads[0][2 * slots : 2 * slots + 1, :]
    low = lax.broadcasted_iota(jnp.int32, (1, chans), 1) < chans // 2
    all_sums = []
    for number in range(slots):
        sides = 2 if number < slots - 1 else 1
        own = [level[number : number + 1, :] for level in levels]
        sums = []
        for place in range(3 * sides):
            codes = [decode(codes_ref[6 * number + place]) for codes_ref in code_refs]
            if place < sides:
                sums.append(sum(code * level for code, level in zip(codes, own)))
            else:
                sums.append(sum(codes) * (1.0 / len(code_refs)))
        if sides == 1:
            sums = [
                jnp.where(low, side, 0.0) for value in sums for side in (value, pltpu.roll(value, chans // 2, 1))
            ]
        all_sums.append(sums)
    line = lax.broadcasted_iota(jnp.int32, levels[0].shape, 0)
    last = slots - 1
    for number in range(slots):
        sums = all_sums[number]
        for other in range(last) if number == last else [last]:
            swap = wide == min(number, other)
            sums = [jnp.where(swap, value, kept) for value, kept in zip(all_sums[other], sums)]
        peak = jnp.max(jnp.maximum(jnp.abs(sums[0]), jnp.abs(sums[1])), axis=0, keepdims=True)
        code = level_code(peak)
        upscale = CODE_TOP / level_of(code)
        head = jnp.where(line == 0, code, offsets[number])
        for part, value in enumerate([sums[0] * upscale, sums[1] * upscale, *sums[2:], head]):
            held_ref[number, part, :, :] = encode(value)
    for place, out_ref in enumerate(out_refs):
        out_ref[...] = held_ref[where_ref[0] ^ partner(orders, place, core_ref[0] & 1)]


def partners(count):
    return sorted(range(1, count), key=lambda k: (-(k >> 1).bit_count(), k & 1, k)) + [0]


def chips(count):
    near = [k for k in range(2, count, 2) if k.bit_count() == 1]
    far = [k for k in range(2, count, 2) if k.bit_count() > 1]
    return near[::-1] + far + [0], near + far + [0]


def planes(count):
    others = partners(count)[:-1]
    return others + [0], others[1:] + others[:1] + [0]


def partner(orders, place, core):
    return jnp.where(core == 0, orders[0][place], orders[1][place])


def exchange(pieces, orders, over_tm=False):
    chan_count, tm_count = lax.axis_size("chan"), lax.axis_size("tm")
    arrived = []
    for place, piece in enumerate(pieces):
        pairs = []
        for source in range(chan_count * tm_count):
            k = orders[source // tm_count % 2][place]
            pairs.append((source, source ^ k if over_tm else source ^ (k * tm_count)))
        moved = any(source != target for source, target in pairs)
        arrived.append(lax.ppermute(piece, ("chan", "tm"), pairs) if moved else piece)
    return arrived


def split_kernel(order, spec_ref, *refs):
    out_refs, sems = refs[:-1], refs[-1]
    me = lax.axis_index("chan").astype(jnp.int32)
    copies = [
        pltpu.make_async_copy(spec_ref.at[:, me ^ k], out_ref, sems.at[number])
        for number, (k, out_ref) in enumerate(zip(order, out_refs))
    ]
    for copy in copies:
        copy.start()
    for copy in copies:
        copy.wait()


def stack_kernel(windows, where_ref, *refs):
    sums_refs, out_ref = refs[:-1], refs[-1]
    blocks, copies, rows, _ = out_ref.shape
    _, lag_rows, chans = sums_refs[0].shape
    per_sum = windows // len(sums_refs)
    heads = [decode(sums_ref[6]) for sums_ref in sums_refs]
    levels = [level_of(head[0:1, :]) * (1.0 / (CODE_TOP * windows)) for head in heads]
    stacks = []
    for side in range(2):
        linear = sum(decode(sums_ref[side]) * level for sums_ref, level in zip(sums_refs, levels))
        real, imag = (
            sum(decode(sums_ref[part + side]) for sums_ref in sums_refs) * (per_sum / (CODE_TOP * windows))
            for part in (2, 4)
        )
        stacks.append(linear * (real * real + imag * imag))
    offset = heads[0][1:2, :]
    lane = lax.broadcasted_iota(jnp.int32, (1, chans), 1)
    behind = [jnp.zeros_like(stack) for stack in stacks]
    for steps in range(1, blocks // 2 + 1):
        ahead = steps * (chans // blocks)
        chosen = (offset == steps) & (lane >= ahead)
        behind = [jnp.where(chosen, pltpu.roll(stack, ahead, 1), kept) for stack, kept in zip(stacks, behind)]
    back = stacks[1] + behind[0]
    back = jnp.concatenate([back[row : row + 1, :] for row in reversed(range(lag_rows))], axis=0)
    me = where_ref[0]
    even = (me & 1) == 0
    ahead = stacks[0] + behind[1]
    both = jnp.concatenate([jnp.where(even, ahead, back), jnp.where(even, back, ahead)], axis=0)
    parts = chans // (2 * lag_rows)
    turned = jnp.concatenate([both] * parts, axis=0).T
    unit = lane // lag_rows
    part_of = jnp.where(((unit ^ me) & 1) == 0, unit - me, unit + me + 1) % blocks // 2
    per_block = chans // blocks
    for block in range(blocks):
        piece = jnp.zeros((rows, chans), jnp.float32)
        for part in range(parts):
            begin = block * per_block + part * rows
            piece = jnp.where(part_of == part, turned[begin : begin + rows, :], piece)
        for copy in range(copies):
            out_ref[block, copy, :, :] = piece


def place_kernel(parts_ref, out_ref):
    groups, offset_count, rows, lanes = parts_ref.shape
    half = out_ref.shape[2] // 2
    lag_rows = half // groups
    parts = out_ref.shape[0] // rows
    unit = lax.broadcasted_iota(jnp.int32, (1, lanes), 1) // lag_rows
    for number in range(offset_count):
        pieces = [parts_ref[group, number] for group in range(groups)]
        for part in range(parts):
            sides = [jnp.zeros((rows, lanes), jnp.float32)] * 2
            for group, piece in enumerate(pieces):
                places = ((groups - 1 - group + 2 * part) % groups, (group + 2 * part) % groups)
                sides = [jnp.where(unit == place, piece, side) for place, side in zip(places, sides)]
            for side, value in enumerate(sides):
                value = pltpu.roll(value, (lanes - 2 * part * lag_rows) % lanes, 1) if part else value
                out_ref[part * rows : (part + 1) * rows, number, side * half : (side + 1) * half] = value


def window_shards(spectra, quality, offsets):
    chan_count = lax.axis_size("chan")
    tm_count = lax.axis_size("tm")
    _, windows, band, chans = spectra.shape
    freqs = band * chan_count
    half = LAGS // 2
    lag_rows = half // chan_count
    offset_count = offsets.shape[0]
    piece_rows = 2 * lag_rows // chan_count
    smem = pl.BlockSpec(memory_space=pltpu.SMEM)
    vmem = pl.BlockSpec(memory_space=pltpu.VMEM)
    params = pltpu.CompilerParams(vmem_limit_bytes=VMEM_LIMIT)
    table = half_table(freqs, LAGS).reshape(2, chan_count, lag_rows, freqs // 128, 128)
    table = jnp.asarray(np.ascontiguousarray(table.transpose(3, 0, 1, 2, 4)))
    chan_index = lax.axis_index("chan").astype(jnp.int32)
    tm_index = lax.axis_index("tm").astype(jnp.int32)
    chan_where, tm_where = chan_index.reshape(1), tm_index.reshape(1)

    chan_order, tm_orders = partners(chan_count), planes(tm_count)
    kept = pl.BlockSpec(memory_space=pltpu.HBM)
    spectra = pltpu.with_memory_space_constraint(spectra, pltpu.HBM)
    pieces = []
    for part in (chan_order[:2], chan_order[2:]):
        pieces += pl.pallas_call(
            functools.partial(split_kernel, part),
            out_shape=[jax.ShapeDtypeStruct((2, band, chans), spectra.dtype)] * len(part),
            in_specs=[kept],
            out_specs=[pl.BlockSpec(memory_space=pl.ANY)] * len(part),
            scratch_shapes=[pltpu.SemaphoreType.DMA((len(part),))],
            compiler_params=params,
            name="split_windows",
        )(spectra)
    chip_count = chan_count // 2
    pair_shape = (6 * offset_count - 2, lag_rows, chans)
    own, far = pl.pallas_call(
        functools.partial(window_kernel, chan_order),
        out_shape=[jax.ShapeDtypeStruct((chip_count, *pair_shape), jnp.int16)] * 2,
        in_specs=[kept, smem] + [vmem] * (chan_count + 2),
        out_specs=[vmem] * 2,
        scratch_shapes=[
            pltpu.VMEM((2, freqs, chans), jnp.bfloat16),
            pltpu.VMEM((offset_count, 2, freqs, chans), jnp.bfloat16),
            pltpu.SMEM(offsets.shape, jnp.int32),
            pltpu.SemaphoreType.DMA(()),
        ],
        compiler_params=params,
        name="window_pairs",
    )(pltpu.with_memory_space_constraint(offsets, pltpu.HBM), chan_where, *exchange(pieces, (chan_order, chan_order)), quality, table)
    pairs = pl.pallas_call(
        functools.partial(merge_kernel, offset_count),
        out_shape=[jax.ShapeDtypeStruct(pair_shape, jnp.int16)] * chip_count,
        in_specs=[vmem] * 2,
        out_specs=[vmem] * chip_count,
        compiler_params=params,
        name="merge_windows",
    )(own, *exchange([far], ([1], [1])))
    sums = pl.pallas_call(
        functools.partial(sum_kernel, tm_orders, 1.0 / (CODE_TOP * math.sqrt(freqs))),
        out_shape=[jax.ShapeDtypeStruct((7, lag_rows, chans), jnp.int16)] * tm_count,
        in_specs=[smem, smem] + [vmem] * chip_count,
        out_specs=[vmem] * tm_count,
        scratch_shapes=[pltpu.VMEM((offset_count, 7, lag_rows, chans), jnp.int16)],
        compiler_params=params,
        name="sum_windows",
    )(tm_where, chan_where, *exchange(pairs, chips(chan_count)))
    pieces = pl.pallas_call(
        functools.partial(stack_kernel, windows * tm_count),
        out_shape=jax.ShapeDtypeStruct((chan_count, tm_count, piece_rows, chans), jnp.float32),
        in_specs=[smem] + [vmem] * tm_count,
        out_specs=vmem,
        compiler_params=params,
        name="stack_pairs",
    )(chan_where, *exchange(sums, tm_orders, over_tm=True))
    shape = (chan_count * tm_count, piece_rows, chans)
    arrived = lax.all_to_all(pieces.reshape(shape), ("chan", "tm"), 0, 0, tiled=True)
    return pl.pallas_call(
        place_kernel,
        out_shape=jax.ShapeDtypeStruct((CH_DEV, offset_count, LAGS), jnp.float32),
        in_specs=[vmem],
        out_specs=vmem,
        compiler_params=params,
        name="place_lags",
    )(arrived.reshape(chan_count, tm_count, piece_rows, chans))


def shifted(value, axis, steps):
    count = lax.axis_size(axis)
    leading, last = (max(0, -steps), min(count, count - steps))
    return lax.ppermute(value, axis, [(source, source + steps) for source in range(leading, last)])


def lag_table(freq_count, lag_count):
    freq_index = jnp.arange(freq_count, dtype=jnp.int32)[:, None]
    double_lag = (2 * jnp.arange(lag_count, dtype=jnp.int32) - lag_count + 1)[None, :]
    turns = jnp.mod(freq_index * double_lag, 4 * freq_count)
    angles = turns.astype(jnp.float32) * (2.0 * math.pi / (4 * freq_count))
    cosine = jnp.cos(angles)
    sine = jnp.sin(angles)
    upper = jnp.concatenate([cosine, sine], axis=1)
    lower = jnp.concatenate([-sine, cosine], axis=1)
    return jnp.stack([upper, lower]).astype(jnp.bfloat16)


def whiten_parts(real_part, imag_part, magnitude, channel_level, usable):
    factor = usable.astype(jnp.float32)[:, None, :] / (magnitude + 0.5 * (channel_level + 1e-05))
    return jnp.stack([real_part * factor, imag_part * factor]).astype(jnp.bfloat16)


def cross_parts(own_real, own_imag, far_real, far_imag):
    own_real = own_real.astype(jnp.float32)
    own_imag = own_imag.astype(jnp.float32)
    far_real = far_real.astype(jnp.float32)
    far_imag = far_imag.astype(jnp.float32)
    return jnp.stack(
        [own_real * far_real + own_imag * far_imag, own_imag * far_real - own_real * far_imag]
    ).astype(jnp.bfloat16)


def pair_terms(corr_all):
    lag_count = corr_all.shape[-1] // 2
    real_corr = corr_all[..., :lag_count]
    imag_corr = corr_all[..., lag_count:]
    power = real_corr * real_corr + imag_corr * imag_corr
    mean_power = jnp.mean(power, axis=-1, keepdims=True)
    denominator = jnp.sqrt(power + 0.25 * (mean_power + 1e-06))
    return (
        jnp.sum(real_corr, axis=-3),
        jnp.sum(real_corr / denominator, axis=-3),
        jnp.sum(imag_corr / denominator, axis=-3),
    )


def shards(spectra, quality, offsets):
    chan_count = lax.axis_size("chan")
    tm_count = lax.axis_size("tm")
    levels = chan_count.bit_length() - 1
    table_bf = lag_table(F, LAGS)
    inv_root = 1.0 / math.sqrt(F)
    real_part = spectra[0].astype(jnp.float32)
    imag_part = spectra[1].astype(jnp.float32)
    magnitude = jnp.sqrt(real_part * real_part + imag_part * imag_part)
    band_total = lax.psum(jnp.sum(magnitude, axis=1), "chan")
    channel_level = (band_total / F)[:, None, :]
    whitened = whiten_parts(real_part, imag_part, magnitude, channel_level, quality)
    width_all = whitened.shape[3]
    padded = jnp.pad(whitened, ((0, 0), (0, 0), (0, 0), (0, width_all)))
    crossed_list = []
    for offset_index in range(NOFF):
        partner = lax.dynamic_slice_in_dim(padded, offsets[offset_index] * CH_DEV, width_all, 3)
        crossed_list.append(cross_parts(whitened[0], whitened[1], partner[0], partner[1]))
    crossed = jnp.stack(crossed_list, axis=1)
    corr_all = jnp.einsum(
        "cnwfh,cfl->nwhl",
        lax.all_to_all(crossed, "chan", split_axis=4, concat_axis=3, tiled=True),
        table_bf,
        preferred_element_type=jnp.float32,
    )
    linear_sum, real_sum, imag_sum = pair_terms(corr_all * inv_root)
    totals = lax.psum((linear_sum, real_sum, imag_sum), "tm")
    window_count = W_DEV * tm_count
    linear = totals[0] / window_count
    real_phase = totals[1] / window_count
    imag_phase = totals[2] / window_count
    stacks = jnp.transpose(linear * (real_phase * real_phase + imag_phase * imag_phase), (1, 0, 2))
    reverse_part = stacks
    for bit_index in range(levels):
        step_size = 1 << bit_index
        arrived = shifted(reverse_part, "chan", step_size)
        chosen = offsets // step_size % 2 == 1
        reverse_part = jnp.where(chosen[None, :, None], arrived, reverse_part)
    return stacks + jnp.flip(reverse_part, axis=2)


def solution(mesh):
    chan_count, tm_count = mesh.shape["chan"], mesh.shape["tm"]
    by_window = chan_count == W_DEV and tm_count == NOFF
    return jax.shard_map(
        window_shards if by_window else shards,
        mesh=mesh,
        in_specs=(P(None, "tm", "chan", None), P("tm", None), P()),
        out_specs=P("chan", None, None),
        check_vma=False,
    )
```

```python
import functools
import math

import jax
import jax.numpy as jnp
import numpy as np
from jax import lax
from jax.experimental import pallas as pl
from jax.experimental.pallas import tpu as pltpu
from jax.sharding import PartitionSpec as P

F = 2048
LAGS = 256
NOFF = 4
CH_DEV = 16
W_DEV = 8
VMEM_LIMIT = 48 * 1024 * 1024
CODE_TOP = 32767.0
OCTAVE = 256.0
LOWEST = -110.0


def encode(value):
    return jnp.round(value).astype(jnp.int32).astype(jnp.int16)


def decode(code):
    return code.astype(jnp.int32).astype(jnp.float32)


def level_code(peak):
    return jnp.ceil(jnp.maximum(jnp.log2(jnp.maximum(peak, 1e-30)), LOWEST) * OCTAVE) + 1.0


def level_of(code):
    return jnp.exp2(code * (1.0 / OCTAVE))


def half_table(freq_count, lag_count):
    freq_index = np.arange(freq_count, dtype=np.int64)[None, :]
    double_lag = (2 * np.arange(lag_count // 2, lag_count, dtype=np.int64) - lag_count + 1)[:, None]
    turns = np.mod(freq_index * double_lag, 4 * freq_count).astype(np.float32)
    angles = turns * np.float32(2.0 * math.pi / (4 * freq_count))
    return np.concatenate([np.cos(angles), np.sin(angles)]).astype(jnp.bfloat16)


def widest(offs_ref, reach):
    last = offs_ref.shape[0] - 1
    found = last
    for number in reversed(range(last)):
        found = jnp.where(offs_ref[number] == reach, number, found)
    return found


def offset_of(slot, offs_ref, reach):
    last, wide = offs_ref.shape[0] - 1, widest(offs_ref, reach)
    return offs_ref[jnp.where(slot == wide, last, jnp.where(slot == last, wide, slot))]


def window_kernel(order, offs_hbm_ref, where_ref, *refs):
    chan_count = len(order)
    spec_refs, (qual_ref, table_ref) = refs[:chan_count], refs[chan_count : chan_count + 2]
    out_refs = refs[chan_count + 2 : chan_count + 6]
    mag_ref, white_ref, cross_ref, offs_ref, offs_sem = refs[chan_count + 6 :]
    fetch = pltpu.make_async_copy(offs_hbm_ref, offs_ref, offs_sem)
    fetch.start()
    me = where_ref[0]
    _, band, chans = spec_refs[0].shape
    freqs = chan_count * band
    chip_count = chan_count // 2
    _, blocks, lag_rows, _ = out_refs[0].shape
    offset_count = offs_ref.shape[0]
    half = chan_count * lag_rows
    step = 64

    total = jnp.zeros((8, chans), jnp.float32)
    for number, spec_ref in enumerate(spec_refs):
        for row in range(0, band, step):
            real, imag = (spec_ref[part, row : row + step, :].astype(jnp.float32) for part in range(2))
            square = real * real + imag * imag
            magnitude = square * lax.rsqrt(jnp.maximum(square, 1e-30))
            held = slice(number * band + row, number * band + row + step)
            mag_ref[held, :] = magnitude
            total += jnp.sum(magnitude.reshape(step // 8, 8, chans), axis=0)
    level = jnp.sum(total, axis=0, keepdims=True) * (1.0 / freqs)
    floor = 0.5 * (level + 1e-05)

    for number, spec_ref in enumerate(spec_refs):
        for row in range(0, band, step):
            held = slice(number * band + row, number * band + row + step)
            factor = pl.reciprocal(mag_ref[held, :] + floor, approx=True)
            for part in range(2):
                value = spec_ref[part, row : row + step, :].astype(jnp.float32) * factor
                white_ref[part, held, :] = value.astype(jnp.bfloat16)

    lane = lax.broadcasted_iota(jnp.int32, (1, chans), 1)
    line = lax.broadcasted_iota(jnp.int32, (lag_rows, chans), 0)
    usable = qual_ref[pl.ds(me, 1), :].astype(jnp.float32)
    levels = jnp.zeros((lag_rows, chans), jnp.float32)
    core = me & 1
    orders = chips(chan_count)
    groups = [partner(orders, place, core) for place in range(chip_count)]
    groups += [partner(orders, place, 1 - core) ^ 1 for place in range(chip_count)]
    fetch.wait()
    per_band = table_ref.shape[0] // chan_count
    chunks = [(me ^ k) * per_band + chunk for k in order for chunk in range(per_band)]
    table = jnp.concatenate(
        [
            jnp.concatenate([table_ref[chunk, side, me ^ group] for side in range(2) for group in groups], axis=0)
            for chunk in chunks
        ],
        axis=1,
    )
    turns = [chans - offset_of(number, offs_ref, chan_count // 2) * (chans // chan_count) for number in range(offset_count)]
    for row in range(0, freqs, step):
        own = [white_ref[part, row : row + step, :] for part in range(2)]
        own_real, own_imag = (value.astype(jnp.float32) for value in own)
        for number, turn in enumerate(turns):
            far_real, far_imag = (pltpu.roll(value, turn, 1).astype(jnp.float32) for value in own)
            real = own_real * far_real + own_imag * far_imag
            imag = own_imag * far_real - own_real * far_imag
            cross_ref[number, 0, row : row + step, :] = real.astype(jnp.bfloat16)
            cross_ref[number, 1, row : row + step, :] = imag.astype(jnp.bfloat16)

    for number, turn in enumerate(turns):
        if number % 2 == 0:
            taken = range(number, min(number + 2, offset_count))
            wide = jnp.concatenate([cross_ref[each, part] for each in taken for part in range(2)], axis=1)
            pair_sums = jnp.dot(table, wide, preferred_element_type=jnp.float32)
        sums = pair_sums[:, number % 2 * 2 * chans : (number % 2 + 1) * 2 * chans]
        cos_real, sin_real = sums[:half, :chans], sums[half:, :chans]
        cos_imag, sin_imag = sums[:half, chans:], sums[half:, chans:]
        corr = (
            (cos_real - sin_imag, sin_real + cos_imag),
            (cos_real + sin_imag, cos_imag - sin_real),
        )
        power = [real * real + imag * imag for real, imag in corr]
        mean_power = jnp.sum(power[0] + power[1], axis=0, keepdims=True) * (1.0 / (2 * half))
        extra = 0.25 * (mean_power + 1e-06 * freqs)
        peak = jnp.max(jnp.maximum(jnp.abs(corr[0][0]), jnp.abs(corr[1][0])), axis=0, keepdims=True)
        code = level_code(peak)
        keep = jnp.where(lane < turn, usable * pltpu.roll(usable, turn, 1), 0.0) * CODE_TOP
        upscale = keep / level_of(code)
        inverse = [lax.rsqrt(side + extra) * keep for side in power]
        kinds = [
            [real * upscale for real, _ in corr],
            [real * scale for (real, _), scale in zip(corr, inverse)],
            [imag * scale for (_, imag), scale in zip(corr, inverse)],
        ]
        if number == offset_count - 1:
            code = jnp.where(lane < chans // 2, code, pltpu.roll(code, chans // 2, 1))
            kinds = [[jnp.where(lane < chans // 2, ahead, pltpu.roll(back, chans // 2, 1))] for ahead, back in kinds]
        levels = jnp.where(line == number, code, levels)
        for place, value in enumerate(value for kind in kinds for value in kind):
            coded = encode(value).reshape(chan_count, lag_rows, chans)
            begin = 0
            for out_ref in out_refs:
                out_ref[:, 6 * number + place, :, :] = coded[begin : begin + out_ref.shape[0]]
                begin += out_ref.shape[0]
    for number in range(offset_count):
        levels = jnp.where(line == offset_count + number, offs_ref[number].astype(jnp.float32), levels)
    wide = widest(offs_ref, chan_count // 2).astype(jnp.float32)
    levels = jnp.where(line == 2 * offset_count, wide, levels)
    for out_ref in out_refs:
        for chip in range(out_ref.shape[0]):
            out_ref[chip, blocks - 1, :, :] = encode(levels)


def merge_kernel(slots, own_ref, far_ref, *out_refs):
    blocks = own_ref.shape[1]
    for chip, out_ref in enumerate(out_refs):
        codes = [decode(ref[chip, blocks - 1]) for ref in (own_ref, far_ref)]
        levels = [level_of(code) for code in codes]
        code = level_code(levels[0] + levels[1])
        shares = [level / level_of(code) for level in levels]
        line = lax.broadcasted_iota(jnp.int32, code.shape, 0)
        out_ref[blocks - 1, :, :] = encode(jnp.where(line < slots, code, codes[0]))
        for block in range(blocks - 1):
            number, part = divmod(block, 6)
            linear = part < (2 if blocks - 1 - 6 * number > 3 else 1)
            own, far = decode(own_ref[chip, block]), decode(far_ref[chip, block])
            if linear:
                total = own * shares[0][number : number + 1, :] + far * shares[1][number : number + 1, :]
            else:
                total = (own + far) * 0.5
            out_ref[block, :, :] = encode(total)


def sum_kernel(orders, scale, where_ref, core_ref, *refs):
    count = len(orders[0])
    code_refs, out_refs, held_ref = refs[: -count - 1], refs[-count - 1 : -1], refs[-1]
    blocks, _, chans = code_refs[0].shape
    slots = held_ref.shape[0]
    heads = [decode(codes_ref[blocks - 1]) for codes_ref in code_refs]
    levels = [level_of(head) * scale for head in heads]
    offsets = [heads[0][slots + number : slots + number + 1, :] for number in range(slots)]
    wide = heads[0][2 * slots : 2 * slots + 1, :]
    low = lax.broadcasted_iota(jnp.int32, (1, chans), 1) < chans // 2
    all_sums = []
    for number in range(slots):
        sides = 2 if number < slots - 1 else 1
        own = [level[number : number + 1, :] for level in levels]
        sums = []
        for place in range(3 * sides):
            codes = [decode(codes_ref[6 * number + place]) for codes_ref in code_refs]
            if place < sides:
                sums.append(sum(code * level for code, level in zip(codes, own)))
            else:
                sums.append(sum(codes) * (1.0 / len(code_refs)))
        if sides == 1:
            sums = [
                jnp.where(low, side, 0.0) for value in sums for side in (value, pltpu.roll(value, chans // 2, 1))
            ]
        all_sums.append(sums)
    line = lax.broadcasted_iota(jnp.int32, levels[0].shape, 0)
    last = slots - 1
    for number in range(slots):
        sums = all_sums[number]
        for other in range(last) if number == last else [last]:
            swap = wide == min(number, other)
            sums = [jnp.where(swap, value, kept) for value, kept in zip(all_sums[other], sums)]
        peak = jnp.max(jnp.maximum(jnp.abs(sums[0]), jnp.abs(sums[1])), axis=0, keepdims=True)
        code = level_code(peak)
        upscale = CODE_TOP / level_of(code)
        head = jnp.where(line == 0, code, offsets[number])
        for part, value in enumerate([sums[0] * upscale, sums[1] * upscale, *sums[2:], head]):
            held_ref[number, part, :, :] = encode(value)
    for place, out_ref in enumerate(out_refs):
        out_ref[...] = held_ref[where_ref[0] ^ partner(orders, place, core_ref[0] & 1)]


def partners(count):
    return sorted(range(1, count), key=lambda k: (-(k >> 1).bit_count(), k & 1, k)) + [0]


def chips(count):
    near = [k for k in range(2, count, 2) if k.bit_count() == 1]
    far = [k for k in range(2, count, 2) if k.bit_count() > 1]
    return near[::-1] + far + [0], near + far + [0]


def planes(count):
    others = partners(count)[:-1]
    return others + [0], others[1:] + others[:1] + [0]


def partner(orders, place, core):
    return jnp.where(core == 0, orders[0][place], orders[1][place])


def exchange(pieces, orders, over_tm=False):
    chan_count, tm_count = lax.axis_size("chan"), lax.axis_size("tm")
    arrived = []
    for place, piece in enumerate(pieces):
        pairs = []
        for source in range(chan_count * tm_count):
            k = orders[source // tm_count % 2][place]
            pairs.append((source, source ^ k if over_tm else source ^ (k * tm_count)))
        moved = any(source != target for source, target in pairs)
        arrived.append(lax.ppermute(piece, ("chan", "tm"), pairs) if moved else piece)
    return arrived


def split_kernel(order, spec_ref, *refs):
    out_refs, sems = refs[:-1], refs[-1]
    me = lax.axis_index("chan").astype(jnp.int32)
    copies = [
        pltpu.make_async_copy(spec_ref.at[:, me ^ k], out_ref, sems.at[number])
        for number, (k, out_ref) in enumerate(zip(order, out_refs))
    ]
    for copy in copies:
        copy.start()
    for copy in copies:
        copy.wait()


def stack_kernel(windows, where_ref, *refs):
    sums_refs, out_ref = refs[:-1], refs[-1]
    blocks, copies, rows, _ = out_ref.shape
    _, lag_rows, chans = sums_refs[0].shape
    per_sum = windows // len(sums_refs)
    heads = [decode(sums_ref[6]) for sums_ref in sums_refs]
    levels = [level_of(head[0:1, :]) * (1.0 / (CODE_TOP * windows)) for head in heads]
    stacks = []
    for side in range(2):
        linear = sum(decode(sums_ref[side]) * level for sums_ref, level in zip(sums_refs, levels))
        real, imag = (
            sum(decode(sums_ref[part + side]) for sums_ref in sums_refs) * (per_sum / (CODE_TOP * windows))
            for part in (2, 4)
        )
        stacks.append(linear * (real * real + imag * imag))
    offset = heads[0][1:2, :]
    lane = lax.broadcasted_iota(jnp.int32, (1, chans), 1)
    behind = [jnp.zeros_like(stack) for stack in stacks]
    for steps in range(1, blocks // 2 + 1):
        ahead = steps * (chans // blocks)
        chosen = (offset == steps) & (lane >= ahead)
        behind = [jnp.where(chosen, pltpu.roll(stack, ahead, 1), kept) for stack, kept in zip(stacks, behind)]
    back = stacks[1] + behind[0]
    back = jnp.concatenate([back[row : row + 1, :] for row in reversed(range(lag_rows))], axis=0)
    me = where_ref[0]
    even = (me & 1) == 0
    ahead = stacks[0] + behind[1]
    both = jnp.concatenate([jnp.where(even, ahead, back), jnp.where(even, back, ahead)], axis=0)
    parts = chans // (2 * lag_rows)
    turned = jnp.concatenate([both] * parts, axis=0).T
    unit = lane // lag_rows
    part_of = jnp.where(((unit ^ me) & 1) == 0, unit - me, unit + me + 1) % blocks // 2
    per_block = chans // blocks
    for block in range(blocks):
        piece = jnp.zeros((rows, chans), jnp.float32)
        for part in range(parts):
            begin = block * per_block + part * rows
            piece = jnp.where(part_of == part, turned[begin : begin + rows, :], piece)
        for copy in range(copies):
            out_ref[block, copy, :, :] = piece


def place_kernel(parts_ref, out_ref):
    groups, offset_count, rows, lanes = parts_ref.shape
    half = out_ref.shape[2] // 2
    lag_rows = half // groups
    parts = out_ref.shape[0] // rows
    unit = lax.broadcasted_iota(jnp.int32, (1, lanes), 1) // lag_rows
    for number in range(offset_count):
        pieces = [parts_ref[group, number] for group in range(groups)]
        for part in range(parts):
            sides = [jnp.zeros((rows, lanes), jnp.float32)] * 2
            for group, piece in enumerate(pieces):
                places = ((groups - 1 - group + 2 * part) % groups, (group + 2 * part) % groups)
                sides = [jnp.where(unit == place, piece, side) for place, side in zip(places, sides)]
            for side, value in enumerate(sides):
                value = pltpu.roll(value, (lanes - 2 * part * lag_rows) % lanes, 1) if part else value
                out_ref[part * rows : (part + 1) * rows, number, side * half : (side + 1) * half] = value


def window_shards(spectra, quality, offsets):
    chan_count = lax.axis_size("chan")
    tm_count = lax.axis_size("tm")
    _, windows, band, chans = spectra.shape
    freqs = band * chan_count
    half = LAGS // 2
    lag_rows = half // chan_count
    offset_count = offsets.shape[0]
    piece_rows = 2 * lag_rows // chan_count
    smem = pl.BlockSpec(memory_space=pltpu.SMEM)
    vmem = pl.BlockSpec(memory_space=pltpu.VMEM)
    params = pltpu.CompilerParams(vmem_limit_bytes=VMEM_LIMIT)
    table = half_table(freqs, LAGS).reshape(2, chan_count, lag_rows, freqs // 128, 128)
    table = jnp.asarray(np.ascontiguousarray(table.transpose(3, 0, 1, 2, 4)))
    chan_index = lax.axis_index("chan").astype(jnp.int32)
    tm_index = lax.axis_index("tm").astype(jnp.int32)
    chan_where, tm_where = chan_index.reshape(1), tm_index.reshape(1)

    chan_order, tm_orders = partners(chan_count), planes(tm_count)
    kept = pl.BlockSpec(memory_space=pltpu.HBM)
    spectra = pltpu.with_memory_space_constraint(spectra, pltpu.HBM)
    pieces = []
    for part in (chan_order[:2], chan_order[2:]):
        pieces += pl.pallas_call(
            functools.partial(split_kernel, part),
            out_shape=[jax.ShapeDtypeStruct((2, band, chans), spectra.dtype)] * len(part),
            in_specs=[kept],
            out_specs=[pl.BlockSpec(memory_space=pl.ANY)] * len(part),
            scratch_shapes=[pltpu.SemaphoreType.DMA((len(part),))],
            compiler_params=params,
            name="split_windows",
        )(spectra)
    chip_count = chan_count // 2
    pair_shape = (6 * offset_count - 2, lag_rows, chans)
    first_half, second_half, *far = pl.pallas_call(
        functools.partial(window_kernel, chan_order),
        out_shape=[jax.ShapeDtypeStruct((chip_count // 2, *pair_shape), jnp.int16)] * 4,
        in_specs=[kept, smem] + [vmem] * (chan_count + 2),
        out_specs=[vmem] * 4,
        scratch_shapes=[
            pltpu.VMEM((freqs, chans), jnp.float32),
            pltpu.VMEM((2, freqs, chans), jnp.bfloat16),
            pltpu.VMEM((offset_count, 2, freqs, chans), jnp.bfloat16),
            pltpu.SMEM(offsets.shape, jnp.int32),
            pltpu.SemaphoreType.DMA(()),
        ],
        compiler_params=params,
        name="window_pairs",
    )(pltpu.with_memory_space_constraint(offsets, pltpu.HBM), chan_where, *exchange(pieces, (chan_order, chan_order)), quality, table)
    pairs = []
    for own, other in zip((first_half, second_half), exchange(far, ([1, 1], [1, 1]))):
        pairs += pl.pallas_call(
            functools.partial(merge_kernel, offset_count),
            out_shape=[jax.ShapeDtypeStruct(pair_shape, jnp.int16)] * (chip_count // 2),
            in_specs=[vmem] * 2,
            out_specs=[vmem] * (chip_count // 2),
            compiler_params=params,
            name="merge_windows",
        )(own, other)
    sums = pl.pallas_call(
        functools.partial(sum_kernel, tm_orders, 1.0 / (CODE_TOP * math.sqrt(freqs))),
        out_shape=[jax.ShapeDtypeStruct((7, lag_rows, chans), jnp.int16)] * tm_count,
        in_specs=[smem, smem] + [vmem] * chip_count,
        out_specs=[vmem] * tm_count,
        scratch_shapes=[pltpu.VMEM((offset_count, 7, lag_rows, chans), jnp.int16)],
        compiler_params=params,
        name="sum_windows",
    )(tm_where, chan_where, *exchange(pairs, chips(chan_count)))
    pieces = pl.pallas_call(
        functools.partial(stack_kernel, windows * tm_count),
        out_shape=jax.ShapeDtypeStruct((chan_count, tm_count, piece_rows, chans), jnp.float32),
        in_specs=[smem] + [vmem] * tm_count,
        out_specs=vmem,
        compiler_params=params,
        name="stack_pairs",
    )(chan_where, *exchange(sums, tm_orders, over_tm=True))
    shape = (chan_count * tm_count, piece_rows, chans)
    arrived = lax.all_to_all(pieces.reshape(shape), ("chan", "tm"), 0, 0, tiled=True)
    return pl.pallas_call(
        place_kernel,
        out_shape=jax.ShapeDtypeStruct((CH_DEV, offset_count, LAGS), jnp.float32),
        in_specs=[vmem],
        out_specs=vmem,
        compiler_params=params,
        name="place_lags",
    )(arrived.reshape(chan_count, tm_count, piece_rows, chans))


def shifted(value, axis, steps):
    count = lax.axis_size(axis)
    leading, last = (max(0, -steps), min(count, count - steps))
    return lax.ppermute(value, axis, [(source, source + steps) for source in range(leading, last)])


def lag_table(freq_count, lag_count):
    freq_index = jnp.arange(freq_count, dtype=jnp.int32)[:, None]
    double_lag = (2 * jnp.arange(lag_count, dtype=jnp.int32) - lag_count + 1)[None, :]
    turns = jnp.mod(freq_index * double_lag, 4 * freq_count)
    angles = turns.astype(jnp.float32) * (2.0 * math.pi / (4 * freq_count))
    cosine = jnp.cos(angles)
    sine = jnp.sin(angles)
    upper = jnp.concatenate([cosine, sine], axis=1)
    lower = jnp.concatenate([-sine, cosine], axis=1)
    return jnp.stack([upper, lower]).astype(jnp.bfloat16)


def whiten_parts(real_part, imag_part, magnitude, channel_level, usable):
    factor = usable.astype(jnp.float32)[:, None, :] / (magnitude + 0.5 * (channel_level + 1e-05))
    return jnp.stack([real_part * factor, imag_part * factor]).astype(jnp.bfloat16)


def cross_parts(own_real, own_imag, far_real, far_imag):
    own_real = own_real.astype(jnp.float32)
    own_imag = own_imag.astype(jnp.float32)
    far_real = far_real.astype(jnp.float32)
    far_imag = far_imag.astype(jnp.float32)
    return jnp.stack(
        [own_real * far_real + own_imag * far_imag, own_imag * far_real - own_real * far_imag]
    ).astype(jnp.bfloat16)


def pair_terms(corr_all):
    lag_count = corr_all.shape[-1] // 2
    real_corr = corr_all[..., :lag_count]
    imag_corr = corr_all[..., lag_count:]
    power = real_corr * real_corr + imag_corr * imag_corr
    mean_power = jnp.mean(power, axis=-1, keepdims=True)
    denominator = jnp.sqrt(power + 0.25 * (mean_power + 1e-06))
    return (
        jnp.sum(real_corr, axis=-3),
        jnp.sum(real_corr / denominator, axis=-3),
        jnp.sum(imag_corr / denominator, axis=-3),
    )


def shards(spectra, quality, offsets):
    chan_count = lax.axis_size("chan")
    tm_count = lax.axis_size("tm")
    levels = chan_count.bit_length() - 1
    table_bf = lag_table(F, LAGS)
    inv_root = 1.0 / math.sqrt(F)
    real_part = spectra[0].astype(jnp.float32)
    imag_part = spectra[1].astype(jnp.float32)
    magnitude = jnp.sqrt(real_part * real_part + imag_part * imag_part)
    band_total = lax.psum(jnp.sum(magnitude, axis=1), "chan")
    channel_level = (band_total / F)[:, None, :]
    whitened = whiten_parts(real_part, imag_part, magnitude, channel_level, quality)
    width_all = whitened.shape[3]
    padded = jnp.pad(whitened, ((0, 0), (0, 0), (0, 0), (0, width_all)))
    crossed_list = []
    for offset_index in range(NOFF):
        partner = lax.dynamic_slice_in_dim(padded, offsets[offset_index] * CH_DEV, width_all, 3)
        crossed_list.append(cross_parts(whitened[0], whitened[1], partner[0], partner[1]))
    crossed = jnp.stack(crossed_list, axis=1)
    corr_all = jnp.einsum(
        "cnwfh,cfl->nwhl",
        lax.all_to_all(crossed, "chan", split_axis=4, concat_axis=3, tiled=True),
        table_bf,
        preferred_element_type=jnp.float32,
    )
    linear_sum, real_sum, imag_sum = pair_terms(corr_all * inv_root)
    totals = lax.psum((linear_sum, real_sum, imag_sum), "tm")
    window_count = W_DEV * tm_count
    linear = totals[0] / window_count
    real_phase = totals[1] / window_count
    imag_phase = totals[2] / window_count
    stacks = jnp.transpose(linear * (real_phase * real_phase + imag_phase * imag_phase), (1, 0, 2))
    reverse_part = stacks
    for bit_index in range(levels):
        step_size = 1 << bit_index
        arrived = shifted(reverse_part, "chan", step_size)
        chosen = offsets // step_size % 2 == 1
        reverse_part = jnp.where(chosen[None, :, None], arrived, reverse_part)
    return stacks + jnp.flip(reverse_part, axis=2)


def solution(mesh):
    chan_count, tm_count = mesh.shape["chan"], mesh.shape["tm"]
    by_window = chan_count == W_DEV and tm_count == NOFF
    return jax.shard_map(
        window_shards if by_window else shards,
        mesh=mesh,
        in_specs=(P(None, "tm", "chan", None), P("tm", None), P()),
        out_specs=P("chan", None, None),
        check_vma=False,
    )
```
